32 devices in a mesh: gx: 4 (over x, core), gy: 2 (over y), gz: 4 (over z).
Axes of the slice: x: 2, y: 2, z: 4, core: 2. Of those that a mesh axis runs over, the one named last changes fastest.
Arguments:
- adjoint: float32 [19, 32, 32, 512], P(None, 'gx', 'gy', 'gz'), may hold values from -6 to 6
- density: float32 [2, 32, 32, 512], P(None, 'gx', 'gy', 'gz'), may hold values from 0.8 to 1.2
- velocity: float32 [2, 3, 32, 32, 512], P(None, None, 'gx', 'gy', 'gz'), may hold values from -0.25 to 0.25
- pore_mask: int32 [32, 32, 512], P('gx', 'gy', 'gz'), may hold values from 0 to 1, as said below
Outputs:
- adjoint_out: float32 [19, 32, 32, 512], P(None, 'gx', 'gy', 'gz')
- sensitivity: float32 [32, 32, 512], P('gx', 'gy', 'gz')
The draws below stay inside these ranges and needn't reach their ends.
Inputs may be any that keep to these rules, and one draw needn't show every extreme that they name: `pore_mask`: 1 marks a pore voxel and 0 a solid one.
All inputs are finite; a program needn't handle non-finite values.
Results may differ from the reference program's by a relative error of at most 0.00002.
Values sent between devices are 32-bit elements; how exact they have to be, the bound alone decides.
No kernel may reach another device: no remote copies, remote signals or barrier semaphores. Data moves between devices by JAX's collectives and lax.ppermute only.
A program may use at most 128 MiB of HBM per device.

```python
import jax
import jax.numpy as jnp

CX = 8
CY = 16
CZ = 128
NX = 32
NY = 32
NZ = 512


def draw_pore_mask(key, part):
    first, second = jax.random.split(jax.random.fold_in(key, 7))
    levels = jax.random.randint(first, (NX // CX, NY // CY, NZ // CZ), 15, 96)
    levels = jnp.repeat(jnp.repeat(jnp.repeat(levels, CX, axis=0), CY, axis=1), CZ, axis=2)
    ticket = jax.random.randint(second, (NX, NY, NZ), 0, 100)
    return jnp.where(ticket < levels, 1, 0).astype(jnp.int32)


def block_levels(key, dims, cuts, low, top_value):
    def one(axis_at, parts):
        draws = jax.random.uniform(jax.random.fold_in(jax.random.fold_in(key, 6), axis_at), (parts,), jnp.float32, low / len(cuts), top_value / len(cuts))
        return jnp.repeat(jnp.exp(draws), dims[axis_at] // parts).reshape((-1,) + (1,) * (len(dims) - axis_at - 1))

    gain = one(*cuts[0])
    for cut in cuts[1:]:
        gain = gain * one(*cut)
    return gain


def bell_draw(rng, extent, scale, limit, shards=(), kind=jnp.bfloat16):
    factor_of = block_levels(rng, extent, shards, -0.22, 0.18) if shards else 1.0
    drawn = jax.random.normal(rng, extent, jnp.float32) * scale * factor_of
    return jnp.minimum(jnp.maximum(drawn, -limit), limit).astype(kind)


def setup_inputs(seed: int = 0) -> dict:
    key_of = jax.random.split(jax.random.key(seed), 5)
    adjoint = bell_draw(key_of[0], (19, NX, NY, NZ), 1.0, 6.0, ((1, 4), (2, 2), (3, 4)), jnp.float32)
    density = jnp.clip(0.8 + 0.40000004 * jax.random.uniform(key_of[1], (2, NX, NY, NZ), jnp.float32) ** block_levels(key_of[1], (2, NX, NY, NZ), ((1, 4), (2, 2), (3, 4)), -0.2, 0.2), 0.8, 1.2)
    velocity = bell_draw(key_of[2], (2, 3, NX, NY, NZ), 0.05, 0.25, ((2, 4), (3, 2), (4, 4)), jnp.float32)
    pore_mask = draw_pore_mask(jax.random.fold_in(key_of[4], 71), 0)
    return dict(adjoint=adjoint, density=density, velocity=velocity, pore_mask=pore_mask)


VELOCITIES = [(0, 0, 0), (1, 0, 0), (-1, 0, 0), (0, 1, 0), (0, -1, 0), (0, 0, 1), (0, 0, -1),
              (1, 1, 0), (-1, -1, 0), (1, -1, 0), (-1, 1, 0), (1, 0, 1), (-1, 0, -1),
              (1, 0, -1), (-1, 0, 1), (0, 1, 1), (0, -1, -1), (0, 1, -1), (0, -1, 1)]
WEIGHTS = [1.0 / 3.0] + [1.0 / 18.0] * 6 + [1.0 / 36.0] * 12
OPPOSITE = [0, 2, 1, 4, 3, 6, 5, 8, 7, 10, 9, 12, 11, 14, 13, 16, 15, 18, 17]
OMEGA = 1.25


def collide(pulled, rho, speed, pores):
    ux, uy, uz = speed[0], speed[1], speed[2]
    usq = ux * ux + uy * uy + uz * uz
    shapes = []
    moment = jnp.zeros_like(rho)
    vec_x = jnp.zeros_like(rho)
    vec_y = jnp.zeros_like(rho)
    vec_z = jnp.zeros_like(rho)
    for index in range(19):
        cx, cy, cz = VELOCITIES[index]
        weight = WEIGHTS[index]
        along = cx * ux + cy * uy + cz * uz
        shaped = weight * (1.0 + 3.0 * along + 4.5 * along * along - 1.5 * usq)
        shapes.append(shaped)
        moment = moment + pulled[index] * shaped
        common = pulled[index] * weight
        vec_x = vec_x + common * (3.0 * cx + 9.0 * along * cx - 3.0 * ux)
        vec_y = vec_y + common * (3.0 * cy + 9.0 * along * cy - 3.0 * uy)
        vec_z = vec_z + common * (3.0 * cz + 9.0 * along * cz - 3.0 * uz)
    fluid = pores > 0
    layers = []
    change = jnp.zeros_like(rho)
    for index in range(19):
        cx, cy, cz = VELOCITIES[index]
        project = vec_x * (cx - ux) + vec_y * (cy - uy) + vec_z * (cz - uz)
        collided = (1.0 - OMEGA) * pulled[index] + OMEGA * (moment + project) + (cx - ux) / rho
        layers.append(jnp.where(fluid, collided, pulled[OPPOSITE[index]]))
        change = change + (pulled[OPPOSITE[index]] - pulled[index]) * rho * shapes[index]
    return jnp.stack(layers), jnp.where(fluid, change, 0.0)


def reference(adjoint, density, velocity, pore_mask):
    field = adjoint
    total = jnp.zeros(pore_mask.shape, jnp.float32)
    ext_x, ext_y, ext_z = pore_mask.shape
    for level in (1, 0):
        padded = jnp.pad(field, ((0, 0), (1, 1), (1, 1), (1, 1)))
        pulled = jnp.stack([padded[index, 1 + VELOCITIES[index][0]:1 + VELOCITIES[index][0] + ext_x,
                                   1 + VELOCITIES[index][1]:1 + VELOCITIES[index][1] + ext_y,
                                   1 + VELOCITIES[index][2]:1 + VELOCITIES[index][2] + ext_z] for index in range(19)])
        field, change = collide(pulled, density[level], velocity[level], pore_mask)
        total = total + change
    return field, total
```

```python
import functools

import jax
import jax.numpy as jnp
from jax import lax
from jax.experimental import pallas as pl
from jax.experimental.pallas import tpu as pltpu
from jax.sharding import PartitionSpec as P

VELOCITIES = [
    (0, 0, 0),
    (1, 0, 0),
    (-1, 0, 0),
    (0, 1, 0),
    (0, -1, 0),
    (0, 0, 1),
    (0, 0, -1),
    (1, 1, 0),
    (-1, -1, 0),
    (1, -1, 0),
    (-1, 1, 0),
    (1, 0, 1),
    (-1, 0, -1),
    (1, 0, -1),
    (-1, 0, 1),
    (0, 1, 1),
    (0, -1, -1),
    (0, 1, -1),
    (0, -1, 1),
]
OPPOSITE = [0, 2, 1, 4, 3, 6, 5, 8, 7, 10, 9, 12, 11, 14, 13, 16, 15, 18, 17]
OMEGA = 1.25
LANES = 128
GROUP = 16


def pops(axis, sign):
    return [j for j in range(19) if VELOCITIES[j][axis] == sign]


def mirrored(j):
    cx, cy, cz = VELOCITIES[j]
    return VELOCITIES.index((cx, cy, -cz))


Z_FLAT = pops(2, 0)
Z_UP = pops(2, 1)
Z_DOWN = [mirrored(j) for j in Z_UP]
RHO, UX, UY, UZ, KIND = range(5)
Z_PLACE = {("pop", j): (0, g) for g, j in enumerate(Z_FLAT[:8])}
Z_PLACE[("pop", Z_FLAT[8])] = (1, 5)
Z_PLACE[("field", RHO)] = (1, 6)
Z_PLACE[("field", KIND)] = (1, 7)
Z_PLACE[("field", UX)] = (2, 5)
Z_PLACE[("field", UY)] = (2, 6)
Z_PLACE[("field", UZ)] = (2, 7)
BELOW, ABOVE, OWN_LOW, OWN_HIGH, Z_TILES = 0, 3, 6, 7, 8


def face_lines(axis, toward):
    near = pops(axis, 0) + pops(axis, toward)
    lines = [("pop", j, 0) for j in near] + [("field", k, 0) for k in range(5)]
    return lines + [("pop", j, 1) for j in pops(axis, toward)]


def edge_lines(toward_x, toward_y):
    lines = [("field", k, 0, 0) for k in range(5)]
    for j in range(19):
        cx, cy, _ = VELOCITIES[j]
        if cx not in (0, toward_x) or cy not in (0, toward_y):
            continue
        lines.append(("pop", j, 0, 0))
        if cx:
            lines.append(("pop", j, 1, 0))
        if cy:
            lines.append(("pop", j, 0, 1))
        if cx and cy:
            lines.append(("pop", j, 1, 1))
    return lines


FACE = 24
EDGE = 24


def lane_ids():
    return lax.broadcasted_iota(jnp.int32, (8, LANES), 1)


def field_of(refs, kind, index, at):
    adj, den, vel, mask = refs
    if kind == "pop":
        return adj[(index, *at)]
    if index == RHO:
        return den[(1, *at)]
    if index == KIND:
        return (mask[at] + 1).astype(jnp.float32)
    return vel[(1, index - UX, *at)]


def pack_z_kernel(adj, den, vel, mask, low, high):
    refs = (adj, den, vel, mask)
    ext_x, ext_y, _ = mask.shape
    lane = lane_ids()
    for part in range(ext_y // 8):
        rows = pl.ds(8 * part, 8)
        zero = jnp.zeros((8, LANES), jnp.float32)
        lows, highs, far_low, far_high = [zero] * 3, [zero] * 3, zero, zero
        for x in range(ext_x):
            at = (x, rows, slice(None))
            for (kind, index), (tile, group) in Z_PLACE.items():
                spot = GROUP * group + 2 + x
                moved = pltpu.roll(field_of(refs, kind, index, at), spot, 1)
                lows[tile] = jnp.where(lane == spot, moved, lows[tile])
                highs[tile] = jnp.where(lane == spot - 1, moved, highs[tile])
            for group in range(5):
                spot = GROUP * group + 2 + x
                moved = pltpu.roll(field_of(refs, "pop", Z_UP[group], at), spot, 1)
                lows[1] = jnp.where(lane == spot, moved, lows[1])
                far_low = jnp.where(lane == spot + 1, moved, far_low)
                moved = pltpu.roll(field_of(refs, "pop", Z_DOWN[group], at), spot, 1)
                highs[1] = jnp.where(lane == spot - 1, moved, highs[1])
                far_high = jnp.where(lane == spot - 2, moved, far_high)
        highs = [pltpu.roll(tile, 1, 1) for tile in highs]
        lows[2] = jnp.where(lane < 5 * GROUP, pltpu.roll(far_low, LANES - 1, 1), lows[2])
        highs[2] = jnp.where(lane < 5 * GROUP, pltpu.roll(far_high, 2, 1), highs[2])
        for tile in range(3):
            low[tile, rows, :] = lows[tile]
            high[tile, rows, :] = highs[tile]


def sides_of(paired, index, act):
    if paired:

        @pl.when(index == 0)
        def _():
            act(0, 1)

        @pl.when(index != 0)
        def _():
            act(0, 0)

    else:
        act(0, 0)
        act(1, 1)


def pack_xy_kernel(paired, adj, den, vel, mask, own_low, own_high, below, above, *packets):
    refs = (adj, den, vel, mask)
    ext_x, ext_y, _ = mask.shape
    slots = 1 if paired else 2
    x_packets, y_packets, xy_packets = packets[:2], packets[2 : 2 + slots], packets[2 + slots :]

    def add_z(packet, first, rows):
        for tile in range(3):
            packet[first + BELOW + tile] = below[tile, rows, :]
            packet[first + ABOVE + tile] = above[tile, rows, :]
        packet[first + OWN_LOW] = own_low[1, rows, :]
        packet[first + OWN_HIGH] = own_high[1, rows, :]

    for side in range(2):
        for line, (kind, index, depth) in enumerate(face_lines(0, 1 - 2 * side)):
            x = ext_x - 1 - depth if side else depth
            x_packets[side][line] = field_of(refs, kind, index, (x, slice(None), slice(None)))
        add_z(x_packets[side], FACE, pl.ds(0, ext_y))

    def pack_y(slot, side):
        rows = pl.ds(ext_y - 8 if side else 0, 8)
        packet = y_packets[slot]
        for line, (kind, index, depth) in enumerate(face_lines(1, 1 - 2 * side)):
            y = ext_y - 1 - depth if side else depth
            for x in range(ext_x):
                packet[line, x : x + 1, :] = field_of(refs, kind, index, (x, slice(y, y + 1), slice(None)))
        add_z(packet, FACE, rows)
        for side_x in range(2):
            packet = xy_packets[2 * slot + side_x]
            for line, (kind, index, far_x, far_y) in enumerate(edge_lines(1 - 2 * side_x, 1 - 2 * side)):
                x = ext_x - 1 - far_x if side_x else far_x
                y = ext_y - 1 - far_y if side else far_y
                spot = line % 8
                packet[line // 8, spot : spot + 1, :] = field_of(
                    refs, kind, index, (x, slice(y, y + 1), slice(None))
                )
            add_z(packet, EDGE // 8, rows)

    sides_of(paired, lax.axis_index("gy"), pack_y)


def collide(pulled, rho, ux, uy, uz, fluid, wanted):
    total = {}
    diff = {}
    for j in range(1, 19, 2):
        total[j] = pulled[j] + pulled[j + 1]
        diff[j] = pulled[j] - pulled[j + 1]
    in_xy, in_xz, in_yz = total[7] + total[9], total[11] + total[13], total[15] + total[17]
    two_x, two_y, two_z = total[1] + total[1], total[3] + total[3], total[5] + total[5]
    count = (12.0 * pulled[0] + (two_x + two_y)) + (two_z + (in_xy + (in_xz + in_yz)))
    flow_x = (diff[1] + diff[1]) + ((diff[7] + diff[9]) + (diff[11] + diff[13]))
    flow_y = (diff[3] + diff[3]) + ((diff[7] - diff[9]) + (diff[15] + diff[17]))
    flow_z = (diff[5] + diff[5]) + ((diff[11] - diff[13]) + (diff[15] - diff[17]))
    xx, yy, zz = two_x + (in_xy + in_xz), two_y + (in_xy + in_yz), two_z + (in_xz + in_yz)
    xy, xz, yz = total[7] - total[9], total[11] - total[13], total[15] - total[17]
    push_x = xx * ux + xy * uy + xz * uz
    push_y = xy * ux + yy * uy + yz * uz
    push_z = xz * ux + yz * uy + zz * uz
    usq = ux * ux + uy * uy + uz * uz
    push = ux * push_x + uy * push_y + uz * push_z
    inverse = 1.0 / rho
    base = count * (OMEGA / 36.0 + (OMEGA / 24.0) * usq) - (OMEGA / 8.0) * push - ux * inverse
    along_x = (OMEGA / 12.0) * (flow_x + 3.0 * push_x - ux * count) + inverse
    along_y = (OMEGA / 12.0) * (flow_y + 3.0 * push_y - uy * count)
    along_z = (OMEGA / 12.0) * (flow_z + 3.0 * push_z - uz * count)
    parts = {
        1: along_x,
        3: along_y,
        5: along_z,
        7: along_x + along_y,
        9: along_x - along_y,
        11: along_x + along_z,
        13: along_x - along_z,
        15: along_y + along_z,
        17: along_y - along_z,
    }
    out = {}
    for j in wanted:
        if j == 0:
            shift = base
        elif j % 2:
            shift = base + parts[j]
        else:
            shift = base - parts[j - 1]
        out[j] = jnp.where(fluid, (1.0 - OMEGA) * pulled[j] + shift, pulled[OPPOSITE[j]])
    change = (-1.0 / 6.0) * rho * (flow_x * ux + flow_y * uy + flow_z * uz)
    return out, jnp.where(fluid, change, 0.0)


def step_kernel(paired, adj, den, vel, mask, own_low, own_high, below, above, *rest):
    slots = 1 if paired else 2
    from_x, from_y, from_xy = rest[:2], rest[2 : 2 + slots], rest[2 + slots : 2 + 3 * slots]
    out, sens, first, fields, second, change, z_first, z_second, held, held_sens, sems = rest[2 + 3 * slots :]
    refs = (adj, den, vel, mask)
    ext_x, ext_y, _ = mask.shape
    lane = lane_ids()
    spot = lane % GROUP
    every = slice(None)
    inner = pl.ds(8, ext_y)

    for j in range(19):
        first[j, 2 : 2 + ext_x, inner, :] = adj[j]
    for k in range(5):
        fields[k, 1 : 1 + ext_x, inner, :] = field_of(refs, "field", k, (every, every, every))
    for side in range(2):
        for line, (kind, index, depth) in enumerate(face_lines(0, 2 * side - 1)):
            x = ext_x + depth if side else -1 - depth
            if kind == "pop":
                first[index, x + 2, inner, :] = from_x[side][line]
            else:
                fields[index, x + 1, inner, :] = from_x[side][line]

    def z_rows(start, size, middle, left, right):
        for tile in range(Z_TILES):
            for part in range(size // 8):
                rows = pl.ds(8 * part, 8)
                value = middle(tile, rows)
                value = jnp.where(spot < 2, pltpu.roll(left(tile, rows), LANES - ext_x, 1), value)
                value = jnp.where(spot >= 2 + ext_x, pltpu.roll(right(tile, rows), ext_x, 1), value)
                z_first[tile, pl.ds(start + 8 * part, 8), :] = value

    def own_z(tile, rows):
        if tile < ABOVE:
            return below[tile - BELOW, rows, :]
        if tile < OWN_LOW:
            return above[tile - ABOVE, rows, :]
        return (own_low if tile == OWN_LOW else own_high)[1, rows, :]

    z_rows(
        8,
        ext_y,
        own_z,
        lambda tile, rows: from_x[0][FACE + tile, rows, :],
        lambda tile, rows: from_x[1][FACE + tile, rows, :],
    )

    def put_row(kind, index, x, y, value):
        row = y + 8
        if kind == "pop":
            first[index, x + 2, row : row + 1, :] = value
        else:
            fields[index, x + 1, row : row + 1, :] = value

    def place_y(slot, side):
        packet = from_y[slot]
        for line, (kind, index, depth) in enumerate(face_lines(1, 2 * side - 1)):
            y = ext_y + depth if side else -1 - depth
            for x in range(ext_x):
                put_row(kind, index, x, y, packet[line, x : x + 1, :])
        for side_x in range(2):
            packet = from_xy[2 * slot + side_x]
            for line, (kind, index, far_x, far_y) in enumerate(edge_lines(2 * side_x - 1, 2 * side - 1)):
                x = ext_x + far_x if side_x else -1 - far_x
                y = ext_y + far_y if side else -1 - far_y
                put_row(kind, index, x, y, packet[line // 8, line % 8 : line % 8 + 1, :])
        z_rows(
            8 + ext_y if side else 0,
            8,
            lambda tile, rows: from_y[slot][FACE + tile, rows, :],
            lambda tile, rows: from_xy[2 * slot][EDGE // 8 + tile, rows, :],
            lambda tile, rows: from_xy[2 * slot + 1][EDGE // 8 + tile, rows, :],
        )
        if paired:
            clear_y(1 - side)

    def clear_y(side):
        nothing = jnp.zeros((1, LANES), jnp.float32)
        for kind, index, depth in face_lines(1, 2 * side - 1):
            y = ext_y + depth if side else -1 - depth
            for x in range(-1, ext_x + 1):
                put_row(kind, index, x, y, nothing)
            if kind == "pop":
                put_row(kind, index, -2, y, nothing)
                put_row(kind, index, ext_x + 1, y, nothing)
        start = 8 + ext_y if side else 0
        for tile in range(Z_TILES):
            z_first[tile, pl.ds(start, 8), :] = jnp.zeros((8, LANES), jnp.float32)

    sides_of(paired, lax.axis_index("gy"), place_y)

    parts = (ext_y + 2 + 7) // 8

    @pl.loop(0, ext_x + 2)
    def _(x):
        for part in range(parts):
            row = 7 + 8 * part
            pulled = []
            for j in range(19):
                cx, cy, cz = VELOCITIES[j]
                rows = pl.ds(row + cy, 8)
                value = first[j, x + 1 + cx, rows, :]
                if cz == 1:
                    group = Z_UP.index(j)
                    edge = z_first[ABOVE + 1, rows, :]
                    edge = pltpu.roll(edge, LANES - 2 - GROUP * group - cx - x, 1)
                    value = jnp.where(lane == LANES - 1, edge, pltpu.roll(value, LANES - 1, 1))
                elif cz == -1:
                    group = Z_DOWN.index(j)
                    edge = z_first[BELOW + 1, rows, :]
                    edge = pltpu.roll(edge, LANES - 1 - GROUP * group - cx - x, 1)
                    value = jnp.where(lane == 0, edge, pltpu.roll(value, 1, 1))
                pulled.append(value)
            rows = pl.ds(row, 8)
            rho, ux, uy, uz, kind = [fields[k, x, rows, :] for k in range(5)]
            after, gain = collide(pulled, rho, ux, uy, uz, kind > 1.5, range(19))
            for j in range(19):
                second[j, x, rows, :] = jnp.where(kind > 0.5, after[j], 0.0)
            change[x, rows, :] = gain

    for part in range(parts):
        row = 7 + 8 * part

        def both(low_tile, high_tile, group, cx, cy):
            rows = pl.ds(row + cy, 8)
            low = pltpu.roll(z_first[low_tile, rows, :], (-GROUP * group - cx) % LANES, 1)
            high = pltpu.roll(z_first[high_tile, rows, :], (LANES // 2 - GROUP * group - cx) % LANES, 1)
            return jnp.where(lane < LANES // 2, low, high)

        pulled = []
        for j in range(19):
            cx, cy, cz = VELOCITIES[j]
            if cz == 0:
                tile, group = Z_PLACE[("pop", j)]
                pulled.append(both(BELOW + tile, ABOVE + tile, group, cx, cy))
            elif cz == 1:
                pulled.append(both(OWN_LOW, ABOVE + 2, Z_UP.index(j), cx, cy))
            else:
                pulled.append(both(BELOW + 2, OWN_HIGH, Z_DOWN.index(j), cx, cy))
        rho, ux, uy, uz, kind = [
            both(BELOW + tile, ABOVE + tile, group, 0, 0)
            for tile, group in [Z_PLACE[("field", k)] for k in range(5)]
        ]
        after, _ = collide(pulled, rho, ux, uy, uz, kind > 1.5, Z_UP + Z_DOWN)
        for group in range(5):
            value = jnp.where(lane < LANES // 2, after[Z_DOWN[group]], after[Z_UP[group]])
            z_second[group, pl.ds(row, 8), :] = jnp.where(kind > 0.5, value, 0.0)

    def copies(x):
        return (
            pltpu.make_async_copy(held.at[:, x], out.at[:, x], sems.at[0, x]),
            pltpu.make_async_copy(held_sens.at[x], sens.at[x], sems.at[1, x]),
        )

    @pl.loop(0, ext_x)
    def _(x):
        for part in range(ext_y // 8):
            row = 8 + 8 * part
            at = (x, pl.ds(8 * part, 8), every)
            pulled = []
            for j in range(19):
                cx, cy, cz = VELOCITIES[j]
                rows = pl.ds(row + cy, 8)
                value = second[j, x + 1 + cx, rows, :]
                if cz == 1:
                    edge = z_second[Z_UP.index(j), rows, :]
                    edge = pltpu.roll(edge, LANES // 2 - 3 - cx - x, 1)
                    value = jnp.where(lane == LANES - 1, edge, pltpu.roll(value, LANES - 1, 1))
                elif cz == -1:
                    edge = z_second[Z_DOWN.index(j), rows, :]
                    edge = pltpu.roll(edge, LANES - 2 - cx - x, 1)
                    value = jnp.where(lane == 0, edge, pltpu.roll(value, 1, 1))
                pulled.append(value)
            after, gain = collide(
                pulled,
                den[(0, *at)],
                vel[(0, 0, *at)],
                vel[(0, 1, *at)],
                vel[(0, 2, *at)],
                mask[at] > 0,
                range(19),
            )
            for j in range(19):
                held[(j, *at)] = after[j]
            held_sens[at] = change[x + 1, pl.ds(row, 8), :] + gain
        for copy in copies(x):
            copy.start()

    for x in range(ext_x):
        for copy in copies(x):
            copy.wait()


def shards(adjoint, density, velocity, pore_mask):
    ext_x, ext_y, ext_z = pore_mask.shape
    assert ext_z == LANES and ext_y % 8 == 0 and ext_x + 4 <= GROUP
    many_x, many_y, many_z = [lax.axis_size(axis) for axis in ("gx", "gy", "gz")]
    paired = many_y == 2
    vmem = pl.BlockSpec(memory_space=pltpu.VMEM)
    params = pltpu.CompilerParams(vmem_limit_bytes=24 * 1024 * 1024)
    inputs = (adjoint, density, velocity, pore_mask)

    def array(*shape):
        return jax.ShapeDtypeStruct(shape, jnp.float32)

    def call(kernel, name, operands, shapes, **more):
        more.setdefault("out_specs", [vmem] * len(shapes))
        return pl.pallas_call(
            kernel,
            out_shape=shapes,
            in_specs=[vmem] * len(operands),
            compiler_params=params,
            name=name,
            **more,
        )(*operands)

    def move(value, axes, step):
        sizes = [lax.axis_size(axis) for axis in axes]
        pairs = []
        if len(axes) == 1:
            for at in range(sizes[0]):
                to = 1 - at if step[0] is None else at + step[0]
                if 0 <= to < sizes[0]:
                    pairs.append((at, to))
            return lax.ppermute(value, axes[0], pairs)
        for at in range(sizes[0]):
            for at_y in range(sizes[1]):
                to = at + step[0]
                to_y = 1 - at_y if step[1] is None else at_y + step[1]
                if 0 <= to < sizes[0] and 0 <= to_y < sizes[1]:
                    pairs.append((at * sizes[1] + at_y, to * sizes[1] + to_y))
        return lax.ppermute(value, axes, pairs)

    own_low, own_high = call(pack_z_kernel, "pack_z", inputs, [array(3, ext_y, LANES)] * 2)
    above = move(own_low, ("gz",), (-1,))
    below = move(own_high, ("gz",), (1,))
    z_faces = (own_low, own_high, below, above)

    slots = 1 if paired else 2
    x_shape = array(FACE + Z_TILES, ext_y, LANES)
    y_shape = array(FACE + Z_TILES, ext_x, LANES)
    xy_shape = array(EDGE // 8 + Z_TILES, 8, LANES)
    packets = call(
        functools.partial(pack_xy_kernel, paired),
        "pack_xy",
        inputs + z_faces,
        [x_shape] * 2 + [y_shape] * slots + [xy_shape] * (2 * slots),
    )
    to_x, to_y, to_xy = packets[:2], packets[2 : 2 + slots], packets[2 + slots :]
    from_x = [move(to_x[1], ("gx",), (1,)), move(to_x[0], ("gx",), (-1,))]
    if paired:
        from_y = [move(to_y[0], ("gy",), (None,))]
        from_xy = [move(to_xy[1], ("gx", "gy"), (1, None)), move(to_xy[0], ("gx", "gy"), (-1, None))]
    else:
        from_y = [move(to_y[1], ("gy",), (1,)), move(to_y[0], ("gy",), (-1,))]
        from_xy = [
            move(to_xy[2 * (1 - side) + 1 - side_x], ("gx", "gy"), (1 - 2 * side_x, 1 - 2 * side))
            for side in range(2)
            for side_x in range(2)
        ]

    rows = ext_y + 16
    scratch = [
        pltpu.VMEM((19, ext_x + 4, rows, LANES), jnp.float32),
        pltpu.VMEM((5, ext_x + 2, rows, LANES), jnp.float32),
        pltpu.VMEM((19, ext_x + 2, rows, LANES), jnp.float32),
        pltpu.VMEM((ext_x + 2, rows, LANES), jnp.float32),
        pltpu.VMEM((Z_TILES, rows, LANES), jnp.float32),
        pltpu.VMEM((5, rows, LANES), jnp.float32),
        pltpu.VMEM((19, ext_x, ext_y, LANES), jnp.float32),
        pltpu.VMEM((ext_x, ext_y, LANES), jnp.float32),
        pltpu.SemaphoreType.DMA((2, ext_x)),
    ]
    return call(
        functools.partial(step_kernel, paired),
        "two_steps",
        inputs + z_faces + (*from_x, *from_y, *from_xy),
        [array(19, ext_x, ext_y, LANES), array(ext_x, ext_y, LANES)],
        out_specs=[pl.BlockSpec(memory_space=pl.ANY)] * 2,
        scratch_shapes=scratch,
    )


def solution(mesh):
    placed = (
        P(None, "gx", "gy", "gz"),
        P(None, "gx", "gy", "gz"),
        P(None, None, "gx", "gy", "gz"),
        P("gx", "gy", "gz"),
    )

    def whole(*arrays):
        return tuple(shards(*arrays))

    return jax.shard_map(
        whole,
        mesh=mesh,
        in_specs=placed,
        out_specs=(P(None, "gx", "gy", "gz"), P("gx", "gy", "gz")),
        check_vma=False,
    )
```

```python
import functools

import jax
import jax.numpy as jnp
from jax import lax
from jax.experimental import pallas as pl
from jax.experimental.pallas import tpu as pltpu
from jax.sharding import PartitionSpec as P

VELOCITIES = [
    (0, 0, 0),
    (1, 0, 0),
    (-1, 0, 0),
    (0, 1, 0),
    (0, -1, 0),
    (0, 0, 1),
    (0, 0, -1),
    (1, 1, 0),
    (-1, -1, 0),
    (1, -1, 0),
    (-1, 1, 0),
    (1, 0, 1),
    (-1, 0, -1),
    (1, 0, -1),
    (-1, 0, 1),
    (0, 1, 1),
    (0, -1, -1),
    (0, 1, -1),
    (0, -1, 1),
]
OPPOSITE = [0, 2, 1, 4, 3, 6, 5, 8, 7, 10, 9, 12, 11, 14, 13, 16, 15, 18, 17]
OMEGA = 1.25
LANES = 128
GROUP = 16


def pops(axis, sign):
    return [j for j in range(19) if VELOCITIES[j][axis] == sign]


def mirrored(j):
    cx, cy, cz = VELOCITIES[j]
    return VELOCITIES.index((cx, cy, -cz))


Z_FLAT = pops(2, 0)
Z_UP = pops(2, 1)
Z_DOWN = [mirrored(j) for j in Z_UP]
RHO, UX, UY, UZ, KIND = range(5)
Z_PLACE = {("pop", j): (0, g) for g, j in enumerate(Z_FLAT[:8])}
Z_PLACE[("pop", Z_FLAT[8])] = (1, 5)
Z_PLACE[("field", RHO)] = (1, 6)
Z_PLACE[("field", KIND)] = (1, 7)
Z_PLACE[("field", UX)] = (2, 5)
Z_PLACE[("field", UY)] = (2, 6)
Z_PLACE[("field", UZ)] = (2, 7)
BELOW, ABOVE, OWN_LOW, OWN_HIGH, Z_TILES = 0, 3, 6, 7, 8


def face_lines(axis, toward):
    near = pops(axis, 0) + pops(axis, toward)
    lines = [("pop", j, 0) for j in near] + [("field", k, 0) for k in range(5)]
    return lines + [("pop", j, 1) for j in pops(axis, toward)]


def edge_lines(toward_x, toward_y):
    lines = [("field", k, 0, 0) for k in range(5)]
    for j in range(19):
        cx, cy, _ = VELOCITIES[j]
        if cx not in (0, toward_x) or cy not in (0, toward_y):
            continue
        lines.append(("pop", j, 0, 0))
        if cx:
            lines.append(("pop", j, 1, 0))
        if cy:
            lines.append(("pop", j, 0, 1))
        if cx and cy:
            lines.append(("pop", j, 1, 1))
    return lines


FACE = 24
EDGE = 24


def lane_ids():
    return lax.broadcasted_iota(jnp.int32, (8, LANES), 1)


def field_of(refs, kind, index, at):
    adj, den, vel, mask = refs
    if kind == "pop":
        return adj[(index, *at)]
    if index == RHO:
        return den[(1, *at)]
    if index == KIND:
        return (mask[at] + 1).astype(jnp.float32)
    return vel[(1, index - UX, *at)]


def parity_of(axis):
    return lax.rem(lax.axis_index(axis), 2)


def on_side(parity, slot, act):
    @pl.when(parity == slot)
    def _():
        act(1)

    @pl.when(parity != slot)
    def _():
        act(0)


def pack_z_kernel(slots, adj_in, den_in, vel_in, mask_in, adj, den, vel, mask, near, *rest):
    packets, sems = rest[:slots], rest[slots]
    refs = (adj, den, vel, mask)
    loads = [
        pltpu.make_async_copy(source, target, sems.at[at])
        for at, (source, target) in enumerate(
            [
                (adj_in, adj),
                (den_in.at[1], den.at[1]),
                (vel_in.at[1], vel.at[1]),
                (mask_in, mask),
                (den_in.at[0], den.at[0]),
                (vel_in.at[0], vel.at[0]),
            ]
        )
    ]
    for load in loads:
        load.start()
    for load in loads[:4]:
        load.wait()
    ext_x, ext_y, _ = mask.shape
    lane = lane_ids()
    parity = parity_of("gz")
    for part in range(ext_y // 8):
        rows = pl.ds(8 * part, 8)
        zero = jnp.zeros((8, LANES), jnp.float32)
        lows, highs, far_low, far_high = [zero] * 3, [zero] * 3, zero, zero
        for x in range(ext_x):
            at = (x, rows, slice(None))
            for (kind, index), (tile, group) in Z_PLACE.items():
                spot = GROUP * group + 2 + x
                moved = pltpu.roll(field_of(refs, kind, index, at), spot, 1)
                lows[tile] = jnp.where(lane == spot, moved, lows[tile])
                highs[tile] = jnp.where(lane == spot - 1, moved, highs[tile])
            for group in range(5):
                spot = GROUP * group + 2 + x
                moved = pltpu.roll(field_of(refs, "pop", Z_UP[group], at), spot, 1)
                lows[1] = jnp.where(lane == spot, moved, lows[1])
                far_low = jnp.where(lane == spot + 1, moved, far_low)
                moved = pltpu.roll(field_of(refs, "pop", Z_DOWN[group], at), spot, 1)
                highs[1] = jnp.where(lane == spot - 1, moved, highs[1])
                far_high = jnp.where(lane == spot - 2, moved, far_high)
        highs = [pltpu.roll(tile, 1, 1) for tile in highs]
        lows[2] = jnp.where(lane < 5 * GROUP, pltpu.roll(far_low, LANES - 1, 1), lows[2])
        highs[2] = jnp.where(lane < 5 * GROUP, pltpu.roll(far_high, 2, 1), highs[2])
        near[0, rows, :] = lows[1]
        near[1, rows, :] = highs[1]
        for slot in range(slots):
            for tile in range(3):
                packets[slot][tile, rows, :] = jnp.where(parity == slot, highs[tile], lows[tile])
    for load in loads[4:]:
        load.wait()


def pack_xy_kernel(slots, adj, den, vel, mask, near, *rest):
    many_x, many_y, many_z = slots
    from_z, z_set = rest[:many_z], rest[many_z]
    to_x = rest[many_z + 1 : many_z + 1 + many_x]
    to_y = rest[many_z + 1 + many_x : many_z + 1 + many_x + many_y]
    to_xy, faces = rest[many_z + 1 + many_x + many_y : -1], rest[-1]
    refs = (adj, den, vel, mask)
    ext_x, ext_y, _ = mask.shape
    spot = lane_ids() % GROUP
    every = slice(None)
    px, py, pz = parity_of("gx"), parity_of("gy"), parity_of("gz")

    z_set[OWN_LOW] = near[0]
    z_set[OWN_HIGH] = near[1]
    for tile in range(3):
        first = from_z[0][tile]
        second = from_z[1][tile] if many_z > 1 else jnp.zeros_like(first)
        z_set[ABOVE + tile] = jnp.where(pz == 0, first, second)
        z_set[BELOW + tile] = jnp.where(pz == 0, second, first)

    for side in range(2):
        for part in range(ext_y // 8):
            rows = pl.ds(8 * part, 8)
            value = jnp.zeros((8, LANES), jnp.float32)
            for tile in range(Z_TILES):
                start = ext_x if side else 2
                moved = pltpu.roll(z_set[tile, rows, :], (2 * tile - start) % LANES, 1)
                value = jnp.where(spot // 2 == tile, moved, value)
            faces[side, rows, :] = value

    def pack_xy(slot_x, slot_y, side_x, side_y):
        packet = to_xy[many_x * slot_y + slot_x]
        for line, (kind, index, far_x, far_y) in enumerate(edge_lines(1 - 2 * side_x, 1 - 2 * side_y)):
            x = ext_x - 1 - far_x if side_x else far_x
            y = ext_y - 1 - far_y if side_y else far_y
            packet[line // 8, line % 8 : line % 8 + 1, :] = field_of(refs, kind, index, (x, slice(y, y + 1), every))
        start = ext_y - 2 if side_y else 0
        packet[EDGE // 8, 0:2, :] = faces[side_x, start : start + 2, :]

    def pack_y(slot, side):
        packet = to_y[slot]
        for line, (kind, index, depth) in enumerate(face_lines(1, 1 - 2 * side)):
            y = ext_y - 1 - depth if side else depth
            for x in range(ext_x):
                packet[line, x : x + 1, :] = field_of(refs, kind, index, (x, slice(y, y + 1), every))
        start = ext_y - 2 if side else 0
        for tile in range(Z_TILES):
            row = 2 * tile % 8
            packet[FACE + tile // 4, row : row + 2, :] = z_set[tile, start : start + 2, :]

    def pack_x(slot, side):
        for line, (kind, index, depth) in enumerate(face_lines(0, 1 - 2 * side)):
            x = ext_x - 1 - depth if side else depth
            to_x[slot][line] = field_of(refs, kind, index, (x, every, every))
        to_x[slot][FACE] = faces[side]

    for slot_y in range(many_y):
        on_side(py, slot_y, functools.partial(pack_y, slot_y))
        for slot_x in range(many_x):
            on_side(
                py,
                slot_y,
                lambda side_y: on_side(px, slot_x, lambda side_x: pack_xy(slot_x, slot_y, side_x, side_y)),
            )
    for slot_x in range(many_x):
        on_side(px, slot_x, functools.partial(pack_x, slot_x))


def collide(pulled, rho, ux, uy, uz, fluid, wanted):
    total = {}
    diff = {}
    for j in range(1, 19, 2):
        total[j] = pulled[j] + pulled[j + 1]
        diff[j] = pulled[j] - pulled[j + 1]
    in_xy, in_xz, in_yz = total[7] + total[9], total[11] + total[13], total[15] + total[17]
    two_x, two_y, two_z = total[1] + total[1], total[3] + total[3], total[5] + total[5]
    count = (12.0 * pulled[0] + (two_x + two_y)) + (two_z + (in_xy + (in_xz + in_yz)))
    flow_x = (diff[1] + diff[1]) + ((diff[7] + diff[9]) + (diff[11] + diff[13]))
    flow_y = (diff[3] + diff[3]) + ((diff[7] - diff[9]) + (diff[15] + diff[17]))
    flow_z = (diff[5] + diff[5]) + ((diff[11] - diff[13]) + (diff[15] - diff[17]))
    xx, yy, zz = two_x + (in_xy + in_xz), two_y + (in_xy + in_yz), two_z + (in_xz + in_yz)
    xy, xz, yz = total[7] - total[9], total[11] - total[13], total[15] - total[17]
    push_x = xx * ux + xy * uy + xz * uz
    push_y = xy * ux + yy * uy + yz * uz
    push_z = xz * ux + yz * uy + zz * uz
    usq = ux * ux + uy * uy + uz * uz
    push = ux * push_x + uy * push_y + uz * push_z
    inverse = 1.0 / rho
    base = count * (OMEGA / 36.0 + (OMEGA / 24.0) * usq) - (OMEGA / 8.0) * push - ux * inverse
    along_x = (OMEGA / 12.0) * (flow_x + 3.0 * push_x - ux * count) + inverse
    along_y = (OMEGA / 12.0) * (flow_y + 3.0 * push_y - uy * count)
    along_z = (OMEGA / 12.0) * (flow_z + 3.0 * push_z - uz * count)
    parts = {
        1: along_x,
        3: along_y,
        5: along_z,
        7: along_x + along_y,
        9: along_x - along_y,
        11: along_x + along_z,
        13: along_x - along_z,
        15: along_y + along_z,
        17: along_y - along_z,
    }
    out = {}
    for j in wanted:
        if j == 0:
            shift = base
        elif j % 2:
            shift = base + parts[j]
        else:
            shift = base - parts[j - 1]
        out[j] = jnp.where(fluid, (1.0 - OMEGA) * pulled[j] + shift, pulled[OPPOSITE[j]])
    change = (-1.0 / 6.0) * rho * (flow_x * ux + flow_y * uy + flow_z * uz)
    return out, jnp.where(fluid, change, 0.0)


def step_kernel(slots, adj, den, vel, mask, z_set, *rest):
    many_x, many_y = slots
    from_x, from_y = rest[:many_x], rest[many_x : many_x + many_y]
    from_xy = rest[many_x + many_y : many_x + many_y + many_x * many_y]
    out, sens, first, fields, second, change, z_first, z_second, held, held_sens, sems = rest[-11:]
    refs = (adj, den, vel, mask)
    ext_x, ext_y, _ = mask.shape
    lane = lane_ids()
    spot = lane % GROUP
    every = slice(None)
    inner = pl.ds(8, ext_y)
    px, py = parity_of("gx"), parity_of("gy")

    def put_row(kind, index, x, y, value):
        row = y + 8
        if kind == "pop":
            first[index, x + 2, row : row + 1, :] = value
        else:
            fields[index, x + 1, row : row + 1, :] = value

    for j in range(19):
        first[j, 2 : 2 + ext_x, inner, :] = adj[j]
    for k in range(5):
        fields[k, 1 : 1 + ext_x, inner, :] = field_of(refs, "field", k, (every, every, every))
    z_first[:, inner, :] = z_set[...]

    def place_y(slot, side):
        packet = from_y[slot]
        for line, (kind, index, depth) in enumerate(face_lines(1, 2 * side - 1)):
            y = ext_y + depth if side else -1 - depth
            for x in range(ext_x):
                put_row(kind, index, x, y, packet[line, x : x + 1, :])
        start = 8 + ext_y if side else 6
        for tile in range(Z_TILES):
            row = 2 * tile % 8
            z_first[tile, start : start + 2, :] = packet[FACE + tile // 4, row : row + 2, :]
        if many_y == 1:
            clear_y(1 - side)

    def clear_y(side):
        nothing = jnp.zeros((1, LANES), jnp.float32)
        for kind, index, depth in face_lines(1, 2 * side - 1):
            y = ext_y + depth if side else -1 - depth
            for x in range(-1, ext_x + 1):
                put_row(kind, index, x, y, nothing)
            if kind == "pop":
                put_row(kind, index, -2, y, nothing)
                put_row(kind, index, ext_x + 1, y, nothing)
        start = 8 + ext_y if side else 6
        for tile in range(Z_TILES):
            z_first[tile, start : start + 2, :] = jnp.zeros((2, LANES), jnp.float32)

    def place_z(value, start, size, side):
        rows = pl.ds(start, size)
        inside = spot[:size] >= 2 + ext_x if side else spot[:size] < 2
        for tile in range(Z_TILES):
            shift = (2 + ext_x if side else 0) - 2 * tile
            moved = pltpu.roll(value, shift % LANES, 1)[:size]
            z_first[tile, rows, :] = jnp.where(inside, moved, z_first[tile, rows, :])

    def place_x(slot, side):
        packet = from_x[slot]
        for line, (kind, index, depth) in enumerate(face_lines(0, 2 * side - 1)):
            x = ext_x + depth if side else -1 - depth
            if kind == "pop":
                first[index, x + 2, inner, :] = packet[line]
            else:
                fields[index, x + 1, inner, :] = packet[line]
        for part in range(ext_y // 8):
            place_z(packet[FACE, pl.ds(8 * part, 8), :], 8 + 8 * part, 8, side)

    def place_xy(slot_x, slot_y, side_x, side_y):
        packet = from_xy[many_x * slot_y + slot_x]
        for line, (kind, index, far_x, far_y) in enumerate(edge_lines(2 * side_x - 1, 2 * side_y - 1)):
            x = ext_x + far_x if side_x else -1 - far_x
            y = ext_y + far_y if side_y else -1 - far_y
            put_row(kind, index, x, y, packet[line // 8, line % 8 : line % 8 + 1, :])
        place_z(packet[EDGE // 8], 8 + ext_y if side_y else 6, 2, side_x)

    for slot_y in range(many_y):
        on_side(py, slot_y, functools.partial(place_y, slot_y))
    for slot_x in range(many_x):
        on_side(px, slot_x, functools.partial(place_x, slot_x))
        for slot_y in range(many_y):
            on_side(
                py,
                slot_y,
                lambda side_y: on_side(px, slot_x, lambda side_x: place_xy(slot_x, slot_y, side_x, side_y)),
            )

    parts = (ext_y + 2 + 7) // 8

    @pl.loop(0, ext_x + 2)
    def _(x):
        for part in range(parts):
            row = 7 + 8 * part
            pulled = []
            for j in range(19):
                cx, cy, cz = VELOCITIES[j]
                rows = pl.ds(row + cy, 8)
                value = first[j, x + 1 + cx, rows, :]
                if cz == 1:
                    group = Z_UP.index(j)
                    edge = z_first[ABOVE + 1, rows, :]
                    edge = pltpu.roll(edge, LANES - 2 - GROUP * group - cx - x, 1)
                    value = jnp.where(lane == LANES - 1, edge, pltpu.roll(value, LANES - 1, 1))
                elif cz == -1:
                    group = Z_DOWN.index(j)
                    edge = z_first[BELOW + 1, rows, :]
                    edge = pltpu.roll(edge, LANES - 1 - GROUP * group - cx - x, 1)
                    value = jnp.where(lane == 0, edge, pltpu.roll(value, 1, 1))
                pulled.append(value)
            rows = pl.ds(row, 8)
            rho, ux, uy, uz, kind = [fields[k, x, rows, :] for k in range(5)]
            after, gain = collide(pulled, rho, ux, uy, uz, kind > 1.5, range(19))
            for j in range(19):
                second[j, x, rows, :] = jnp.where(kind > 0.5, after[j], 0.0)
            change[x, rows, :] = gain

    for part in range(parts):
        row = 7 + 8 * part

        def both(low_tile, high_tile, group, cx, cy):
            rows = pl.ds(row + cy, 8)
            low = pltpu.roll(z_first[low_tile, rows, :], (-GROUP * group - cx) % LANES, 1)
            high = pltpu.roll(z_first[high_tile, rows, :], (LANES // 2 - GROUP * group - cx) % LANES, 1)
            return jnp.where(lane < LANES // 2, low, high)

        pulled = []
        for j in range(19):
            cx, cy, cz = VELOCITIES[j]
            if cz == 0:
                tile, group = Z_PLACE[("pop", j)]
                pulled.append(both(BELOW + tile, ABOVE + tile, group, cx, cy))
            elif cz == 1:
                pulled.append(both(OWN_LOW, ABOVE + 2, Z_UP.index(j), cx, cy))
            else:
                pulled.append(both(BELOW + 2, OWN_HIGH, Z_DOWN.index(j), cx, cy))
        rho, ux, uy, uz, kind = [
            both(BELOW + tile, ABOVE + tile, group, 0, 0)
            for tile, group in [Z_PLACE[("field", k)] for k in range(5)]
        ]
        after, _ = collide(pulled, rho, ux, uy, uz, kind > 1.5, Z_UP + Z_DOWN)
        for group in range(5):
            value = jnp.where(lane < LANES // 2, after[Z_DOWN[group]], after[Z_UP[group]])
            z_second[group, pl.ds(row, 8), :] = jnp.where(kind > 0.5, value, 0.0)

    def copies(x):
        return (
            pltpu.make_async_copy(held.at[:, x], out.at[:, x], sems.at[0, x]),
            pltpu.make_async_copy(held_sens.at[x], sens.at[x], sems.at[1, x]),
        )

    @pl.loop(0, ext_x)
    def _(x):
        for part in range(ext_y // 8):
            row = 8 + 8 * part
            at = (x, pl.ds(8 * part, 8), every)
            pulled = []
            for j in range(19):
                cx, cy, cz = VELOCITIES[j]
                rows = pl.ds(row + cy, 8)
                value = second[j, x + 1 + cx, rows, :]
                if cz == 1:
                    edge = z_second[Z_UP.index(j), rows, :]
                    edge = pltpu.roll(edge, LANES // 2 - 3 - cx - x, 1)
                    value = jnp.where(lane == LANES - 1, edge, pltpu.roll(value, LANES - 1, 1))
                elif cz == -1:
                    edge = z_second[Z_DOWN.index(j), rows, :]
                    edge = pltpu.roll(edge, LANES - 2 - cx - x, 1)
                    value = jnp.where(lane == 0, edge, pltpu.roll(value, 1, 1))
                pulled.append(value)
            after, gain = collide(
                pulled,
                den[(0, *at)],
                vel[(0, 0, *at)],
                vel[(0, 1, *at)],
                vel[(0, 2, *at)],
                mask[at] > 0,
                range(19),
            )
            for j in range(19):
                held[(j, *at)] = after[j]
            held_sens[at] = change[x + 1, pl.ds(row, 8), :] + gain
        for copy in copies(x):
            copy.start()

    for x in range(ext_x):
        for copy in copies(x):
            copy.wait()


def shards(adjoint, density, velocity, pore_mask):
    ext_x, ext_y, ext_z = pore_mask.shape
    assert ext_z == LANES and ext_y % 8 == 0 and ext_x + 4 <= GROUP and ext_x == 8
    many_x = 2
    many_y, many_z = [1 if lax.axis_size(axis) == 2 else 2 for axis in ("gy", "gz")]
    vmem = pl.BlockSpec(memory_space=pltpu.VMEM)
    hbm = pl.BlockSpec(memory_space=pl.ANY)
    params = pltpu.CompilerParams(vmem_limit_bytes=24 * 1024 * 1024)
    inputs = (adjoint, density, velocity, pore_mask)

    def array(*shape):
        return jax.ShapeDtypeStruct(shape, jnp.float32)

    def call(kernel, name, operands, shapes, **more):
        more.setdefault("out_specs", [vmem] * len(shapes))
        more.setdefault("in_specs", [vmem] * len(operands))
        return pl.pallas_call(kernel, out_shape=shapes, compiler_params=params, name=name, **more)(*operands)

    def partners(axis, slot):
        size = lax.axis_size(axis)
        found = {}
        for at in range(slot, size - 1, 2):
            found[at], found[at + 1] = at + 1, at
        return found

    def swap(value, *places):
        axes = [axis for axis, _ in places]
        tables = [partners(axis, slot) for axis, slot in places]
        if len(places) == 1:
            return lax.ppermute(value, axes[0], sorted(tables[0].items()))
        size = lax.axis_size(axes[1])
        pairs = [
            (at * size + at_y, to * size + to_y)
            for at, to in sorted(tables[0].items())
            for at_y, to_y in sorted(tables[1].items())
        ]
        return lax.ppermute(value, tuple(axes), pairs)

    loaded = [jax.ShapeDtypeStruct(value.shape, value.dtype) for value in inputs]
    *held, near, a_z, b_z = (
        *call(
            functools.partial(pack_z_kernel, many_z),
            "pack_z",
            inputs,
            loaded + [array(2, ext_y, LANES)] + [array(3, ext_y, LANES)] * many_z,
            in_specs=[hbm] * 4,
            scratch_shapes=[pltpu.SemaphoreType.DMA((6,))],
        ),
        *[None] * (2 - many_z),
    )
    from_z = [swap(value, ("gz", slot)) for slot, value in enumerate((a_z, b_z)[:many_z])]

    z_set, *packets = call(
        functools.partial(pack_xy_kernel, (many_x, many_y, many_z)),
        "pack_xy",
        (*held, near, *from_z),
        [array(Z_TILES, ext_y, LANES)]
        + [array(FACE + 1, ext_y, LANES)] * many_x
        + [array(FACE + 2, ext_x, LANES)] * many_y
        + [array(EDGE // 8 + 1, 8, LANES)] * (many_x * many_y),
        scratch_shapes=[pltpu.VMEM((2, ext_y, LANES), jnp.float32)],
    )
    to_x, to_y, to_xy = packets[:many_x], packets[many_x : many_x + many_y], packets[many_x + many_y :]
    from_xy = [
        swap(to_xy[many_x * slot_y + slot_x], ("gx", slot_x), ("gy", slot_y))
        for slot_y in range(many_y)
        for slot_x in range(many_x)
    ]
    from_y = [swap(value, ("gy", slot)) for slot, value in enumerate(to_y)]
    from_x = [swap(value, ("gx", slot)) for slot, value in enumerate(to_x)]

    rows = ext_y + 16
    scratch = [
        pltpu.VMEM((19, ext_x + 4, rows, LANES), jnp.float32),
        pltpu.VMEM((5, ext_x + 2, rows, LANES), jnp.float32),
        pltpu.VMEM((19, ext_x + 2, rows, LANES), jnp.float32),
        pltpu.VMEM((ext_x + 2, rows, LANES), jnp.float32),
        pltpu.VMEM((Z_TILES, rows, LANES), jnp.float32),
        pltpu.VMEM((5, rows, LANES), jnp.float32),
        pltpu.VMEM((19, ext_x, ext_y, LANES), jnp.float32),
        pltpu.VMEM((ext_x, ext_y, LANES), jnp.float32),
        pltpu.SemaphoreType.DMA((2, ext_x)),
    ]
    return call(
        functools.partial(step_kernel, (many_x, many_y)),
        "two_steps",
        (*held, z_set, *from_x, *from_y, *from_xy),
        [array(19, ext_x, ext_y, LANES), array(ext_x, ext_y, LANES)],
        out_specs=[pl.BlockSpec(memory_space=pl.ANY)] * 2,
        scratch_shapes=scratch,
    )


def solution(mesh):
    placed = (
        P(None, "gx", "gy", "gz"),
        P(None, "gx", "gy", "gz"),
        P(None, None, "gx", "gy", "gz"),
        P("gx", "gy", "gz"),
    )

    def whole(*arrays):
        return tuple(shards(*arrays))

    return jax.shard_map(
        whole,
        mesh=mesh,
        in_specs=placed,
        out_specs=(P(None, "gx", "gy", "gz"), P("gx", "gy", "gz")),
        check_vma=False,
    )
```

```python
import functools

import jax
import jax.numpy as jnp
from jax import lax
from jax.experimental import pallas as pl
from jax.experimental.pallas import tpu as pltpu
from jax.sharding import PartitionSpec as P

VELOCITIES = [
    (0, 0, 0),
    (1, 0, 0),
    (-1, 0, 0),
    (0, 1, 0),
    (0, -1, 0),
    (0, 0, 1),
    (0, 0, -1),
    (1, 1, 0),
    (-1, -1, 0),
    (1, -1, 0),
    (-1, 1, 0),
    (1, 0, 1),
    (-1, 0, -1),
    (1, 0, -1),
    (-1, 0, 1),
    (0, 1, 1),
    (0, -1, -1),
    (0, 1, -1),
    (0, -1, 1),
]
OPPOSITE = [0, 2, 1, 4, 3, 6, 5, 8, 7, 10, 9, 12, 11, 14, 13, 16, 15, 18, 17]
OMEGA = 1.25
LANES = 128
GROUP = 16


def pops(axis, sign):
    return [j for j in range(19) if VELOCITIES[j][axis] == sign]


def mirrored(j):
    cx, cy, cz = VELOCITIES[j]
    return VELOCITIES.index((cx, cy, -cz))


Z_FLAT = pops(2, 0)
Z_UP = pops(2, 1)
Z_DOWN = [mirrored(j) for j in Z_UP]
RHO, UX, UY, UZ, KIND = range(5)
Z_PLACE = {("pop", j): (0, g) for g, j in enumerate(Z_FLAT[:8])}
Z_PLACE[("pop", Z_FLAT[8])] = (1, 5)
Z_PLACE[("field", RHO)] = (1, 6)
Z_PLACE[("field", KIND)] = (1, 7)
Z_PLACE[("field", UX)] = (2, 5)
Z_PLACE[("field", UY)] = (2, 6)
Z_PLACE[("field", UZ)] = (2, 7)
BELOW, ABOVE, OWN_LOW, OWN_HIGH, Z_TILES = 0, 3, 6, 7, 8


def face_lines(axis, toward):
    near = pops(axis, 0) + pops(axis, toward)
    lines = [("pop", j, 0) for j in near] + [("field", k, 0) for k in range(5)]
    return lines + [("pop", j, 1) for j in pops(axis, toward)]


def edge_lines(toward_x, toward_y):
    lines = [("field", k, 0, 0) for k in range(5)]
    for j in range(19):
        cx, cy, _ = VELOCITIES[j]
        if cx not in (0, toward_x) or cy not in (0, toward_y):
            continue
        lines.append(("pop", j, 0, 0))
        if cx:
            lines.append(("pop", j, 1, 0))
        if cy:
            lines.append(("pop", j, 0, 1))
        if cx and cy:
            lines.append(("pop", j, 1, 1))
    return lines


FACE = 24
EDGE = 24


def lane_ids():
    return lax.broadcasted_iota(jnp.int32, (8, LANES), 1)


def field_of(refs, kind, index, at):
    adj, den, vel, mask = refs
    if kind == "pop":
        return adj[(index, *at)]
    if index == RHO:
        return den[(1, *at)]
    if index == KIND:
        return (mask[at] + 1).astype(jnp.float32)
    return vel[(1, index - UX, *at)]


def parity_of(axis):
    return lax.rem(lax.axis_index(axis), 2)


def on_side(parity, slot, act):
    @pl.when(parity == slot)
    def _():
        act(1)

    @pl.when(parity != slot)
    def _():
        act(0)


def has_partner(axis, slot):
    at = lax.axis_index(axis)
    to = at + jnp.where(lax.rem(at, 2) == slot, 1, -1)
    return (to >= 0) & (to < lax.axis_size(axis))


def pack_z_kernel(slots, adj_in, den_in, vel_in, mask_in, near, *rest):
    packets, (adj, den, vel, mask, sems) = rest[:slots], rest[slots:]
    refs = (adj, den, vel, mask)
    ext_x, ext_y, _ = mask.shape
    loads = [
        pltpu.make_async_copy(source, target, sems.at[ext_x + at])
        for at, (source, target) in enumerate([(den_in.at[1], den.at[1]), (vel_in.at[1], vel.at[1]), (mask_in, mask)])
    ]
    plane_loads = [pltpu.make_async_copy(adj_in.at[:, x], adj.at[:, x], sems.at[x]) for x in range(ext_x)]
    for load in loads + plane_loads:
        load.start()
    for load in loads:
        load.wait()
    lane = lane_ids()
    parity = parity_of("gz")
    parts = range(ext_y // 8)
    zero = jnp.zeros((8, LANES), jnp.float32)
    lows, highs = [[zero] * 3 for _ in parts], [[zero] * 3 for _ in parts]
    far_low, far_high = [zero for _ in parts], [zero for _ in parts]
    for x in range(ext_x):
        plane_loads[x].wait()
        for part in parts:
            at = (x, pl.ds(8 * part, 8), slice(None))
            for (kind, index), (tile, group) in Z_PLACE.items():
                spot = GROUP * group + 2 + x
                moved = pltpu.roll(field_of(refs, kind, index, at), spot, 1)
                lows[part][tile] = jnp.where(lane == spot, moved, lows[part][tile])
                highs[part][tile] = jnp.where(lane == spot - 1, moved, highs[part][tile])
            for group in range(5):
                spot = GROUP * group + 2 + x
                moved = pltpu.roll(field_of(refs, "pop", Z_UP[group], at), spot, 1)
                lows[part][1] = jnp.where(lane == spot, moved, lows[part][1])
                far_low[part] = jnp.where(lane == spot + 1, moved, far_low[part])
                moved = pltpu.roll(field_of(refs, "pop", Z_DOWN[group], at), spot, 1)
                highs[part][1] = jnp.where(lane == spot - 1, moved, highs[part][1])
                far_high[part] = jnp.where(lane == spot - 2, moved, far_high[part])
    for part in parts:
        rows = pl.ds(8 * part, 8)
        low = lows[part]
        high = [pltpu.roll(tile, 1, 1) for tile in highs[part]]
        low[2] = jnp.where(lane < 5 * GROUP, pltpu.roll(far_low[part], LANES - 1, 1), low[2])
        high[2] = jnp.where(lane < 5 * GROUP, pltpu.roll(far_high[part], 2, 1), high[2])
        near[0, rows, :] = low[1]
        near[1, rows, :] = high[1]
        for slot in range(slots):
            there = has_partner("gz", slot)
            for tile in range(3):
                value = jnp.where(parity == slot, high[tile], low[tile])
                packets[slot][tile, rows, :] = jnp.where(there, value, 0.0)


def pack_xy_kernel(slots, adj, den, vel, mask, near, *rest):
    many_x, many_y, many_z = slots
    from_z, z_set = rest[:many_z], rest[many_z]
    to_x = rest[many_z + 1 : many_z + 1 + many_x]
    to_y = rest[many_z + 1 + many_x : many_z + 1 + many_x + many_y]
    to_xy, faces = rest[many_z + 1 + many_x + many_y : -1], rest[-1]
    refs = (adj, den, vel, mask)
    ext_x, ext_y, _ = mask.shape
    spot = lane_ids() % GROUP
    every = slice(None)
    px, py, pz = parity_of("gx"), parity_of("gy"), parity_of("gz")

    z_set[OWN_LOW] = near[0]
    z_set[OWN_HIGH] = near[1]
    for tile in range(3):
        first = from_z[0][tile]
        second = from_z[1][tile] if many_z > 1 else jnp.zeros_like(first)
        z_set[ABOVE + tile] = jnp.where(pz == 0, first, second)
        z_set[BELOW + tile] = jnp.where(pz == 0, second, first)

    for side in range(2):
        for part in range(ext_y // 8):
            rows = pl.ds(8 * part, 8)
            value = jnp.zeros((8, LANES), jnp.float32)
            for tile in range(Z_TILES):
                start = ext_x if side else 2
                moved = pltpu.roll(z_set[tile, rows, :], (2 * tile - start) % LANES, 1)
                value = jnp.where(spot // 2 == tile, moved, value)
            faces[side, rows, :] = value

    def pack_xy(slot_x, slot_y, side_x, side_y):
        packet = to_xy[many_x * slot_y + slot_x]
        for line, (kind, index, far_x, far_y) in enumerate(edge_lines(1 - 2 * side_x, 1 - 2 * side_y)):
            x = ext_x - 1 - far_x if side_x else far_x
            y = ext_y - 1 - far_y if side_y else far_y
            packet[line // 8, line % 8 : line % 8 + 1, :] = field_of(refs, kind, index, (x, slice(y, y + 1), every))
        start = ext_y - 2 if side_y else 0
        packet[EDGE // 8, 0:2, :] = faces[side_x, start : start + 2, :]

    def pack_y(slot, side):
        packet = to_y[slot]
        for line, (kind, index, depth) in enumerate(face_lines(1, 1 - 2 * side)):
            y = ext_y - 1 - depth if side else depth
            for x in range(ext_x):
                packet[line, x : x + 1, :] = field_of(refs, kind, index, (x, slice(y, y + 1), every))
        start = ext_y - 2 if side else 0
        for tile in range(Z_TILES):
            row = 2 * tile % 8
            packet[FACE + tile // 4, row : row + 2, :] = z_set[tile, start : start + 2, :]

    def pack_x(slot, side):
        for line, (kind, index, depth) in enumerate(face_lines(0, 1 - 2 * side)):
            x = ext_x - 1 - depth if side else depth
            to_x[slot][line] = field_of(refs, kind, index, (x, every, every))
        to_x[slot][FACE] = faces[side]

    def when_there(there, packet, act):
        pl.when(there)(act)

        @pl.when(jnp.logical_not(there))
        def _():
            packet[...] = jnp.zeros(packet.shape, jnp.float32)

    for slot_y in range(many_y):
        there_y = has_partner("gy", slot_y)
        when_there(there_y, to_y[slot_y], lambda: on_side(py, slot_y, functools.partial(pack_y, slot_y)))
        for slot_x in range(many_x):
            when_there(
                there_y & has_partner("gx", slot_x),
                to_xy[many_x * slot_y + slot_x],
                lambda: on_side(
                    py,
                    slot_y,
                    lambda side_y: on_side(px, slot_x, lambda side_x: pack_xy(slot_x, slot_y, side_x, side_y)),
                ),
            )
    for slot_x in range(many_x):
        when_there(
            has_partner("gx", slot_x), to_x[slot_x], lambda: on_side(px, slot_x, functools.partial(pack_x, slot_x))
        )


def collide(pulled, rho, ux, uy, uz, fluid, wanted):
    total = {}
    diff = {}
    for j in range(1, 19, 2):
        total[j] = pulled[j] + pulled[j + 1]
        diff[j] = pulled[j] - pulled[j + 1]
    in_xy, in_xz, in_yz = total[7] + total[9], total[11] + total[13], total[15] + total[17]
    two_x, two_y, two_z = total[1] + total[1], total[3] + total[3], total[5] + total[5]
    count = (12.0 * pulled[0] + (two_x + two_y)) + (two_z + (in_xy + (in_xz + in_yz)))
    flow_x = (diff[1] + diff[1]) + ((diff[7] + diff[9]) + (diff[11] + diff[13]))
    flow_y = (diff[3] + diff[3]) + ((diff[7] - diff[9]) + (diff[15] + diff[17]))
    flow_z = (diff[5] + diff[5]) + ((diff[11] - diff[13]) + (diff[15] - diff[17]))
    xx, yy, zz = two_x + (in_xy + in_xz), two_y + (in_xy + in_yz), two_z + (in_xz + in_yz)
    xy, xz, yz = total[7] - total[9], total[11] - total[13], total[15] - total[17]
    push_x = xx * ux + xy * uy + xz * uz
    push_y = xy * ux + yy * uy + yz * uz
    push_z = xz * ux + yz * uy + zz * uz
    usq = ux * ux + uy * uy + uz * uz
    push = ux * push_x + uy * push_y + uz * push_z
    inverse = 1.0 / rho
    base = count * (OMEGA / 36.0 + (OMEGA / 24.0) * usq) - (OMEGA / 8.0) * push - ux * inverse
    along_x = (OMEGA / 12.0) * (flow_x + 3.0 * push_x - ux * count) + inverse
    along_y = (OMEGA / 12.0) * (flow_y + 3.0 * push_y - uy * count)
    along_z = (OMEGA / 12.0) * (flow_z + 3.0 * push_z - uz * count)
    parts = {
        1: along_x,
        3: along_y,
        5: along_z,
        7: along_x + along_y,
        9: along_x - along_y,
        11: along_x + along_z,
        13: along_x - along_z,
        15: along_y + along_z,
        17: along_y - along_z,
    }
    out = {}
    for j in wanted:
        if j == 0:
            shift = base
        elif j % 2:
            shift = base + parts[j]
        else:
            shift = base - parts[j - 1]
        out[j] = jnp.where(fluid, (1.0 - OMEGA) * pulled[j] + shift, pulled[OPPOSITE[j]])
    change = (-1.0 / 6.0) * rho * (flow_x * ux + flow_y * uy + flow_z * uz)
    return out, jnp.where(fluid, change, 0.0)


def step_kernel(slots, adj, den, vel, mask, z_set, *rest):
    many_x, many_y = slots
    from_x, from_y = rest[:many_x], rest[many_x : many_x + many_y]
    from_xy = rest[many_x + many_y : many_x + many_y + many_x * many_y]
    out, sens, first, fields, second, change, z_first, z_second, held, held_sens, sems = rest[-11:]
    refs = (adj, den, vel, mask)
    ext_x, ext_y, _ = mask.shape
    lane = lane_ids()
    spot = lane % GROUP
    every = slice(None)
    inner = pl.ds(8, ext_y)
    px, py = parity_of("gx"), parity_of("gy")

    def put_row(kind, index, x, y, value):
        row = y + 8
        if kind == "pop":
            first[index, x + 2, row : row + 1, :] = value
        else:
            fields[index, x + 1, row : row + 1, :] = value

    for j in range(19):
        first[j, 2 : 2 + ext_x, inner, :] = adj[j]
    for k in range(5):
        fields[k, 1 : 1 + ext_x, inner, :] = field_of(refs, "field", k, (every, every, every))
    z_first[:, inner, :] = z_set[...]

    def place_y(slot, side):
        packet = from_y[slot]
        for line, (kind, index, depth) in enumerate(face_lines(1, 2 * side - 1)):
            y = ext_y + depth if side else -1 - depth
            for x in range(ext_x):
                put_row(kind, index, x, y, packet[line, x : x + 1, :])
        start = 8 + ext_y if side else 6
        for tile in range(Z_TILES):
            row = 2 * tile % 8
            z_first[tile, start : start + 2, :] = packet[FACE + tile // 4, row : row + 2, :]
        if many_y == 1:
            clear_y(1 - side)

    def clear_y(side):
        nothing = jnp.zeros((1, LANES), jnp.float32)
        for kind, index, depth in face_lines(1, 2 * side - 1):
            y = ext_y + depth if side else -1 - depth
            for x in range(-1, ext_x + 1):
                put_row(kind, index, x, y, nothing)
            if kind == "pop":
                put_row(kind, index, -2, y, nothing)
                put_row(kind, index, ext_x + 1, y, nothing)
        start = 8 + ext_y if side else 6
        for tile in range(Z_TILES):
            z_first[tile, start : start + 2, :] = jnp.zeros((2, LANES), jnp.float32)

    def place_z(value, start, size, side):
        rows = pl.ds(start, size)
        inside = spot[:size] >= 2 + ext_x if side else spot[:size] < 2
        for tile in range(Z_TILES):
            shift = (2 + ext_x if side else 0) - 2 * tile
            moved = pltpu.roll(value, shift % LANES, 1)[:size]
            z_first[tile, rows, :] = jnp.where(inside, moved, z_first[tile, rows, :])

    def place_x(slot, side):
        packet = from_x[slot]
        for line, (kind, index, depth) in enumerate(face_lines(0, 2 * side - 1)):
            x = ext_x + depth if side else -1 - depth
            if kind == "pop":
                first[index, x + 2, inner, :] = packet[line]
            else:
                fields[index, x + 1, inner, :] = packet[line]
        for part in range(ext_y // 8):
            place_z(packet[FACE, pl.ds(8 * part, 8), :], 8 + 8 * part, 8, side)

    def place_xy(slot_x, slot_y, side_x, side_y):
        packet = from_xy[many_x * slot_y + slot_x]
        for line, (kind, index, far_x, far_y) in enumerate(edge_lines(2 * side_x - 1, 2 * side_y - 1)):
            x = ext_x + far_x if side_x else -1 - far_x
            y = ext_y + far_y if side_y else -1 - far_y
            put_row(kind, index, x, y, packet[line // 8, line % 8 : line % 8 + 1, :])
        place_z(packet[EDGE // 8], 8 + ext_y if side_y else 6, 2, side_x)

    for slot_y in range(many_y):
        on_side(py, slot_y, functools.partial(place_y, slot_y))
    for slot_x in range(many_x):
        on_side(px, slot_x, functools.partial(place_x, slot_x))
        for slot_y in range(many_y):
            on_side(
                py,
                slot_y,
                lambda side_y: on_side(px, slot_x, lambda side_x: place_xy(slot_x, slot_y, side_x, side_y)),
            )

    parts = (ext_y + 2 + 7) // 8

    @pl.loop(0, ext_x + 2)
    def _(x):
        for part in range(parts):
            row = 7 + 8 * part
            pulled = []
            for j in range(19):
                cx, cy, cz = VELOCITIES[j]
                rows = pl.ds(row + cy, 8)
                value = first[j, x + 1 + cx, rows, :]
                if cz == 1:
                    group = Z_UP.index(j)
                    edge = z_first[ABOVE + 1, rows, :]
                    edge = pltpu.roll(edge, LANES - 2 - GROUP * group - cx - x, 1)
                    value = jnp.where(lane == LANES - 1, edge, pltpu.roll(value, LANES - 1, 1))
                elif cz == -1:
                    group = Z_DOWN.index(j)
                    edge = z_first[BELOW + 1, rows, :]
                    edge = pltpu.roll(edge, LANES - 1 - GROUP * group - cx - x, 1)
                    value = jnp.where(lane == 0, edge, pltpu.roll(value, 1, 1))
                pulled.append(value)
            rows = pl.ds(row, 8)
            rho, ux, uy, uz, kind = [fields[k, x, rows, :] for k in range(5)]
            after, gain = collide(pulled, rho, ux, uy, uz, kind > 1.5, range(19))
            for j in range(19):
                second[j, x, rows, :] = jnp.where(kind > 0.5, after[j], 0.0)
            change[x, rows, :] = gain

    for part in range(parts):
        row = 7 + 8 * part

        def both(low_tile, high_tile, group, cx, cy):
            rows = pl.ds(row + cy, 8)
            low = pltpu.roll(z_first[low_tile, rows, :], (-GROUP * group - cx) % LANES, 1)
            high = pltpu.roll(z_first[high_tile, rows, :], (LANES // 2 - GROUP * group - cx) % LANES, 1)
            return jnp.where(lane < LANES // 2, low, high)

        pulled = []
        for j in range(19):
            cx, cy, cz = VELOCITIES[j]
            if cz == 0:
                tile, group = Z_PLACE[("pop", j)]
                pulled.append(both(BELOW + tile, ABOVE + tile, group, cx, cy))
            elif cz == 1:
                pulled.append(both(OWN_LOW, ABOVE + 2, Z_UP.index(j), cx, cy))
            else:
                pulled.append(both(BELOW + 2, OWN_HIGH, Z_DOWN.index(j), cx, cy))
        rho, ux, uy, uz, kind = [
            both(BELOW + tile, ABOVE + tile, group, 0, 0)
            for tile, group in [Z_PLACE[("field", k)] for k in range(5)]
        ]
        after, _ = collide(pulled, rho, ux, uy, uz, kind > 1.5, Z_UP + Z_DOWN)
        for group in range(5):
            value = jnp.where(lane < LANES // 2, after[Z_DOWN[group]], after[Z_UP[group]])
            z_second[group, pl.ds(row, 8), :] = jnp.where(kind > 0.5, value, 0.0)

    def copies(x):
        return (
            pltpu.make_async_copy(held.at[:, x], out.at[:, x], sems.at[0, x]),
            pltpu.make_async_copy(held_sens.at[x], sens.at[x], sems.at[1, x]),
        )

    @pl.loop(0, ext_x)
    def _(x):
        for part in range(ext_y // 8):
            row = 8 + 8 * part
            at = (x, pl.ds(8 * part, 8), every)
            pulled = []
            for j in range(19):
                cx, cy, cz = VELOCITIES[j]
                rows = pl.ds(row + cy, 8)
                value = second[j, x + 1 + cx, rows, :]
                if cz == 1:
                    edge = z_second[Z_UP.index(j), rows, :]
                    edge = pltpu.roll(edge, LANES // 2 - 3 - cx - x, 1)
                    value = jnp.where(lane == LANES - 1, edge, pltpu.roll(value, LANES - 1, 1))
                elif cz == -1:
                    edge = z_second[Z_DOWN.index(j), rows, :]
                    edge = pltpu.roll(edge, LANES - 2 - cx - x, 1)
                    value = jnp.where(lane == 0, edge, pltpu.roll(value, 1, 1))
                pulled.append(value)
            after, gain = collide(
                pulled,
                den[(0, *at)],
                vel[(0, 0, *at)],
                vel[(0, 1, *at)],
                vel[(0, 2, *at)],
                mask[at] > 0,
                range(19),
            )
            for j in range(19):
                held[(j, *at)] = after[j]
            held_sens[at] = change[x + 1, pl.ds(row, 8), :] + gain
        for copy in copies(x):
            copy.start()

    for x in range(ext_x):
        for copy in copies(x):
            copy.wait()


def shards(adjoint, density, velocity, pore_mask):
    ext_x, ext_y, ext_z = pore_mask.shape
    assert ext_z == LANES and ext_y % 8 == 0 and ext_x + 4 <= GROUP and ext_x == 8
    many_x = 2
    many_y, many_z = [1 if lax.axis_size(axis) == 2 else 2 for axis in ("gy", "gz")]
    vmem = pl.BlockSpec(memory_space=pltpu.VMEM)
    hbm = pl.BlockSpec(memory_space=pltpu.HBM)
    inputs = (adjoint, density, velocity, pore_mask)

    def array(*shape):
        return jax.ShapeDtypeStruct(shape, jnp.float32)

    def call(kernel, name, operands, shapes, limit, **more):
        more.setdefault("out_specs", [vmem] * len(shapes))
        more.setdefault("in_specs", [vmem] * len(operands))
        params = pltpu.CompilerParams(vmem_limit_bytes=limit * 1024 * 1024)
        return pl.pallas_call(kernel, out_shape=shapes, compiler_params=params, name=name, **more)(*operands)

    def partners(axis, slot):
        size = lax.axis_size(axis)
        found = {at: at for at in range(size)}
        for at in range(slot, size - 1, 2):
            found[at], found[at + 1] = at + 1, at
        return found

    def swap(value, *places):
        axes = [axis for axis, _ in places]
        tables = [partners(axis, slot) for axis, slot in places]
        if len(places) == 1:
            return lax.ppermute(value, axes[0], sorted(tables[0].items()))
        size = lax.axis_size(axes[1])
        pairs = [
            (at * size + at_y, to * size + to_y)
            for at, to in sorted(tables[0].items())
            for at_y, to_y in sorted(tables[1].items())
        ]
        return lax.ppermute(value, tuple(axes), pairs)

    near, *to_z = call(
        functools.partial(pack_z_kernel, many_z),
        "pack_z",
        inputs,
        [array(2, ext_y, LANES)] + [array(3, ext_y, LANES)] * many_z,
        56,
        in_specs=[hbm] * 4,
        scratch_shapes=[pltpu.VMEM(value.shape, value.dtype) for value in inputs]
        + [pltpu.SemaphoreType.DMA((ext_x + 3,))],
    )
    from_z = [swap(value, ("gz", slot)) for slot, value in enumerate(to_z)]

    z_set, *packets = call(
        functools.partial(pack_xy_kernel, (many_x, many_y, many_z)),
        "pack_xy",
        (*inputs, near, *from_z),
        [array(Z_TILES, ext_y, LANES)]
        + [array(FACE + 1, ext_y, LANES)] * many_x
        + [array(FACE + 2, ext_x, LANES)] * many_y
        + [array(EDGE // 8 + 1, 8, LANES)] * (many_x * many_y),
        8,
        scratch_shapes=[pltpu.VMEM((2, ext_y, LANES), jnp.float32)],
    )
    to_x, to_y, to_xy = packets[:many_x], packets[many_x : many_x + many_y], packets[many_x + many_y :]
    from_xy = [
        swap(to_xy[many_x * slot_y + slot_x], ("gx", slot_x), ("gy", slot_y))
        for slot_y in range(many_y)
        for slot_x in range(many_x)
    ]
    from_y = [swap(value, ("gy", slot)) for slot, value in enumerate(to_y)]
    from_x = [swap(value, ("gx", slot)) for slot, value in enumerate(to_x)]

    rows = ext_y + 16
    scratch = [
        pltpu.VMEM((19, ext_x + 4, rows, LANES), jnp.float32),
        pltpu.VMEM((5, ext_x + 2, rows, LANES), jnp.float32),
        pltpu.VMEM((19, ext_x + 2, rows, LANES), jnp.float32),
        pltpu.VMEM((ext_x + 2, rows, LANES), jnp.float32),
        pltpu.VMEM((Z_TILES, rows, LANES), jnp.float32),
        pltpu.VMEM((5, rows, LANES), jnp.float32),
        pltpu.VMEM((19, ext_x, ext_y, LANES), jnp.float32),
        pltpu.VMEM((ext_x, ext_y, LANES), jnp.float32),
        pltpu.SemaphoreType.DMA((2, ext_x)),
    ]
    return call(
        functools.partial(step_kernel, (many_x, many_y)),
        "two_steps",
        (*inputs, z_set, *from_x, *from_y, *from_xy),
        [array(19, ext_x, ext_y, LANES), array(ext_x, ext_y, LANES)],
        24,
        out_specs=[hbm] * 2,
        scratch_shapes=scratch,
    )


def solution(mesh):
    placed = (
        P(None, "gx", "gy", "gz"),
        P(None, "gx", "gy", "gz"),
        P(None, None, "gx", "gy", "gz"),
        P("gx", "gy", "gz"),
    )

    def whole(*arrays):
        return tuple(shards(*arrays))

    return jax.shard_map(
        whole,
        mesh=mesh,
        in_specs=placed,
        out_specs=(P(None, "gx", "gy", "gz"), P("gx", "gy", "gz")),
        check_vma=False,
    )
```

```python
import functools

import jax
import jax.numpy as jnp
from jax import lax
from jax.experimental import pallas as pl
from jax.experimental.pallas import tpu as pltpu
from jax.sharding import PartitionSpec as P

VELOCITIES = [
    (0, 0, 0),
    (1, 0, 0),
    (-1, 0, 0),
    (0, 1, 0),
    (0, -1, 0),
    (0, 0, 1),
    (0, 0, -1),
    (1, 1, 0),
    (-1, -1, 0),
    (1, -1, 0),
    (-1, 1, 0),
    (1, 0, 1),
    (-1, 0, -1),
    (1, 0, -1),
    (-1, 0, 1),
    (0, 1, 1),
    (0, -1, -1),
    (0, 1, -1),
    (0, -1, 1),
]
OPPOSITE = [0, 2, 1, 4, 3, 6, 5, 8, 7, 10, 9, 12, 11, 14, 13, 16, 15, 18, 17]
OMEGA = 1.25
LANES = 128
GROUP = 16


def pops(axis, sign):
    return [j for j in range(19) if VELOCITIES[j][axis] == sign]


def mirrored(j):
    cx, cy, cz = VELOCITIES[j]
    return VELOCITIES.index((cx, cy, -cz))


Z_FLAT = pops(2, 0)
Z_UP = pops(2, 1)
Z_DOWN = [mirrored(j) for j in Z_UP]
RHO, UX, UY, UZ, KIND = range(5)
Z_PLACE = {("pop", j): (0, g) for g, j in enumerate(Z_FLAT[:8])}
Z_PLACE[("pop", Z_FLAT[8])] = (1, 5)
Z_PLACE[("field", RHO)] = (1, 6)
Z_PLACE[("field", KIND)] = (1, 7)
Z_PLACE[("field", UX)] = (2, 5)
Z_PLACE[("field", UY)] = (2, 6)
Z_PLACE[("field", UZ)] = (2, 7)
BELOW, ABOVE, OWN_LOW, OWN_HIGH, Z_TILES = 0, 3, 6, 7, 8


def face_lines(axis, toward):
    near = pops(axis, 0) + pops(axis, toward)
    lines = [("pop", j, 0) for j in near] + [("field", k, 0) for k in range(5)]
    return lines + [("pop", j, 1) for j in pops(axis, toward)]


def edge_lines(toward_x, toward_y):
    lines = [("field", k, 0, 0) for k in range(5)]
    for j in range(19):
        cx, cy, _ = VELOCITIES[j]
        if cx not in (0, toward_x) or cy not in (0, toward_y):
            continue
        lines.append(("pop", j, 0, 0))
        if cx:
            lines.append(("pop", j, 1, 0))
        if cy:
            lines.append(("pop", j, 0, 1))
        if cx and cy:
            lines.append(("pop", j, 1, 1))
    return lines


FACE = 24
EDGE = 24


def lane_ids():
    return lax.broadcasted_iota(jnp.int32, (8, LANES), 1)


def field_of(refs, kind, index, at):
    adj, den, vel, mask = refs
    if kind == "pop":
        return adj[(index, *at)]
    if index == RHO:
        return den[(1, *at)]
    if index == KIND:
        return (mask[at] + 1).astype(jnp.float32)
    return vel[(1, index - UX, *at)]


def parity_of(axis):
    return lax.rem(lax.axis_index(axis), 2)


def on_side(parity, slot, act):
    @pl.when(parity == slot)
    def _():
        act(1)

    @pl.when(parity != slot)
    def _():
        act(0)


def has_partner(axis, slot):
    at = lax.axis_index(axis)
    to = at + jnp.where(lax.rem(at, 2) == slot, 1, -1)
    return (to >= 0) & (to < lax.axis_size(axis))


def pack_z_kernel(slots, adj_in, den_in, vel_in, mask_in, near, *rest):
    packets, (adj, den, vel, mask, sems) = rest[:slots], rest[slots:]
    refs = (adj, den, vel, mask)
    ext_x, ext_y, _ = mask.shape
    loads = [
        pltpu.make_async_copy(source, target, sems.at[ext_x + at])
        for at, (source, target) in enumerate([(den_in.at[1], den.at[1]), (vel_in.at[1], vel.at[1]), (mask_in, mask)])
    ]
    plane_loads = [pltpu.make_async_copy(adj_in.at[:, x], adj.at[:, x], sems.at[x]) for x in range(ext_x)]
    for load in loads + plane_loads:
        load.start()
    for load in loads:
        load.wait()
    lane = lane_ids()
    parity = parity_of("gz")
    parts = range(ext_y // 8)
    zero = jnp.zeros((8, LANES), jnp.float32)
    lows, highs = [[zero] * 3 for _ in parts], [[zero] * 3 for _ in parts]
    far_low, far_high = [zero for _ in parts], [zero for _ in parts]
    for x in range(ext_x):
        plane_loads[x].wait()
        for part in parts:
            at = (x, pl.ds(8 * part, 8), slice(None))
            for (kind, index), (tile, group) in Z_PLACE.items():
                spot = GROUP * group + 2 + x
                moved = pltpu.roll(field_of(refs, kind, index, at), spot, 1)
                lows[part][tile] = jnp.where(lane == spot, moved, lows[part][tile])
                highs[part][tile] = jnp.where(lane == spot - 1, moved, highs[part][tile])
            for group in range(5):
                spot = GROUP * group + 2 + x
                moved = pltpu.roll(field_of(refs, "pop", Z_UP[group], at), spot, 1)
                lows[part][1] = jnp.where(lane == spot, moved, lows[part][1])
                far_low[part] = jnp.where(lane == spot + 1, moved, far_low[part])
                moved = pltpu.roll(field_of(refs, "pop", Z_DOWN[group], at), spot, 1)
                highs[part][1] = jnp.where(lane == spot - 1, moved, highs[part][1])
                far_high[part] = jnp.where(lane == spot - 2, moved, far_high[part])
    for part in parts:
        rows = pl.ds(8 * part, 8)
        low = lows[part]
        high = [pltpu.roll(tile, 1, 1) for tile in highs[part]]
        low[2] = jnp.where(lane < 5 * GROUP, pltpu.roll(far_low[part], LANES - 1, 1), low[2])
        high[2] = jnp.where(lane < 5 * GROUP, pltpu.roll(far_high[part], 2, 1), high[2])
        near[0, rows, :] = low[1]
        near[1, rows, :] = high[1]
        for slot in range(slots):
            there = has_partner("gz", slot)
            for tile in range(3):
                value = jnp.where(parity == slot, high[tile], low[tile])
                packets[slot][tile, rows, :] = jnp.where(there, value, 0.0)


def pack_xy_kernel(slots, adj, den, vel, mask, near, *rest):
    many_x, many_y, many_z = slots
    from_z, z_set = rest[:many_z], rest[many_z]
    to_x = rest[many_z + 1 : many_z + 1 + many_x]
    to_y = rest[many_z + 1 + many_x : many_z + 1 + many_x + many_y]
    to_xy, faces = rest[many_z + 1 + many_x + many_y : -1], rest[-1]
    refs = (adj, den, vel, mask)
    ext_x, ext_y, _ = mask.shape
    spot = lane_ids() % GROUP
    every = slice(None)
    px, py, pz = parity_of("gx"), parity_of("gy"), parity_of("gz")

    z_set[OWN_LOW] = near[0]
    z_set[OWN_HIGH] = near[1]
    for tile in range(3):
        first = from_z[0][tile]
        second = from_z[1][tile] if many_z > 1 else jnp.zeros_like(first)
        z_set[ABOVE + tile] = jnp.where(pz == 0, first, second)
        z_set[BELOW + tile] = jnp.where(pz == 0, second, first)

    for side in range(2):
        for part in range(ext_y // 8):
            rows = pl.ds(8 * part, 8)
            value = jnp.zeros((8, LANES), jnp.float32)
            for tile in range(Z_TILES):
                start = ext_x if side else 2
                moved = pltpu.roll(z_set[tile, rows, :], (2 * tile - start) % LANES, 1)
                value = jnp.where(spot // 2 == tile, moved, value)
            faces[side, rows, :] = value

    def pack_xy(slot_x, slot_y, side_x, side_y):
        packet = to_xy[many_x * slot_y + slot_x]
        for line, (kind, index, far_x, far_y) in enumerate(edge_lines(1 - 2 * side_x, 1 - 2 * side_y)):
            x = ext_x - 1 - far_x if side_x else far_x
            y = ext_y - 1 - far_y if side_y else far_y
            packet[line // 8, line % 8 : line % 8 + 1, :] = field_of(refs, kind, index, (x, slice(y, y + 1), every))
        start = ext_y - 2 if side_y else 0
        packet[EDGE // 8, 0:2, :] = faces[side_x, start : start + 2, :]

    def pack_y(slot, side):
        packet = to_y[slot]
        for line, (kind, index, depth) in enumerate(face_lines(1, 1 - 2 * side)):
            y = ext_y - 1 - depth if side else depth
            for x in range(ext_x):
                packet[line, x : x + 1, :] = field_of(refs, kind, index, (x, slice(y, y + 1), every))
        start = ext_y - 2 if side else 0
        for tile in range(Z_TILES):
            row = 2 * tile % 8
            packet[FACE + tile // 4, row : row + 2, :] = z_set[tile, start : start + 2, :]

    def pack_x(slot, side):
        for line, (kind, index, depth) in enumerate(face_lines(0, 1 - 2 * side)):
            x = ext_x - 1 - depth if side else depth
            to_x[slot][line] = field_of(refs, kind, index, (x, every, every))
        to_x[slot][FACE] = faces[side]

    def when_there(there, packet, act):
        pl.when(there)(act)

        @pl.when(jnp.logical_not(there))
        def _():
            packet[...] = jnp.zeros(packet.shape, jnp.float32)

    for slot_y in range(many_y):
        there_y = has_partner("gy", slot_y)
        when_there(there_y, to_y[slot_y], lambda: on_side(py, slot_y, functools.partial(pack_y, slot_y)))
        for slot_x in range(many_x):
            when_there(
                there_y & has_partner("gx", slot_x),
                to_xy[many_x * slot_y + slot_x],
                lambda: on_side(
                    py,
                    slot_y,
                    lambda side_y: on_side(px, slot_x, lambda side_x: pack_xy(slot_x, slot_y, side_x, side_y)),
                ),
            )
    for slot_x in range(many_x):
        when_there(
            has_partner("gx", slot_x), to_x[slot_x], lambda: on_side(px, slot_x, functools.partial(pack_x, slot_x))
        )


def collide(pulled, rho, ux, uy, uz, fluid, wanted):
    total = {}
    diff = {}
    for j in range(1, 19, 2):
        total[j] = pulled[j] + pulled[j + 1]
        diff[j] = pulled[j] - pulled[j + 1]
    in_xy, in_xz, in_yz = total[7] + total[9], total[11] + total[13], total[15] + total[17]
    two_x, two_y, two_z = total[1] + total[1], total[3] + total[3], total[5] + total[5]
    count = (12.0 * pulled[0] + (two_x + two_y)) + (two_z + (in_xy + (in_xz + in_yz)))
    flow_x = (diff[1] + diff[1]) + ((diff[7] + diff[9]) + (diff[11] + diff[13]))
    flow_y = (diff[3] + diff[3]) + ((diff[7] - diff[9]) + (diff[15] + diff[17]))
    flow_z = (diff[5] + diff[5]) + ((diff[11] - diff[13]) + (diff[15] - diff[17]))
    xx, yy, zz = two_x + (in_xy + in_xz), two_y + (in_xy + in_yz), two_z + (in_xz + in_yz)
    xy, xz, yz = total[7] - total[9], total[11] - total[13], total[15] - total[17]
    push_x = xx * ux + xy * uy + xz * uz
    push_y = xy * ux + yy * uy + yz * uz
    push_z = xz * ux + yz * uy + zz * uz
    usq = ux * ux + uy * uy + uz * uz
    push = ux * push_x + uy * push_y + uz * push_z
    inverse = 1.0 / rho
    base = count * (OMEGA / 36.0 + (OMEGA / 24.0) * usq) - (OMEGA / 8.0) * push - ux * inverse
    along_x = (OMEGA / 12.0) * (flow_x + 3.0 * push_x - ux * count) + inverse
    along_y = (OMEGA / 12.0) * (flow_y + 3.0 * push_y - uy * count)
    along_z = (OMEGA / 12.0) * (flow_z + 3.0 * push_z - uz * count)
    parts = {
        1: along_x,
        3: along_y,
        5: along_z,
        7: along_x + along_y,
        9: along_x - along_y,
        11: along_x + along_z,
        13: along_x - along_z,
        15: along_y + along_z,
        17: along_y - along_z,
    }
    out = {}
    for j in wanted:
        if j == 0:
            shift = base
        elif j % 2:
            shift = base + parts[j]
        else:
            shift = base - parts[j - 1]
        out[j] = jnp.where(fluid, (1.0 - OMEGA) * pulled[j] + shift, pulled[OPPOSITE[j]])
    change = (-1.0 / 6.0) * rho * (flow_x * ux + flow_y * uy + flow_z * uz)
    return out, jnp.where(fluid, change, 0.0)


def step_kernel(slots, adj, den, vel, mask, z_set, *rest):
    many_x, many_y = slots
    from_x, from_y = rest[:many_x], rest[many_x : many_x + many_y]
    from_xy = rest[many_x + many_y : many_x + many_y + many_x * many_y]
    out, sens, first, fields, second, change, z_first, z_second, held, held_sens, sems = rest[-11:]
    refs = (adj, den, vel, mask)
    ext_x, ext_y, _ = mask.shape
    lane = lane_ids()
    spot = lane % GROUP
    every = slice(None)
    inner = pl.ds(8, ext_y)
    px, py = parity_of("gx"), parity_of("gy")

    def put_row(kind, index, x, y, value):
        row = y + 8
        if kind == "pop":
            first[index, x + 2, row : row + 1, :] = value
        else:
            fields[index, x + 1, row : row + 1, :] = value

    for j in range(19):
        first[j, 2 : 2 + ext_x, inner, :] = adj[j]
    for k in range(5):
        fields[k, 1 : 1 + ext_x, inner, :] = field_of(refs, "field", k, (every, every, every))
    z_first[:, inner, :] = z_set[...]

    def place_y(slot, side):
        packet = from_y[slot]
        for line, (kind, index, depth) in enumerate(face_lines(1, 2 * side - 1)):
            y = ext_y + depth if side else -1 - depth
            for x in range(ext_x):
                put_row(kind, index, x, y, packet[line, x : x + 1, :])
        start = 8 + ext_y if side else 6
        for tile in range(Z_TILES):
            row = 2 * tile % 8
            z_first[tile, start : start + 2, :] = packet[FACE + tile // 4, row : row + 2, :]
        if many_y == 1:
            clear_y(1 - side)

    def clear_y(side):
        nothing = jnp.zeros((1, LANES), jnp.float32)
        for kind, index, depth in face_lines(1, 2 * side - 1):
            y = ext_y + depth if side else -1 - depth
            for x in range(-1, ext_x + 1):
                put_row(kind, index, x, y, nothing)
            if kind == "pop":
                put_row(kind, index, -2, y, nothing)
                put_row(kind, index, ext_x + 1, y, nothing)
        start = 8 + ext_y if side else 6
        for tile in range(Z_TILES):
            z_first[tile, start : start + 2, :] = jnp.zeros((2, LANES), jnp.float32)

    def place_z(value, start, size, side):
        rows = pl.ds(start, size)
        inside = spot[:size] >= 2 + ext_x if side else spot[:size] < 2
        for tile in range(Z_TILES):
            shift = (2 + ext_x if side else 0) - 2 * tile
            moved = pltpu.roll(value, shift % LANES, 1)[:size]
            z_first[tile, rows, :] = jnp.where(inside, moved, z_first[tile, rows, :])

    def place_x(slot, side):
        packet = from_x[slot]
        for line, (kind, index, depth) in enumerate(face_lines(0, 2 * side - 1)):
            x = ext_x + depth if side else -1 - depth
            if kind == "pop":
                first[index, x + 2, inner, :] = packet[line]
            else:
                fields[index, x + 1, inner, :] = packet[line]
        for part in range(ext_y // 8):
            place_z(packet[FACE, pl.ds(8 * part, 8), :], 8 + 8 * part, 8, side)

    def place_xy(slot_x, slot_y, side_x, side_y):
        packet = from_xy[many_x * slot_y + slot_x]
        for line, (kind, index, far_x, far_y) in enumerate(edge_lines(2 * side_x - 1, 2 * side_y - 1)):
            x = ext_x + far_x if side_x else -1 - far_x
            y = ext_y + far_y if side_y else -1 - far_y
            put_row(kind, index, x, y, packet[line // 8, line % 8 : line % 8 + 1, :])
        place_z(packet[EDGE // 8], 8 + ext_y if side_y else 6, 2, side_x)

    for slot_y in range(many_y):
        on_side(py, slot_y, functools.partial(place_y, slot_y))
    for slot_x in range(many_x):
        on_side(px, slot_x, functools.partial(place_x, slot_x))
        for slot_y in range(many_y):
            on_side(
                py,
                slot_y,
                lambda side_y: on_side(px, slot_x, lambda side_x: place_xy(slot_x, slot_y, side_x, side_y)),
            )

    parts = (ext_y + 2 + 7) // 8

    @pl.loop(0, ext_x + 2)
    def _(x):
        for part in range(parts):
            row = 7 + 8 * part
            pulled = []
            for j in range(19):
                cx, cy, cz = VELOCITIES[j]
                rows = pl.ds(row + cy, 8)
                value = first[j, x + 1 + cx, rows, :]
                if cz == 1:
                    group = Z_UP.index(j)
                    edge = z_first[ABOVE + 1, rows, :]
                    edge = pltpu.roll(edge, LANES - 2 - GROUP * group - cx - x, 1)
                    value = jnp.where(lane == LANES - 1, edge, pltpu.roll(value, LANES - 1, 1))
                elif cz == -1:
                    group = Z_DOWN.index(j)
                    edge = z_first[BELOW + 1, rows, :]
                    edge = pltpu.roll(edge, LANES - 1 - GROUP * group - cx - x, 1)
                    value = jnp.where(lane == 0, edge, pltpu.roll(value, 1, 1))
                pulled.append(value)
            rows = pl.ds(row, 8)
            rho, ux, uy, uz, kind = [fields[k, x, rows, :] for k in range(5)]
            after, gain = collide(pulled, rho, ux, uy, uz, kind > 1.5, range(19))
            for j in range(19):
                second[j, x, rows, :] = jnp.where(kind > 0.5, after[j], 0.0)
            change[x, rows, :] = gain

    for part in range(parts):
        row = 7 + 8 * part

        def both(low_tile, high_tile, group, cx, cy):
            rows = pl.ds(row + cy, 8)
            low = pltpu.roll(z_first[low_tile, rows, :], (-GROUP * group - cx) % LANES, 1)
            high = pltpu.roll(z_first[high_tile, rows, :], (LANES // 2 - GROUP * group - cx) % LANES, 1)
            return jnp.where(lane < LANES // 2, low, high)

        pulled = []
        for j in range(19):
            cx, cy, cz = VELOCITIES[j]
            if cz == 0:
                tile, group = Z_PLACE[("pop", j)]
                pulled.append(both(BELOW + tile, ABOVE + tile, group, cx, cy))
            elif cz == 1:
                pulled.append(both(OWN_LOW, ABOVE + 2, Z_UP.index(j), cx, cy))
            else:
                pulled.append(both(BELOW + 2, OWN_HIGH, Z_DOWN.index(j), cx, cy))
        rho, ux, uy, uz, kind = [
            both(BELOW + tile, ABOVE + tile, group, 0, 0)
            for tile, group in [Z_PLACE[("field", k)] for k in range(5)]
        ]
        after, _ = collide(pulled, rho, ux, uy, uz, kind > 1.5, Z_UP + Z_DOWN)
        for group in range(5):
            value = jnp.where(lane < LANES // 2, after[Z_DOWN[group]], after[Z_UP[group]])
            z_second[group, pl.ds(row, 8), :] = jnp.where(kind > 0.5, value, 0.0)

    def copies(x):
        return (
            pltpu.make_async_copy(held.at[:, x], out.at[:, x], sems.at[0, x]),
            pltpu.make_async_copy(held_sens.at[x], sens.at[x], sems.at[1, x]),
        )

    @pl.loop(0, ext_x)
    def _(x):
        for part in range(ext_y // 8):
            row = 8 + 8 * part
            at = (x, pl.ds(8 * part, 8), every)
            pulled = []
            for j in range(19):
                cx, cy, cz = VELOCITIES[j]
                rows = pl.ds(row + cy, 8)
                value = second[j, x + 1 + cx, rows, :]
                if cz == 1:
                    edge = z_second[Z_UP.index(j), rows, :]
                    edge = pltpu.roll(edge, LANES // 2 - 3 - cx - x, 1)
                    value = jnp.where(lane == LANES - 1, edge, pltpu.roll(value, LANES - 1, 1))
                elif cz == -1:
                    edge = z_second[Z_DOWN.index(j), rows, :]
                    edge = pltpu.roll(edge, LANES - 2 - cx - x, 1)
                    value = jnp.where(lane == 0, edge, pltpu.roll(value, 1, 1))
                pulled.append(value)
            after, gain = collide(
                pulled,
                den[(0, *at)],
                vel[(0, 0, *at)],
                vel[(0, 1, *at)],
                vel[(0, 2, *at)],
                mask[at] > 0,
                range(19),
            )
            for j in range(19):
                held[(j, *at)] = after[j]
            held_sens[at] = change[x + 1, pl.ds(row, 8), :] + gain
        for copy in copies(x):
            copy.start()

    for x in range(ext_x):
        for copy in copies(x):
            copy.wait()


def shards(adjoint, density, velocity, pore_mask):
    ext_x, ext_y, ext_z = pore_mask.shape
    assert ext_z == LANES and ext_y % 8 == 0 and ext_x + 4 <= GROUP and ext_x == 8
    many_x = 2
    many_y, many_z = [1 if lax.axis_size(axis) == 2 else 2 for axis in ("gy", "gz")]
    vmem = pl.BlockSpec(memory_space=pltpu.VMEM)
    hbm = pl.BlockSpec(memory_space=pltpu.HBM)
    inputs = (adjoint, density, velocity, pore_mask)

    def array(*shape):
        return jax.ShapeDtypeStruct(shape, jnp.float32)

    def call(kernel, name, operands, shapes, limit, **more):
        more.setdefault("out_specs", [vmem] * len(shapes))
        more.setdefault("in_specs", [vmem] * len(operands))
        params = pltpu.CompilerParams(vmem_limit_bytes=limit * 1024 * 1024)
        return pl.pallas_call(kernel, out_shape=shapes, compiler_params=params, name=name, **more)(*operands)

    def partners(axis, slot):
        size = lax.axis_size(axis)
        found = {at: at for at in range(size)}
        for at in range(slot, size, 2):
            to = (at + 1) % size
            if found[at] == at and found[to] == to:
                found[at], found[to] = to, at
        return found

    def swap(value, *places):
        axes = [axis for axis, _ in places]
        tables = [partners(axis, slot) for axis, slot in places]
        if len(places) == 1:
            return lax.ppermute(value, axes[0], sorted(tables[0].items()))
        size = lax.axis_size(axes[1])
        pairs = [
            (at * size + at_y, to * size + to_y)
            for at, to in sorted(tables[0].items())
            for at_y, to_y in sorted(tables[1].items())
        ]
        return lax.ppermute(value, tuple(axes), pairs)

    near, *to_z = call(
        functools.partial(pack_z_kernel, many_z),
        "pack_z",
        inputs,
        [array(2, ext_y, LANES)] + [array(3, ext_y, LANES)] * many_z,
        56,
        in_specs=[hbm] * 4,
        scratch_shapes=[pltpu.VMEM(value.shape, value.dtype) for value in inputs]
        + [pltpu.SemaphoreType.DMA((ext_x + 3,))],
    )
    from_z = [swap(value, ("gz", slot)) for slot, value in enumerate(to_z)]

    z_set, *packets = call(
        functools.partial(pack_xy_kernel, (many_x, many_y, many_z)),
        "pack_xy",
        (*inputs, near, *from_z),
        [array(Z_TILES, ext_y, LANES)]
        + [array(FACE + 1, ext_y, LANES)] * many_x
        + [array(FACE + 2, ext_x, LANES)] * many_y
        + [array(EDGE // 8 + 1, 8, LANES)] * (many_x * many_y),
        8,
        scratch_shapes=[pltpu.VMEM((2, ext_y, LANES), jnp.float32)],
    )
    to_x, to_y, to_xy = packets[:many_x], packets[many_x : many_x + many_y], packets[many_x + many_y :]
    from_xy = [
        swap(to_xy[many_x * slot_y + slot_x], ("gx", slot_x), ("gy", slot_y))
        for slot_y in range(many_y)
        for slot_x in range(many_x)
    ]
    from_y = [swap(value, ("gy", slot)) for slot, value in enumerate(to_y)]
    from_x = [swap(value, ("gx", slot)) for slot, value in enumerate(to_x)]

    rows = ext_y + 16
    scratch = [
        pltpu.VMEM((19, ext_x + 4, rows, LANES), jnp.float32),
        pltpu.VMEM((5, ext_x + 2, rows, LANES), jnp.float32),
        pltpu.VMEM((19, ext_x + 2, rows, LANES), jnp.float32),
        pltpu.VMEM((ext_x + 2, rows, LANES), jnp.float32),
        pltpu.VMEM((Z_TILES, rows, LANES), jnp.float32),
        pltpu.VMEM((5, rows, LANES), jnp.float32),
        pltpu.VMEM((19, ext_x, ext_y, LANES), jnp.float32),
        pltpu.VMEM((ext_x, ext_y, LANES), jnp.float32),
        pltpu.SemaphoreType.DMA((2, ext_x)),
    ]
    return call(
        functools.partial(step_kernel, (many_x, many_y)),
        "two_steps",
        (*inputs, z_set, *from_x, *from_y, *from_xy),
        [array(19, ext_x, ext_y, LANES), array(ext_x, ext_y, LANES)],
        24,
        out_specs=[hbm] * 2,
        scratch_shapes=scratch,
    )


def solution(mesh):
    placed = (
        P(None, "gx", "gy", "gz"),
        P(None, "gx", "gy", "gz"),
        P(None, None, "gx", "gy", "gz"),
        P("gx", "gy", "gz"),
    )

    def whole(*arrays):
        return tuple(shards(*arrays))

    return jax.shard_map(
        whole,
        mesh=mesh,
        in_specs=placed,
        out_specs=(P(None, "gx", "gy", "gz"), P("gx", "gy", "gz")),
        check_vma=False,
    )
```

```python
import functools
import itertools

import jax
import jax.numpy as jnp
from jax import lax
from jax.experimental import pallas as pl
from jax.experimental.pallas import tpu as pltpu
from jax.sharding import PartitionSpec as P

VELOCITIES = [
    (0, 0, 0),
    (1, 0, 0),
    (-1, 0, 0),
    (0, 1, 0),
    (0, -1, 0),
    (0, 0, 1),
    (0, 0, -1),
    (1, 1, 0),
    (-1, -1, 0),
    (1, -1, 0),
    (-1, 1, 0),
    (1, 0, 1),
    (-1, 0, -1),
    (1, 0, -1),
    (-1, 0, 1),
    (0, 1, 1),
    (0, -1, -1),
    (0, 1, -1),
    (0, -1, 1),
]
OPPOSITE = [0, 2, 1, 4, 3, 6, 5, 8, 7, 10, 9, 12, 11, 14, 13, 16, 15, 18, 17]
OMEGA = 1.25
LANES = 128
GROUP = 16


def pops(axis, sign):
    return [j for j in range(19) if VELOCITIES[j][axis] == sign]


def mirrored(j):
    cx, cy, cz = VELOCITIES[j]
    return VELOCITIES.index((cx, cy, -cz))


Z_FLAT = pops(2, 0)
Z_UP = pops(2, 1)
Z_DOWN = [mirrored(j) for j in Z_UP]
RHO, UX, UY, UZ, KIND = range(5)
Z_PLACE = {("pop", j): (0, g) for g, j in enumerate(Z_FLAT[:8])}
Z_PLACE[("pop", Z_FLAT[8])] = (1, 5)
Z_PLACE[("field", RHO)] = (1, 6)
Z_PLACE[("field", KIND)] = (1, 7)
Z_PLACE[("field", UX)] = (2, 5)
Z_PLACE[("field", UY)] = (2, 6)
Z_PLACE[("field", UZ)] = (2, 7)
BELOW, ABOVE, OWN_LOW, OWN_HIGH, Z_TILES = 0, 3, 6, 7, 8


def face_lines(axis, toward):
    near = pops(axis, 0) + pops(axis, toward)
    lines = [("pop", j, 0) for j in near] + [("field", k, 0) for k in range(5)]
    return lines + [("pop", j, 1) for j in pops(axis, toward)]


def edge_lines(toward_x, toward_y):
    lines = [("field", k, 0, 0) for k in range(5)]
    for j in range(19):
        cx, cy, _ = VELOCITIES[j]
        if cx not in (0, toward_x) or cy not in (0, toward_y):
            continue
        lines.append(("pop", j, 0, 0))
        if cx:
            lines.append(("pop", j, 1, 0))
        if cy:
            lines.append(("pop", j, 0, 1))
        if cx and cy:
            lines.append(("pop", j, 1, 1))
    return lines


FACE = 24
EDGE = 24


def lane_ids():
    return lax.broadcasted_iota(jnp.int32, (8, LANES), 1)


def field_of(refs, kind, index, at):
    adj, den, vel, mask = refs
    if kind == "pop":
        return adj[(index, *at)]
    if index == RHO:
        return den[(1, *at)]
    if index == KIND:
        return (mask[at] + 1).astype(jnp.float32)
    return vel[(1, index - UX, *at)]


def parity_of(axis):
    return lax.rem(lax.axis_index(axis), 2)


def on_side(parity, slot, act):
    @pl.when(parity == slot)
    def _():
        act(1)

    @pl.when(parity != slot)
    def _():
        act(0)


def has_partner(axis, slot):
    at = lax.axis_index(axis)
    to = at + jnp.where(lax.rem(at, 2) == slot, 1, -1)
    return (to >= 0) & (to < lax.axis_size(axis))


def pack_z_kernel(slots, adj_in, den_in, vel_in, mask_in, adj, den, vel, mask, near, *rest):
    packets, sems = rest[:slots], rest[slots]
    refs = (adj, den, vel, mask)
    ext_x, ext_y, _ = mask.shape
    loads = [
        pltpu.make_async_copy(source, target, sems.at[ext_x + at])
        for at, (source, target) in enumerate([(den_in.at[1], den.at[1]), (vel_in.at[1], vel.at[1]), (mask_in, mask)])
    ]
    plane_loads = [pltpu.make_async_copy(adj_in.at[:, x], adj.at[:, x], sems.at[x]) for x in range(ext_x)]
    last_loads = [
        pltpu.make_async_copy(source, target, sems.at[ext_x + 3 + at])
        for at, (source, target) in enumerate([(den_in.at[0], den.at[0]), (vel_in.at[0], vel.at[0])])
    ]
    for load in loads + plane_loads + last_loads:
        load.start()
    for load in loads:
        load.wait()
    lane = lane_ids()
    parity = parity_of("gz")
    parts = range(ext_y // 8)
    zero = jnp.zeros((8, LANES), jnp.float32)
    lows, highs = [[zero] * 3 for _ in parts], [[zero] * 3 for _ in parts]
    far_low, far_high = [zero for _ in parts], [zero for _ in parts]
    for x in range(ext_x):
        plane_loads[x].wait()
        for part in parts:
            at = (x, pl.ds(8 * part, 8), slice(None))
            for (kind, index), (tile, group) in Z_PLACE.items():
                spot = GROUP * group + 2 + x
                moved = pltpu.roll(field_of(refs, kind, index, at), spot, 1)
                lows[part][tile] = jnp.where(lane == spot, moved, lows[part][tile])
                highs[part][tile] = jnp.where(lane == spot - 1, moved, highs[part][tile])
            for group in range(5):
                spot = GROUP * group + 2 + x
                moved = pltpu.roll(field_of(refs, "pop", Z_UP[group], at), spot, 1)
                lows[part][1] = jnp.where(lane == spot, moved, lows[part][1])
                far_low[part] = jnp.where(lane == spot + 1, moved, far_low[part])
                moved = pltpu.roll(field_of(refs, "pop", Z_DOWN[group], at), spot, 1)
                highs[part][1] = jnp.where(lane == spot - 1, moved, highs[part][1])
                far_high[part] = jnp.where(lane == spot - 2, moved, far_high[part])
    for part in parts:
        rows = pl.ds(8 * part, 8)
        low = lows[part]
        high = [pltpu.roll(tile, 1, 1) for tile in highs[part]]
        low[2] = jnp.where(lane < 5 * GROUP, pltpu.roll(far_low[part], LANES - 1, 1), low[2])
        high[2] = jnp.where(lane < 5 * GROUP, pltpu.roll(far_high[part], 2, 1), high[2])
        near[0, rows, :] = low[1]
        near[1, rows, :] = high[1]
        for slot in range(slots):
            there = has_partner("gz", slot)
            for tile in range(3):
                value = jnp.where(parity == slot, high[tile], low[tile])
                packets[slot][tile, rows, :] = jnp.where(there, value, 0.0)
    for load in last_loads:
        load.wait()


def pack_xy_kernel(slots, adj, den, vel, mask, near, *rest):
    many_x, many_y, many_z = slots
    from_z, z_set = rest[:many_z], rest[many_z]
    to_x = rest[many_z + 1 : many_z + 1 + many_x]
    to_y = rest[many_z + 1 + many_x : many_z + 1 + many_x + many_y]
    to_xy, faces = rest[many_z + 1 + many_x + many_y : -1], rest[-1]
    refs = (adj, den, vel, mask)
    ext_x, ext_y, _ = mask.shape
    spot = lane_ids() % GROUP
    every = slice(None)
    px, py, pz = parity_of("gx"), parity_of("gy"), parity_of("gz")

    z_set[OWN_LOW] = near[0]
    z_set[OWN_HIGH] = near[1]
    for tile in range(3):
        first = from_z[0][tile]
        second = from_z[1][tile] if many_z > 1 else jnp.zeros_like(first)
        z_set[ABOVE + tile] = jnp.where(pz == 0, first, second)
        z_set[BELOW + tile] = jnp.where(pz == 0, second, first)

    for side in range(2):
        for part in range(ext_y // 8):
            rows = pl.ds(8 * part, 8)
            value = jnp.zeros((8, LANES), jnp.float32)
            for tile in range(Z_TILES):
                start = ext_x if side else 2
                moved = pltpu.roll(z_set[tile, rows, :], (2 * tile - start) % LANES, 1)
                value = jnp.where(spot // 2 == tile, moved, value)
            faces[side, rows, :] = value

    def pack_xy(slot_x, slot_y, side_x, side_y):
        packet = to_xy[many_x * slot_y + slot_x]
        for line, (kind, index, far_x, far_y) in enumerate(edge_lines(1 - 2 * side_x, 1 - 2 * side_y)):
            x = ext_x - 1 - far_x if side_x else far_x
            y = ext_y - 1 - far_y if side_y else far_y
            packet[line // 8, line % 8 : line % 8 + 1, :] = field_of(refs, kind, index, (x, slice(y, y + 1), every))
        start = ext_y - 2 if side_y else 0
        packet[EDGE // 8, 0:2, :] = faces[side_x, start : start + 2, :]

    def pack_y(slot, side):
        packet = to_y[slot]
        for line, (kind, index, depth) in enumerate(face_lines(1, 1 - 2 * side)):
            y = ext_y - 1 - depth if side else depth
            for x in range(ext_x):
                packet[line, x : x + 1, :] = field_of(refs, kind, index, (x, slice(y, y + 1), every))
        start = ext_y - 2 if side else 0
        for tile in range(Z_TILES):
            row = 2 * tile % 8
            packet[FACE + tile // 4, row : row + 2, :] = z_set[tile, start : start + 2, :]

    def pack_x(slot, side):
        for line, (kind, index, depth) in enumerate(face_lines(0, 1 - 2 * side)):
            x = ext_x - 1 - depth if side else depth
            to_x[slot][line] = field_of(refs, kind, index, (x, every, every))
        to_x[slot][FACE] = faces[side]

    def when_there(there, packet, act):
        pl.when(there)(act)

        @pl.when(jnp.logical_not(there))
        def _():
            packet[...] = jnp.zeros(packet.shape, jnp.float32)

    for slot_y in range(many_y):
        there_y = has_partner("gy", slot_y)
        when_there(there_y, to_y[slot_y], lambda: on_side(py, slot_y, functools.partial(pack_y, slot_y)))
        for slot_x in range(many_x):
            when_there(
                there_y & has_partner("gx", slot_x),
                to_xy[many_x * slot_y + slot_x],
                lambda: on_side(
                    py,
                    slot_y,
                    lambda side_y: on_side(px, slot_x, lambda side_x: pack_xy(slot_x, slot_y, side_x, side_y)),
                ),
            )
    for slot_x in range(many_x):
        when_there(
            has_partner("gx", slot_x), to_x[slot_x], lambda: on_side(px, slot_x, functools.partial(pack_x, slot_x))
        )


def collide(pulled, rho, ux, uy, uz, fluid, wanted):
    total = {}
    diff = {}
    for j in range(1, 19, 2):
        total[j] = pulled[j] + pulled[j + 1]
        diff[j] = pulled[j] - pulled[j + 1]
    in_xy, in_xz, in_yz = total[7] + total[9], total[11] + total[13], total[15] + total[17]
    two_x, two_y, two_z = total[1] + total[1], total[3] + total[3], total[5] + total[5]
    count = (12.0 * pulled[0] + (two_x + two_y)) + (two_z + (in_xy + (in_xz + in_yz)))
    flow_x = (diff[1] + diff[1]) + ((diff[7] + diff[9]) + (diff[11] + diff[13]))
    flow_y = (diff[3] + diff[3]) + ((diff[7] - diff[9]) + (diff[15] + diff[17]))
    flow_z = (diff[5] + diff[5]) + ((diff[11] - diff[13]) + (diff[15] - diff[17]))
    xx, yy, zz = two_x + (in_xy + in_xz), two_y + (in_xy + in_yz), two_z + (in_xz + in_yz)
    xy, xz, yz = total[7] - total[9], total[11] - total[13], total[15] - total[17]
    push_x = xx * ux + xy * uy + xz * uz
    push_y = xy * ux + yy * uy + yz * uz
    push_z = xz * ux + yz * uy + zz * uz
    usq = ux * ux + uy * uy + uz * uz
    push = ux * push_x + uy * push_y + uz * push_z
    inverse = 1.0 / rho
    base = count * (OMEGA / 36.0 + (OMEGA / 24.0) * usq) - (OMEGA / 8.0) * push - ux * inverse
    along_x = (OMEGA / 12.0) * (flow_x + 3.0 * push_x - ux * count) + inverse
    along_y = (OMEGA / 12.0) * (flow_y + 3.0 * push_y - uy * count)
    along_z = (OMEGA / 12.0) * (flow_z + 3.0 * push_z - uz * count)
    parts = {
        1: along_x,
        3: along_y,
        5: along_z,
        7: along_x + along_y,
        9: along_x - along_y,
        11: along_x + along_z,
        13: along_x - along_z,
        15: along_y + along_z,
        17: along_y - along_z,
    }
    out = {}
    for j in wanted:
        if j == 0:
            shift = base
        elif j % 2:
            shift = base + parts[j]
        else:
            shift = base - parts[j - 1]
        out[j] = jnp.where(fluid, (1.0 - OMEGA) * pulled[j] + shift, pulled[OPPOSITE[j]])
    change = (-1.0 / 6.0) * rho * (flow_x * ux + flow_y * uy + flow_z * uz)
    return out, jnp.where(fluid, change, 0.0)


def step_kernel(slots, adj, den, vel, mask, z_set, *rest):
    many_x, many_y = slots
    from_x, from_y = rest[:many_x], rest[many_x : many_x + many_y]
    from_xy = rest[many_x + many_y : many_x + many_y + many_x * many_y]
    out, sens, first, fields, second, change, z_first, z_second, held, held_sens, sems = rest[-11:]
    refs = (adj, den, vel, mask)
    ext_x, ext_y, _ = mask.shape
    lane = lane_ids()
    spot = lane % GROUP
    every = slice(None)
    inner = pl.ds(8, ext_y)
    px, py = parity_of("gx"), parity_of("gy")

    def put_row(kind, index, x, y, value):
        row = y + 8
        if kind == "pop":
            first[index, x + 2, row : row + 1, :] = value
        else:
            fields[index, x + 1, row : row + 1, :] = value

    for j in range(19):
        first[j, 2 : 2 + ext_x, inner, :] = adj[j]
    for k in range(5):
        fields[k, 1 : 1 + ext_x, inner, :] = field_of(refs, "field", k, (every, every, every))
    z_first[:, inner, :] = z_set[...]

    def place_y(slot, side):
        packet = from_y[slot]
        for line, (kind, index, depth) in enumerate(face_lines(1, 2 * side - 1)):
            y = ext_y + depth if side else -1 - depth
            for x in range(ext_x):
                put_row(kind, index, x, y, packet[line, x : x + 1, :])
        start = 8 + ext_y if side else 6
        for tile in range(Z_TILES):
            row = 2 * tile % 8
            z_first[tile, start : start + 2, :] = packet[FACE + tile // 4, row : row + 2, :]
        if many_y == 1:
            clear_y(1 - side)

    def clear_y(side):
        nothing = jnp.zeros((1, LANES), jnp.float32)
        for kind, index, depth in face_lines(1, 2 * side - 1):
            y = ext_y + depth if side else -1 - depth
            for x in range(-1, ext_x + 1):
                put_row(kind, index, x, y, nothing)
            if kind == "pop":
                put_row(kind, index, -2, y, nothing)
                put_row(kind, index, ext_x + 1, y, nothing)
        start = 8 + ext_y if side else 6
        for tile in range(Z_TILES):
            z_first[tile, start : start + 2, :] = jnp.zeros((2, LANES), jnp.float32)

    def place_z(value, start, size, side):
        rows = pl.ds(start, size)
        inside = spot[:size] >= 2 + ext_x if side else spot[:size] < 2
        for tile in range(Z_TILES):
            shift = (2 + ext_x if side else 0) - 2 * tile
            moved = pltpu.roll(value, shift % LANES, 1)[:size]
            z_first[tile, rows, :] = jnp.where(inside, moved, z_first[tile, rows, :])

    def place_x(slot, side):
        packet = from_x[slot]
        for line, (kind, index, depth) in enumerate(face_lines(0, 2 * side - 1)):
            x = ext_x + depth if side else -1 - depth
            if kind == "pop":
                first[index, x + 2, inner, :] = packet[line]
            else:
                fields[index, x + 1, inner, :] = packet[line]
        for part in range(ext_y // 8):
            place_z(packet[FACE, pl.ds(8 * part, 8), :], 8 + 8 * part, 8, side)

    def place_xy(slot_x, slot_y, side_x, side_y):
        packet = from_xy[many_x * slot_y + slot_x]
        for line, (kind, index, far_x, far_y) in enumerate(edge_lines(2 * side_x - 1, 2 * side_y - 1)):
            x = ext_x + far_x if side_x else -1 - far_x
            y = ext_y + far_y if side_y else -1 - far_y
            put_row(kind, index, x, y, packet[line // 8, line % 8 : line % 8 + 1, :])
        place_z(packet[EDGE // 8], 8 + ext_y if side_y else 6, 2, side_x)

    for slot_y in range(many_y):
        on_side(py, slot_y, functools.partial(place_y, slot_y))
    for slot_x in range(many_x):
        on_side(px, slot_x, functools.partial(place_x, slot_x))
        for slot_y in range(many_y):
            on_side(
                py,
                slot_y,
                lambda side_y: on_side(px, slot_x, lambda side_x: place_xy(slot_x, slot_y, side_x, side_y)),
            )

    parts = (ext_y + 2 + 7) // 8

    @pl.loop(0, ext_x + 2)
    def _(x):
        for part in range(parts):
            row = 7 + 8 * part
            pulled = []
            for j in range(19):
                cx, cy, cz = VELOCITIES[j]
                rows = pl.ds(row + cy, 8)
                value = first[j, x + 1 + cx, rows, :]
                if cz == 1:
                    group = Z_UP.index(j)
                    edge = z_first[ABOVE + 1, rows, :]
                    edge = pltpu.roll(edge, LANES - 2 - GROUP * group - cx - x, 1)
                    value = jnp.where(lane == LANES - 1, edge, pltpu.roll(value, LANES - 1, 1))
                elif cz == -1:
                    group = Z_DOWN.index(j)
                    edge = z_first[BELOW + 1, rows, :]
                    edge = pltpu.roll(edge, LANES - 1 - GROUP * group - cx - x, 1)
                    value = jnp.where(lane == 0, edge, pltpu.roll(value, 1, 1))
                pulled.append(value)
            rows = pl.ds(row, 8)
            rho, ux, uy, uz, kind = [fields[k, x, rows, :] for k in range(5)]
            after, gain = collide(pulled, rho, ux, uy, uz, kind > 1.5, range(19))
            for j in range(19):
                second[j, x, rows, :] = jnp.where(kind > 0.5, after[j], 0.0)
            change[x, rows, :] = gain

    for part in range(parts):
        row = 7 + 8 * part

        def both(low_tile, high_tile, group, cx, cy):
            rows = pl.ds(row + cy, 8)
            low = pltpu.roll(z_first[low_tile, rows, :], (-GROUP * group - cx) % LANES, 1)
            high = pltpu.roll(z_first[high_tile, rows, :], (LANES // 2 - GROUP * group - cx) % LANES, 1)
            return jnp.where(lane < LANES // 2, low, high)

        pulled = []
        for j in range(19):
            cx, cy, cz = VELOCITIES[j]
            if cz == 0:
                tile, group = Z_PLACE[("pop", j)]
                pulled.append(both(BELOW + tile, ABOVE + tile, group, cx, cy))
            elif cz == 1:
                pulled.append(both(OWN_LOW, ABOVE + 2, Z_UP.index(j), cx, cy))
            else:
                pulled.append(both(BELOW + 2, OWN_HIGH, Z_DOWN.index(j), cx, cy))
        rho, ux, uy, uz, kind = [
            both(BELOW + tile, ABOVE + tile, group, 0, 0)
            for tile, group in [Z_PLACE[("field", k)] for k in range(5)]
        ]
        after, _ = collide(pulled, rho, ux, uy, uz, kind > 1.5, Z_UP + Z_DOWN)
        for group in range(5):
            value = jnp.where(lane < LANES // 2, after[Z_DOWN[group]], after[Z_UP[group]])
            z_second[group, pl.ds(row, 8), :] = jnp.where(kind > 0.5, value, 0.0)

    def copies(x):
        return (
            pltpu.make_async_copy(held.at[:, x], out.at[:, x], sems.at[0, x]),
            pltpu.make_async_copy(held_sens.at[x], sens.at[x], sems.at[1, x]),
        )

    @pl.loop(0, ext_x)
    def _(x):
        for part in range(ext_y // 8):
            row = 8 + 8 * part
            at = (x, pl.ds(8 * part, 8), every)
            pulled = []
            for j in range(19):
                cx, cy, cz = VELOCITIES[j]
                rows = pl.ds(row + cy, 8)
                value = second[j, x + 1 + cx, rows, :]
                if cz == 1:
                    edge = z_second[Z_UP.index(j), rows, :]
                    edge = pltpu.roll(edge, LANES // 2 - 3 - cx - x, 1)
                    value = jnp.where(lane == LANES - 1, edge, pltpu.roll(value, LANES - 1, 1))
                elif cz == -1:
                    edge = z_second[Z_DOWN.index(j), rows, :]
                    edge = pltpu.roll(edge, LANES - 2 - cx - x, 1)
                    value = jnp.where(lane == 0, edge, pltpu.roll(value, 1, 1))
                pulled.append(value)
            after, gain = collide(
                pulled,
                den[(0, *at)],
                vel[(0, 0, *at)],
                vel[(0, 1, *at)],
                vel[(0, 2, *at)],
                mask[at] > 0,
                range(19),
            )
            for j in range(19):
                held[(j, *at)] = after[j]
            held_sens[at] = change[x + 1, pl.ds(row, 8), :] + gain
        for copy in copies(x):
            copy.start()

    for x in range(ext_x):
        for copy in copies(x):
            copy.wait()


def shards(adjoint, density, velocity, pore_mask):
    ext_x, ext_y, ext_z = pore_mask.shape
    assert ext_z == LANES and ext_y % 8 == 0 and ext_x + 4 <= GROUP and ext_x == 8
    many_x = 2
    many_y, many_z = [1 if lax.axis_size(axis) == 2 else 2 for axis in ("gy", "gz")]
    vmem = pl.BlockSpec(memory_space=pltpu.VMEM)
    hbm = pl.BlockSpec(memory_space=pltpu.HBM)
    inputs = (adjoint, density, velocity, pore_mask)

    def array(*shape):
        return jax.ShapeDtypeStruct(shape, jnp.float32)

    def call(kernel, name, operands, shapes, limit, **more):
        more.setdefault("out_specs", [vmem] * len(shapes))
        more.setdefault("in_specs", [vmem] * len(operands))
        params = pltpu.CompilerParams(vmem_limit_bytes=limit * 1024 * 1024)
        return pl.pallas_call(kernel, out_shape=shapes, compiler_params=params, name=name, **more)(*operands)

    def partners(axis, slot):
        size = lax.axis_size(axis)
        found = {}
        for at in range(slot, size - 1, 2):
            found[at], found[at + 1] = at + 1, at
        return found

    def swap(value, spare, *places):
        tables = {axis: partners(axis, slot) for axis, slot in places}
        axes = [axis for axis in ("gx", "gy", "gz") if axis in tables or axis == spare]
        sizes = [lax.axis_size(axis) for axis in axes]
        pairs = []
        for at in itertools.product(*[range(size) for size in sizes]):
            to = [tables.get(axis, {}).get(spot, spot) for axis, spot in zip(axes, at)]
            if spare is not None and tuple(to) == at:
                to = [partners(spare, 0).get(spot, spot) if axis == spare else spot for axis, spot in zip(axes, at)]
            flat = []
            for spots in (at, to):
                index = 0
                for size, spot in zip(sizes, spots):
                    index = index * size + spot
                flat.append(index)
            pairs.append(tuple(flat))
        return lax.ppermute(value, tuple(axes), pairs)

    loaded = [jax.ShapeDtypeStruct(value.shape, value.dtype) for value in inputs]
    *held, near, a_z, b_z = (
        *call(
            functools.partial(pack_z_kernel, many_z),
            "pack_z",
            [pltpu.with_memory_space_constraint(value, pltpu.HBM) for value in inputs],
            loaded + [array(2, ext_y, LANES)] + [array(3, ext_y, LANES)] * many_z,
            8,
            in_specs=[hbm] * 4,
            scratch_shapes=[pltpu.SemaphoreType.DMA((ext_x + 5,))],
        ),
        *[None] * (2 - many_z),
    )
    from_z = [swap(value, "gx", ("gz", slot)) for slot, value in enumerate((a_z, b_z)[:many_z])]

    z_set, *packets = call(
        functools.partial(pack_xy_kernel, (many_x, many_y, many_z)),
        "pack_xy",
        (*held, near, *from_z),
        [array(Z_TILES, ext_y, LANES)]
        + [array(FACE + 1, ext_y, LANES)] * many_x
        + [array(FACE + 2, ext_x, LANES)] * many_y
        + [array(EDGE // 8 + 1, 8, LANES)] * (many_x * many_y),
        8,
        scratch_shapes=[pltpu.VMEM((2, ext_y, LANES), jnp.float32)],
    )
    to_x, to_y, to_xy = packets[:many_x], packets[many_x : many_x + many_y], packets[many_x + many_y :]
    from_xy = [
        swap(to_xy[many_x * slot_y + slot_x], None, ("gx", slot_x), ("gy", slot_y))
        for slot_y in range(many_y)
        for slot_x in range(many_x)
    ]
    from_y = [swap(value, "gz", ("gy", slot)) for slot, value in enumerate(to_y)]
    from_x = [swap(value, "gz", ("gx", slot)) for slot, value in enumerate(to_x)]

    rows = ext_y + 16
    scratch = [
        pltpu.VMEM((19, ext_x + 4, rows, LANES), jnp.float32),
        pltpu.VMEM((5, ext_x + 2, rows, LANES), jnp.float32),
        pltpu.VMEM((19, ext_x + 2, rows, LANES), jnp.float32),
        pltpu.VMEM((ext_x + 2, rows, LANES), jnp.float32),
        pltpu.VMEM((Z_TILES, rows, LANES), jnp.float32),
        pltpu.VMEM((5, rows, LANES), jnp.float32),
        pltpu.VMEM((19, ext_x, ext_y, LANES), jnp.float32),
        pltpu.VMEM((ext_x, ext_y, LANES), jnp.float32),
        pltpu.SemaphoreType.DMA((2, ext_x)),
    ]
    return call(
        functools.partial(step_kernel, (many_x, many_y)),
        "two_steps",
        (*held, z_set, *from_x, *from_y, *from_xy),
        [array(19, ext_x, ext_y, LANES), array(ext_x, ext_y, LANES)],
        24,
        out_specs=[hbm] * 2,
        scratch_shapes=scratch,
    )


def solution(mesh):
    placed = (
        P(None, "gx", "gy", "gz"),
        P(None, "gx", "gy", "gz"),
        P(None, None, "gx", "gy", "gz"),
        P("gx", "gy", "gz"),
    )

    def whole(*arrays):
        return tuple(shards(*arrays))

    return jax.shard_map(
        whole,
        mesh=mesh,
        in_specs=placed,
        out_specs=(P(None, "gx", "gy", "gz"), P("gx", "gy", "gz")),
        check_vma=False,
    )
```

```python
import functools
import itertools

import jax
import jax.numpy as jnp
from jax import lax
from jax.experimental import pallas as pl
from jax.experimental.pallas import tpu as pltpu
from jax.sharding import PartitionSpec as P

VELOCITIES = [
    (0, 0, 0),
    (1, 0, 0),
    (-1, 0, 0),
    (0, 1, 0),
    (0, -1, 0),
    (0, 0, 1),
    (0, 0, -1),
    (1, 1, 0),
    (-1, -1, 0),
    (1, -1, 0),
    (-1, 1, 0),
    (1, 0, 1),
    (-1, 0, -1),
    (1, 0, -1),
    (-1, 0, 1),
    (0, 1, 1),
    (0, -1, -1),
    (0, 1, -1),
    (0, -1, 1),
]
OPPOSITE = [0, 2, 1, 4, 3, 6, 5, 8, 7, 10, 9, 12, 11, 14, 13, 16, 15, 18, 17]
OMEGA = 1.25
LANES = 128
GROUP = 16


def pops(axis, sign):
    return [j for j in range(19) if VELOCITIES[j][axis] == sign]


def mirrored(j):
    cx, cy, cz = VELOCITIES[j]
    return VELOCITIES.index((cx, cy, -cz))


Z_FLAT = pops(2, 0)
Z_UP = pops(2, 1)
Z_DOWN = [mirrored(j) for j in Z_UP]
RHO, UX, UY, UZ, KIND = range(5)
Z_PLACE = {("pop", j): (0, g) for g, j in enumerate(Z_FLAT[:8])}
Z_PLACE[("pop", Z_FLAT[8])] = (1, 5)
Z_PLACE[("field", RHO)] = (1, 6)
Z_PLACE[("field", KIND)] = (1, 7)
Z_PLACE[("field", UX)] = (2, 5)
Z_PLACE[("field", UY)] = (2, 6)
Z_PLACE[("field", UZ)] = (2, 7)
BELOW, ABOVE, OWN_LOW, OWN_HIGH, Z_TILES = 0, 3, 6, 7, 8


def face_lines(axis, toward):
    near = pops(axis, 0) + pops(axis, toward)
    lines = [("pop", j, 0) for j in near] + [("field", k, 0) for k in range(5)]
    return lines + [("pop", j, 1) for j in pops(axis, toward)]


def edge_lines(toward_x, toward_y):
    lines = [("field", k, 0, 0) for k in range(5)]
    for j in range(19):
        cx, cy, _ = VELOCITIES[j]
        if cx not in (0, toward_x) or cy not in (0, toward_y):
            continue
        lines.append(("pop", j, 0, 0))
        if cx:
            lines.append(("pop", j, 1, 0))
        if cy:
            lines.append(("pop", j, 0, 1))
        if cx and cy:
            lines.append(("pop", j, 1, 1))
    return lines


FACE = 24
EDGE = 24


def lane_ids():
    return lax.broadcasted_iota(jnp.int32, (8, LANES), 1)


def field_of(refs, kind, index, at):
    adj, den, vel, mask = refs
    if kind == "pop":
        return adj[(index, *at)]
    if index == RHO:
        return den[(1, *at)]
    if index == KIND:
        return (mask[at] + 1).astype(jnp.float32)
    return vel[(1, index - UX, *at)]


def parity_of(axis):
    return lax.rem(lax.axis_index(axis), 2)


def on_side(parity, slot, act):
    @pl.when(parity == slot)
    def _():
        act(1)

    @pl.when(parity != slot)
    def _():
        act(0)


def has_partner(axis, slot):
    at = lax.axis_index(axis)
    to = at + jnp.where(lax.rem(at, 2) == slot, 1, -1)
    return (to >= 0) & (to < lax.axis_size(axis))


def pack_z_kernel(slots, adj_in, den_in, vel_in, mask_in, adj, den, vel, mask, near, *rest):
    packets, sems = rest[:slots], rest[slots]
    refs = (adj, den, vel, mask)
    ext_x, ext_y, _ = mask.shape
    loads = [
        pltpu.make_async_copy(source, target, sems.at[ext_x + at])
        for at, (source, target) in enumerate([(den_in.at[1], den.at[1]), (vel_in.at[1], vel.at[1]), (mask_in, mask)])
    ]
    plane_loads = [pltpu.make_async_copy(adj_in.at[:, x], adj.at[:, x], sems.at[x]) for x in range(ext_x)]
    last_loads = [
        pltpu.make_async_copy(source, target, sems.at[ext_x + 3 + at])
        for at, (source, target) in enumerate([(den_in.at[0], den.at[0]), (vel_in.at[0], vel.at[0])])
    ]
    for load in loads + plane_loads + last_loads:
        load.start()
    for load in loads:
        load.wait()
    lane = lane_ids()
    parity = parity_of("gz")
    parts = range(ext_y // 8)
    zero = jnp.zeros((8, LANES), jnp.float32)
    lows, highs = [[zero] * 3 for _ in parts], [[zero] * 3 for _ in parts]
    far_low, far_high = [zero for _ in parts], [zero for _ in parts]
    for x in range(ext_x):
        plane_loads[x].wait()
        for part in parts:
            at = (x, pl.ds(8 * part, 8), slice(None))
            for (kind, index), (tile, group) in Z_PLACE.items():
                spot = GROUP * group + 2 + x
                moved = pltpu.roll(field_of(refs, kind, index, at), spot, 1)
                lows[part][tile] = jnp.where(lane == spot, moved, lows[part][tile])
                highs[part][tile] = jnp.where(lane == spot - 1, moved, highs[part][tile])
            for group in range(5):
                spot = GROUP * group + 2 + x
                moved = pltpu.roll(field_of(refs, "pop", Z_UP[group], at), spot, 1)
                lows[part][1] = jnp.where(lane == spot, moved, lows[part][1])
                far_low[part] = jnp.where(lane == spot + 1, moved, far_low[part])
                moved = pltpu.roll(field_of(refs, "pop", Z_DOWN[group], at), spot, 1)
                highs[part][1] = jnp.where(lane == spot - 1, moved, highs[part][1])
                far_high[part] = jnp.where(lane == spot - 2, moved, far_high[part])
    for part in parts:
        rows = pl.ds(8 * part, 8)
        low = lows[part]
        high = [pltpu.roll(tile, 1, 1) for tile in highs[part]]
        low[2] = jnp.where(lane < 5 * GROUP, pltpu.roll(far_low[part], LANES - 1, 1), low[2])
        high[2] = jnp.where(lane < 5 * GROUP, pltpu.roll(far_high[part], 2, 1), high[2])
        near[0, rows, :] = low[1]
        near[1, rows, :] = high[1]
        for slot in range(slots):
            there = has_partner("gz", slot)
            for tile in range(3):
                value = jnp.where(parity == slot, high[tile], low[tile])
                packets[slot][tile, rows, :] = jnp.where(there, value, 0.0)
    for load in last_loads:
        load.wait()


def pack_xy_kernel(slots, adj, den, vel, mask, near, *rest):
    many_x, many_y, many_z = slots
    from_z, z_set, first, packets = rest[:many_z], rest[many_z], rest[many_z + 1], rest[many_z + 2 :]
    to_x, to_y = packets[:many_x], packets[many_x : many_x + many_y]
    to_xy, faces = packets[many_x + many_y : -1], packets[-1]
    refs = (adj, den, vel, mask)
    ext_x, ext_y, _ = mask.shape
    lane = lane_ids()
    spot = lane % GROUP
    every = slice(None)
    px, py, pz = parity_of("gx"), parity_of("gy"), parity_of("gz")

    z_set[OWN_LOW] = near[0]
    z_set[OWN_HIGH] = near[1]
    for tile in range(3):
        even = from_z[0][tile]
        odd = from_z[1][tile] if many_z > 1 else jnp.zeros_like(even)
        z_set[ABOVE + tile] = jnp.where(pz == 0, even, odd)
        z_set[BELOW + tile] = jnp.where(pz == 0, odd, even)

    for j in range(19):
        cz = VELOCITIES[j][2]
        if cz == 0:
            first[j, 2 : 2 + ext_x, pl.ds(8, ext_y), :] = adj[j]
            continue
        group = (Z_UP if cz > 0 else Z_DOWN).index(j)
        for part in range(ext_y // 8):
            rows = pl.ds(8 * part, 8)
            halo = z_set[(ABOVE if cz > 0 else BELOW) + 1, rows, :]
            last = LANES - 1 if cz > 0 else 0
            for x in range(ext_x):
                edge = pltpu.roll(halo, (last - 2 - GROUP * group - x) % LANES, 1)
                value = pltpu.roll(adj[j, x, rows, :], -cz % LANES, 1)
                first[j, 2 + x, pl.ds(8 + 8 * part, 8), :] = jnp.where(lane == last, edge, value)

    def line_of(kind, index, x, y):
        if kind == "pop":
            return first[index, x + 2, y + 8 : y + 9, :]
        return field_of(refs, kind, index, (x, slice(y, y + 1), every))

    for side in range(2):
        for part in range(ext_y // 8):
            rows = pl.ds(8 * part, 8)
            value = jnp.zeros((8, LANES), jnp.float32)
            for tile in range(Z_TILES):
                start = ext_x if side else 2
                moved = pltpu.roll(z_set[tile, rows, :], (2 * tile - start) % LANES, 1)
                value = jnp.where(spot // 2 == tile, moved, value)
            faces[side, rows, :] = value

    def pack_xy(slot_x, slot_y, side_x, side_y):
        packet = to_xy[many_x * slot_y + slot_x]
        for line, (kind, index, far_x, far_y) in enumerate(edge_lines(1 - 2 * side_x, 1 - 2 * side_y)):
            x = ext_x - 1 - far_x if side_x else far_x
            y = ext_y - 1 - far_y if side_y else far_y
            packet[line // 8, line % 8 : line % 8 + 1, :] = line_of(kind, index, x, y)
        start = ext_y - 2 if side_y else 0
        packet[EDGE // 8, 0:2, :] = faces[side_x, start : start + 2, :]

    def pack_y(slot, side):
        packet = to_y[slot]
        for line, (kind, index, depth) in enumerate(face_lines(1, 1 - 2 * side)):
            y = ext_y - 1 - depth if side else depth
            for x in range(ext_x):
                packet[line, x : x + 1, :] = line_of(kind, index, x, y)
        start = ext_y - 2 if side else 0
        for tile in range(Z_TILES):
            row = 2 * tile % 8
            packet[FACE + tile // 4, row : row + 2, :] = z_set[tile, start : start + 2, :]

    def pack_x(slot, side):
        for line, (kind, index, depth) in enumerate(face_lines(0, 1 - 2 * side)):
            x = ext_x - 1 - depth if side else depth
            if kind == "pop":
                to_x[slot][line] = first[index, x + 2, pl.ds(8, ext_y), :]
            else:
                to_x[slot][line] = field_of(refs, kind, index, (x, every, every))
        to_x[slot][FACE] = faces[side]

    def when_there(there, packet, act):
        pl.when(there)(act)

        @pl.when(jnp.logical_not(there))
        def _():
            packet[...] = jnp.zeros(packet.shape, jnp.float32)

    for slot_y in range(many_y):
        there_y = has_partner("gy", slot_y)
        when_there(there_y, to_y[slot_y], lambda: on_side(py, slot_y, functools.partial(pack_y, slot_y)))
        for slot_x in range(many_x):
            when_there(
                there_y & has_partner("gx", slot_x),
                to_xy[many_x * slot_y + slot_x],
                lambda: on_side(
                    py,
                    slot_y,
                    lambda side_y: on_side(px, slot_x, lambda side_x: pack_xy(slot_x, slot_y, side_x, side_y)),
                ),
            )
    for slot_x in range(many_x):
        when_there(
            has_partner("gx", slot_x), to_x[slot_x], lambda: on_side(px, slot_x, functools.partial(pack_x, slot_x))
        )


def collide(pulled, rho, ux, uy, uz, fluid, wanted):
    total = {}
    diff = {}
    for j in range(1, 19, 2):
        total[j] = pulled[j] + pulled[j + 1]
        diff[j] = pulled[j] - pulled[j + 1]
    in_xy, in_xz, in_yz = total[7] + total[9], total[11] + total[13], total[15] + total[17]
    two_x, two_y, two_z = total[1] + total[1], total[3] + total[3], total[5] + total[5]
    count = (12.0 * pulled[0] + (two_x + two_y)) + (two_z + (in_xy + (in_xz + in_yz)))
    flow_x = (diff[1] + diff[1]) + ((diff[7] + diff[9]) + (diff[11] + diff[13]))
    flow_y = (diff[3] + diff[3]) + ((diff[7] - diff[9]) + (diff[15] + diff[17]))
    flow_z = (diff[5] + diff[5]) + ((diff[11] - diff[13]) + (diff[15] - diff[17]))
    xx, yy, zz = two_x + (in_xy + in_xz), two_y + (in_xy + in_yz), two_z + (in_xz + in_yz)
    xy, xz, yz = total[7] - total[9], total[11] - total[13], total[15] - total[17]
    push_x = xx * ux + xy * uy + xz * uz
    push_y = xy * ux + yy * uy + yz * uz
    push_z = xz * ux + yz * uy + zz * uz
    usq = ux * ux + uy * uy + uz * uz
    push = ux * push_x + uy * push_y + uz * push_z
    inverse = 1.0 / rho
    base = count * (OMEGA / 36.0 + (OMEGA / 24.0) * usq) - (OMEGA / 8.0) * push - ux * inverse
    along_x = (OMEGA / 12.0) * (flow_x + 3.0 * push_x - ux * count) + inverse
    along_y = (OMEGA / 12.0) * (flow_y + 3.0 * push_y - uy * count)
    along_z = (OMEGA / 12.0) * (flow_z + 3.0 * push_z - uz * count)
    parts = {
        1: along_x,
        3: along_y,
        5: along_z,
        7: along_x + along_y,
        9: along_x - along_y,
        11: along_x + along_z,
        13: along_x - along_z,
        15: along_y + along_z,
        17: along_y - along_z,
    }
    out = {}
    for j in wanted:
        if j == 0:
            shift = base
        elif j % 2:
            shift = base + parts[j]
        else:
            shift = base - parts[j - 1]
        out[j] = jnp.where(fluid, (1.0 - OMEGA) * pulled[j] + shift, pulled[OPPOSITE[j]])
    change = (-1.0 / 6.0) * rho * (flow_x * ux + flow_y * uy + flow_z * uz)
    return out, jnp.where(fluid, change, 0.0)


def first_step(first, fields, second, change, take):
    pulled = [take(first, j, 2, *VELOCITIES[j][:2])[...] for j in range(19)]
    rho, ux, uy, uz, kind = [take(fields, k, 1, 0, 0)[...] for k in range(5)]
    after, gain = collide(pulled, rho, ux, uy, uz, kind > 1.5, range(19))
    for j in range(19):
        value = jnp.where(kind > 0.5, after[j], 0.0)
        cz = VELOCITIES[j][2]
        take(second, j, 1, 0, 0)[...] = pltpu.roll(value, -cz % LANES, 1) if cz else value
    take(change, None, 1, 0, 0)[...] = gain


def inner_kernel(den, vel, mask, first, fields, second, change):
    refs = (None, den, vel, mask)
    ext_x, ext_y, _ = mask.shape
    every = slice(None)
    for k in range(5):
        fields[k, 1 : 1 + ext_x, pl.ds(8, ext_y), :] = field_of(refs, "field", k, (every, every, every))

    @pl.loop(1, ext_x - 1)
    def _(x):
        for part in range(ext_y // 8):

            def take(ref, lead, margin, cx, cy):
                at = (x + margin + cx, pl.ds(9 + 8 * part + cy, 8), every)
                return ref.at[at if lead is None else (lead, *at)]

            first_step(first, fields, second, change, take)


def outer_kernel(slots, den, vel, mask, z_set, *rest):
    many_x, many_y = slots
    from_x, from_y = rest[4 : 4 + many_x], rest[4 + many_x : 4 + many_x + many_y]
    from_xy = rest[4 + many_x + many_y : 4 + many_x + many_y + many_x * many_y]
    out, sens, first, fields, second, change, z_first, z_second, held, held_sens, sems = rest[-11:]
    ext_x, ext_y, _ = mask.shape
    lane = lane_ids()
    spot = lane % GROUP
    every = slice(None)
    inner = pl.ds(8, ext_y)
    px, py = parity_of("gx"), parity_of("gy")

    def put_row(kind, index, x, y, value):
        row = y + 8
        if kind == "pop":
            first[index, x + 2, row : row + 1, :] = value
        else:
            fields[index, x + 1, row : row + 1, :] = value

    z_first[:, inner, :] = z_set[...]

    def place_y(slot, side):
        packet = from_y[slot]
        for line, (kind, index, depth) in enumerate(face_lines(1, 2 * side - 1)):
            y = ext_y + depth if side else -1 - depth
            for x in range(ext_x):
                put_row(kind, index, x, y, packet[line, x : x + 1, :])
        start = 8 + ext_y if side else 6
        for tile in range(Z_TILES):
            row = 2 * tile % 8
            z_first[tile, start : start + 2, :] = packet[FACE + tile // 4, row : row + 2, :]
        if many_y == 1:
            clear_y(1 - side)

    def clear_y(side):
        nothing = jnp.zeros((1, LANES), jnp.float32)
        for kind, index, depth in face_lines(1, 2 * side - 1):
            y = ext_y + depth if side else -1 - depth
            for x in range(-1, ext_x + 1):
                put_row(kind, index, x, y, nothing)
            if kind == "pop":
                put_row(kind, index, -2, y, nothing)
                put_row(kind, index, ext_x + 1, y, nothing)
        start = 8 + ext_y if side else 6
        for tile in range(Z_TILES):
            z_first[tile, start : start + 2, :] = jnp.zeros((2, LANES), jnp.float32)

    def place_z(value, start, size, side):
        rows = pl.ds(start, size)
        inside = spot[:size] >= 2 + ext_x if side else spot[:size] < 2
        for tile in range(Z_TILES):
            shift = (2 + ext_x if side else 0) - 2 * tile
            moved = pltpu.roll(value, shift % LANES, 1)[:size]
            z_first[tile, rows, :] = jnp.where(inside, moved, z_first[tile, rows, :])

    def place_x(slot, side):
        packet = from_x[slot]
        for line, (kind, index, depth) in enumerate(face_lines(0, 2 * side - 1)):
            x = ext_x + depth if side else -1 - depth
            if kind == "pop":
                first[index, x + 2, inner, :] = packet[line]
            else:
                fields[index, x + 1, inner, :] = packet[line]
        for part in range(ext_y // 8):
            place_z(packet[FACE, pl.ds(8 * part, 8), :], 8 + 8 * part, 8, side)

    def place_xy(slot_x, slot_y, side_x, side_y):
        packet = from_xy[many_x * slot_y + slot_x]
        for line, (kind, index, far_x, far_y) in enumerate(edge_lines(2 * side_x - 1, 2 * side_y - 1)):
            x = ext_x + far_x if side_x else -1 - far_x
            y = ext_y + far_y if side_y else -1 - far_y
            put_row(kind, index, x, y, packet[line // 8, line % 8 : line % 8 + 1, :])
        place_z(packet[EDGE // 8], 8 + ext_y if side_y else 6, 2, side_x)

    for slot_y in range(many_y):
        on_side(py, slot_y, functools.partial(place_y, slot_y))
    for slot_x in range(many_x):
        on_side(px, slot_x, functools.partial(place_x, slot_x))
        for slot_y in range(many_y):
            on_side(
                py,
                slot_y,
                lambda side_y: on_side(px, slot_x, lambda side_x: place_xy(slot_x, slot_y, side_x, side_y)),
            )

    parts = (ext_y + 2 + 7) // 8

    for x in (-1, 0, ext_x - 1, ext_x):
        for part in range(parts):

            def take(ref, lead, margin, cx, cy):
                at = (x + margin + cx, pl.ds(7 + 8 * part + cy, 8), every)
                return ref.at[at if lead is None else (lead, *at)]

            first_step(first, fields, second, change, take)
    for y in (-1, 0, ext_y - 1, ext_y):

        def take(ref, lead, margin, cx, cy):
            at = (pl.ds(margin + cx, ext_x), y + 8 + cy, every)
            return ref.at[at if lead is None else (lead, *at)]

        first_step(first, fields, second, change, take)

    for part in range(parts):
        row = 7 + 8 * part

        def both(low_tile, high_tile, group, cx, cy):
            rows = pl.ds(row + cy, 8)
            low = pltpu.roll(z_first[low_tile, rows, :], (-GROUP * group - cx) % LANES, 1)
            high = pltpu.roll(z_first[high_tile, rows, :], (LANES // 2 - GROUP * group - cx) % LANES, 1)
            return jnp.where(lane < LANES // 2, low, high)

        pulled = []
        for j in range(19):
            cx, cy, cz = VELOCITIES[j]
            if cz == 0:
                tile, group = Z_PLACE[("pop", j)]
                pulled.append(both(BELOW + tile, ABOVE + tile, group, cx, cy))
            elif cz == 1:
                pulled.append(both(OWN_LOW, ABOVE + 2, Z_UP.index(j), cx, cy))
            else:
                pulled.append(both(BELOW + 2, OWN_HIGH, Z_DOWN.index(j), cx, cy))
        rho, ux, uy, uz, kind = [
            both(BELOW + tile, ABOVE + tile, group, 0, 0)
            for tile, group in [Z_PLACE[("field", k)] for k in range(5)]
        ]
        after, _ = collide(pulled, rho, ux, uy, uz, kind > 1.5, Z_UP + Z_DOWN)
        for group in range(5):
            value = jnp.where(lane < LANES // 2, after[Z_DOWN[group]], after[Z_UP[group]])
            z_second[group, pl.ds(row, 8), :] = jnp.where(kind > 0.5, value, 0.0)

    def copies(x):
        return (
            pltpu.make_async_copy(held.at[:, x], out.at[:, x], sems.at[0, x]),
            pltpu.make_async_copy(held_sens.at[x], sens.at[x], sems.at[1, x]),
        )

    @pl.loop(0, ext_x)
    def _(x):
        for part in range(ext_y // 8):
            row = 8 + 8 * part
            at = (x, pl.ds(8 * part, 8), every)
            pulled = []
            for j in range(19):
                cx, cy, cz = VELOCITIES[j]
                rows = pl.ds(row + cy, 8)
                value = second[j, x + 1 + cx, rows, :]
                if cz == 1:
                    edge = z_second[Z_UP.index(j), rows, :]
                    edge = pltpu.roll(edge, LANES // 2 - 3 - cx - x, 1)
                    value = jnp.where(lane == LANES - 1, edge, value)
                elif cz == -1:
                    edge = z_second[Z_DOWN.index(j), rows, :]
                    edge = pltpu.roll(edge, LANES - 2 - cx - x, 1)
                    value = jnp.where(lane == 0, edge, value)
                pulled.append(value)
            after, gain = collide(
                pulled,
                den[(0, *at)],
                vel[(0, 0, *at)],
                vel[(0, 1, *at)],
                vel[(0, 2, *at)],
                mask[at] > 0,
                range(19),
            )
            for j in range(19):
                held[(j, *at)] = after[j]
            held_sens[at] = change[x + 1, pl.ds(row, 8), :] + gain
        for copy in copies(x):
            copy.start()

    for x in range(ext_x):
        for copy in copies(x):
            copy.wait()


def shards(adjoint, density, velocity, pore_mask):
    ext_x, ext_y, ext_z = pore_mask.shape
    assert ext_z == LANES and ext_y % 8 == 0 and ext_x + 4 <= GROUP and ext_x == 8
    many_x = 2
    many_y, many_z = [1 if lax.axis_size(axis) == 2 else 2 for axis in ("gy", "gz")]
    vmem = pl.BlockSpec(memory_space=pltpu.VMEM)
    hbm = pl.BlockSpec(memory_space=pltpu.HBM)
    inputs = (adjoint, density, velocity, pore_mask)

    def array(*shape):
        return jax.ShapeDtypeStruct(shape, jnp.float32)

    def call(kernel, name, operands, shapes, limit, **more):
        more.setdefault("out_specs", [vmem] * len(shapes))
        more.setdefault("in_specs", [vmem] * len(operands))
        params = pltpu.CompilerParams(vmem_limit_bytes=limit * 1024 * 1024)
        return pl.pallas_call(kernel, out_shape=shapes, compiler_params=params, name=name, **more)(*operands)

    def partners(axis, slot, ends=False):
        size = lax.axis_size(axis)
        found = {}
        for at in range(slot, size - 1, 2):
            found[at], found[at + 1] = at + 1, at
        if ends and slot and size % 2 == 0:
            found[0], found[size - 1] = size - 1, 0
        return found

    def swap(value, spare, *places):
        tables = {axis: partners(axis, slot, spare == axis) for axis, slot in places}
        axes = [axis for axis in ("gx", "gy", "gz") if axis in tables or axis == spare]
        sizes = [lax.axis_size(axis) for axis in axes]
        pairs = []
        for at in itertools.product(*[range(size) for size in sizes]):
            to = [tables.get(axis, {}).get(spot, spot) for axis, spot in zip(axes, at)]
            if spare is not None and tuple(to) == at:
                to = [partners(spare, 0).get(spot, spot) if axis == spare else spot for axis, spot in zip(axes, at)]
            flat = []
            for spots in (at, to):
                index = 0
                for size, spot in zip(sizes, spots):
                    index = index * size + spot
                flat.append(index)
            pairs.append(tuple(flat))
        return lax.ppermute(value, tuple(axes), pairs)

    loaded = [jax.ShapeDtypeStruct(value.shape, value.dtype) for value in inputs]
    *held, near, a_z, b_z = (
        *call(
            functools.partial(pack_z_kernel, many_z),
            "pack_z",
            [pltpu.with_memory_space_constraint(value, pltpu.HBM) for value in inputs],
            loaded + [array(2, ext_y, LANES)] + [array(3, ext_y, LANES)] * many_z,
            8,
            in_specs=[hbm] * 4,
            scratch_shapes=[pltpu.SemaphoreType.DMA((ext_x + 5,))],
        ),
        *[None] * (2 - many_z),
    )
    from_z = [swap(value, "gx", ("gz", slot)) for slot, value in enumerate((a_z, b_z)[:many_z])]

    rows = ext_y + 16
    z_set, first, *packets = call(
        functools.partial(pack_xy_kernel, (many_x, many_y, many_z)),
        "pack_xy",
        (*held, near, *from_z),
        [array(Z_TILES, ext_y, LANES), array(19, ext_x + 4, rows, LANES)]
        + [array(FACE + 1, ext_y, LANES)] * many_x
        + [array(FACE + 2, ext_x, LANES)] * many_y
        + [array(EDGE // 8 + 1, 8, LANES)] * (many_x * many_y),
        8,
        scratch_shapes=[pltpu.VMEM((2, ext_y, LANES), jnp.float32)],
    )
    to_x, to_y, to_xy = packets[:many_x], packets[many_x : many_x + many_y], packets[many_x + many_y :]
    from_xy = [
        swap(to_xy[many_x * slot_y + slot_x], None, ("gx", slot_x), ("gy", slot_y))
        for slot_y in range(many_y)
        for slot_x in range(many_x)
    ]
    from_y = [swap(value, "gz", ("gy", slot)) for slot, value in enumerate(to_y)]
    from_x = [swap(value, "gx", ("gx", slot)) for slot, value in enumerate(to_x)]

    _, den, vel, mask = held
    fields, second, change = call(
        inner_kernel,
        "inner_step",
        (den, vel, mask, first),
        [array(5, ext_x + 2, rows, LANES), array(19, ext_x + 2, rows, LANES), array(ext_x + 2, rows, LANES)],
        8,
        cost_estimate=pl.CostEstimate(flops=40_000_000, bytes_accessed=8_000_000, transcendentals=0),
    )
    inout = (first, fields, second, change)
    return call(
        functools.partial(outer_kernel, (many_x, many_y)),
        "outer_steps",
        (den, vel, mask, z_set, *inout, *from_x, *from_y, *from_xy),
        [array(19, ext_x, ext_y, LANES), array(ext_x, ext_y, LANES)] + [array(*value.shape) for value in inout],
        8,
        out_specs=[hbm] * 2 + [vmem] * 4,
        input_output_aliases={4 + at: 2 + at for at in range(4)},
        scratch_shapes=[
            pltpu.VMEM((Z_TILES, rows, LANES), jnp.float32),
            pltpu.VMEM((5, rows, LANES), jnp.float32),
            pltpu.VMEM((19, ext_x, ext_y, LANES), jnp.float32),
            pltpu.VMEM((ext_x, ext_y, LANES), jnp.float32),
            pltpu.SemaphoreType.DMA((2, ext_x)),
        ],
    )[:2]


def solution(mesh):
    placed = (
        P(None, "gx", "gy", "gz"),
        P(None, "gx", "gy", "gz"),
        P(None, None, "gx", "gy", "gz"),
        P("gx", "gy", "gz"),
    )

    def whole(*arrays):
        return tuple(shards(*arrays))

    return jax.shard_map(
        whole,
        mesh=mesh,
        in_specs=placed,
        out_specs=(P(None, "gx", "gy", "gz"), P("gx", "gy", "gz")),
        check_vma=False,
    )
```

```python
import functools
import itertools

import jax
import jax.numpy as jnp
from jax import lax
from jax.experimental import pallas as pl
from jax.experimental.pallas import tpu as pltpu
from jax.sharding import PartitionSpec as P

VELOCITIES = [
    (0, 0, 0),
    (1, 0, 0),
    (-1, 0, 0),
    (0, 1, 0),
    (0, -1, 0),
    (0, 0, 1),
    (0, 0, -1),
    (1, 1, 0),
    (-1, -1, 0),
    (1, -1, 0),
    (-1, 1, 0),
    (1, 0, 1),
    (-1, 0, -1),
    (1, 0, -1),
    (-1, 0, 1),
    (0, 1, 1),
    (0, -1, -1),
    (0, 1, -1),
    (0, -1, 1),
]
OPPOSITE = [0, 2, 1, 4, 3, 6, 5, 8, 7, 10, 9, 12, 11, 14, 13, 16, 15, 18, 17]
OMEGA = 1.25
LANES = 128
GROUP = 16


def pops(axis, sign):
    return [j for j in range(19) if VELOCITIES[j][axis] == sign]


def mirrored(j):
    cx, cy, cz = VELOCITIES[j]
    return VELOCITIES.index((cx, cy, -cz))


Z_FLAT = pops(2, 0)
Z_UP = pops(2, 1)
Z_DOWN = [mirrored(j) for j in Z_UP]
RHO, UX, UY, UZ, KIND = range(5)
Z_PLACE = {("pop", j): (0, g) for g, j in enumerate(Z_FLAT[:8])}
Z_PLACE[("pop", Z_FLAT[8])] = (1, 5)
Z_PLACE[("field", RHO)] = (1, 6)
Z_PLACE[("field", KIND)] = (1, 7)
Z_PLACE[("field", UX)] = (2, 5)
Z_PLACE[("field", UY)] = (2, 6)
Z_PLACE[("field", UZ)] = (2, 7)
BELOW, ABOVE, OWN_LOW, OWN_HIGH, Z_TILES = 0, 3, 6, 7, 8


def face_lines(axis, toward):
    near = pops(axis, 0) + pops(axis, toward)
    lines = [("pop", j, 0) for j in near] + [("field", k, 0) for k in range(5)]
    return lines + [("pop", j, 1) for j in pops(axis, toward)]


def edge_lines(toward_x, toward_y):
    lines = [("field", k, 0, 0) for k in range(5)]
    for j in range(19):
        cx, cy, _ = VELOCITIES[j]
        if cx not in (0, toward_x) or cy not in (0, toward_y):
            continue
        lines.append(("pop", j, 0, 0))
        if cx:
            lines.append(("pop", j, 1, 0))
        if cy:
            lines.append(("pop", j, 0, 1))
        if cx and cy:
            lines.append(("pop", j, 1, 1))
    return lines


FACE = 24
EDGE = 24


def lane_ids():
    return lax.broadcasted_iota(jnp.int32, (8, LANES), 1)


def field_of(refs, kind, index, at):
    adj, den, vel, mask = refs
    if kind == "pop":
        return adj[(index, *at)]
    if index == RHO:
        return den[(1, *at)]
    if index == KIND:
        return (mask[at] + 1).astype(jnp.float32)
    return vel[(1, index - UX, *at)]


def parity_of(axis):
    return lax.rem(lax.axis_index(axis), 2)


def on_side(parity, slot, act):
    @pl.when(parity == slot)
    def _():
        act(1)

    @pl.when(parity != slot)
    def _():
        act(0)


def has_partner(axis, slot):
    at = lax.axis_index(axis)
    to = at + jnp.where(lax.rem(at, 2) == slot, 1, -1)
    return (to >= 0) & (to < lax.axis_size(axis))


def pack_z_kernel(slots, adj_in, den_in, vel_in, mask_in, adj, den, vel, mask, near, *rest):
    packets, sems = rest[:slots], rest[slots]
    refs = (adj, den, vel, mask)
    ext_x, ext_y, _ = mask.shape
    starts = range(0, 19, 5)
    loads = [
        pltpu.make_async_copy(source, target, sems.at[len(starts) + at])
        for at, (source, target) in enumerate([(den_in.at[1], den.at[1]), (vel_in.at[1], vel.at[1]), (mask_in, mask)])
    ]
    group_loads = [
        pltpu.make_async_copy(adj_in.at[start : min(start + 5, 19)], adj.at[start : min(start + 5, 19)], sems.at[at])
        for at, start in enumerate(starts)
    ]
    last_loads = [
        pltpu.make_async_copy(source, target, sems.at[len(starts) + 3 + at])
        for at, (source, target) in enumerate([(den_in.at[0], den.at[0]), (vel_in.at[0], vel.at[0])])
    ]
    for load in loads + group_loads + last_loads:
        load.start()
    for load in loads:
        load.wait()
    lane = lane_ids()
    parity = parity_of("gz")
    parts = range(ext_y // 8)
    zero = jnp.zeros((8, LANES), jnp.float32)
    lows, highs = [[zero] * 3 for _ in parts], [[zero] * 3 for _ in parts]
    far_low, far_high = [zero for _ in parts], [zero for _ in parts]

    def gather(kind, index):
        for x, part in itertools.product(range(ext_x), parts):
            value = field_of(refs, kind, index, (x, pl.ds(8 * part, 8), slice(None)))
            if kind == "pop" and VELOCITIES[index][2] == 1:
                spot = GROUP * Z_UP.index(index) + 2 + x
                moved = pltpu.roll(value, spot, 1)
                lows[part][1] = jnp.where(lane == spot, moved, lows[part][1])
                far_low[part] = jnp.where(lane == spot + 1, moved, far_low[part])
            elif kind == "pop" and VELOCITIES[index][2] == -1:
                spot = GROUP * Z_DOWN.index(index) + 2 + x
                moved = pltpu.roll(value, spot, 1)
                highs[part][1] = jnp.where(lane == spot - 1, moved, highs[part][1])
                far_high[part] = jnp.where(lane == spot - 2, moved, far_high[part])
            else:
                tile, group = Z_PLACE[(kind, index)]
                spot = GROUP * group + 2 + x
                moved = pltpu.roll(value, spot, 1)
                lows[part][tile] = jnp.where(lane == spot, moved, lows[part][tile])
                highs[part][tile] = jnp.where(lane == spot - 1, moved, highs[part][tile])

    for k in range(5):
        gather("field", k)
    for start, load in zip(starts, group_loads):
        load.wait()
        for j in range(start, min(start + 5, 19)):
            gather("pop", j)
    for part in parts:
        rows = pl.ds(8 * part, 8)
        low = lows[part]
        high = [pltpu.roll(tile, 1, 1) for tile in highs[part]]
        low[2] = jnp.where(lane < 5 * GROUP, pltpu.roll(far_low[part], LANES - 1, 1), low[2])
        high[2] = jnp.where(lane < 5 * GROUP, pltpu.roll(far_high[part], 2, 1), high[2])
        near[0, rows, :] = low[1]
        near[1, rows, :] = high[1]
        for slot in range(slots):
            there = has_partner("gz", slot)
            for tile in range(3):
                value = jnp.where(parity == slot, high[tile], low[tile])
                packets[slot][tile, rows, :] = jnp.where(there, value, 0.0)
    for load in last_loads:
        load.wait()


def shift_kernel(adj, first):
    _, ext_x, ext_y, _ = adj.shape
    for j in range(19):
        cz = VELOCITIES[j][2]
        for x, part in itertools.product(range(ext_x), range(ext_y // 8)):
            value = adj[j, x, pl.ds(8 * part, 8), :]
            first[j, 2 + x, pl.ds(8 + 8 * part, 8), :] = pltpu.roll(value, -cz % LANES, 1) if cz else value


def pack_xy_kernel(slots, den, vel, mask, near, shifted, *rest):
    many_x, many_y, many_z = slots
    from_z, z_set, first, packets = rest[:many_z], rest[many_z], rest[many_z + 1], rest[many_z + 2 :]
    to_x, to_y = packets[:many_x], packets[many_x : many_x + many_y]
    to_xy, faces = packets[many_x + many_y : -1], packets[-1]
    refs = (None, den, vel, mask)
    ext_x, ext_y, _ = mask.shape
    spot = lane_ids() % GROUP
    every = slice(None)
    px, py, pz = parity_of("gx"), parity_of("gy"), parity_of("gz")

    z_set[OWN_LOW] = near[0]
    z_set[OWN_HIGH] = near[1]
    for tile in range(3):
        even = from_z[0][tile]
        odd = from_z[1][tile] if many_z > 1 else jnp.zeros_like(even)
        z_set[ABOVE + tile] = jnp.where(pz == 0, even, odd)
        z_set[BELOW + tile] = jnp.where(pz == 0, odd, even)

    for j in Z_UP + Z_DOWN:
        up = VELOCITIES[j][2] > 0
        group = (Z_UP if up else Z_DOWN).index(j)
        last = LANES - 1 if up else 0
        for part in range(ext_y // 8):
            halo = z_set[(ABOVE if up else BELOW) + 1, pl.ds(8 * part, 8), :]
            for x in range(ext_x):
                edge = pltpu.roll(halo, (last - 2 - GROUP * group - x) % LANES, 1)
                first[j, 2 + x, pl.ds(8 + 8 * part, 8), last : last + 1] = edge[:, last : last + 1]

    def line_of(kind, index, x, y):
        if kind == "pop":
            return first[index, x + 2, y + 8 : y + 9, :]
        return field_of(refs, kind, index, (x, slice(y, y + 1), every))

    for side in range(2):
        for part in range(ext_y // 8):
            rows = pl.ds(8 * part, 8)
            value = jnp.zeros((8, LANES), jnp.float32)
            for tile in range(Z_TILES):
                start = ext_x if side else 2
                moved = pltpu.roll(z_set[tile, rows, :], (2 * tile - start) % LANES, 1)
                value = jnp.where(spot // 2 == tile, moved, value)
            faces[side, rows, :] = value

    def pack_xy(slot_x, slot_y, side_x, side_y):
        packet = to_xy[many_x * slot_y + slot_x]
        for line, (kind, index, far_x, far_y) in enumerate(edge_lines(1 - 2 * side_x, 1 - 2 * side_y)):
            x = ext_x - 1 - far_x if side_x else far_x
            y = ext_y - 1 - far_y if side_y else far_y
            packet[line // 8, line % 8 : line % 8 + 1, :] = line_of(kind, index, x, y)
        start = ext_y - 2 if side_y else 0
        packet[EDGE // 8, 0:2, :] = faces[side_x, start : start + 2, :]

    def pack_y(slot, side):
        packet = to_y[slot]
        for line, (kind, index, depth) in enumerate(face_lines(1, 1 - 2 * side)):
            y = ext_y - 1 - depth if side else depth
            for x in range(ext_x):
                packet[line, x : x + 1, :] = line_of(kind, index, x, y)
        start = ext_y - 2 if side else 0
        for tile in range(Z_TILES):
            row = 2 * tile % 8
            packet[FACE + tile // 4, row : row + 2, :] = z_set[tile, start : start + 2, :]

    def pack_x(slot, side):
        for line, (kind, index, depth) in enumerate(face_lines(0, 1 - 2 * side)):
            x = ext_x - 1 - depth if side else depth
            if kind == "pop":
                to_x[slot][line] = first[index, x + 2, pl.ds(8, ext_y), :]
            else:
                to_x[slot][line] = field_of(refs, kind, index, (x, every, every))
        to_x[slot][FACE] = faces[side]

    def when_there(there, packet, act):
        pl.when(there)(act)

        @pl.when(jnp.logical_not(there))
        def _():
            packet[...] = jnp.zeros(packet.shape, jnp.float32)

    for slot_y in range(many_y):
        there_y = has_partner("gy", slot_y)
        when_there(there_y, to_y[slot_y], lambda: on_side(py, slot_y, functools.partial(pack_y, slot_y)))
        for slot_x in range(many_x):
            when_there(
                there_y & has_partner("gx", slot_x),
                to_xy[many_x * slot_y + slot_x],
                lambda: on_side(
                    py,
                    slot_y,
                    lambda side_y: on_side(px, slot_x, lambda side_x: pack_xy(slot_x, slot_y, side_x, side_y)),
                ),
            )
    for slot_x in range(many_x):
        when_there(
            has_partner("gx", slot_x), to_x[slot_x], lambda: on_side(px, slot_x, functools.partial(pack_x, slot_x))
        )


def collide(pulled, rho, ux, uy, uz, fluid, wanted):
    total = {}
    diff = {}
    for j in range(1, 19, 2):
        total[j] = pulled[j] + pulled[j + 1]
        diff[j] = pulled[j] - pulled[j + 1]
    in_xy, in_xz, in_yz = total[7] + total[9], total[11] + total[13], total[15] + total[17]
    two_x, two_y, two_z = total[1] + total[1], total[3] + total[3], total[5] + total[5]
    count = (12.0 * pulled[0] + (two_x + two_y)) + (two_z + (in_xy + (in_xz + in_yz)))
    flow_x = (diff[1] + diff[1]) + ((diff[7] + diff[9]) + (diff[11] + diff[13]))
    flow_y = (diff[3] + diff[3]) + ((diff[7] - diff[9]) + (diff[15] + diff[17]))
    flow_z = (diff[5] + diff[5]) + ((diff[11] - diff[13]) + (diff[15] - diff[17]))
    xx, yy, zz = two_x + (in_xy + in_xz), two_y + (in_xy + in_yz), two_z + (in_xz + in_yz)
    xy, xz, yz = total[7] - total[9], total[11] - total[13], total[15] - total[17]
    push_x = xx * ux + xy * uy + xz * uz
    push_y = xy * ux + yy * uy + yz * uz
    push_z = xz * ux + yz * uy + zz * uz
    usq = ux * ux + uy * uy + uz * uz
    push = ux * push_x + uy * push_y + uz * push_z
    inverse = 1.0 / rho
    base = count * (OMEGA / 36.0 + (OMEGA / 24.0) * usq) - (OMEGA / 8.0) * push - ux * inverse
    along_x = (OMEGA / 12.0) * (flow_x + 3.0 * push_x - ux * count) + inverse
    along_y = (OMEGA / 12.0) * (flow_y + 3.0 * push_y - uy * count)
    along_z = (OMEGA / 12.0) * (flow_z + 3.0 * push_z - uz * count)
    parts = {
        1: along_x,
        3: along_y,
        5: along_z,
        7: along_x + along_y,
        9: along_x - along_y,
        11: along_x + along_z,
        13: along_x - along_z,
        15: along_y + along_z,
        17: along_y - along_z,
    }
    out = {}
    for j in wanted:
        if j == 0:
            shift = base
        elif j % 2:
            shift = base + parts[j]
        else:
            shift = base - parts[j - 1]
        out[j] = jnp.where(fluid, (1.0 - OMEGA) * pulled[j] + shift, pulled[OPPOSITE[j]])
    change = (-1.0 / 6.0) * rho * (flow_x * ux + flow_y * uy + flow_z * uz)
    return out, jnp.where(fluid, change, 0.0)


def first_step(first, fields, second, change, take):
    pulled = [take(first, j, 2, *VELOCITIES[j][:2])[...] for j in range(19)]
    rho, ux, uy, uz, kind = [take(fields, k, 1, 0, 0)[...] for k in range(5)]
    after, gain = collide(pulled, rho, ux, uy, uz, kind > 1.5, range(19))
    for j in range(19):
        value = jnp.where(kind > 0.5, after[j], 0.0)
        cz = VELOCITIES[j][2]
        take(second, j, 1, 0, 0)[...] = pltpu.roll(value, -cz % LANES, 1) if cz else value
    take(change, None, 1, 0, 0)[...] = gain


def inner_kernel(den, vel, mask, first, fields, second, change):
    refs = (None, den, vel, mask)
    ext_x, ext_y, _ = mask.shape
    every = slice(None)
    for k in range(5):
        fields[k, 1 : 1 + ext_x, pl.ds(8, ext_y), :] = field_of(refs, "field", k, (every, every, every))

    @pl.loop(1, ext_x - 1)
    def _(x):
        for part in range(ext_y // 8):
            first_step(first, fields, second, change, plane_tile(x, 1 + 8 * part))


def plane_tile(x, row):
    def take(ref, lead, margin, cx, cy):
        at = (x + margin + cx, pl.ds(8 + row + cy, 8), slice(None))
        return ref.at[at if lead is None else (lead, *at)]

    return take


def row_tile(y, ext_x):
    def take(ref, lead, margin, cx, cy):
        at = (pl.ds(margin + cx, ext_x), y + 8 + cy, slice(None))
        return ref.at[at if lead is None else (lead, *at)]

    return take


def put_row(first, fields, kind, index, x, y, value):
    row = y + 8
    if kind == "pop":
        first[index, x + 2, row : row + 1, :] = value
    else:
        fields[index, x + 1, row : row + 1, :] = value


def place_z(z_first, value, start, size, side, ext_x):
    rows = pl.ds(start, size)
    spot = lane_ids()[:size] % GROUP
    inside = spot >= 2 + ext_x if side else spot < 2
    for tile in range(Z_TILES):
        shift = (2 + ext_x if side else 0) - 2 * tile
        moved = pltpu.roll(value, shift % LANES, 1)[:size]
        z_first[tile, rows, :] = jnp.where(inside, moved, z_first[tile, rows, :])


def side_kernel(slots, z_set, *rest):
    many_x, many_y = slots
    from_x, from_y = rest[4 : 4 + many_x], rest[4 + many_x : 4 + many_x + many_y]
    first, fields, second, change, z_first = rest[-5:]
    _, ext_y, _ = z_set.shape
    ext_x = change.shape[0] - 2
    inner = pl.ds(8, ext_y)
    put = functools.partial(put_row, first, fields)
    z_first[:, inner, :] = z_set[...]

    def place_y(slot, side):
        packet = from_y[slot]
        for line, (kind, index, depth) in enumerate(face_lines(1, 2 * side - 1)):
            y = ext_y + depth if side else -1 - depth
            for x in range(ext_x):
                put(kind, index, x, y, packet[line, x : x + 1, :])
        start = 8 + ext_y if side else 6
        for tile in range(Z_TILES):
            row = 2 * tile % 8
            z_first[tile, start : start + 2, :] = packet[FACE + tile // 4, row : row + 2, :]
        if many_y == 1:
            clear_y(1 - side)

    def clear_y(side):
        nothing = jnp.zeros((1, LANES), jnp.float32)
        for kind, index, depth in face_lines(1, 2 * side - 1):
            y = ext_y + depth if side else -1 - depth
            for x in range(-1, ext_x + 1):
                put(kind, index, x, y, nothing)
            if kind == "pop":
                put(kind, index, -2, y, nothing)
                put(kind, index, ext_x + 1, y, nothing)
        start = 8 + ext_y if side else 6
        for tile in range(Z_TILES):
            z_first[tile, start : start + 2, :] = jnp.zeros((2, LANES), jnp.float32)

    def place_x(slot, side):
        packet = from_x[slot]
        for line, (kind, index, depth) in enumerate(face_lines(0, 2 * side - 1)):
            x = ext_x + depth if side else -1 - depth
            if kind == "pop":
                first[index, x + 2, inner, :] = packet[line]
            else:
                fields[index, x + 1, inner, :] = packet[line]
        for part in range(ext_y // 8):
            place_z(z_first, packet[FACE, pl.ds(8 * part, 8), :], 8 + 8 * part, 8, side, ext_x)

    for slot_y in range(many_y):
        on_side(parity_of("gy"), slot_y, functools.partial(place_y, slot_y))
    for slot_x in range(many_x):
        on_side(parity_of("gx"), slot_x, functools.partial(place_x, slot_x))

    for x in (-1, 0, ext_x - 1, ext_x):
        for row in range(7, ext_y - 8, 8):
            first_step(first, fields, second, change, plane_tile(x, row))
    for y in (-1, 0, ext_y - 1, ext_y):
        first_step(first, fields, second, change, row_tile(y, ext_x))


def last_kernel(slots, den, vel, mask, *rest):
    many_x, many_y = slots
    from_xy = rest[5 : 5 + many_x * many_y]
    out, sens, first, fields, second, change, z_first, z_second, held, held_sens, sems = rest[-11:]
    ext_x, ext_y, _ = mask.shape
    lane = lane_ids()
    every = slice(None)
    px, py = parity_of("gx"), parity_of("gy")

    def place_xy(slot_x, slot_y, side_x, side_y):
        packet = from_xy[many_x * slot_y + slot_x]
        for line, (kind, index, far_x, far_y) in enumerate(edge_lines(2 * side_x - 1, 2 * side_y - 1)):
            x = ext_x + far_x if side_x else -1 - far_x
            y = ext_y + far_y if side_y else -1 - far_y
            put_row(first, fields, kind, index, x, y, packet[line // 8, line % 8 : line % 8 + 1, :])
        place_z(z_first, packet[EDGE // 8], 8 + ext_y if side_y else 6, 2, side_x, ext_x)

    for slot_x in range(many_x):
        for slot_y in range(many_y):
            on_side(
                py,
                slot_y,
                lambda side_y: on_side(px, slot_x, lambda side_x: place_xy(slot_x, slot_y, side_x, side_y)),
            )

    for x in (-1, 0, ext_x - 1, ext_x):
        for row in (-1, ext_y - 1):
            first_step(first, fields, second, change, plane_tile(x, row))

    for part in range((ext_y + 2 + 7) // 8):
        row = 7 + 8 * part

        def both(low_tile, high_tile, group, cx, cy):
            rows = pl.ds(row + cy, 8)
            low = pltpu.roll(z_first[low_tile, rows, :], (-GROUP * group - cx) % LANES, 1)
            high = pltpu.roll(z_first[high_tile, rows, :], (LANES // 2 - GROUP * group - cx) % LANES, 1)
            return jnp.where(lane < LANES // 2, low, high)

        pulled = []
        for j in range(19):
            cx, cy, cz = VELOCITIES[j]
            if cz == 0:
                tile, group = Z_PLACE[("pop", j)]
                pulled.append(both(BELOW + tile, ABOVE + tile, group, cx, cy))
            elif cz == 1:
                pulled.append(both(OWN_LOW, ABOVE + 2, Z_UP.index(j), cx, cy))
            else:
                pulled.append(both(BELOW + 2, OWN_HIGH, Z_DOWN.index(j), cx, cy))
        rho, ux, uy, uz, kind = [
            both(BELOW + tile, ABOVE + tile, group, 0, 0)
            for tile, group in [Z_PLACE[("field", k)] for k in range(5)]
        ]
        after, _ = collide(pulled, rho, ux, uy, uz, kind > 1.5, Z_UP + Z_DOWN)
        for group in range(5):
            value = jnp.where(lane < LANES // 2, after[Z_DOWN[group]], after[Z_UP[group]])
            z_second[group, pl.ds(row, 8), :] = jnp.where(kind > 0.5, value, 0.0)

    def copies(x):
        return (
            pltpu.make_async_copy(held.at[:, x], out.at[:, x], sems.at[0, x]),
            pltpu.make_async_copy(held_sens.at[x], sens.at[x], sems.at[1, x]),
        )

    @pl.loop(0, ext_x)
    def _(x):
        for part in range(ext_y // 8):
            row = 8 + 8 * part
            at = (x, pl.ds(8 * part, 8), every)
            pulled = []
            for j in range(19):
                cx, cy, cz = VELOCITIES[j]
                rows = pl.ds(row + cy, 8)
                value = second[j, x + 1 + cx, rows, :]
                if cz == 1:
                    edge = z_second[Z_UP.index(j), rows, :]
                    edge = pltpu.roll(edge, LANES // 2 - 3 - cx - x, 1)
                    value = jnp.where(lane == LANES - 1, edge, value)
                elif cz == -1:
                    edge = z_second[Z_DOWN.index(j), rows, :]
                    edge = pltpu.roll(edge, LANES - 2 - cx - x, 1)
                    value = jnp.where(lane == 0, edge, value)
                pulled.append(value)
            after, gain = collide(
                pulled,
                den[(0, *at)],
                vel[(0, 0, *at)],
                vel[(0, 1, *at)],
                vel[(0, 2, *at)],
                mask[at] > 0,
                range(19),
            )
            for j in range(19):
                held[(j, *at)] = after[j]
            held_sens[at] = change[x + 1, pl.ds(row, 8), :] + gain
        for copy in copies(x):
            copy.start()

    for x in range(ext_x):
        for copy in copies(x):
            copy.wait()


def shards(adjoint, density, velocity, pore_mask):
    ext_x, ext_y, ext_z = pore_mask.shape
    assert ext_z == LANES and ext_y % 8 == 0 and ext_x + 4 <= GROUP and ext_x == 8
    many_x = 2
    many_y, many_z = [1 if lax.axis_size(axis) == 2 else 2 for axis in ("gy", "gz")]
    vmem = pl.BlockSpec(memory_space=pltpu.VMEM)
    hbm = pl.BlockSpec(memory_space=pltpu.HBM)
    inputs = (adjoint, density, velocity, pore_mask)

    def array(*shape):
        return jax.ShapeDtypeStruct(shape, jnp.float32)

    def call(kernel, name, operands, shapes, limit, **more):
        more.setdefault("out_specs", [vmem] * len(shapes))
        more.setdefault("in_specs", [vmem] * len(operands))
        params = pltpu.CompilerParams(vmem_limit_bytes=limit * 1024 * 1024)
        return pl.pallas_call(kernel, out_shape=shapes, compiler_params=params, name=name, **more)(*operands)

    def partners(axis, slot, ends=False):
        size = lax.axis_size(axis)
        found = {}
        for at in range(slot, size - 1, 2):
            found[at], found[at + 1] = at + 1, at
        if ends and slot and size % 2 == 0:
            found[0], found[size - 1] = size - 1, 0
        return found

    def swap(value, spare, *places):
        tables = {axis: partners(axis, slot, spare == axis) for axis, slot in places}
        axes = [axis for axis in ("gx", "gy", "gz") if axis in tables or axis == spare]
        sizes = [lax.axis_size(axis) for axis in axes]
        pairs = []
        for at in itertools.product(*[range(size) for size in sizes]):
            to = [tables.get(axis, {}).get(spot, spot) for axis, spot in zip(axes, at)]
            if spare is not None and tuple(to) == at:
                to = [partners(spare, 0).get(spot, spot) if axis == spare else spot for axis, spot in zip(axes, at)]
            flat = []
            for spots in (at, to):
                index = 0
                for size, spot in zip(sizes, spots):
                    index = index * size + spot
                flat.append(index)
            pairs.append(tuple(flat))
        return lax.ppermute(value, tuple(axes), pairs)

    loaded = [jax.ShapeDtypeStruct(value.shape, value.dtype) for value in inputs]
    *held, near, a_z, b_z = (
        *call(
            functools.partial(pack_z_kernel, many_z),
            "pack_z",
            [pltpu.with_memory_space_constraint(value, pltpu.HBM) for value in inputs],
            loaded + [array(2, ext_y, LANES)] + [array(3, ext_y, LANES)] * many_z,
            8,
            in_specs=[hbm] * 4,
            scratch_shapes=[pltpu.SemaphoreType.DMA((9,))],
        ),
        *[None] * (2 - many_z),
    )
    from_z = [swap(value, "gx", ("gz", slot)) for slot, value in enumerate((a_z, b_z)[:many_z])]

    rows = ext_y + 16
    adj, den, vel, mask = held
    (shifted,) = call(
        shift_kernel,
        "shift",
        (adj,),
        [array(19, ext_x + 4, rows, LANES)],
        8,
        cost_estimate=pl.CostEstimate(flops=1_000_000, bytes_accessed=2_500_000, transcendentals=0),
    )
    z_set, first, *packets = call(
        functools.partial(pack_xy_kernel, (many_x, many_y, many_z)),
        "pack_xy",
        (den, vel, mask, near, shifted, *from_z),
        [array(Z_TILES, ext_y, LANES), array(19, ext_x + 4, rows, LANES)]
        + [array(FACE + 1, ext_y, LANES)] * many_x
        + [array(FACE + 2, ext_x, LANES)] * many_y
        + [array(EDGE // 8 + 1, 8, LANES)] * (many_x * many_y),
        8,
        input_output_aliases={4: 1},
        scratch_shapes=[pltpu.VMEM((2, ext_y, LANES), jnp.float32)],
    )
    to_x, to_y, to_xy = packets[:many_x], packets[many_x : many_x + many_y], packets[many_x + many_y :]
    from_xy = [
        swap(to_xy[many_x * slot_y + slot_x], None, ("gx", slot_x), ("gy", slot_y))
        for slot_y in range(many_y)
        for slot_x in range(many_x)
    ]
    from_y = [swap(value, "gz", ("gy", slot)) for slot, value in enumerate(to_y)]
    from_x = [swap(value, "gy", ("gx", slot)) for slot, value in enumerate(to_x)]

    fields, second, change = call(
        inner_kernel,
        "inner_step",
        (den, vel, mask, first),
        [array(5, ext_x + 2, rows, LANES), array(19, ext_x + 2, rows, LANES), array(ext_x + 2, rows, LANES)],
        8,
        cost_estimate=pl.CostEstimate(flops=40_000_000, bytes_accessed=8_000_000, transcendentals=0),
    )
    inout = (first, fields, second, change)
    inout = call(
        functools.partial(side_kernel, (many_x, many_y)),
        "side_step",
        (z_set, *inout, *from_x, *from_y),
        [array(*value.shape) for value in inout] + [array(Z_TILES, rows, LANES)],
        8,
        input_output_aliases={1 + at: at for at in range(4)},
        cost_estimate=pl.CostEstimate(flops=40_000_000, bytes_accessed=8_000_000, transcendentals=0),
    )
    return call(
        functools.partial(last_kernel, (many_x, many_y)),
        "last_steps",
        (den, vel, mask, *inout, *from_xy),
        [array(19, ext_x, ext_y, LANES), array(ext_x, ext_y, LANES)] + [array(*value.shape) for value in inout],
        8,
        out_specs=[hbm] * 2 + [vmem] * 5,
        input_output_aliases={3 + at: 2 + at for at in range(5)},
        scratch_shapes=[
            pltpu.VMEM((5, rows, LANES), jnp.float32),
            pltpu.VMEM((19, ext_x, ext_y, LANES), jnp.float32),
            pltpu.VMEM((ext_x, ext_y, LANES), jnp.float32),
            pltpu.SemaphoreType.DMA((2, ext_x)),
        ],
    )[:2]


def solution(mesh):
    placed = (
        P(None, "gx", "gy", "gz"),
        P(None, "gx", "gy", "gz"),
        P(None, None, "gx", "gy", "gz"),
        P("gx", "gy", "gz"),
    )

    def whole(*arrays):
        return tuple(shards(*arrays))

    return jax.shard_map(
        whole,
        mesh=mesh,
        in_specs=placed,
        out_specs=(P(None, "gx", "gy", "gz"), P("gx", "gy", "gz")),
        check_vma=False,
    )
```

```python
import functools
import itertools

import jax
import jax.numpy as jnp
from jax import lax
from jax.experimental import pallas as pl
from jax.experimental.pallas import tpu as pltpu
from jax.sharding import PartitionSpec as P

VELOCITIES = [
    (0, 0, 0),
    (1, 0, 0),
    (-1, 0, 0),
    (0, 1, 0),
    (0, -1, 0),
    (0, 0, 1),
    (0, 0, -1),
    (1, 1, 0),
    (-1, -1, 0),
    (1, -1, 0),
    (-1, 1, 0),
    (1, 0, 1),
    (-1, 0, -1),
    (1, 0, -1),
    (-1, 0, 1),
    (0, 1, 1),
    (0, -1, -1),
    (0, 1, -1),
    (0, -1, 1),
]
OPPOSITE = [0, 2, 1, 4, 3, 6, 5, 8, 7, 10, 9, 12, 11, 14, 13, 16, 15, 18, 17]
OMEGA = 1.25
LANES = 128
GROUP = 16


def pops(axis, sign):
    return [j for j in range(19) if VELOCITIES[j][axis] == sign]


def mirrored(j):
    cx, cy, cz = VELOCITIES[j]
    return VELOCITIES.index((cx, cy, -cz))


Z_FLAT = pops(2, 0)
Z_UP = pops(2, 1)
Z_DOWN = [mirrored(j) for j in Z_UP]
RHO, UX, UY, UZ, KIND = range(5)
Z_PLACE = {("pop", j): (0, g) for g, j in enumerate(Z_FLAT[:8])}
Z_PLACE[("pop", Z_FLAT[8])] = (1, 5)
Z_PLACE[("field", RHO)] = (1, 6)
Z_PLACE[("field", KIND)] = (1, 7)
Z_PLACE[("field", UX)] = (2, 5)
Z_PLACE[("field", UY)] = (2, 6)
Z_PLACE[("field", UZ)] = (2, 7)
BELOW, ABOVE, OWN_LOW, OWN_HIGH, Z_TILES = 0, 3, 6, 7, 8


def face_lines(axis, toward):
    near = pops(axis, 0) + pops(axis, toward)
    lines = [("pop", j, 0) for j in near] + [("field", k, 0) for k in range(5)]
    return lines + [("pop", j, 1) for j in pops(axis, toward)]


def edge_lines(toward_x, toward_y):
    lines = [("field", k, 0, 0) for k in range(5)]
    for j in range(19):
        cx, cy, _ = VELOCITIES[j]
        if cx not in (0, toward_x) or cy not in (0, toward_y):
            continue
        lines.append(("pop", j, 0, 0))
        if cx:
            lines.append(("pop", j, 1, 0))
        if cy:
            lines.append(("pop", j, 0, 1))
        if cx and cy:
            lines.append(("pop", j, 1, 1))
    return lines


FACE = 24
EDGE = 24


def lane_ids():
    return lax.broadcasted_iota(jnp.int32, (8, LANES), 1)


def field_of(refs, kind, index, at):
    adj, den, vel, mask = refs
    if kind == "pop":
        return adj[(index, *at)]
    if index == RHO:
        return den[(1, *at)]
    if index == KIND:
        return (mask[at] + 1).astype(jnp.float32)
    return vel[(1, index - UX, *at)]


def parity_of(axis):
    return lax.rem(lax.axis_index(axis), 2)


def on_side(parity, slot, act):
    @pl.when(parity == slot)
    def _():
        act(1)

    @pl.when(parity != slot)
    def _():
        act(0)


def has_partner(axis, slot):
    at = lax.axis_index(axis)
    to = at + jnp.where(lax.rem(at, 2) == slot, 1, -1)
    return (to >= 0) & (to < lax.axis_size(axis))


def pack_z_kernel(slots, adj_in, den_in, vel_in, mask_in, adj, den, vel, mask, near, *rest):
    packets, sems = rest[:slots], rest[slots]
    refs = (adj, den, vel, mask)
    ext_x, ext_y, _ = mask.shape
    starts = range(0, 19, 5)
    loads = [
        pltpu.make_async_copy(source, target, sems.at[len(starts) + at])
        for at, (source, target) in enumerate([(den_in.at[1], den.at[1]), (vel_in.at[1], vel.at[1]), (mask_in, mask)])
    ]
    group_loads = [
        pltpu.make_async_copy(adj_in.at[start : min(start + 5, 19)], adj.at[start : min(start + 5, 19)], sems.at[at])
        for at, start in enumerate(starts)
    ]
    last_loads = [
        pltpu.make_async_copy(source, target, sems.at[len(starts) + 3 + at])
        for at, (source, target) in enumerate([(den_in.at[0], den.at[0]), (vel_in.at[0], vel.at[0])])
    ]
    for load in loads + group_loads + last_loads:
        load.start()
    for load in loads:
        load.wait()
    lane = lane_ids()
    parity = parity_of("gz")
    parts = range(ext_y // 8)
    zero = jnp.zeros((8, LANES), jnp.float32)
    lows, highs = [[zero] * 3 for _ in parts], [[zero] * 3 for _ in parts]
    far_low, far_high = [zero for _ in parts], [zero for _ in parts]

    def gather(kind, index):
        for x, part in itertools.product(range(ext_x), parts):
            value = field_of(refs, kind, index, (x, pl.ds(8 * part, 8), slice(None)))
            if kind == "pop" and VELOCITIES[index][2] == 1:
                spot = GROUP * Z_UP.index(index) + 2 + x
                moved = pltpu.roll(value, spot, 1)
                lows[part][1] = jnp.where(lane == spot, moved, lows[part][1])
                far_low[part] = jnp.where(lane == spot + 1, moved, far_low[part])
            elif kind == "pop" and VELOCITIES[index][2] == -1:
                spot = GROUP * Z_DOWN.index(index) + 2 + x
                moved = pltpu.roll(value, spot, 1)
                highs[part][1] = jnp.where(lane == spot - 1, moved, highs[part][1])
                far_high[part] = jnp.where(lane == spot - 2, moved, far_high[part])
            else:
                tile, group = Z_PLACE[(kind, index)]
                spot = GROUP * group + 2 + x
                moved = pltpu.roll(value, spot, 1)
                lows[part][tile] = jnp.where(lane == spot, moved, lows[part][tile])
                highs[part][tile] = jnp.where(lane == spot - 1, moved, highs[part][tile])

    for k in range(5):
        gather("field", k)
    for start, load in zip(starts, group_loads):
        load.wait()
        for j in range(start, min(start + 5, 19)):
            gather("pop", j)
    for part in parts:
        rows = pl.ds(8 * part, 8)
        low = lows[part]
        high = [pltpu.roll(tile, 1, 1) for tile in highs[part]]
        low[2] = jnp.where(lane < 5 * GROUP, pltpu.roll(far_low[part], LANES - 1, 1), low[2])
        high[2] = jnp.where(lane < 5 * GROUP, pltpu.roll(far_high[part], 2, 1), high[2])
        near[0, rows, :] = low[1]
        near[1, rows, :] = high[1]
        for slot in range(slots):
            there = has_partner("gz", slot)
            for tile in range(3):
                value = jnp.where(parity == slot, high[tile], low[tile])
                packets[slot][tile, rows, :] = jnp.where(there, value, 0.0)
    for load in last_loads:
        load.wait()


def shift_kernel(adj, first):
    _, ext_x, ext_y, _ = adj.shape
    for j in range(19):
        cz = VELOCITIES[j][2]
        for x, part in itertools.product(range(ext_x), range(ext_y // 8)):
            value = adj[j, x, pl.ds(8 * part, 8), :]
            first[j, 2 + x, pl.ds(8 + 8 * part, 8), :] = pltpu.roll(value, -cz % LANES, 1) if cz else value


def pack_xy_kernel(slots, den, vel, mask, near, shifted, *rest):
    many_x, many_y, many_z = slots
    from_z, z_set, first, packets = rest[:many_z], rest[many_z], rest[many_z + 1], rest[many_z + 2 :]
    to_x, to_y = packets[:many_x], packets[many_x : many_x + many_y]
    to_xy, faces = packets[many_x + many_y : -1], packets[-1]
    refs = (None, den, vel, mask)
    ext_x, ext_y, _ = mask.shape
    spot = lane_ids() % GROUP
    every = slice(None)
    px, py, pz = parity_of("gx"), parity_of("gy"), parity_of("gz")

    z_set[OWN_LOW] = near[0]
    z_set[OWN_HIGH] = near[1]
    for tile in range(3):
        even = from_z[0][tile]
        odd = from_z[1][tile] if many_z > 1 else jnp.zeros_like(even)
        z_set[ABOVE + tile] = jnp.where(pz == 0, even, odd)
        z_set[BELOW + tile] = jnp.where(pz == 0, odd, even)

    for j in Z_UP + Z_DOWN:
        up = VELOCITIES[j][2] > 0
        group = (Z_UP if up else Z_DOWN).index(j)
        last = LANES - 1 if up else 0
        for part in range(ext_y // 8):
            halo = z_set[(ABOVE if up else BELOW) + 1, pl.ds(8 * part, 8), :]
            for x in range(ext_x):
                edge = pltpu.roll(halo, (last - 2 - GROUP * group - x) % LANES, 1)
                first[j, 2 + x, pl.ds(8 + 8 * part, 8), last : last + 1] = edge[:, last : last + 1]

    def line_of(kind, index, x, y):
        if kind == "pop":
            return first[index, x + 2, y + 8 : y + 9, :]
        return field_of(refs, kind, index, (x, slice(y, y + 1), every))

    for side in range(2):
        for part in range(ext_y // 8):
            rows = pl.ds(8 * part, 8)
            value = jnp.zeros((8, LANES), jnp.float32)
            for tile in range(Z_TILES):
                start = ext_x if side else 2
                moved = pltpu.roll(z_set[tile, rows, :], (2 * tile - start) % LANES, 1)
                value = jnp.where(spot // 2 == tile, moved, value)
            faces[side, rows, :] = value

    def pack_xy(slot_x, slot_y, side_x, side_y):
        packet = to_xy[many_x * slot_y + slot_x]
        for line, (kind, index, far_x, far_y) in enumerate(edge_lines(1 - 2 * side_x, 1 - 2 * side_y)):
            x = ext_x - 1 - far_x if side_x else far_x
            y = ext_y - 1 - far_y if side_y else far_y
            packet[line // 8, line % 8 : line % 8 + 1, :] = line_of(kind, index, x, y)
        start = ext_y - 2 if side_y else 0
        packet[EDGE // 8, 0:2, :] = faces[side_x, start : start + 2, :]

    def pack_y(slot, side):
        packet = to_y[slot]
        for line, (kind, index, depth) in enumerate(face_lines(1, 1 - 2 * side)):
            y = ext_y - 1 - depth if side else depth
            for x in range(ext_x):
                packet[line, x : x + 1, :] = line_of(kind, index, x, y)
        start = ext_y - 2 if side else 0
        for tile in range(Z_TILES):
            row = 2 * tile % 8
            packet[FACE + tile // 4, row : row + 2, :] = z_set[tile, start : start + 2, :]

    def pack_x(slot, side):
        for line, (kind, index, depth) in enumerate(face_lines(0, 1 - 2 * side)):
            x = ext_x - 1 - depth if side else depth
            if kind == "pop":
                to_x[slot][line] = first[index, x + 2, pl.ds(8, ext_y), :]
            else:
                to_x[slot][line] = field_of(refs, kind, index, (x, every, every))
        to_x[slot][FACE] = faces[side]

    def when_there(there, packet, act):
        pl.when(there)(act)

        @pl.when(jnp.logical_not(there))
        def _():
            packet[...] = jnp.zeros(packet.shape, jnp.float32)

    for slot_y in range(many_y):
        there_y = has_partner("gy", slot_y)
        when_there(there_y, to_y[slot_y], lambda: on_side(py, slot_y, functools.partial(pack_y, slot_y)))
        for slot_x in range(many_x):
            when_there(
                there_y & has_partner("gx", slot_x),
                to_xy[many_x * slot_y + slot_x],
                lambda: on_side(
                    py,
                    slot_y,
                    lambda side_y: on_side(px, slot_x, lambda side_x: pack_xy(slot_x, slot_y, side_x, side_y)),
                ),
            )
    for slot_x in range(many_x):
        when_there(
            has_partner("gx", slot_x), to_x[slot_x], lambda: on_side(px, slot_x, functools.partial(pack_x, slot_x))
        )


def collide(pulled, rho, ux, uy, uz, fluid, wanted):
    total = {}
    diff = {}
    for j in range(1, 19, 2):
        total[j] = pulled[j] + pulled[j + 1]
        diff[j] = pulled[j] - pulled[j + 1]
    in_xy, in_xz, in_yz = total[7] + total[9], total[11] + total[13], total[15] + total[17]
    two_x, two_y, two_z = total[1] + total[1], total[3] + total[3], total[5] + total[5]
    count = (12.0 * pulled[0] + (two_x + two_y)) + (two_z + (in_xy + (in_xz + in_yz)))
    flow_x = (diff[1] + diff[1]) + ((diff[7] + diff[9]) + (diff[11] + diff[13]))
    flow_y = (diff[3] + diff[3]) + ((diff[7] - diff[9]) + (diff[15] + diff[17]))
    flow_z = (diff[5] + diff[5]) + ((diff[11] - diff[13]) + (diff[15] - diff[17]))
    xx, yy, zz = two_x + (in_xy + in_xz), two_y + (in_xy + in_yz), two_z + (in_xz + in_yz)
    xy, xz, yz = total[7] - total[9], total[11] - total[13], total[15] - total[17]
    push_x = xx * ux + xy * uy + xz * uz
    push_y = xy * ux + yy * uy + yz * uz
    push_z = xz * ux + yz * uy + zz * uz
    usq = ux * ux + uy * uy + uz * uz
    push = ux * push_x + uy * push_y + uz * push_z
    inverse = 1.0 / rho
    base = count * (OMEGA / 36.0 + (OMEGA / 24.0) * usq) - (OMEGA / 8.0) * push - ux * inverse
    along_x = (OMEGA / 12.0) * (flow_x + 3.0 * push_x - ux * count) + inverse
    along_y = (OMEGA / 12.0) * (flow_y + 3.0 * push_y - uy * count)
    along_z = (OMEGA / 12.0) * (flow_z + 3.0 * push_z - uz * count)
    parts = {
        1: along_x,
        3: along_y,
        5: along_z,
        7: along_x + along_y,
        9: along_x - along_y,
        11: along_x + along_z,
        13: along_x - along_z,
        15: along_y + along_z,
        17: along_y - along_z,
    }
    out = {}
    for j in wanted:
        if j == 0:
            shift = base
        elif j % 2:
            shift = base + parts[j]
        else:
            shift = base - parts[j - 1]
        out[j] = jnp.where(fluid, (1.0 - OMEGA) * pulled[j] + shift, pulled[OPPOSITE[j]])
    change = (-1.0 / 6.0) * rho * (flow_x * ux + flow_y * uy + flow_z * uz)
    return out, jnp.where(fluid, change, 0.0)


def first_step(first, fields, second, change, take):
    pulled = [take(first, j, 2, *VELOCITIES[j][:2])[...] for j in range(19)]
    rho, ux, uy, uz, kind = [take(fields, k, 1, 0, 0)[...] for k in range(5)]
    after, gain = collide(pulled, rho, ux, uy, uz, kind > 1.5, range(19))
    for j in range(19):
        value = jnp.where(kind > 0.5, after[j], 0.0)
        cz = VELOCITIES[j][2]
        take(second, j, 1, 0, 0)[...] = pltpu.roll(value, -cz % LANES, 1) if cz else value
    take(change, None, 1, 0, 0)[...] = gain


def inner_kernel(den, vel, mask, first, fields, second, change):
    refs = (None, den, vel, mask)
    ext_x, ext_y, _ = mask.shape
    every = slice(None)
    for k in range(5):
        fields[k, 1 : 1 + ext_x, pl.ds(8, ext_y), :] = field_of(refs, "field", k, (every, every, every))

    @pl.loop(1, ext_x - 1)
    def _(x):
        for part in range(ext_y // 8):
            first_step(first, fields, second, change, plane_tile(x, 1 + 8 * part))


def plane_tile(x, row):
    def take(ref, lead, margin, cx, cy):
        at = (x + margin + cx, pl.ds(8 + row + cy, 8), slice(None))
        return ref.at[at if lead is None else (lead, *at)]

    return take


def row_tile(y, ext_x):
    def take(ref, lead, margin, cx, cy):
        at = (pl.ds(margin + cx, ext_x), y + 8 + cy, slice(None))
        return ref.at[at if lead is None else (lead, *at)]

    return take


def put_row(first, fields, kind, index, x, y, value):
    row = y + 8
    if kind == "pop":
        first[index, x + 2, row : row + 1, :] = value
    else:
        fields[index, x + 1, row : row + 1, :] = value


def place_z(z_first, value, start, size, side, ext_x):
    rows = pl.ds(start, size)
    spot = lane_ids()[:size] % GROUP
    inside = spot >= 2 + ext_x if side else spot < 2
    for tile in range(Z_TILES):
        shift = (2 + ext_x if side else 0) - 2 * tile
        moved = pltpu.roll(value, shift % LANES, 1)[:size]
        z_first[tile, rows, :] = jnp.where(inside, moved, z_first[tile, rows, :])


def side_kernel(slots, z_set, *rest):
    many_x, many_y = slots
    from_x, from_y = rest[4 : 4 + many_x], rest[4 + many_x : 4 + many_x + many_y]
    first, fields, second, change, z_first = rest[-5:]
    _, ext_y, _ = z_set.shape
    ext_x = change.shape[0] - 2
    inner = pl.ds(8, ext_y)
    put = functools.partial(put_row, first, fields)
    z_first[:, inner, :] = z_set[...]

    def place_y(slot, side):
        packet = from_y[slot]
        for line, (kind, index, depth) in enumerate(face_lines(1, 2 * side - 1)):
            y = ext_y + depth if side else -1 - depth
            for x in range(ext_x):
                put(kind, index, x, y, packet[line, x : x + 1, :])
        start = 8 + ext_y if side else 6
        for tile in range(Z_TILES):
            row = 2 * tile % 8
            z_first[tile, start : start + 2, :] = packet[FACE + tile // 4, row : row + 2, :]
        if many_y == 1:
            clear_y(1 - side)

    def clear_y(side):
        nothing = jnp.zeros((1, LANES), jnp.float32)
        for kind, index, depth in face_lines(1, 2 * side - 1):
            y = ext_y + depth if side else -1 - depth
            for x in range(-1, ext_x + 1):
                put(kind, index, x, y, nothing)
            if kind == "pop":
                put(kind, index, -2, y, nothing)
                put(kind, index, ext_x + 1, y, nothing)
        start = 8 + ext_y if side else 6
        for tile in range(Z_TILES):
            z_first[tile, start : start + 2, :] = jnp.zeros((2, LANES), jnp.float32)

    def place_x(slot, side):
        packet = from_x[slot]
        for line, (kind, index, depth) in enumerate(face_lines(0, 2 * side - 1)):
            x = ext_x + depth if side else -1 - depth
            if kind == "pop":
                first[index, x + 2, inner, :] = packet[line]
            else:
                fields[index, x + 1, inner, :] = packet[line]
        for part in range(ext_y // 8):
            place_z(z_first, packet[FACE, pl.ds(8 * part, 8), :], 8 + 8 * part, 8, side, ext_x)

    for slot_y in range(many_y):
        on_side(parity_of("gy"), slot_y, functools.partial(place_y, slot_y))
    for slot_x in range(many_x):
        on_side(parity_of("gx"), slot_x, functools.partial(place_x, slot_x))

    for x in (-1, 0, ext_x - 1, ext_x):
        for row in range(7, ext_y - 8, 8):
            first_step(first, fields, second, change, plane_tile(x, row))
    for y in (-1, 0, ext_y - 1, ext_y):
        first_step(first, fields, second, change, row_tile(y, ext_x))


def last_kernel(slots, den, vel, mask, *rest):
    many_x, many_y = slots
    from_xy = rest[5 : 5 + many_x * many_y]
    out, sens, first, fields, second, change, z_first, z_second, held, held_sens, sems = rest[-11:]
    ext_x, ext_y, _ = mask.shape
    lane = lane_ids()
    every = slice(None)
    px, py = parity_of("gx"), parity_of("gy")

    def place_xy(slot_x, slot_y, side_x, side_y):
        packet = from_xy[many_x * slot_y + slot_x]
        for line, (kind, index, far_x, far_y) in enumerate(edge_lines(2 * side_x - 1, 2 * side_y - 1)):
            x = ext_x + far_x if side_x else -1 - far_x
            y = ext_y + far_y if side_y else -1 - far_y
            put_row(first, fields, kind, index, x, y, packet[line // 8, line % 8 : line % 8 + 1, :])
        place_z(z_first, packet[EDGE // 8], 8 + ext_y if side_y else 6, 2, side_x, ext_x)

    for slot_x in range(many_x):
        for slot_y in range(many_y):
            on_side(
                py,
                slot_y,
                lambda side_y: on_side(px, slot_x, lambda side_x: place_xy(slot_x, slot_y, side_x, side_y)),
            )

    for x in (-1, 0, ext_x - 1, ext_x):
        for row in (-1, ext_y - 1):
            first_step(first, fields, second, change, plane_tile(x, row))

    for part in range((ext_y + 2 + 7) // 8):
        row = 7 + 8 * part

        def both(low_tile, high_tile, group, cx, cy):
            rows = pl.ds(row + cy, 8)
            low = pltpu.roll(z_first[low_tile, rows, :], (-GROUP * group - cx) % LANES, 1)
            high = pltpu.roll(z_first[high_tile, rows, :], (LANES // 2 - GROUP * group - cx) % LANES, 1)
            return jnp.where(lane < LANES // 2, low, high)

        pulled = []
        for j in range(19):
            cx, cy, cz = VELOCITIES[j]
            if cz == 0:
                tile, group = Z_PLACE[("pop", j)]
                pulled.append(both(BELOW + tile, ABOVE + tile, group, cx, cy))
            elif cz == 1:
                pulled.append(both(OWN_LOW, ABOVE + 2, Z_UP.index(j), cx, cy))
            else:
                pulled.append(both(BELOW + 2, OWN_HIGH, Z_DOWN.index(j), cx, cy))
        rho, ux, uy, uz, kind = [
            both(BELOW + tile, ABOVE + tile, group, 0, 0)
            for tile, group in [Z_PLACE[("field", k)] for k in range(5)]
        ]
        after, _ = collide(pulled, rho, ux, uy, uz, kind > 1.5, Z_UP + Z_DOWN)
        for group in range(5):
            value = jnp.where(lane < LANES // 2, after[Z_DOWN[group]], after[Z_UP[group]])
            z_second[group, pl.ds(row, 8), :] = jnp.where(kind > 0.5, value, 0.0)

    def copies(x):
        return (
            pltpu.make_async_copy(held.at[:, x], out.at[:, x], sems.at[0, x]),
            pltpu.make_async_copy(held_sens.at[x], sens.at[x], sems.at[1, x]),
        )

    @pl.loop(0, ext_x)
    def _(x):
        for part in range(ext_y // 8):
            row = 8 + 8 * part
            at = (x, pl.ds(8 * part, 8), every)
            pulled = []
            for j in range(19):
                cx, cy, cz = VELOCITIES[j]
                rows = pl.ds(row + cy, 8)
                value = second[j, x + 1 + cx, rows, :]
                if cz == 1:
                    edge = z_second[Z_UP.index(j), rows, :]
                    edge = pltpu.roll(edge, LANES // 2 - 3 - cx - x, 1)
                    value = jnp.where(lane == LANES - 1, edge, value)
                elif cz == -1:
                    edge = z_second[Z_DOWN.index(j), rows, :]
                    edge = pltpu.roll(edge, LANES - 2 - cx - x, 1)
                    value = jnp.where(lane == 0, edge, value)
                pulled.append(value)
            after, gain = collide(
                pulled,
                den[(0, *at)],
                vel[(0, 0, *at)],
                vel[(0, 1, *at)],
                vel[(0, 2, *at)],
                mask[at] > 0,
                range(19),
            )
            for j in range(19):
                held[(j, *at)] = after[j]
            held_sens[at] = change[x + 1, pl.ds(row, 8), :] + gain
        for copy in copies(x):
            copy.start()

    for x in range(ext_x):
        for copy in copies(x):
            copy.wait()


def shards(adjoint, density, velocity, pore_mask):
    ext_x, ext_y, ext_z = pore_mask.shape
    assert ext_z == LANES and ext_y % 8 == 0 and ext_x + 4 <= GROUP and ext_x == 8
    many_x = 2
    many_y, many_z = [1 if lax.axis_size(axis) == 2 else 2 for axis in ("gy", "gz")]
    vmem = pl.BlockSpec(memory_space=pltpu.VMEM)
    hbm = pl.BlockSpec(memory_space=pltpu.HBM)
    inputs = (adjoint, density, velocity, pore_mask)

    def array(*shape):
        return jax.ShapeDtypeStruct(shape, jnp.float32)

    def call(kernel, name, operands, shapes, limit, **more):
        more.setdefault("out_specs", [vmem] * len(shapes))
        more.setdefault("in_specs", [vmem] * len(operands))
        params = pltpu.CompilerParams(vmem_limit_bytes=limit * 1024 * 1024)
        return pl.pallas_call(kernel, out_shape=shapes, compiler_params=params, name=name, **more)(*operands)

    def partners(axis, slot):
        found = {}
        for at in range(slot, lax.axis_size(axis) - 1, 2):
            found[at], found[at + 1] = at + 1, at
        return found

    def ends(axis):
        last = lax.axis_size(axis) - 1
        return {0: last, last: 0}

    def swap(value, spares, *places):
        tables = {axis: partners(axis, slot) for axis, slot in places}
        axes = [axis for axis in ("gx", "gy", "gz") if axis in tables or axis in dict(spares)]
        sizes = [lax.axis_size(axis) for axis in axes]
        pairs = []
        for at in itertools.product(*[range(size) for size in sizes]):
            to = [tables.get(axis, {}).get(spot, spot) for axis, spot in zip(axes, at)]
            for spare, table in spares:
                if tuple(to) == at:
                    to = [table.get(spot, spot) if axis == spare else spot for axis, spot in zip(axes, at)]
            flat = []
            for spots in (at, to):
                index = 0
                for size, spot in zip(sizes, spots):
                    index = index * size + spot
                flat.append(index)
            pairs.append(tuple(flat))
        return lax.ppermute(value, tuple(axes), pairs)

    loaded = [jax.ShapeDtypeStruct(value.shape, value.dtype) for value in inputs]
    *held, near, a_z, b_z = (
        *call(
            functools.partial(pack_z_kernel, many_z),
            "pack_z",
            [pltpu.with_memory_space_constraint(value, pltpu.HBM) for value in inputs],
            loaded + [array(2, ext_y, LANES)] + [array(3, ext_y, LANES)] * many_z,
            8,
            in_specs=[hbm] * 4,
            scratch_shapes=[pltpu.SemaphoreType.DMA((9,))],
        ),
        *[None] * (2 - many_z),
    )
    from_z = [swap(value, [("gx", partners("gx", 0))], ("gz", slot)) for slot, value in enumerate((a_z, b_z)[:many_z])]

    rows = ext_y + 16
    adj, den, vel, mask = held
    (shifted,) = call(
        shift_kernel,
        "shift",
        (adj,),
        [array(19, ext_x + 4, rows, LANES)],
        8,
        cost_estimate=pl.CostEstimate(flops=1_000_000, bytes_accessed=2_500_000, transcendentals=0),
    )
    z_set, first, *packets = call(
        functools.partial(pack_xy_kernel, (many_x, many_y, many_z)),
        "pack_xy",
        (den, vel, mask, near, shifted, *from_z),
        [array(Z_TILES, ext_y, LANES), array(19, ext_x + 4, rows, LANES)]
        + [array(FACE + 1, ext_y, LANES)] * many_x
        + [array(FACE + 2, ext_x, LANES)] * many_y
        + [array(EDGE // 8 + 1, 8, LANES)] * (many_x * many_y),
        8,
        input_output_aliases={4: 1},
        scratch_shapes=[pltpu.VMEM((2, ext_y, LANES), jnp.float32)],
    )
    to_x, to_y, to_xy = packets[:many_x], packets[many_x : many_x + many_y], packets[many_x + many_y :]
    from_xy = [
        swap(to_xy[many_x * slot_y + slot_x], [], ("gx", slot_x), ("gy", slot_y))
        for slot_y in range(many_y)
        for slot_x in range(many_x)
    ]
    from_y = [swap(value, [("gz", partners("gz", 0))], ("gy", slot)) for slot, value in enumerate(to_y)]
    spares = [("gz", partners("gz", 1)), ("gx", ends("gx"))]
    from_x = [swap(value, spares, ("gx", slot)) for slot, value in enumerate(to_x)]

    fields, second, change = call(
        inner_kernel,
        "inner_step",
        (den, vel, mask, first),
        [array(5, ext_x + 2, rows, LANES), array(19, ext_x + 2, rows, LANES), array(ext_x + 2, rows, LANES)],
        8,
        cost_estimate=pl.CostEstimate(flops=40_000_000, bytes_accessed=8_000_000, transcendentals=0),
    )
    inout = (first, fields, second, change)
    inout = call(
        functools.partial(side_kernel, (many_x, many_y)),
        "side_step",
        (z_set, *inout, *from_x, *from_y),
        [array(*value.shape) for value in inout] + [array(Z_TILES, rows, LANES)],
        8,
        input_output_aliases={1 + at: at for at in range(4)},
        cost_estimate=pl.CostEstimate(flops=40_000_000, bytes_accessed=8_000_000, transcendentals=0),
    )
    return call(
        functools.partial(last_kernel, (many_x, many_y)),
        "last_steps",
        (den, vel, mask, *inout, *from_xy),
        [array(19, ext_x, ext_y, LANES), array(ext_x, ext_y, LANES)] + [array(*value.shape) for value in inout],
        8,
        out_specs=[hbm] * 2 + [vmem] * 5,
        input_output_aliases={3 + at: 2 + at for at in range(5)},
        scratch_shapes=[
            pltpu.VMEM((5, rows, LANES), jnp.float32),
            pltpu.VMEM((19, ext_x, ext_y, LANES), jnp.float32),
            pltpu.VMEM((ext_x, ext_y, LANES), jnp.float32),
            pltpu.SemaphoreType.DMA((2, ext_x)),
        ],
    )[:2]


def solution(mesh):
    placed = (
        P(None, "gx", "gy", "gz"),
        P(None, "gx", "gy", "gz"),
        P(None, None, "gx", "gy", "gz"),
        P("gx", "gy", "gz"),
    )

    def whole(*arrays):
        return tuple(shards(*arrays))

    return jax.shard_map(
        whole,
        mesh=mesh,
        in_specs=placed,
        out_specs=(P(None, "gx", "gy", "gz"), P("gx", "gy", "gz")),
        check_vma=False,
    )
```

```python
import functools
import itertools

import jax
import jax.numpy as jnp
from jax import lax
from jax.experimental import pallas as pl
from jax.experimental.pallas import tpu as pltpu
from jax.sharding import PartitionSpec as P

VELOCITIES = [
    (0, 0, 0),
    (1, 0, 0),
    (-1, 0, 0),
    (0, 1, 0),
    (0, -1, 0),
    (0, 0, 1),
    (0, 0, -1),
    (1, 1, 0),
    (-1, -1, 0),
    (1, -1, 0),
    (-1, 1, 0),
    (1, 0, 1),
    (-1, 0, -1),
    (1, 0, -1),
    (-1, 0, 1),
    (0, 1, 1),
    (0, -1, -1),
    (0, 1, -1),
    (0, -1, 1),
]
OPPOSITE = [0, 2, 1, 4, 3, 6, 5, 8, 7, 10, 9, 12, 11, 14, 13, 16, 15, 18, 17]
OMEGA = 1.25
LANES = 128
GROUP = 16


def pops(axis, sign):
    return [j for j in range(19) if VELOCITIES[j][axis] == sign]


def mirrored(j):
    cx, cy, cz = VELOCITIES[j]
    return VELOCITIES.index((cx, cy, -cz))


Z_FLAT = pops(2, 0)
Z_UP = pops(2, 1)
Z_DOWN = [mirrored(j) for j in Z_UP]
RHO, UX, UY, UZ, KIND = range(5)
Z_PLACE = {("pop", j): (0, g) for g, j in enumerate(Z_FLAT[:8])}
Z_PLACE[("pop", Z_FLAT[8])] = (1, 5)
Z_PLACE[("field", RHO)] = (1, 6)
Z_PLACE[("field", KIND)] = (1, 7)
Z_PLACE[("field", UX)] = (2, 5)
Z_PLACE[("field", UY)] = (2, 6)
Z_PLACE[("field", UZ)] = (2, 7)
BELOW, ABOVE, OWN_LOW, OWN_HIGH, Z_TILES = 0, 3, 6, 7, 8


def face_lines(axis, toward):
    near = pops(axis, 0) + pops(axis, toward)
    lines = [("pop", j, 0) for j in near] + [("field", k, 0) for k in range(5)]
    return lines + [("pop", j, 1) for j in pops(axis, toward)]


def edge_lines(toward_x, toward_y):
    lines = [("field", k, 0, 0) for k in range(5)]
    for j in range(19):
        cx, cy, _ = VELOCITIES[j]
        if cx not in (0, toward_x) or cy not in (0, toward_y):
            continue
        lines.append(("pop", j, 0, 0))
        if cx:
            lines.append(("pop", j, 1, 0))
        if cy:
            lines.append(("pop", j, 0, 1))
        if cx and cy:
            lines.append(("pop", j, 1, 1))
    return lines


FACE = 24
EDGE = 24


def lane_ids():
    return lax.broadcasted_iota(jnp.int32, (8, LANES), 1)


def field_of(refs, kind, index, at):
    adj, den, vel, mask = refs
    if kind == "pop":
        return adj[(index, *at)]
    if index == RHO:
        return den[(1, *at)]
    if index == KIND:
        return (mask[at] + 1).astype(jnp.float32)
    return vel[(1, index - UX, *at)]


def parity_of(axis):
    return lax.rem(lax.axis_index(axis), 2)


def on_side(parity, slot, act):
    @pl.when(parity == slot)
    def _():
        act(1)

    @pl.when(parity != slot)
    def _():
        act(0)


def has_partner(axis, slot):
    at = lax.axis_index(axis)
    to = at + jnp.where(lax.rem(at, 2) == slot, 1, -1)
    return (to >= 0) & (to < lax.axis_size(axis))


def pack_z_kernel(slots, adj_in, den_in, vel_in, mask_in, adj, den, vel, mask, near, *rest):
    packets, sems = rest[:slots], rest[slots]
    refs = (adj, den, vel, mask)
    ext_x, ext_y, _ = mask.shape
    starts = range(0, 19, 5)
    loads = [
        pltpu.make_async_copy(source, target, sems.at[len(starts) + at])
        for at, (source, target) in enumerate([(den_in.at[1], den.at[1]), (vel_in.at[1], vel.at[1]), (mask_in, mask)])
    ]
    group_loads = [
        pltpu.make_async_copy(adj_in.at[start : min(start + 5, 19)], adj.at[start : min(start + 5, 19)], sems.at[at])
        for at, start in enumerate(starts)
    ]
    last_loads = [
        pltpu.make_async_copy(source, target, sems.at[len(starts) + 3 + at])
        for at, (source, target) in enumerate([(den_in.at[0], den.at[0]), (vel_in.at[0], vel.at[0])])
    ]
    for load in loads + group_loads + last_loads:
        load.start()
    for load in loads:
        load.wait()
    lane = lane_ids()
    parity = parity_of("gz")
    parts = range(ext_y // 8)
    zero = jnp.zeros((8, LANES), jnp.float32)
    lows, highs = [[zero] * 3 for _ in parts], [[zero] * 3 for _ in parts]
    far_low, far_high = [zero for _ in parts], [zero for _ in parts]

    def gather(kind, index):
        for x, part in itertools.product(range(ext_x), parts):
            value = field_of(refs, kind, index, (x, pl.ds(8 * part, 8), slice(None)))
            if kind == "pop" and VELOCITIES[index][2] == 1:
                spot = GROUP * Z_UP.index(index) + 2 + x
                moved = pltpu.roll(value, spot, 1)
                lows[part][1] = jnp.where(lane == spot, moved, lows[part][1])
                far_low[part] = jnp.where(lane == spot + 1, moved, far_low[part])
            elif kind == "pop" and VELOCITIES[index][2] == -1:
                spot = GROUP * Z_DOWN.index(index) + 2 + x
                moved = pltpu.roll(value, spot, 1)
                highs[part][1] = jnp.where(lane == spot - 1, moved, highs[part][1])
                far_high[part] = jnp.where(lane == spot - 2, moved, far_high[part])
            else:
                tile, group = Z_PLACE[(kind, index)]
                spot = GROUP * group + 2 + x
                moved = pltpu.roll(value, spot, 1)
                lows[part][tile] = jnp.where(lane == spot, moved, lows[part][tile])
                highs[part][tile] = jnp.where(lane == spot - 1, moved, highs[part][tile])

    for k in range(5):
        gather("field", k)
    for start, load in zip(starts, group_loads):
        load.wait()
        for j in range(start, min(start + 5, 19)):
            gather("pop", j)
    for part in parts:
        rows = pl.ds(8 * part, 8)
        low = lows[part]
        high = [pltpu.roll(tile, 1, 1) for tile in highs[part]]
        low[2] = jnp.where(lane < 5 * GROUP, pltpu.roll(far_low[part], LANES - 1, 1), low[2])
        high[2] = jnp.where(lane < 5 * GROUP, pltpu.roll(far_high[part], 2, 1), high[2])
        near[0, rows, :] = low[1]
        near[1, rows, :] = high[1]
        for slot in range(slots):
            there = has_partner("gz", slot)
            for tile in range(3):
                value = jnp.where(parity == slot, high[tile], low[tile])
                packets[slot][tile, rows, :] = jnp.where(there, value, 0.0)
    for load in last_loads:
        load.wait()


def shift_kernel(adj, first):
    _, ext_x, ext_y, _ = adj.shape
    for j in range(19):
        cz = VELOCITIES[j][2]
        for x, part in itertools.product(range(ext_x), range(ext_y // 8)):
            value = adj[j, x, pl.ds(8 * part, 8), :]
            first[j, 2 + x, pl.ds(8 + 8 * part, 8), :] = pltpu.roll(value, -cz % LANES, 1) if cz else value


def pack_xy_kernel(slots, den, vel, mask, near, shifted, *rest):
    many_x, many_y, many_z = slots
    from_z, z_set, first, packets = rest[:many_z], rest[many_z], rest[many_z + 1], rest[many_z + 2 :]
    to_x, to_y = packets[:many_x], packets[many_x : many_x + many_y]
    to_xy, faces = packets[many_x + many_y : -1], packets[-1]
    refs = (None, den, vel, mask)
    ext_x, ext_y, _ = mask.shape
    spot = lane_ids() % GROUP
    every = slice(None)
    px, py, pz = parity_of("gx"), parity_of("gy"), parity_of("gz")

    z_set[OWN_LOW] = near[0]
    z_set[OWN_HIGH] = near[1]
    for tile in range(3):
        even = from_z[0][tile]
        odd = from_z[1][tile] if many_z > 1 else jnp.zeros_like(even)
        z_set[ABOVE + tile] = jnp.where(pz == 0, even, odd)
        z_set[BELOW + tile] = jnp.where(pz == 0, odd, even)

    for j in Z_UP + Z_DOWN:
        up = VELOCITIES[j][2] > 0
        group = (Z_UP if up else Z_DOWN).index(j)
        last = LANES - 1 if up else 0
        for part in range(ext_y // 8):
            halo = z_set[(ABOVE if up else BELOW) + 1, pl.ds(8 * part, 8), :]
            for x in range(ext_x):
                edge = pltpu.roll(halo, (last - 2 - GROUP * group - x) % LANES, 1)
                first[j, 2 + x, pl.ds(8 + 8 * part, 8), last : last + 1] = edge[:, last : last + 1]

    def line_of(kind, index, x, y):
        if kind == "pop":
            return first[index, x + 2, y + 8 : y + 9, :]
        return field_of(refs, kind, index, (x, slice(y, y + 1), every))

    for side in range(2):
        for part in range(ext_y // 8):
            rows = pl.ds(8 * part, 8)
            value = jnp.zeros((8, LANES), jnp.float32)
            for tile in range(Z_TILES):
                start = ext_x if side else 2
                moved = pltpu.roll(z_set[tile, rows, :], (2 * tile - start) % LANES, 1)
                value = jnp.where(spot // 2 == tile, moved, value)
            faces[side, rows, :] = value

    def pack_xy(slot_x, slot_y, side_x, side_y):
        packet = to_xy[many_x * slot_y + slot_x]
        for line, (kind, index, far_x, far_y) in enumerate(edge_lines(1 - 2 * side_x, 1 - 2 * side_y)):
            x = ext_x - 1 - far_x if side_x else far_x
            y = ext_y - 1 - far_y if side_y else far_y
            packet[line // 8, line % 8 : line % 8 + 1, :] = line_of(kind, index, x, y)
        start = ext_y - 2 if side_y else 0
        packet[EDGE // 8, 0:2, :] = faces[side_x, start : start + 2, :]

    def pack_y(slot, side):
        packet = to_y[slot]
        for line, (kind, index, depth) in enumerate(face_lines(1, 1 - 2 * side)):
            y = ext_y - 1 - depth if side else depth
            for x in range(ext_x):
                packet[line, x : x + 1, :] = line_of(kind, index, x, y)
        start = ext_y - 2 if side else 0
        for tile in range(Z_TILES):
            row = 2 * tile % 8
            packet[FACE + tile // 4, row : row + 2, :] = z_set[tile, start : start + 2, :]

    def pack_x(slot, side):
        for line, (kind, index, depth) in enumerate(face_lines(0, 1 - 2 * side)):
            x = ext_x - 1 - depth if side else depth
            if kind == "pop":
                to_x[slot][line] = first[index, x + 2, pl.ds(8, ext_y), :]
            else:
                to_x[slot][line] = field_of(refs, kind, index, (x, every, every))
        to_x[slot][FACE] = faces[side]

    def when_there(there, packet, act):
        pl.when(there)(act)

        @pl.when(jnp.logical_not(there))
        def _():
            packet[...] = jnp.zeros(packet.shape, jnp.float32)

    for slot_y in range(many_y):
        there_y = has_partner("gy", slot_y)
        when_there(there_y, to_y[slot_y], lambda: on_side(py, slot_y, functools.partial(pack_y, slot_y)))
        for slot_x in range(many_x):
            when_there(
                there_y & has_partner("gx", slot_x),
                to_xy[many_x * slot_y + slot_x],
                lambda: on_side(
                    py,
                    slot_y,
                    lambda side_y: on_side(px, slot_x, lambda side_x: pack_xy(slot_x, slot_y, side_x, side_y)),
                ),
            )
    for slot_x in range(many_x):
        when_there(
            has_partner("gx", slot_x), to_x[slot_x], lambda: on_side(px, slot_x, functools.partial(pack_x, slot_x))
        )


def collide(pulled, rho, ux, uy, uz, fluid, wanted):
    total = {}
    diff = {}
    for j in range(1, 19, 2):
        total[j] = pulled[j] + pulled[j + 1]
        diff[j] = pulled[j] - pulled[j + 1]
    in_xy, in_xz, in_yz = total[7] + total[9], total[11] + total[13], total[15] + total[17]
    two_x, two_y, two_z = total[1] + total[1], total[3] + total[3], total[5] + total[5]
    count = (12.0 * pulled[0] + (two_x + two_y)) + (two_z + (in_xy + (in_xz + in_yz)))
    flow_x = (diff[1] + diff[1]) + ((diff[7] + diff[9]) + (diff[11] + diff[13]))
    flow_y = (diff[3] + diff[3]) + ((diff[7] - diff[9]) + (diff[15] + diff[17]))
    flow_z = (diff[5] + diff[5]) + ((diff[11] - diff[13]) + (diff[15] - diff[17]))
    xx, yy, zz = two_x + (in_xy + in_xz), two_y + (in_xy + in_yz), two_z + (in_xz + in_yz)
    xy, xz, yz = total[7] - total[9], total[11] - total[13], total[15] - total[17]
    push_x = xx * ux + xy * uy + xz * uz
    push_y = xy * ux + yy * uy + yz * uz
    push_z = xz * ux + yz * uy + zz * uz
    usq = ux * ux + uy * uy + uz * uz
    push = ux * push_x + uy * push_y + uz * push_z
    inverse = 1.0 / rho
    base = count * (OMEGA / 36.0 + (OMEGA / 24.0) * usq) - (OMEGA / 8.0) * push - ux * inverse
    along_x = (OMEGA / 12.0) * (flow_x + 3.0 * push_x - ux * count) + inverse
    along_y = (OMEGA / 12.0) * (flow_y + 3.0 * push_y - uy * count)
    along_z = (OMEGA / 12.0) * (flow_z + 3.0 * push_z - uz * count)
    parts = {
        1: along_x,
        3: along_y,
        5: along_z,
        7: along_x + along_y,
        9: along_x - along_y,
        11: along_x + along_z,
        13: along_x - along_z,
        15: along_y + along_z,
        17: along_y - along_z,
    }
    out = {}
    for j in wanted:
        if j == 0:
            shift = base
        elif j % 2:
            shift = base + parts[j]
        else:
            shift = base - parts[j - 1]
        out[j] = jnp.where(fluid, (1.0 - OMEGA) * pulled[j] + shift, pulled[OPPOSITE[j]])
    change = (-1.0 / 6.0) * rho * (flow_x * ux + flow_y * uy + flow_z * uz)
    return out, jnp.where(fluid, change, 0.0)


class Plane:
    def __init__(self, x, row):
        self.x, self.row = x, row

    def load(self, ref, lead, margin, cx=0, cy=0):
        return ref[lead, self.x + margin + cx, pl.ds(8 + self.row + cy, 8), :]

    def store(self, ref, lead, margin, value):
        ref[lead, self.x + margin, pl.ds(8 + self.row, 8), :] = value


class Rim:
    def __init__(self, x, ext_y):
        self.x, self.ext_y = x, ext_y

    def load(self, ref, lead, margin, cx=0, cy=0):
        at = self.x + margin + cx
        upper = ref[lead, at, pl.ds(8 + self.ext_y - 1 + cy, 8), :]
        lower = ref[lead, at, pl.ds(1 + cy, 8), :]
        return jnp.where(lax.broadcasted_iota(jnp.int32, (8, LANES), 0) < 4, upper, lower)

    def store(self, ref, lead, margin, value):
        at = self.x + margin
        ref[lead, at, pl.ds(8 + self.ext_y - 1, 2), :] = value[0:2]
        ref[lead, at, pl.ds(7, 2), :] = value[6:8]


def first_step(first, fields, second, change, tiles, outside=True):
    loaded = [
        (
            [tile.load(first, j, 2, *VELOCITIES[j][:2]) for j in range(19)],
            [tile.load(fields, k, 1) for k in range(5)],
        )
        for tile in tiles
    ]
    done = [
        collide(pulled, rho, ux, uy, uz, kind > 1.5, range(19)) for pulled, (rho, ux, uy, uz, kind) in loaded
    ]
    for tile, (_, here), (after, gain) in zip(tiles, loaded, done):
        inside = here[KIND] > 0.5
        for j in range(19):
            value = jnp.where(inside, after[j], 0.0) if outside else after[j]
            cz = VELOCITIES[j][2]
            tile.store(second, j, 1, pltpu.roll(value, -cz % LANES, 1) if cz else value)
        tile.store(change, 0, 1, gain)


def inner_kernel(den, vel, mask, first, fields, second, change):
    refs = (None, den, vel, mask)
    ext_x, ext_y, _ = mask.shape
    every = slice(None)
    for k in range(5):
        fields[k, 1 : 1 + ext_x, pl.ds(8, ext_y), :] = field_of(refs, "field", k, (every, every, every))

    @pl.loop(1, ext_x - 1)
    def _(x):
        tiles = [Plane(x, 1 + 8 * part) for part in range(ext_y // 8)]
        first_step(first, fields, second, change, tiles, outside=False)


def put_row(first, fields, kind, index, x, y, value):
    row = y + 8
    if kind == "pop":
        first[index, x + 2, row : row + 1, :] = value
    else:
        fields[index, x + 1, row : row + 1, :] = value


def place_z(z_first, value, start, size, side, ext_x):
    rows = pl.ds(start, size)
    spot = lane_ids()[:size] % GROUP
    inside = spot >= 2 + ext_x if side else spot < 2
    for tile in range(Z_TILES):
        shift = (2 + ext_x if side else 0) - 2 * tile
        moved = pltpu.roll(value, shift % LANES, 1)[:size]
        z_first[tile, rows, :] = jnp.where(inside, moved, z_first[tile, rows, :])


def side_kernel(slots, z_set, *rest):
    many_x, many_y = slots
    from_x, from_y = rest[4 : 4 + many_x], rest[4 + many_x : 4 + many_x + many_y]
    first, fields, second, change, z_first = rest[-5:]
    _, ext_y, _ = z_set.shape
    ext_x = change.shape[1] - 2
    inner = pl.ds(8, ext_y)
    put = functools.partial(put_row, first, fields)
    z_first[:, inner, :] = z_set[...]

    def place_y(slot, side):
        packet = from_y[slot]
        for line, (kind, index, depth) in enumerate(face_lines(1, 2 * side - 1)):
            y = ext_y + depth if side else -1 - depth
            for x in range(ext_x):
                put(kind, index, x, y, packet[line, x : x + 1, :])
        start = 8 + ext_y if side else 6
        for tile in range(Z_TILES):
            row = 2 * tile % 8
            z_first[tile, start : start + 2, :] = packet[FACE + tile // 4, row : row + 2, :]
        if many_y == 1:
            clear_y(1 - side)

    def clear_y(side):
        nothing = jnp.zeros((1, LANES), jnp.float32)
        for kind, index, depth in face_lines(1, 2 * side - 1):
            y = ext_y + depth if side else -1 - depth
            for x in range(-1, ext_x + 1):
                put(kind, index, x, y, nothing)
            if kind == "pop":
                put(kind, index, -2, y, nothing)
                put(kind, index, ext_x + 1, y, nothing)
        start = 8 + ext_y if side else 6
        for tile in range(Z_TILES):
            z_first[tile, start : start + 2, :] = jnp.zeros((2, LANES), jnp.float32)

    def place_x(slot, side):
        packet = from_x[slot]
        for line, (kind, index, depth) in enumerate(face_lines(0, 2 * side - 1)):
            x = ext_x + depth if side else -1 - depth
            if kind == "pop":
                first[index, x + 2, inner, :] = packet[line]
            else:
                fields[index, x + 1, inner, :] = packet[line]
        for part in range(ext_y // 8):
            place_z(z_first, packet[FACE, pl.ds(8 * part, 8), :], 8 + 8 * part, 8, side, ext_x)

    for slot_y in range(many_y):
        on_side(parity_of("gy"), slot_y, functools.partial(place_y, slot_y))
    for slot_x in range(many_x):
        on_side(parity_of("gx"), slot_x, functools.partial(place_x, slot_x))

    for x in (-1, 0, ext_x - 1, ext_x):
        for row in range(7, ext_y - 8, 8):
            first_step(first, fields, second, change, [Plane(x, row)], outside=x in (-1, ext_x))

    @pl.loop(1, ext_x - 1)
    def _(x):
        first_step(first, fields, second, change, [Rim(x, ext_y)])


def last_kernel(slots, den, vel, mask, *rest):
    many_x, many_y = slots
    from_xy = rest[5 : 5 + many_x * many_y]
    out, sens, first, fields, second, change, z_first, z_second, held, held_sens, sems = rest[-11:]
    ext_x, ext_y, _ = mask.shape
    lane = lane_ids()
    every = slice(None)
    px, py = parity_of("gx"), parity_of("gy")

    def place_xy(slot_x, slot_y, side_x, side_y):
        packet = from_xy[many_x * slot_y + slot_x]
        for line, (kind, index, far_x, far_y) in enumerate(edge_lines(2 * side_x - 1, 2 * side_y - 1)):
            x = ext_x + far_x if side_x else -1 - far_x
            y = ext_y + far_y if side_y else -1 - far_y
            put_row(first, fields, kind, index, x, y, packet[line // 8, line % 8 : line % 8 + 1, :])
        place_z(z_first, packet[EDGE // 8], 8 + ext_y if side_y else 6, 2, side_x, ext_x)

    for slot_x in range(many_x):
        for slot_y in range(many_y):
            on_side(
                py,
                slot_y,
                lambda side_y: on_side(px, slot_x, lambda side_x: place_xy(slot_x, slot_y, side_x, side_y)),
            )

    for x in (-1, 0, ext_x - 1, ext_x):
        first_step(first, fields, second, change, [Plane(x, -1), Plane(x, ext_y - 1)])

    for part in range((ext_y + 2 + 7) // 8):
        row = 7 + 8 * part

        def both(low_tile, high_tile, group, cx, cy):
            rows = pl.ds(row + cy, 8)
            low = pltpu.roll(z_first[low_tile, rows, :], (-GROUP * group - cx) % LANES, 1)
            high = pltpu.roll(z_first[high_tile, rows, :], (LANES // 2 - GROUP * group - cx) % LANES, 1)
            return jnp.where(lane < LANES // 2, low, high)

        pulled = []
        for j in range(19):
            cx, cy, cz = VELOCITIES[j]
            if cz == 0:
                tile, group = Z_PLACE[("pop", j)]
                pulled.append(both(BELOW + tile, ABOVE + tile, group, cx, cy))
            elif cz == 1:
                pulled.append(both(OWN_LOW, ABOVE + 2, Z_UP.index(j), cx, cy))
            else:
                pulled.append(both(BELOW + 2, OWN_HIGH, Z_DOWN.index(j), cx, cy))
        rho, ux, uy, uz, kind = [
            both(BELOW + tile, ABOVE + tile, group, 0, 0)
            for tile, group in [Z_PLACE[("field", k)] for k in range(5)]
        ]
        after, _ = collide(pulled, rho, ux, uy, uz, kind > 1.5, Z_UP + Z_DOWN)
        for group in range(5):
            value = jnp.where(lane < LANES // 2, after[Z_DOWN[group]], after[Z_UP[group]])
            z_second[group, pl.ds(row, 8), :] = jnp.where(kind > 0.5, value, 0.0)

    def copies(x):
        return (
            pltpu.make_async_copy(held.at[:, x], out.at[:, x], sems.at[0, x]),
            pltpu.make_async_copy(held_sens.at[x], sens.at[x], sems.at[1, x]),
        )

    @pl.loop(0, ext_x)
    def _(x):
        loaded = []
        for part in range(ext_y // 8):
            row = 8 + 8 * part
            pulled = []
            for j in range(19):
                cx, cy, cz = VELOCITIES[j]
                rows = pl.ds(row + cy, 8)
                value = second[j, x + 1 + cx, rows, :]
                if cz == 1:
                    edge = z_second[Z_UP.index(j), rows, :]
                    edge = pltpu.roll(edge, LANES // 2 - 3 - cx - x, 1)
                    value = jnp.where(lane == LANES - 1, edge, value)
                elif cz == -1:
                    edge = z_second[Z_DOWN.index(j), rows, :]
                    edge = pltpu.roll(edge, LANES - 2 - cx - x, 1)
                    value = jnp.where(lane == 0, edge, value)
                pulled.append(value)
            at = (x, pl.ds(8 * part, 8), every)
            here = [den[(0, *at)], vel[(0, 0, *at)], vel[(0, 1, *at)], vel[(0, 2, *at)], mask[at] > 0]
            loaded.append((at, pulled, here, change[0, x + 1, pl.ds(row, 8), :]))
        done = [collide(pulled, *here, range(19)) for _, pulled, here, _ in loaded]
        for (at, _, _, before), (after, gain) in zip(loaded, done):
            for j in range(19):
                held[(j, *at)] = after[j]
            held_sens[at] = before + gain
        for copy in copies(x):
            copy.start()

    for x in range(ext_x):
        for copy in copies(x):
            copy.wait()


def shards(adjoint, density, velocity, pore_mask):
    ext_x, ext_y, ext_z = pore_mask.shape
    assert ext_z == LANES and ext_y % 8 == 0 and ext_x + 4 <= GROUP and ext_x == 8
    many_x = 2
    many_y, many_z = [1 if lax.axis_size(axis) == 2 else 2 for axis in ("gy", "gz")]
    vmem = pl.BlockSpec(memory_space=pltpu.VMEM)
    hbm = pl.BlockSpec(memory_space=pltpu.HBM)
    inputs = (adjoint, density, velocity, pore_mask)

    def array(*shape):
        return jax.ShapeDtypeStruct(shape, jnp.float32)

    def call(kernel, name, operands, shapes, limit, **more):
        more.setdefault("out_specs", [vmem] * len(shapes))
        more.setdefault("in_specs", [vmem] * len(operands))
        params = pltpu.CompilerParams(vmem_limit_bytes=limit * 1024 * 1024)
        return pl.pallas_call(kernel, out_shape=shapes, compiler_params=params, name=name, **more)(*operands)

    def partners(axis, slot):
        found = {}
        for at in range(slot, lax.axis_size(axis) - 1, 2):
            found[at], found[at + 1] = at + 1, at
        return found

    def ends(axis):
        last = lax.axis_size(axis) - 1
        return {0: last, last: 0}

    def swap(value, spares, *places):
        tables = {axis: partners(axis, slot) for axis, slot in places}
        axes = [axis for axis in ("gx", "gy", "gz") if axis in tables or axis in dict(spares)]
        sizes = [lax.axis_size(axis) for axis in axes]
        pairs = []
        for at in itertools.product(*[range(size) for size in sizes]):
            to = [tables.get(axis, {}).get(spot, spot) for axis, spot in zip(axes, at)]
            for spare, table in spares:
                if tuple(to) == at:
                    to = [table.get(spot, spot) if axis == spare else spot for axis, spot in zip(axes, at)]
            flat = []
            for spots in (at, to):
                index = 0
                for size, spot in zip(sizes, spots):
                    index = index * size + spot
                flat.append(index)
            pairs.append(tuple(flat))
        return lax.ppermute(value, tuple(axes), pairs)

    loaded = [jax.ShapeDtypeStruct(value.shape, value.dtype) for value in inputs]
    *held, near, a_z, b_z = (
        *call(
            functools.partial(pack_z_kernel, many_z),
            "pack_z",
            [pltpu.with_memory_space_constraint(value, pltpu.HBM) for value in inputs],
            loaded + [array(2, ext_y, LANES)] + [array(3, ext_y, LANES)] * many_z,
            8,
            in_specs=[hbm] * 4,
            scratch_shapes=[pltpu.SemaphoreType.DMA((9,))],
        ),
        *[None] * (2 - many_z),
    )
    from_z = [swap(value, [("gx", partners("gx", 0))], ("gz", slot)) for slot, value in enumerate((a_z, b_z)[:many_z])]

    rows = ext_y + 16
    adj, den, vel, mask = held
    (shifted,) = call(
        shift_kernel,
        "shift",
        (adj,),
        [array(19, ext_x + 4, rows, LANES)],
        8,
        cost_estimate=pl.CostEstimate(flops=1_000_000, bytes_accessed=2_500_000, transcendentals=0),
    )
    z_set, first, *packets = call(
        functools.partial(pack_xy_kernel, (many_x, many_y, many_z)),
        "pack_xy",
        (den, vel, mask, near, shifted, *from_z),
        [array(Z_TILES, ext_y, LANES), array(19, ext_x + 4, rows, LANES)]
        + [array(FACE + 1, ext_y, LANES)] * many_x
        + [array(FACE + 2, ext_x, LANES)] * many_y
        + [array(EDGE // 8 + 1, 8, LANES)] * (many_x * many_y),
        8,
        input_output_aliases={4: 1},
        scratch_shapes=[pltpu.VMEM((2, ext_y, LANES), jnp.float32)],
    )
    to_x, to_y, to_xy = packets[:many_x], packets[many_x : many_x + many_y], packets[many_x + many_y :]
    from_xy = [
        swap(to_xy[many_x * slot_y + slot_x], [], ("gx", slot_x), ("gy", slot_y))
        for slot_y in range(many_y)
        for slot_x in range(many_x)
    ]
    from_y = [swap(value, [("gz", partners("gz", 0))], ("gy", slot)) for slot, value in enumerate(to_y)]
    spares = [("gz", partners("gz", 1)), ("gx", ends("gx"))]
    from_x = [swap(value, spares, ("gx", slot)) for slot, value in enumerate(to_x)]

    fields, second, change = call(
        inner_kernel,
        "inner_step",
        (den, vel, mask, first),
        [array(5, ext_x + 2, rows, LANES), array(19, ext_x + 2, rows, LANES), array(1, ext_x + 2, rows, LANES)],
        8,
        cost_estimate=pl.CostEstimate(flops=40_000_000, bytes_accessed=8_000_000, transcendentals=0),
    )
    inout = (first, fields, second, change)
    inout = call(
        functools.partial(side_kernel, (many_x, many_y)),
        "side_step",
        (z_set, *inout, *from_x, *from_y),
        [array(*value.shape) for value in inout] + [array(Z_TILES, rows, LANES)],
        8,
        input_output_aliases={1 + at: at for at in range(4)},
        cost_estimate=pl.CostEstimate(flops=40_000_000, bytes_accessed=8_000_000, transcendentals=0),
    )
    return call(
        functools.partial(last_kernel, (many_x, many_y)),
        "last_steps",
        (den, vel, mask, *inout, *from_xy),
        [array(19, ext_x, ext_y, LANES), array(ext_x, ext_y, LANES)] + [array(*value.shape) for value in inout],
        8,
        out_specs=[hbm] * 2 + [vmem] * 5,
        input_output_aliases={3 + at: 2 + at for at in range(5)},
        scratch_shapes=[
            pltpu.VMEM((5, rows, LANES), jnp.float32),
            pltpu.VMEM((19, ext_x, ext_y, LANES), jnp.float32),
            pltpu.VMEM((ext_x, ext_y, LANES), jnp.float32),
            pltpu.SemaphoreType.DMA((2, ext_x)),
        ],
    )[:2]


def solution(mesh):
    placed = (
        P(None, "gx", "gy", "gz"),
        P(None, "gx", "gy", "gz"),
        P(None, None, "gx", "gy", "gz"),
        P("gx", "gy", "gz"),
    )

    def whole(*arrays):
        return tuple(shards(*arrays))

    return jax.shard_map(
        whole,
        mesh=mesh,
        in_specs=placed,
        out_specs=(P(None, "gx", "gy", "gz"), P("gx", "gy", "gz")),
        check_vma=False,
    )
```

```python
import functools
import itertools

import jax
import jax.numpy as jnp
from jax import lax
from jax.experimental import pallas as pl
from jax.experimental.pallas import tpu as pltpu
from jax.sharding import PartitionSpec as P

VELOCITIES = [
    (0, 0, 0),
    (1, 0, 0),
    (-1, 0, 0),
    (0, 1, 0),
    (0, -1, 0),
    (0, 0, 1),
    (0, 0, -1),
    (1, 1, 0),
    (-1, -1, 0),
    (1, -1, 0),
    (-1, 1, 0),
    (1, 0, 1),
    (-1, 0, -1),
    (1, 0, -1),
    (-1, 0, 1),
    (0, 1, 1),
    (0, -1, -1),
    (0, 1, -1),
    (0, -1, 1),
]
OPPOSITE = [0, 2, 1, 4, 3, 6, 5, 8, 7, 10, 9, 12, 11, 14, 13, 16, 15, 18, 17]
OMEGA = 1.25
LANES = 128
GROUP = 16


def pops(axis, sign):
    return [j for j in range(19) if VELOCITIES[j][axis] == sign]


def mirrored(j):
    cx, cy, cz = VELOCITIES[j]
    return VELOCITIES.index((cx, cy, -cz))


Z_FLAT = pops(2, 0)
Z_UP = pops(2, 1)
Z_DOWN = [mirrored(j) for j in Z_UP]
RHO, UX, UY, UZ, KIND = range(5)
Z_PLACE = {("pop", j): (0, g) for g, j in enumerate(Z_FLAT[:8])}
Z_PLACE[("pop", Z_FLAT[8])] = (1, 5)
Z_PLACE[("field", RHO)] = (1, 6)
Z_PLACE[("field", KIND)] = (1, 7)
Z_PLACE[("field", UX)] = (2, 5)
Z_PLACE[("field", UY)] = (2, 6)
Z_PLACE[("field", UZ)] = (2, 7)
BELOW, ABOVE, OWN_LOW, OWN_HIGH, Z_TILES = 0, 3, 6, 7, 8


def face_lines(axis, toward):
    near = pops(axis, 0) + pops(axis, toward)
    lines = [("pop", j, 0) for j in near] + [("field", k, 0) for k in range(5)]
    return lines + [("pop", j, 1) for j in pops(axis, toward)]


def edge_lines(toward_x, toward_y):
    lines = [("field", k, 0, 0) for k in range(5)]
    for j in range(19):
        cx, cy, _ = VELOCITIES[j]
        if cx not in (0, toward_x) or cy not in (0, toward_y):
            continue
        lines.append(("pop", j, 0, 0))
        if cx:
            lines.append(("pop", j, 1, 0))
        if cy:
            lines.append(("pop", j, 0, 1))
        if cx and cy:
            lines.append(("pop", j, 1, 1))
    return lines


FACE = 24
EDGE = 24


def lane_ids():
    return lax.broadcasted_iota(jnp.int32, (8, LANES), 1)


def field_of(refs, kind, index, at):
    adj, den, vel, mask = refs
    if kind == "pop":
        return adj[(index, *at)]
    if index == RHO:
        return den[(1, *at)]
    if index == KIND:
        return (mask[at] + 1).astype(jnp.float32)
    return vel[(1, index - UX, *at)]


def parity_of(axis):
    return lax.rem(lax.axis_index(axis), 2)


def on_side(parity, slot, act):
    @pl.when(parity == slot)
    def _():
        act(1)

    @pl.when(parity != slot)
    def _():
        act(0)


def has_partner(axis, slot):
    at = lax.axis_index(axis)
    to = at + jnp.where(lax.rem(at, 2) == slot, 1, -1)
    return (to >= 0) & (to < lax.axis_size(axis))


def pack_z_kernel(slots, adj_in, den_in, vel_in, mask_in, adj, den, vel, mask, near, *rest):
    packets, sems = rest[:slots], rest[slots]
    refs = (adj, den, vel, mask)
    ext_x, ext_y, _ = mask.shape
    starts = range(0, 19, 5)
    loads = [
        pltpu.make_async_copy(adj_in.at[start : min(start + 5, 19)], adj.at[start : min(start + 5, 19)], sems.at[at])
        for at, start in enumerate(starts)
    ] + [
        pltpu.make_async_copy(source, target, sems.at[len(starts) + at])
        for at, (source, target) in enumerate([(den_in, den), (vel_in, vel), (mask_in, mask)])
    ]
    for load in loads:
        load.start()
    lane = lane_ids()
    parity = parity_of("gz")
    parts = range(ext_y // 8)
    zero = jnp.zeros((8, LANES), jnp.float32)
    lows, highs = [[zero] * 3 for _ in parts], [[zero] * 3 for _ in parts]
    far_low, far_high = [zero for _ in parts], [zero for _ in parts]

    def gather(kind, index):
        for x, part in itertools.product(range(ext_x), parts):
            value = field_of(refs, kind, index, (x, pl.ds(8 * part, 8), slice(None)))
            if kind == "pop" and VELOCITIES[index][2] == 1:
                spot = GROUP * Z_UP.index(index) + 2 + x
                moved = pltpu.roll(value, spot, 1)
                lows[part][1] = jnp.where(lane == spot, moved, lows[part][1])
                far_low[part] = jnp.where(lane == spot + 1, moved, far_low[part])
            elif kind == "pop" and VELOCITIES[index][2] == -1:
                spot = GROUP * Z_DOWN.index(index) + 2 + x
                moved = pltpu.roll(value, spot, 1)
                highs[part][1] = jnp.where(lane == spot - 1, moved, highs[part][1])
                far_high[part] = jnp.where(lane == spot - 2, moved, far_high[part])
            else:
                tile, group = Z_PLACE[(kind, index)]
                spot = GROUP * group + 2 + x
                moved = pltpu.roll(value, spot, 1)
                lows[part][tile] = jnp.where(lane == spot, moved, lows[part][tile])
                highs[part][tile] = jnp.where(lane == spot - 1, moved, highs[part][tile])

    for start, load in zip(starts, loads):
        load.wait()
        for j in range(start, min(start + 5, 19)):
            gather("pop", j)
    for load in loads[len(starts) :]:
        load.wait()
    for k in range(5):
        gather("field", k)
    for part in parts:
        rows = pl.ds(8 * part, 8)
        low = lows[part]
        high = [pltpu.roll(tile, 1, 1) for tile in highs[part]]
        low[2] = jnp.where(lane < 5 * GROUP, pltpu.roll(far_low[part], LANES - 1, 1), low[2])
        high[2] = jnp.where(lane < 5 * GROUP, pltpu.roll(far_high[part], 2, 1), high[2])
        near[0, rows, :] = low[1]
        near[1, rows, :] = high[1]
        for slot in range(slots):
            there = has_partner("gz", slot)
            for tile in range(3):
                value = jnp.where(parity == slot, high[tile], low[tile])
                packets[slot][tile, rows, :] = jnp.where(there, value, 0.0)


def pack_lines(refs, first, packets, many_x, many_y, wanted, clear):
    to_x, to_y = packets[:many_x], packets[many_x : many_x + many_y]
    to_xy = packets[many_x + many_y :]
    ext_x, ext_y, _ = refs[-1].shape
    every = slice(None)
    px, py = parity_of("gx"), parity_of("gy")

    def line_of(kind, index, x, y):
        if kind == "pop":
            return first[index, x + 2, y + 8 : y + 9, :]
        return field_of(refs, kind, index, (x, slice(y, y + 1), every))

    def pack_xy(slot_x, slot_y, side_x, side_y):
        packet = to_xy[many_x * slot_y + slot_x]
        for line, (kind, index, far_x, far_y) in enumerate(edge_lines(1 - 2 * side_x, 1 - 2 * side_y)):
            if wanted(kind, index):
                x = ext_x - 1 - far_x if side_x else far_x
                y = ext_y - 1 - far_y if side_y else far_y
                packet[line // 8, line % 8 : line % 8 + 1, :] = line_of(kind, index, x, y)

    def pack_y(slot, side):
        for line, (kind, index, depth) in enumerate(face_lines(1, 1 - 2 * side)):
            if wanted(kind, index):
                y = ext_y - 1 - depth if side else depth
                for x in range(ext_x):
                    to_y[slot][line, x : x + 1, :] = line_of(kind, index, x, y)

    def pack_x(slot, side):
        for line, (kind, index, depth) in enumerate(face_lines(0, 1 - 2 * side)):
            if wanted(kind, index):
                x = ext_x - 1 - depth if side else depth
                if kind == "pop":
                    to_x[slot][line] = first[index, x + 2, pl.ds(8, ext_y), :]
                else:
                    to_x[slot][line] = field_of(refs, kind, index, (x, every, every))

    def when_there(there, packet, act):
        pl.when(there)(act)
        if clear:

            @pl.when(jnp.logical_not(there))
            def _():
                packet[...] = jnp.zeros(packet.shape, jnp.float32)

    for slot_y in range(many_y):
        there_y = has_partner("gy", slot_y)
        when_there(there_y, to_y[slot_y], lambda: on_side(py, slot_y, functools.partial(pack_y, slot_y)))
        for slot_x in range(many_x):
            when_there(
                there_y & has_partner("gx", slot_x),
                to_xy[many_x * slot_y + slot_x],
                lambda: on_side(
                    py,
                    slot_y,
                    lambda side_y: on_side(px, slot_x, lambda side_x: pack_xy(slot_x, slot_y, side_x, side_y)),
                ),
            )
    for slot_x in range(many_x):
        when_there(
            has_partner("gx", slot_x), to_x[slot_x], lambda: on_side(px, slot_x, functools.partial(pack_x, slot_x))
        )


def is_flat(kind, index):
    return kind == "field" or VELOCITIES[index][2] == 0


def shift_kernel(slots, adj, den, vel, mask, first, *packets):
    many_x, many_y = slots
    _, ext_x, ext_y, _ = adj.shape
    for j in range(19):
        cz = VELOCITIES[j][2]
        for x, part in itertools.product(range(ext_x), range(ext_y // 8)):
            value = adj[j, x, pl.ds(8 * part, 8), :]
            first[j, 2 + x, pl.ds(8 + 8 * part, 8), :] = pltpu.roll(value, -cz % LANES, 1) if cz else value
    pack_lines((None, den, vel, mask), first, packets, many_x, many_y, is_flat, True)


def pack_xy_kernel(slots, near, *rest):
    many_x, many_y, many_z = slots
    count = many_x + many_y + many_x * many_y
    from_z, rest = rest[:many_z], rest[many_z + 1 + count :]
    z_set, first, packets, faces = rest[0], rest[1], rest[2:-1], rest[-1]
    to_x, to_y, to_xy = packets[:many_x], packets[many_x : many_x + many_y], packets[many_x + many_y :]
    ext_x, ext_y = first.shape[1] - 4, near.shape[1]
    spot = lane_ids() % GROUP
    px, py, pz = parity_of("gx"), parity_of("gy"), parity_of("gz")

    z_set[OWN_LOW] = near[0]
    z_set[OWN_HIGH] = near[1]
    for tile in range(3):
        even = from_z[0][tile]
        odd = from_z[1][tile] if many_z > 1 else jnp.zeros_like(even)
        z_set[ABOVE + tile] = jnp.where(pz == 0, even, odd)
        z_set[BELOW + tile] = jnp.where(pz == 0, odd, even)

    for j in Z_UP + Z_DOWN:
        up = VELOCITIES[j][2] > 0
        group = (Z_UP if up else Z_DOWN).index(j)
        last = LANES - 1 if up else 0
        for part in range(ext_y // 8):
            halo = z_set[(ABOVE if up else BELOW) + 1, pl.ds(8 * part, 8), :]
            for x in range(ext_x):
                edge = pltpu.roll(halo, (last - 2 - GROUP * group - x) % LANES, 1)
                first[j, 2 + x, pl.ds(8 + 8 * part, 8), last : last + 1] = edge[:, last : last + 1]

    mask_like = jax.ShapeDtypeStruct((ext_x, ext_y, LANES), jnp.int32)
    pack_lines((mask_like,), first, packets, many_x, many_y, lambda kind, index: not is_flat(kind, index), False)

    for side in range(2):
        for part in range(ext_y // 8):
            rows = pl.ds(8 * part, 8)
            value = jnp.zeros((8, LANES), jnp.float32)
            for tile in range(Z_TILES):
                start = ext_x if side else 2
                moved = pltpu.roll(z_set[tile, rows, :], (2 * tile - start) % LANES, 1)
                value = jnp.where(spot // 2 == tile, moved, value)
            faces[side, rows, :] = value

    def add_xy(slot_x, slot_y, side_x, side_y):
        start = ext_y - 2 if side_y else 0
        to_xy[many_x * slot_y + slot_x][EDGE // 8, 0:2, :] = faces[side_x, start : start + 2, :]

    def add_y(slot, side):
        start = ext_y - 2 if side else 0
        for tile in range(Z_TILES):
            row = 2 * tile % 8
            to_y[slot][FACE + tile // 4, row : row + 2, :] = z_set[tile, start : start + 2, :]

    def add_x(slot, side):
        to_x[slot][FACE] = faces[side]

    for slot_y in range(many_y):
        there_y = has_partner("gy", slot_y)
        pl.when(there_y)(lambda: on_side(py, slot_y, functools.partial(add_y, slot_y)))
        for slot_x in range(many_x):
            pl.when(there_y & has_partner("gx", slot_x))(
                lambda: on_side(
                    py,
                    slot_y,
                    lambda side_y: on_side(px, slot_x, lambda side_x: add_xy(slot_x, slot_y, side_x, side_y)),
                )
            )
    for slot_x in range(many_x):
        pl.when(has_partner("gx", slot_x))(lambda: on_side(px, slot_x, functools.partial(add_x, slot_x)))


def collide(pulled, rho, ux, uy, uz, fluid, wanted):
    total = {}
    diff = {}
    for j in range(1, 19, 2):
        total[j] = pulled[j] + pulled[j + 1]
        diff[j] = pulled[j] - pulled[j + 1]
    in_xy, in_xz, in_yz = total[7] + total[9], total[11] + total[13], total[15] + total[17]
    two_x, two_y, two_z = total[1] + total[1], total[3] + total[3], total[5] + total[5]
    count = (12.0 * pulled[0] + (two_x + two_y)) + (two_z + (in_xy + (in_xz + in_yz)))
    flow_x = (diff[1] + diff[1]) + ((diff[7] + diff[9]) + (diff[11] + diff[13]))
    flow_y = (diff[3] + diff[3]) + ((diff[7] - diff[9]) + (diff[15] + diff[17]))
    flow_z = (diff[5] + diff[5]) + ((diff[11] - diff[13]) + (diff[15] - diff[17]))
    xx, yy, zz = two_x + (in_xy + in_xz), two_y + (in_xy + in_yz), two_z + (in_xz + in_yz)
    xy, xz, yz = total[7] - total[9], total[11] - total[13], total[15] - total[17]
    push_x = xx * ux + xy * uy + xz * uz
    push_y = xy * ux + yy * uy + yz * uz
    push_z = xz * ux + yz * uy + zz * uz
    usq = ux * ux + uy * uy + uz * uz
    push = ux * push_x + uy * push_y + uz * push_z
    inverse = 1.0 / rho
    base = count * (OMEGA / 36.0 + (OMEGA / 24.0) * usq) - (OMEGA / 8.0) * push - ux * inverse
    along_x = (OMEGA / 12.0) * (flow_x + 3.0 * push_x - ux * count) + inverse
    along_y = (OMEGA / 12.0) * (flow_y + 3.0 * push_y - uy * count)
    along_z = (OMEGA / 12.0) * (flow_z + 3.0 * push_z - uz * count)
    parts = {
        1: along_x,
        3: along_y,
        5: along_z,
        7: along_x + along_y,
        9: along_x - along_y,
        11: along_x + along_z,
        13: along_x - along_z,
        15: along_y + along_z,
        17: along_y - along_z,
    }
    out = {}
    for j in wanted:
        if j == 0:
            shift = base
        elif j % 2:
            shift = base + parts[j]
        else:
            shift = base - parts[j - 1]
        out[j] = jnp.where(fluid, (1.0 - OMEGA) * pulled[j] + shift, pulled[OPPOSITE[j]])
    change = (-1.0 / 6.0) * rho * (flow_x * ux + flow_y * uy + flow_z * uz)
    return out, jnp.where(fluid, change, 0.0)


class Plane:
    def __init__(self, x, row):
        self.x, self.row = x, row

    def load(self, ref, lead, margin, cx=0, cy=0):
        return ref[lead, self.x + margin + cx, pl.ds(8 + self.row + cy, 8), :]

    def store(self, ref, lead, margin, value):
        ref[lead, self.x + margin, pl.ds(8 + self.row, 8), :] = value


class Rim:
    def __init__(self, x, ext_y):
        self.x, self.ext_y = x, ext_y

    def load(self, ref, lead, margin, cx=0, cy=0):
        at = self.x + margin + cx
        upper = ref[lead, at, pl.ds(8 + self.ext_y - 1 + cy, 8), :]
        lower = ref[lead, at, pl.ds(1 + cy, 8), :]
        return jnp.where(lax.broadcasted_iota(jnp.int32, (8, LANES), 0) < 4, upper, lower)

    def store(self, ref, lead, margin, value):
        at = self.x + margin
        ref[lead, at, pl.ds(8 + self.ext_y - 1, 2), :] = value[0:2]
        ref[lead, at, pl.ds(7, 2), :] = value[6:8]


def first_step(first, fields, second, change, tiles, outside=True):
    loaded = [
        (
            [tile.load(first, j, 2, *VELOCITIES[j][:2]) for j in range(19)],
            [tile.load(fields, k, 1) for k in range(5)],
        )
        for tile in tiles
    ]
    done = [
        collide(pulled, rho, ux, uy, uz, kind > 1.5, range(19)) for pulled, (rho, ux, uy, uz, kind) in loaded
    ]
    for tile, (_, here), (after, gain) in zip(tiles, loaded, done):
        inside = here[KIND] > 0.5
        for j in range(19):
            value = jnp.where(inside, after[j], 0.0) if outside else after[j]
            cz = VELOCITIES[j][2]
            tile.store(second, j, 1, pltpu.roll(value, -cz % LANES, 1) if cz else value)
        tile.store(change, 0, 1, gain)


def inner_kernel(den, vel, mask, first, fields, second, change):
    refs = (None, den, vel, mask)
    ext_x, ext_y, _ = mask.shape
    every = slice(None)
    for k in range(5):
        fields[k, 1 : 1 + ext_x, pl.ds(8, ext_y), :] = field_of(refs, "field", k, (every, every, every))

    @pl.loop(0, ext_x // 2 - 1)
    def _(pair):
        tiles = [Plane(2 * pair + at, 1 + 8 * part) for at in (1, 2) for part in range(ext_y // 8)]
        first_step(first, fields, second, change, tiles, outside=False)


def put_row(first, fields, kind, index, x, y, value):
    row = y + 8
    if kind == "pop":
        first[index, x + 2, row : row + 1, :] = value
    else:
        fields[index, x + 1, row : row + 1, :] = value


def place_z(z_first, value, start, size, side, ext_x):
    rows = pl.ds(start, size)
    spot = lane_ids()[:size] % GROUP
    inside = spot >= 2 + ext_x if side else spot < 2
    for tile in range(Z_TILES):
        shift = (2 + ext_x if side else 0) - 2 * tile
        moved = pltpu.roll(value, shift % LANES, 1)[:size]
        z_first[tile, rows, :] = jnp.where(inside, moved, z_first[tile, rows, :])


def side_kernel(slots, z_set, *rest):
    many_x, many_y = slots
    from_x, from_y = rest[4 : 4 + many_x], rest[4 + many_x : 4 + many_x + many_y]
    first, fields, second, change, z_first = rest[-5:]
    _, ext_y, _ = z_set.shape
    ext_x = change.shape[1] - 2
    inner = pl.ds(8, ext_y)
    put = functools.partial(put_row, first, fields)
    z_first[:, inner, :] = z_set[...]

    def place_y(slot, side):
        packet = from_y[slot]
        for line, (kind, index, depth) in enumerate(face_lines(1, 2 * side - 1)):
            y = ext_y + depth if side else -1 - depth
            for x in range(ext_x):
                put(kind, index, x, y, packet[line, x : x + 1, :])
        start = 8 + ext_y if side else 6
        for tile in range(Z_TILES):
            row = 2 * tile % 8
            z_first[tile, start : start + 2, :] = packet[FACE + tile // 4, row : row + 2, :]
        if many_y == 1:
            clear_y(1 - side)

    def clear_y(side):
        nothing = jnp.zeros((1, LANES), jnp.float32)
        for kind, index, depth in face_lines(1, 2 * side - 1):
            y = ext_y + depth if side else -1 - depth
            for x in range(-1, ext_x + 1):
                put(kind, index, x, y, nothing)
            if kind == "pop":
                put(kind, index, -2, y, nothing)
                put(kind, index, ext_x + 1, y, nothing)
        start = 8 + ext_y if side else 6
        for tile in range(Z_TILES):
            z_first[tile, start : start + 2, :] = jnp.zeros((2, LANES), jnp.float32)

    def place_x(slot, side):
        packet = from_x[slot]
        for line, (kind, index, depth) in enumerate(face_lines(0, 2 * side - 1)):
            x = ext_x + depth if side else -1 - depth
            if kind == "pop":
                first[index, x + 2, inner, :] = packet[line]
            else:
                fields[index, x + 1, inner, :] = packet[line]
        for part in range(ext_y // 8):
            place_z(z_first, packet[FACE, pl.ds(8 * part, 8), :], 8 + 8 * part, 8, side, ext_x)

    for slot_y in range(many_y):
        on_side(parity_of("gy"), slot_y, functools.partial(place_y, slot_y))
    for slot_x in range(many_x):
        on_side(parity_of("gx"), slot_x, functools.partial(place_x, slot_x))

    for x in (-1, 0, ext_x - 1, ext_x):
        for row in range(7, ext_y - 8, 8):
            first_step(first, fields, second, change, [Plane(x, row)], outside=x in (-1, ext_x))

    @pl.loop(0, ext_x // 2 - 1)
    def _(pair):
        first_step(first, fields, second, change, [Rim(2 * pair + 1, ext_y), Rim(2 * pair + 2, ext_y)])


def last_kernel(slots, den, vel, mask, *rest):
    many_x, many_y = slots
    from_xy = rest[5 : 5 + many_x * many_y]
    out, sens, first, fields, second, change, z_first, z_second, held, held_sens, sems = rest[-11:]
    ext_x, ext_y, _ = mask.shape
    lane = lane_ids()
    every = slice(None)
    px, py = parity_of("gx"), parity_of("gy")

    def place_xy(slot_x, slot_y, side_x, side_y):
        packet = from_xy[many_x * slot_y + slot_x]
        for line, (kind, index, far_x, far_y) in enumerate(edge_lines(2 * side_x - 1, 2 * side_y - 1)):
            x = ext_x + far_x if side_x else -1 - far_x
            y = ext_y + far_y if side_y else -1 - far_y
            put_row(first, fields, kind, index, x, y, packet[line // 8, line % 8 : line % 8 + 1, :])
        place_z(z_first, packet[EDGE // 8], 8 + ext_y if side_y else 6, 2, side_x, ext_x)

    for slot_x in range(many_x):
        for slot_y in range(many_y):
            on_side(
                py,
                slot_y,
                lambda side_y: on_side(px, slot_x, lambda side_x: place_xy(slot_x, slot_y, side_x, side_y)),
            )

    for x in (-1, 0, ext_x - 1, ext_x):
        first_step(first, fields, second, change, [Plane(x, -1), Plane(x, ext_y - 1)])

    for part in range((ext_y + 2 + 7) // 8):
        row = 7 + 8 * part

        def both(low_tile, high_tile, group, cx, cy):
            rows = pl.ds(row + cy, 8)
            low = pltpu.roll(z_first[low_tile, rows, :], (-GROUP * group - cx) % LANES, 1)
            high = pltpu.roll(z_first[high_tile, rows, :], (LANES // 2 - GROUP * group - cx) % LANES, 1)
            return jnp.where(lane < LANES // 2, low, high)

        pulled = []
        for j in range(19):
            cx, cy, cz = VELOCITIES[j]
            if cz == 0:
                tile, group = Z_PLACE[("pop", j)]
                pulled.append(both(BELOW + tile, ABOVE + tile, group, cx, cy))
            elif cz == 1:
                pulled.append(both(OWN_LOW, ABOVE + 2, Z_UP.index(j), cx, cy))
            else:
                pulled.append(both(BELOW + 2, OWN_HIGH, Z_DOWN.index(j), cx, cy))
        rho, ux, uy, uz, kind = [
            both(BELOW + tile, ABOVE + tile, group, 0, 0)
            for tile, group in [Z_PLACE[("field", k)] for k in range(5)]
        ]
        after, _ = collide(pulled, rho, ux, uy, uz, kind > 1.5, Z_UP + Z_DOWN)
        for group in range(5):
            value = jnp.where(lane < LANES // 2, after[Z_DOWN[group]], after[Z_UP[group]])
            z_second[group, pl.ds(row, 8), :] = jnp.where(kind > 0.5, value, 0.0)

    def copies(x):
        return (
            pltpu.make_async_copy(held.at[:, x], out.at[:, x], sems.at[0, x]),
            pltpu.make_async_copy(held_sens.at[x], sens.at[x], sems.at[1, x]),
        )

    @pl.loop(0, ext_x // 2)
    def _(pair):
        loaded = []
        for x, part in itertools.product((2 * pair, 2 * pair + 1), range(ext_y // 8)):
            row = 8 + 8 * part
            pulled = []
            for j in range(19):
                cx, cy, cz = VELOCITIES[j]
                rows = pl.ds(row + cy, 8)
                value = second[j, x + 1 + cx, rows, :]
                if cz == 1:
                    edge = z_second[Z_UP.index(j), rows, :]
                    edge = pltpu.roll(edge, LANES // 2 - 3 - cx - x, 1)
                    value = jnp.where(lane == LANES - 1, edge, value)
                elif cz == -1:
                    edge = z_second[Z_DOWN.index(j), rows, :]
                    edge = pltpu.roll(edge, LANES - 2 - cx - x, 1)
                    value = jnp.where(lane == 0, edge, value)
                pulled.append(value)
            at = (x, pl.ds(8 * part, 8), every)
            here = [den[(0, *at)], vel[(0, 0, *at)], vel[(0, 1, *at)], vel[(0, 2, *at)], mask[at] > 0]
            loaded.append((at, pulled, here, change[0, x + 1, pl.ds(row, 8), :]))
        done = [collide(pulled, *here, range(19)) for _, pulled, here, _ in loaded]
        for (at, _, _, before), (after, gain) in zip(loaded, done):
            for j in range(19):
                held[(j, *at)] = after[j]
            held_sens[at] = before + gain
        for copy in copies(2 * pair) + copies(2 * pair + 1):
            copy.start()

    for x in range(ext_x):
        for copy in copies(x):
            copy.wait()


def shards(adjoint, density, velocity, pore_mask):
    ext_x, ext_y, ext_z = pore_mask.shape
    assert ext_z == LANES and ext_y % 8 == 0 and ext_x + 4 <= GROUP and ext_x == 8
    many_x = 2
    many_y, many_z = [1 if lax.axis_size(axis) == 2 else 2 for axis in ("gy", "gz")]
    vmem = pl.BlockSpec(memory_space=pltpu.VMEM)
    hbm = pl.BlockSpec(memory_space=pltpu.HBM)
    inputs = (adjoint, density, velocity, pore_mask)

    def array(*shape):
        return jax.ShapeDtypeStruct(shape, jnp.float32)

    def call(kernel, name, operands, shapes, limit, **more):
        more.setdefault("out_specs", [vmem] * len(shapes))
        more.setdefault("in_specs", [vmem] * len(operands))
        params = pltpu.CompilerParams(vmem_limit_bytes=limit * 1024 * 1024)
        return pl.pallas_call(kernel, out_shape=shapes, compiler_params=params, name=name, **more)(*operands)

    def partners(axis, slot):
        found = {}
        for at in range(slot, lax.axis_size(axis) - 1, 2):
            found[at], found[at + 1] = at + 1, at
        return found

    def ends(axis):
        last = lax.axis_size(axis) - 1
        return {0: last, last: 0}

    def swap(value, spares, *places):
        tables = {axis: partners(axis, slot) for axis, slot in places}
        axes = [axis for axis in ("gx", "gy", "gz") if axis in tables or axis in dict(spares)]
        sizes = [lax.axis_size(axis) for axis in axes]
        pairs = []
        for at in itertools.product(*[range(size) for size in sizes]):
            to = [tables.get(axis, {}).get(spot, spot) for axis, spot in zip(axes, at)]
            for spare, table in spares:
                if tuple(to) == at:
                    to = [table.get(spot, spot) if axis == spare else spot for axis, spot in zip(axes, at)]
            flat = []
            for spots in (at, to):
                index = 0
                for size, spot in zip(sizes, spots):
                    index = index * size + spot
                flat.append(index)
            pairs.append(tuple(flat))
        return lax.ppermute(value, tuple(axes), pairs)

    loaded = [jax.ShapeDtypeStruct(value.shape, value.dtype) for value in inputs]
    *held, near, a_z, b_z = (
        *call(
            functools.partial(pack_z_kernel, many_z),
            "pack_z",
            [pltpu.with_memory_space_constraint(value, pltpu.HBM) for value in inputs],
            loaded + [array(2, ext_y, LANES)] + [array(3, ext_y, LANES)] * many_z,
            8,
            in_specs=[hbm] * 4,
            scratch_shapes=[pltpu.SemaphoreType.DMA((7,))],
        ),
        *[None] * (2 - many_z),
    )
    from_z = [swap(value, [("gx", partners("gx", 0))], ("gz", slot)) for slot, value in enumerate((a_z, b_z)[:many_z])]

    rows = ext_y + 16
    adj, den, vel, mask = held
    shapes = (
        [array(19, ext_x + 4, rows, LANES)]
        + [array(FACE + 1, ext_y, LANES)] * many_x
        + [array(FACE + 2, ext_x, LANES)] * many_y
        + [array(EDGE // 8 + 1, 8, LANES)] * (many_x * many_y)
    )
    shifted = call(
        functools.partial(shift_kernel, (many_x, many_y)),
        "shift",
        (adj, den, vel, mask),
        shapes,
        8,
        cost_estimate=pl.CostEstimate(flops=1_000_000, bytes_accessed=2_500_000, transcendentals=0),
    )
    z_set, first, *packets = call(
        functools.partial(pack_xy_kernel, (many_x, many_y, many_z)),
        "pack_xy",
        (near, *from_z, *shifted),
        [array(Z_TILES, ext_y, LANES)] + shapes,
        8,
        input_output_aliases={1 + many_z + at: 1 + at for at in range(len(shapes))},
        scratch_shapes=[pltpu.VMEM((2, ext_y, LANES), jnp.float32)],
    )
    to_x, to_y, to_xy = packets[:many_x], packets[many_x : many_x + many_y], packets[many_x + many_y :]
    from_xy = [
        swap(to_xy[many_x * slot_y + slot_x], [], ("gx", slot_x), ("gy", slot_y))
        for slot_y in range(many_y)
        for slot_x in range(many_x)
    ]
    from_y = [swap(value, [("gz", partners("gz", 0))], ("gy", slot)) for slot, value in enumerate(to_y)]
    spares = [("gz", partners("gz", 1)), ("gx", ends("gx"))]
    from_x = [swap(value, spares, ("gx", slot)) for slot, value in enumerate(to_x)]

    fields, second, change = call(
        inner_kernel,
        "inner_step",
        (den, vel, mask, first),
        [array(5, ext_x + 2, rows, LANES), array(19, ext_x + 2, rows, LANES), array(1, ext_x + 2, rows, LANES)],
        8,
        cost_estimate=pl.CostEstimate(flops=40_000_000, bytes_accessed=8_000_000, transcendentals=0),
    )
    inout = (first, fields, second, change)
    inout = call(
        functools.partial(side_kernel, (many_x, many_y)),
        "side_step",
        (z_set, *inout, *from_x, *from_y),
        [array(*value.shape) for value in inout] + [array(Z_TILES, rows, LANES)],
        8,
        input_output_aliases={1 + at: at for at in range(4)},
        cost_estimate=pl.CostEstimate(flops=40_000_000, bytes_accessed=8_000_000, transcendentals=0),
    )
    return call(
        functools.partial(last_kernel, (many_x, many_y)),
        "last_steps",
        (den, vel, mask, *inout, *from_xy),
        [array(19, ext_x, ext_y, LANES), array(ext_x, ext_y, LANES)] + [array(*value.shape) for value in inout],
        8,
        out_specs=[hbm] * 2 + [vmem] * 5,
        input_output_aliases={3 + at: 2 + at for at in range(5)},
        scratch_shapes=[
            pltpu.VMEM((5, rows, LANES), jnp.float32),
            pltpu.VMEM((19, ext_x, ext_y, LANES), jnp.float32),
            pltpu.VMEM((ext_x, ext_y, LANES), jnp.float32),
            pltpu.SemaphoreType.DMA((2, ext_x)),
        ],
    )[:2]


def solution(mesh):
    placed = (
        P(None, "gx", "gy", "gz"),
        P(None, "gx", "gy", "gz"),
        P(None, None, "gx", "gy", "gz"),
        P("gx", "gy", "gz"),
    )

    def whole(*arrays):
        return tuple(shards(*arrays))

    return jax.shard_map(
        whole,
        mesh=mesh,
        in_specs=placed,
        out_specs=(P(None, "gx", "gy", "gz"), P("gx", "gy", "gz")),
        check_vma=False,
    )
```

```python
import functools
import itertools

import jax
import jax.numpy as jnp
from jax import lax
from jax.experimental import pallas as pl
from jax.experimental.pallas import tpu as pltpu
from jax.sharding import PartitionSpec as P

VELOCITIES = [
    (0, 0, 0),
    (1, 0, 0),
    (-1, 0, 0),
    (0, 1, 0),
    (0, -1, 0),
    (0, 0, 1),
    (0, 0, -1),
    (1, 1, 0),
    (-1, -1, 0),
    (1, -1, 0),
    (-1, 1, 0),
    (1, 0, 1),
    (-1, 0, -1),
    (1, 0, -1),
    (-1, 0, 1),
    (0, 1, 1),
    (0, -1, -1),
    (0, 1, -1),
    (0, -1, 1),
]
OPPOSITE = [0, 2, 1, 4, 3, 6, 5, 8, 7, 10, 9, 12, 11, 14, 13, 16, 15, 18, 17]
OMEGA = 1.25
LANES = 128
GROUP = 16


def pops(axis, sign):
    return [j for j in range(19) if VELOCITIES[j][axis] == sign]


def mirrored(j):
    cx, cy, cz = VELOCITIES[j]
    return VELOCITIES.index((cx, cy, -cz))


Z_FLAT = pops(2, 0)
Z_UP = pops(2, 1)
Z_DOWN = [mirrored(j) for j in Z_UP]
RHO, UX, UY, UZ, KIND = range(5)
Z_PLACE = {("pop", j): (0, g) for g, j in enumerate(Z_FLAT[:8])}
Z_PLACE[("pop", Z_FLAT[8])] = (1, 5)
Z_PLACE[("field", RHO)] = (1, 6)
Z_PLACE[("field", KIND)] = (1, 7)
Z_PLACE[("field", UX)] = (2, 5)
Z_PLACE[("field", UY)] = (2, 6)
Z_PLACE[("field", UZ)] = (2, 7)
BELOW, ABOVE, OWN_LOW, OWN_HIGH, Z_TILES = 0, 3, 6, 7, 8


def face_lines(axis, toward):
    near = pops(axis, 0) + pops(axis, toward)
    lines = [("pop", j, 0) for j in near] + [("field", k, 0) for k in range(5)]
    return lines + [("pop", j, 1) for j in pops(axis, toward)]


def edge_lines(toward_x, toward_y):
    lines = [("field", k, 0, 0) for k in range(5)]
    for j in range(19):
        cx, cy, _ = VELOCITIES[j]
        if cx not in (0, toward_x) or cy not in (0, toward_y):
            continue
        lines.append(("pop", j, 0, 0))
        if cx:
            lines.append(("pop", j, 1, 0))
        if cy:
            lines.append(("pop", j, 0, 1))
        if cx and cy:
            lines.append(("pop", j, 1, 1))
    return lines


FACE = 24
EDGE = 24


def lane_ids():
    return lax.broadcasted_iota(jnp.int32, (8, LANES), 1)


def field_of(refs, kind, index, at):
    adj, den, vel, mask = refs
    if kind == "pop":
        return adj[(index, *at)]
    if index == RHO:
        return den[(1, *at)]
    if index == KIND:
        return (mask[at] + 1).astype(jnp.float32)
    return vel[(1, index - UX, *at)]


def parity_of(axis):
    return lax.rem(lax.axis_index(axis), 2)


def on_side(parity, slot, act):
    @pl.when(parity == slot)
    def _():
        act(1)

    @pl.when(parity != slot)
    def _():
        act(0)


def has_partner(axis, slot):
    at = lax.axis_index(axis)
    to = at + jnp.where(lax.rem(at, 2) == slot, 1, -1)
    return (to >= 0) & (to < lax.axis_size(axis))


def pack_z_kernel(slots, adj_in, den_in, vel_in, mask_in, adj, den, vel, mask, near, *rest):
    packets, sems = rest[:slots], rest[slots]
    refs = (adj, den, vel, mask)
    ext_x, ext_y, _ = mask.shape
    starts = range(0, 19, 5)
    loads = [
        pltpu.make_async_copy(adj_in.at[start : min(start + 5, 19)], adj.at[start : min(start + 5, 19)], sems.at[at])
        for at, start in enumerate(starts)
    ] + [
        pltpu.make_async_copy(source, target, sems.at[len(starts) + at])
        for at, (source, target) in enumerate([(den_in, den), (vel_in, vel), (mask_in, mask)])
    ]
    for load in loads:
        load.start()
    lane = lane_ids()
    parity = parity_of("gz")
    parts = range(ext_y // 8)
    zero = jnp.zeros((8, LANES), jnp.float32)
    lows, highs = [[zero] * 3 for _ in parts], [[zero] * 3 for _ in parts]
    far_low, far_high = [zero for _ in parts], [zero for _ in parts]

    def gather(kind, index):
        for x, part in itertools.product(range(ext_x), parts):
            value = field_of(refs, kind, index, (x, pl.ds(8 * part, 8), slice(None)))
            if kind == "pop" and VELOCITIES[index][2] == 1:
                spot = GROUP * Z_UP.index(index) + 2 + x
                moved = pltpu.roll(value, spot, 1)
                lows[part][1] = jnp.where(lane == spot, moved, lows[part][1])
                far_low[part] = jnp.where(lane == spot + 1, moved, far_low[part])
            elif kind == "pop" and VELOCITIES[index][2] == -1:
                spot = GROUP * Z_DOWN.index(index) + 2 + x
                moved = pltpu.roll(value, spot, 1)
                highs[part][1] = jnp.where(lane == spot - 1, moved, highs[part][1])
                far_high[part] = jnp.where(lane == spot - 2, moved, far_high[part])
            else:
                tile, group = Z_PLACE[(kind, index)]
                spot = GROUP * group + 2 + x
                moved = pltpu.roll(value, spot, 1)
                lows[part][tile] = jnp.where(lane == spot, moved, lows[part][tile])
                highs[part][tile] = jnp.where(lane == spot - 1, moved, highs[part][tile])

    for start, load in zip(starts, loads):
        load.wait()
        for j in range(start, min(start + 5, 19)):
            gather("pop", j)
    for load in loads[len(starts) :]:
        load.wait()
    for k in range(5):
        gather("field", k)
    for part in parts:
        rows = pl.ds(8 * part, 8)
        low = lows[part]
        high = [pltpu.roll(tile, 1, 1) for tile in highs[part]]
        low[2] = jnp.where(lane < 5 * GROUP, pltpu.roll(far_low[part], LANES - 1, 1), low[2])
        high[2] = jnp.where(lane < 5 * GROUP, pltpu.roll(far_high[part], 2, 1), high[2])
        near[0, rows, :] = low[1]
        near[1, rows, :] = high[1]
        for slot in range(slots):
            there = has_partner("gz", slot)
            for tile in range(3):
                value = jnp.where(parity == slot, high[tile], low[tile])
                packets[slot][tile, rows, :] = jnp.where(there, value, 0.0)


def pack_lines(refs, first, packets, many_x, many_y, wanted, clear):
    to_x, to_y = packets[:many_x], packets[many_x : many_x + many_y]
    to_xy = packets[many_x + many_y :]
    ext_x, ext_y, _ = refs[-1].shape
    every = slice(None)
    px, py = parity_of("gx"), parity_of("gy")

    def line_of(kind, index, x, y):
        if kind == "pop":
            return first[index, x + 2, y + 8 : y + 9, :]
        return field_of(refs, kind, index, (x, slice(y, y + 1), every))

    def pack_xy(slot_x, slot_y, side_x, side_y):
        packet = to_xy[many_x * slot_y + slot_x]
        for line, (kind, index, far_x, far_y) in enumerate(edge_lines(1 - 2 * side_x, 1 - 2 * side_y)):
            if wanted(kind, index):
                x = ext_x - 1 - far_x if side_x else far_x
                y = ext_y - 1 - far_y if side_y else far_y
                packet[line // 8, line % 8 : line % 8 + 1, :] = line_of(kind, index, x, y)

    def pack_y(slot, side):
        for line, (kind, index, depth) in enumerate(face_lines(1, 1 - 2 * side)):
            if wanted(kind, index):
                y = ext_y - 1 - depth if side else depth
                for x in range(ext_x):
                    to_y[slot][line, x : x + 1, :] = line_of(kind, index, x, y)

    def pack_x(slot, side):
        for line, (kind, index, depth) in enumerate(face_lines(0, 1 - 2 * side)):
            if wanted(kind, index):
                x = ext_x - 1 - depth if side else depth
                if kind == "pop":
                    to_x[slot][line] = first[index, x + 2, pl.ds(8, ext_y), :]
                else:
                    to_x[slot][line] = field_of(refs, kind, index, (x, every, every))

    def when_there(there, packet, act):
        pl.when(there)(act)
        if clear:

            @pl.when(jnp.logical_not(there))
            def _():
                packet[...] = jnp.zeros(packet.shape, jnp.float32)

    for slot_y in range(many_y):
        there_y = has_partner("gy", slot_y)
        when_there(there_y, to_y[slot_y], lambda: on_side(py, slot_y, functools.partial(pack_y, slot_y)))
        for slot_x in range(many_x):
            when_there(
                there_y & has_partner("gx", slot_x),
                to_xy[many_x * slot_y + slot_x],
                lambda: on_side(
                    py,
                    slot_y,
                    lambda side_y: on_side(px, slot_x, lambda side_x: pack_xy(slot_x, slot_y, side_x, side_y)),
                ),
            )
    for slot_x in range(many_x):
        when_there(
            has_partner("gx", slot_x), to_x[slot_x], lambda: on_side(px, slot_x, functools.partial(pack_x, slot_x))
        )


def is_flat(kind, index):
    return kind == "field" or VELOCITIES[index][2] == 0


def shift_kernel(slots, adj, den, vel, mask, first, *packets):
    many_x, many_y = slots
    _, ext_x, ext_y, _ = adj.shape
    for j in range(19):
        cz = VELOCITIES[j][2]
        for x, part in itertools.product(range(ext_x), range(ext_y // 8)):
            value = adj[j, x, pl.ds(8 * part, 8), :]
            first[j, 2 + x, pl.ds(8 + 8 * part, 8), :] = pltpu.roll(value, -cz % LANES, 1) if cz else value
    pack_lines((None, den, vel, mask), first, packets, many_x, many_y, is_flat, True)


def pack_xy_kernel(slots, near, *rest):
    many_x, many_y, many_z = slots
    count = many_x + many_y + many_x * many_y
    from_z, rest = rest[:many_z], rest[many_z + 1 + count :]
    z_set, first, packets, faces = rest[0], rest[1], rest[2:-1], rest[-1]
    to_x, to_y, to_xy = packets[:many_x], packets[many_x : many_x + many_y], packets[many_x + many_y :]
    ext_x, ext_y = first.shape[1] - 4, near.shape[1]
    spot = lane_ids() % GROUP
    px, py, pz = parity_of("gx"), parity_of("gy"), parity_of("gz")

    z_set[OWN_LOW] = near[0]
    z_set[OWN_HIGH] = near[1]
    for tile in range(3):
        even = from_z[0][tile]
        odd = from_z[1][tile] if many_z > 1 else jnp.zeros_like(even)
        z_set[ABOVE + tile] = jnp.where(pz == 0, even, odd)
        z_set[BELOW + tile] = jnp.where(pz == 0, odd, even)

    for j in Z_UP + Z_DOWN:
        up = VELOCITIES[j][2] > 0
        group = (Z_UP if up else Z_DOWN).index(j)
        last = LANES - 1 if up else 0
        for part in range(ext_y // 8):
            halo = z_set[(ABOVE if up else BELOW) + 1, pl.ds(8 * part, 8), :]
            for x in range(ext_x):
                edge = pltpu.roll(halo, (last - 2 - GROUP * group - x) % LANES, 1)
                first[j, 2 + x, pl.ds(8 + 8 * part, 8), last : last + 1] = edge[:, last : last + 1]

    mask_like = jax.ShapeDtypeStruct((ext_x, ext_y, LANES), jnp.int32)
    pack_lines((mask_like,), first, packets, many_x, many_y, lambda kind, index: not is_flat(kind, index), False)

    for side in range(2):
        for part in range(ext_y // 8):
            rows = pl.ds(8 * part, 8)
            value = jnp.zeros((8, LANES), jnp.float32)
            for tile in range(Z_TILES):
                start = ext_x if side else 2
                moved = pltpu.roll(z_set[tile, rows, :], (2 * tile - start) % LANES, 1)
                value = jnp.where(spot // 2 == tile, moved, value)
            faces[side, rows, :] = value

    def add_xy(slot_x, slot_y, side_x, side_y):
        start = ext_y - 2 if side_y else 0
        to_xy[many_x * slot_y + slot_x][EDGE // 8, 0:2, :] = faces[side_x, start : start + 2, :]

    def add_y(slot, side):
        start = ext_y - 2 if side else 0
        for tile in range(Z_TILES):
            row = 2 * tile % 8
            to_y[slot][FACE + tile // 4, row : row + 2, :] = z_set[tile, start : start + 2, :]

    def add_x(slot, side):
        to_x[slot][FACE] = faces[side]

    for slot_y in range(many_y):
        there_y = has_partner("gy", slot_y)
        pl.when(there_y)(lambda: on_side(py, slot_y, functools.partial(add_y, slot_y)))
        for slot_x in range(many_x):
            pl.when(there_y & has_partner("gx", slot_x))(
                lambda: on_side(
                    py,
                    slot_y,
                    lambda side_y: on_side(px, slot_x, lambda side_x: add_xy(slot_x, slot_y, side_x, side_y)),
                )
            )
    for slot_x in range(many_x):
        pl.when(has_partner("gx", slot_x))(lambda: on_side(px, slot_x, functools.partial(add_x, slot_x)))


def collide(pulled, rho, ux, uy, uz, fluid, wanted):
    total = {}
    diff = {}
    for j in range(1, 19, 2):
        total[j] = pulled[j] + pulled[j + 1]
        diff[j] = pulled[j] - pulled[j + 1]
    in_xy, in_xz, in_yz = total[7] + total[9], total[11] + total[13], total[15] + total[17]
    two_x, two_y, two_z = total[1] + total[1], total[3] + total[3], total[5] + total[5]
    count = (12.0 * pulled[0] + (two_x + two_y)) + (two_z + (in_xy + (in_xz + in_yz)))
    flow_x = (diff[1] + diff[1]) + ((diff[7] + diff[9]) + (diff[11] + diff[13]))
    flow_y = (diff[3] + diff[3]) + ((diff[7] - diff[9]) + (diff[15] + diff[17]))
    flow_z = (diff[5] + diff[5]) + ((diff[11] - diff[13]) + (diff[15] - diff[17]))
    xx, yy, zz = two_x + (in_xy + in_xz), two_y + (in_xy + in_yz), two_z + (in_xz + in_yz)
    xy, xz, yz = total[7] - total[9], total[11] - total[13], total[15] - total[17]
    push_x = xx * ux + xy * uy + xz * uz
    push_y = xy * ux + yy * uy + yz * uz
    push_z = xz * ux + yz * uy + zz * uz
    usq = ux * ux + uy * uy + uz * uz
    push = ux * push_x + uy * push_y + uz * push_z
    inverse = 1.0 / rho
    base = count * (OMEGA / 36.0 + (OMEGA / 24.0) * usq) - (OMEGA / 8.0) * push - ux * inverse
    along_x = (OMEGA / 12.0) * (flow_x + 3.0 * push_x - ux * count) + inverse
    along_y = (OMEGA / 12.0) * (flow_y + 3.0 * push_y - uy * count)
    along_z = (OMEGA / 12.0) * (flow_z + 3.0 * push_z - uz * count)
    parts = {
        1: along_x,
        3: along_y,
        5: along_z,
        7: along_x + along_y,
        9: along_x - along_y,
        11: along_x + along_z,
        13: along_x - along_z,
        15: along_y + along_z,
        17: along_y - along_z,
    }
    out = {}
    for j in wanted:
        if j == 0:
            shift = base
        elif j % 2:
            shift = base + parts[j]
        else:
            shift = base - parts[j - 1]
        out[j] = jnp.where(fluid, (1.0 - OMEGA) * pulled[j] + shift, pulled[OPPOSITE[j]])
    change = (-1.0 / 6.0) * rho * (flow_x * ux + flow_y * uy + flow_z * uz)
    return out, jnp.where(fluid, change, 0.0)


class Plane:
    def __init__(self, x, row):
        self.x, self.row = x, row

    def load(self, ref, lead, margin, cx=0, cy=0):
        return ref[lead, self.x + margin + cx, pl.ds(8 + self.row + cy, 8), :]

    def store(self, ref, lead, margin, value):
        ref[lead, self.x + margin, pl.ds(8 + self.row, 8), :] = value


class Rim:
    def __init__(self, x, ext_y):
        self.x, self.ext_y = x, ext_y

    def load(self, ref, lead, margin, cx=0, cy=0):
        at = self.x + margin + cx
        upper = ref[lead, at, pl.ds(8 + self.ext_y - 1 + cy, 8), :]
        lower = ref[lead, at, pl.ds(1 + cy, 8), :]
        return jnp.where(lax.broadcasted_iota(jnp.int32, (8, LANES), 0) < 4, upper, lower)

    def store(self, ref, lead, margin, value):
        at = self.x + margin
        ref[lead, at, pl.ds(8 + self.ext_y - 1, 2), :] = value[0:2]
        ref[lead, at, pl.ds(7, 2), :] = value[6:8]


def first_step(first, fields, second, change, tiles, outside=True):
    loaded = [
        (
            [tile.load(first, j, 2, *VELOCITIES[j][:2]) for j in range(19)],
            [tile.load(fields, k, 1) for k in range(5)],
        )
        for tile in tiles
    ]
    done = [
        collide(pulled, rho, ux, uy, uz, kind > 1.5, range(19)) for pulled, (rho, ux, uy, uz, kind) in loaded
    ]
    for tile, (_, here), (after, gain) in zip(tiles, loaded, done):
        inside = here[KIND] > 0.5
        for j in range(19):
            value = jnp.where(inside, after[j], 0.0) if outside else after[j]
            cz = VELOCITIES[j][2]
            tile.store(second, j, 1, pltpu.roll(value, -cz % LANES, 1) if cz else value)
        tile.store(change, 0, 1, gain)


def inner_kernel(den, vel, mask, first, fields, second, change):
    refs = (None, den, vel, mask)
    ext_x, ext_y, _ = mask.shape
    every = slice(None)
    for k in range(5):
        fields[k, 1 : 1 + ext_x, pl.ds(8, ext_y), :] = field_of(refs, "field", k, (every, every, every))

    many = 3 if (ext_x - 2) % 3 == 0 else 1

    @pl.loop(0, (ext_x - 2) // many)
    def _(group):
        tiles = [Plane(many * group + at + 1, 1 + 8 * part) for at in range(many) for part in range(ext_y // 8)]
        first_step(first, fields, second, change, tiles, outside=False)


def put_row(first, fields, kind, index, x, y, value):
    row = y + 8
    if kind == "pop":
        first[index, x + 2, row : row + 1, :] = value
    else:
        fields[index, x + 1, row : row + 1, :] = value


def place_z(z_first, value, start, size, side, ext_x):
    rows = pl.ds(start, size)
    spot = lane_ids()[:size] % GROUP
    inside = spot >= 2 + ext_x if side else spot < 2
    for tile in range(Z_TILES):
        shift = (2 + ext_x if side else 0) - 2 * tile
        moved = pltpu.roll(value, shift % LANES, 1)[:size]
        z_first[tile, rows, :] = jnp.where(inside, moved, z_first[tile, rows, :])


def side_kernel(slots, z_set, *rest):
    many_x, many_y = slots
    from_x, from_y = rest[4 : 4 + many_x], rest[4 + many_x : 4 + many_x + many_y]
    first, fields, second, change, z_first = rest[-5:]
    _, ext_y, _ = z_set.shape
    ext_x = change.shape[1] - 2
    inner = pl.ds(8, ext_y)
    put = functools.partial(put_row, first, fields)
    z_first[:, inner, :] = z_set[...]

    def place_y(slot, side):
        packet = from_y[slot]
        for line, (kind, index, depth) in enumerate(face_lines(1, 2 * side - 1)):
            y = ext_y + depth if side else -1 - depth
            for x in range(ext_x):
                put(kind, index, x, y, packet[line, x : x + 1, :])
        start = 8 + ext_y if side else 6
        for tile in range(Z_TILES):
            row = 2 * tile % 8
            z_first[tile, start : start + 2, :] = packet[FACE + tile // 4, row : row + 2, :]
        if many_y == 1:
            clear_y(1 - side)

    def clear_y(side):
        nothing = jnp.zeros((1, LANES), jnp.float32)
        for kind, index, depth in face_lines(1, 2 * side - 1):
            y = ext_y + depth if side else -1 - depth
            for x in range(-1, ext_x + 1):
                put(kind, index, x, y, nothing)
            if kind == "pop":
                put(kind, index, -2, y, nothing)
                put(kind, index, ext_x + 1, y, nothing)
        start = 8 + ext_y if side else 6
        for tile in range(Z_TILES):
            z_first[tile, start : start + 2, :] = jnp.zeros((2, LANES), jnp.float32)

    def place_x(slot, side):
        packet = from_x[slot]
        for line, (kind, index, depth) in enumerate(face_lines(0, 2 * side - 1)):
            x = ext_x + depth if side else -1 - depth
            if kind == "pop":
                first[index, x + 2, inner, :] = packet[line]
            else:
                fields[index, x + 1, inner, :] = packet[line]
        for part in range(ext_y // 8):
            place_z(z_first, packet[FACE, pl.ds(8 * part, 8), :], 8 + 8 * part, 8, side, ext_x)

    for slot_y in range(many_y):
        on_side(parity_of("gy"), slot_y, functools.partial(place_y, slot_y))
    for slot_x in range(many_x):
        on_side(parity_of("gx"), slot_x, functools.partial(place_x, slot_x))

    rims = range(7, ext_y - 8, 8)
    first_step(first, fields, second, change, [Plane(x, row) for x in (0, ext_x - 1) for row in rims], outside=False)
    first_step(first, fields, second, change, [Plane(x, row) for x in (-1, ext_x) for row in rims])

    many = 3 if (ext_x - 2) % 3 == 0 else 1

    @pl.loop(0, (ext_x - 2) // many)
    def _(group):
        first_step(first, fields, second, change, [Rim(many * group + at + 1, ext_y) for at in range(many)])


def last_kernel(slots, den, vel, mask, *rest):
    many_x, many_y = slots
    from_xy = rest[5 : 5 + many_x * many_y]
    out, sens, first, fields, second, change, z_first, z_second, held, held_sens, sems = rest[-11:]
    ext_x, ext_y, _ = mask.shape
    lane = lane_ids()
    every = slice(None)
    px, py = parity_of("gx"), parity_of("gy")

    def place_xy(slot_x, slot_y, side_x, side_y):
        packet = from_xy[many_x * slot_y + slot_x]
        for line, (kind, index, far_x, far_y) in enumerate(edge_lines(2 * side_x - 1, 2 * side_y - 1)):
            x = ext_x + far_x if side_x else -1 - far_x
            y = ext_y + far_y if side_y else -1 - far_y
            put_row(first, fields, kind, index, x, y, packet[line // 8, line % 8 : line % 8 + 1, :])
        place_z(z_first, packet[EDGE // 8], 8 + ext_y if side_y else 6, 2, side_x, ext_x)

    for slot_x in range(many_x):
        for slot_y in range(many_y):
            on_side(
                py,
                slot_y,
                lambda side_y: on_side(px, slot_x, lambda side_x: place_xy(slot_x, slot_y, side_x, side_y)),
            )

    for pair in ((-1, 0), (ext_x - 1, ext_x)):
        first_step(first, fields, second, change, [Plane(x, row) for x in pair for row in (-1, ext_y - 1)])

    starts = [7 + 8 * part for part in range((ext_y + 2 + 7) // 8)]
    loaded = []
    for row in starts:

        def both(low_tile, high_tile, group, cx, cy):
            rows = pl.ds(row + cy, 8)
            low = pltpu.roll(z_first[low_tile, rows, :], (-GROUP * group - cx) % LANES, 1)
            high = pltpu.roll(z_first[high_tile, rows, :], (LANES // 2 - GROUP * group - cx) % LANES, 1)
            return jnp.where(lane < LANES // 2, low, high)

        pulled = []
        for j in range(19):
            cx, cy, cz = VELOCITIES[j]
            if cz == 0:
                tile, group = Z_PLACE[("pop", j)]
                pulled.append(both(BELOW + tile, ABOVE + tile, group, cx, cy))
            elif cz == 1:
                pulled.append(both(OWN_LOW, ABOVE + 2, Z_UP.index(j), cx, cy))
            else:
                pulled.append(both(BELOW + 2, OWN_HIGH, Z_DOWN.index(j), cx, cy))
        places = [Z_PLACE[("field", k)] for k in range(5)]
        loaded.append((pulled, [both(BELOW + tile, ABOVE + tile, group, 0, 0) for tile, group in places]))
    done = [
        collide(pulled, rho, ux, uy, uz, kind > 1.5, Z_UP + Z_DOWN)[0] for pulled, (rho, ux, uy, uz, kind) in loaded
    ]
    for row, (_, here), after in zip(starts, loaded, done):
        for group in range(5):
            value = jnp.where(lane < LANES // 2, after[Z_DOWN[group]], after[Z_UP[group]])
            z_second[group, pl.ds(row, 8), :] = jnp.where(here[KIND] > 0.5, value, 0.0)

    def copies(x):
        return (
            pltpu.make_async_copy(held.at[:, x], out.at[:, x], sems.at[0, x]),
            pltpu.make_async_copy(held_sens.at[x], sens.at[x], sems.at[1, x]),
        )

    many = 4 if ext_x % 4 == 0 else 1

    @pl.loop(0, ext_x // many)
    def _(group):
        loaded = []
        planes = [many * group + at for at in range(many)]
        for x, part in itertools.product(planes, range(ext_y // 8)):
            row = 8 + 8 * part
            pulled = []
            for j in range(19):
                cx, cy, cz = VELOCITIES[j]
                rows = pl.ds(row + cy, 8)
                value = second[j, x + 1 + cx, rows, :]
                if cz == 1:
                    edge = z_second[Z_UP.index(j), rows, :]
                    edge = pltpu.roll(edge, LANES // 2 - 3 - cx - x, 1)
                    value = jnp.where(lane == LANES - 1, edge, value)
                elif cz == -1:
                    edge = z_second[Z_DOWN.index(j), rows, :]
                    edge = pltpu.roll(edge, LANES - 2 - cx - x, 1)
                    value = jnp.where(lane == 0, edge, value)
                pulled.append(value)
            at = (x, pl.ds(8 * part, 8), every)
            here = [den[(0, *at)], vel[(0, 0, *at)], vel[(0, 1, *at)], vel[(0, 2, *at)], mask[at] > 0]
            loaded.append((at, pulled, here, change[0, x + 1, pl.ds(row, 8), :]))
        done = [collide(pulled, *here, range(19)) for _, pulled, here, _ in loaded]
        for (at, _, _, before), (after, gain) in zip(loaded, done):
            for j in range(19):
                held[(j, *at)] = after[j]
            held_sens[at] = before + gain
        for x in planes:
            for copy in copies(x):
                copy.start()

    for x in range(ext_x):
        for copy in copies(x):
            copy.wait()


def shards(adjoint, density, velocity, pore_mask):
    ext_x, ext_y, ext_z = pore_mask.shape
    assert ext_z == LANES and ext_y % 8 == 0 and ext_x + 4 <= GROUP and ext_x == 8
    many_x = 2
    many_y, many_z = [1 if lax.axis_size(axis) == 2 else 2 for axis in ("gy", "gz")]
    vmem = pl.BlockSpec(memory_space=pltpu.VMEM)
    hbm = pl.BlockSpec(memory_space=pltpu.HBM)
    inputs = (adjoint, density, velocity, pore_mask)

    def array(*shape):
        return jax.ShapeDtypeStruct(shape, jnp.float32)

    def call(kernel, name, operands, shapes, limit, **more):
        more.setdefault("out_specs", [vmem] * len(shapes))
        more.setdefault("in_specs", [vmem] * len(operands))
        params = pltpu.CompilerParams(vmem_limit_bytes=limit * 1024 * 1024)
        return pl.pallas_call(kernel, out_shape=shapes, compiler_params=params, name=name, **more)(*operands)

    def partners(axis, slot):
        found = {}
        for at in range(slot, lax.axis_size(axis) - 1, 2):
            found[at], found[at + 1] = at + 1, at
        return found

    def ends(axis):
        last = lax.axis_size(axis) - 1
        return {0: last, last: 0}

    def swap(value, spares, *places):
        tables = {axis: partners(axis, slot) for axis, slot in places}
        axes = [axis for axis in ("gx", "gy", "gz") if axis in tables or axis in dict(spares)]
        sizes = [lax.axis_size(axis) for axis in axes]
        pairs = []
        for at in itertools.product(*[range(size) for size in sizes]):
            to = [tables.get(axis, {}).get(spot, spot) for axis, spot in zip(axes, at)]
            for spare, table in spares:
                if tuple(to) == at:
                    to = [table.get(spot, spot) if axis == spare else spot for axis, spot in zip(axes, at)]
            flat = []
            for spots in (at, to):
                index = 0
                for size, spot in zip(sizes, spots):
                    index = index * size + spot
                flat.append(index)
            pairs.append(tuple(flat))
        return lax.ppermute(value, tuple(axes), pairs)

    loaded = [jax.ShapeDtypeStruct(value.shape, value.dtype) for value in inputs]
    *held, near, a_z, b_z = (
        *call(
            functools.partial(pack_z_kernel, many_z),
            "pack_z",
            [pltpu.with_memory_space_constraint(value, pltpu.HBM) for value in inputs],
            loaded + [array(2, ext_y, LANES)] + [array(3, ext_y, LANES)] * many_z,
            8,
            in_specs=[hbm] * 4,
            scratch_shapes=[pltpu.SemaphoreType.DMA((7,))],
        ),
        *[None] * (2 - many_z),
    )
    from_z = [swap(value, [("gx", partners("gx", 0))], ("gz", slot)) for slot, value in enumerate((a_z, b_z)[:many_z])]

    rows = ext_y + 16
    adj, den, vel, mask = held
    shapes = (
        [array(19, ext_x + 4, rows, LANES)]
        + [array(FACE + 1, ext_y, LANES)] * many_x
        + [array(FACE + 2, ext_x, LANES)] * many_y
        + [array(EDGE // 8 + 1, 8, LANES)] * (many_x * many_y)
    )
    shifted = call(
        functools.partial(shift_kernel, (many_x, many_y)),
        "shift",
        (adj, den, vel, mask),
        shapes,
        8,
        cost_estimate=pl.CostEstimate(flops=1_000_000, bytes_accessed=2_500_000, transcendentals=0),
    )
    z_set, first, *packets = call(
        functools.partial(pack_xy_kernel, (many_x, many_y, many_z)),
        "pack_xy",
        (near, *from_z, *shifted),
        [array(Z_TILES, ext_y, LANES)] + shapes,
        8,
        input_output_aliases={1 + many_z + at: 1 + at for at in range(len(shapes))},
        scratch_shapes=[pltpu.VMEM((2, ext_y, LANES), jnp.float32)],
    )
    to_x, to_y, to_xy = packets[:many_x], packets[many_x : many_x + many_y], packets[many_x + many_y :]
    from_xy = [
        swap(to_xy[many_x * slot_y + slot_x], [], ("gx", slot_x), ("gy", slot_y))
        for slot_y in range(many_y)
        for slot_x in range(many_x)
    ]
    from_y = [swap(value, [("gz", partners("gz", 0))], ("gy", slot)) for slot, value in enumerate(to_y)]
    spares = [("gz", partners("gz", 1)), ("gx", ends("gx"))]
    from_x = [swap(value, spares, ("gx", slot)) for slot, value in enumerate(to_x)]

    fields, second, change = call(
        inner_kernel,
        "inner_step",
        (den, vel, mask, first),
        [array(5, ext_x + 2, rows, LANES), array(19, ext_x + 2, rows, LANES), array(1, ext_x + 2, rows, LANES)],
        8,
        cost_estimate=pl.CostEstimate(flops=40_000_000, bytes_accessed=8_000_000, transcendentals=0),
    )
    inout = (first, fields, second, change)
    inout = call(
        functools.partial(side_kernel, (many_x, many_y)),
        "side_step",
        (z_set, *inout, *from_x, *from_y),
        [array(*value.shape) for value in inout] + [array(Z_TILES, rows, LANES)],
        8,
        input_output_aliases={1 + at: at for at in range(4)},
        cost_estimate=pl.CostEstimate(flops=40_000_000, bytes_accessed=8_000_000, transcendentals=0),
    )
    return call(
        functools.partial(last_kernel, (many_x, many_y)),
        "last_steps",
        (den, vel, mask, *inout, *from_xy),
        [array(19, ext_x, ext_y, LANES), array(ext_x, ext_y, LANES)] + [array(*value.shape) for value in inout],
        8,
        out_specs=[hbm] * 2 + [vmem] * 5,
        input_output_aliases={3 + at: 2 + at for at in range(5)},
        scratch_shapes=[
            pltpu.VMEM((5, rows, LANES), jnp.float32),
            pltpu.VMEM((19, ext_x, ext_y, LANES), jnp.float32),
            pltpu.VMEM((ext_x, ext_y, LANES), jnp.float32),
            pltpu.SemaphoreType.DMA((2, ext_x)),
        ],
    )[:2]


def solution(mesh):
    placed = (
        P(None, "gx", "gy", "gz"),
        P(None, "gx", "gy", "gz"),
        P(None, None, "gx", "gy", "gz"),
        P("gx", "gy", "gz"),
    )

    def whole(*arrays):
        return tuple(shards(*arrays))

    return jax.shard_map(
        whole,
        mesh=mesh,
        in_specs=placed,
        out_specs=(P(None, "gx", "gy", "gz"), P("gx", "gy", "gz")),
        check_vma=False,
    )
```

```python
import functools
import itertools

import jax
import jax.numpy as jnp
from jax import lax
from jax.experimental import pallas as pl
from jax.experimental.pallas import tpu as pltpu
from jax.sharding import PartitionSpec as P

VELOCITIES = [
    (0, 0, 0),
    (1, 0, 0),
    (-1, 0, 0),
    (0, 1, 0),
    (0, -1, 0),
    (0, 0, 1),
    (0, 0, -1),
    (1, 1, 0),
    (-1, -1, 0),
    (1, -1, 0),
    (-1, 1, 0),
    (1, 0, 1),
    (-1, 0, -1),
    (1, 0, -1),
    (-1, 0, 1),
    (0, 1, 1),
    (0, -1, -1),
    (0, 1, -1),
    (0, -1, 1),
]
OPPOSITE = [0, 2, 1, 4, 3, 6, 5, 8, 7, 10, 9, 12, 11, 14, 13, 16, 15, 18, 17]
OMEGA = 1.25
LANES = 128
GROUP = 16


def pops(axis, sign):
    return [j for j in range(19) if VELOCITIES[j][axis] == sign]


def mirrored(j):
    cx, cy, cz = VELOCITIES[j]
    return VELOCITIES.index((cx, cy, -cz))


Z_FLAT = pops(2, 0)
Z_UP = pops(2, 1)
Z_DOWN = [mirrored(j) for j in Z_UP]
RHO, UX, UY, UZ, KIND = range(5)
Z_PLACE = {("pop", j): (0, g) for g, j in enumerate(Z_FLAT[:8])}
Z_PLACE[("pop", Z_FLAT[8])] = (1, 5)
Z_PLACE[("field", RHO)] = (1, 6)
Z_PLACE[("field", KIND)] = (1, 7)
Z_PLACE[("field", UX)] = (2, 5)
Z_PLACE[("field", UY)] = (2, 6)
Z_PLACE[("field", UZ)] = (2, 7)
BELOW, ABOVE, OWN_LOW, OWN_HIGH, Z_TILES = 0, 3, 6, 7, 8


def face_lines(axis, toward):
    near = pops(axis, 0) + pops(axis, toward)
    lines = [("pop", j, 0) for j in near] + [("field", k, 0) for k in range(5)]
    return lines + [("pop", j, 1) for j in pops(axis, toward)]


def edge_lines(toward_x, toward_y):
    lines = [("field", k, 0, 0) for k in range(5)]
    for j in range(19):
        cx, cy, _ = VELOCITIES[j]
        if cx not in (0, toward_x) or cy not in (0, toward_y):
            continue
        lines.append(("pop", j, 0, 0))
        if cx:
            lines.append(("pop", j, 1, 0))
        if cy:
            lines.append(("pop", j, 0, 1))
        if cx and cy:
            lines.append(("pop", j, 1, 1))
    return lines


FACE = 24
EDGE = 24
SIDE = 15


def side_lines(toward):
    full = [("pop", j) for j in pops(0, toward)] + [("share", p) for p in range(5)]
    full += [("field", k) for k in (UX, UY, UZ, KIND)]
    ends = []
    for end in range(2):
        for j in pops(1, 1 - 2 * end):
            cx = VELOCITIES[j][0]
            if cx in (0, toward):
                ends.append((j, abs(cx), end))
    return full, ends


def lane_ids():
    return lax.broadcasted_iota(jnp.int32, (8, LANES), 1)


def field_of(refs, kind, index, at):
    adj, den, vel, mask = refs
    if kind == "pop":
        return adj[(index, *at)]
    if index == RHO:
        return den[(1, *at)]
    if index == KIND:
        return (mask[at] + 1).astype(jnp.float32)
    return vel[(1, index - UX, *at)]


def parity_of(axis):
    return lax.rem(lax.axis_index(axis), 2)


def on_side(parity, slot, act):
    @pl.when(parity == slot)
    def _():
        act(1)

    @pl.when(parity != slot)
    def _():
        act(0)


def has_partner(axis, slot):
    at = lax.axis_index(axis)
    to = at + jnp.where(lax.rem(at, 2) == slot, 1, -1)
    return (to >= 0) & (to < lax.axis_size(axis))


def pack_z_kernel(slots, adj_in, den_in, vel_in, mask_in, adj, den, vel, mask, near, *rest):
    packets, sems = rest[:slots], rest[slots]
    refs = (adj, den, vel, mask)
    ext_x, ext_y, _ = mask.shape
    starts = range(0, 19, 5)
    loads = [
        pltpu.make_async_copy(adj_in.at[start : min(start + 5, 19)], adj.at[start : min(start + 5, 19)], sems.at[at])
        for at, start in enumerate(starts)
    ] + [
        pltpu.make_async_copy(source, target, sems.at[len(starts) + at])
        for at, (source, target) in enumerate([(den_in, den), (vel_in, vel), (mask_in, mask)])
    ]
    for load in loads:
        load.start()
    lane = lane_ids()
    parity = parity_of("gz")
    parts = range(ext_y // 8)
    zero = jnp.zeros((8, LANES), jnp.float32)
    lows, highs = [[zero] * 3 for _ in parts], [[zero] * 3 for _ in parts]
    far_low, far_high = [zero for _ in parts], [zero for _ in parts]

    def gather(kind, index):
        for x, part in itertools.product(range(ext_x), parts):
            value = field_of(refs, kind, index, (x, pl.ds(8 * part, 8), slice(None)))
            if kind == "pop" and VELOCITIES[index][2] == 1:
                spot = GROUP * Z_UP.index(index) + 2 + x
                moved = pltpu.roll(value, spot, 1)
                lows[part][1] = jnp.where(lane == spot, moved, lows[part][1])
                far_low[part] = jnp.where(lane == spot + 1, moved, far_low[part])
            elif kind == "pop" and VELOCITIES[index][2] == -1:
                spot = GROUP * Z_DOWN.index(index) + 2 + x
                moved = pltpu.roll(value, spot, 1)
                highs[part][1] = jnp.where(lane == spot - 1, moved, highs[part][1])
                far_high[part] = jnp.where(lane == spot - 2, moved, far_high[part])
            else:
                tile, group = Z_PLACE[(kind, index)]
                spot = GROUP * group + 2 + x
                moved = pltpu.roll(value, spot, 1)
                lows[part][tile] = jnp.where(lane == spot, moved, lows[part][tile])
                highs[part][tile] = jnp.where(lane == spot - 1, moved, highs[part][tile])

    for start, load in zip(starts, loads):
        load.wait()
        for j in range(start, min(start + 5, 19)):
            gather("pop", j)
    for load in loads[len(starts) :]:
        load.wait()
    for k in range(5):
        gather("field", k)
    for part in parts:
        rows = pl.ds(8 * part, 8)
        low = lows[part]
        high = [pltpu.roll(tile, 1, 1) for tile in highs[part]]
        low[2] = jnp.where(lane < 5 * GROUP, pltpu.roll(far_low[part], LANES - 1, 1), low[2])
        high[2] = jnp.where(lane < 5 * GROUP, pltpu.roll(far_high[part], 2, 1), high[2])
        near[0, rows, :] = low[1]
        near[1, rows, :] = high[1]
        for slot in range(slots):
            there = has_partner("gz", slot)
            for tile in range(3):
                value = jnp.where(parity == slot, high[tile], low[tile])
                packets[slot][tile, rows, :] = jnp.where(there, value, 0.0)


def pack_lines(refs, first, packets, many_x, many_y, wanted, shares):
    to_x, to_y = packets[:many_x], packets[many_x : many_x + many_y]
    to_xy = packets[many_x + many_y :]
    ext_x, ext_y, _ = refs[-1].shape
    every = slice(None)
    px, py = parity_of("gx"), parity_of("gy")

    def line_of(kind, index, x, y):
        if kind == "pop":
            return first[index, x + 2, y + 8 : y + 9, :]
        return field_of(refs, kind, index, (x, slice(y, y + 1), every))

    def pack_xy(slot_x, slot_y, side_x, side_y):
        packet = to_xy[many_x * slot_y + slot_x]
        for line, (kind, index, far_x, far_y) in enumerate(edge_lines(1 - 2 * side_x, 1 - 2 * side_y)):
            if wanted(kind, index):
                x = ext_x - 1 - far_x if side_x else far_x
                y = ext_y - 1 - far_y if side_y else far_y
                packet[line // 8, line % 8 : line % 8 + 1, :] = line_of(kind, index, x, y)

    def pack_y(slot, side):
        for line, (kind, index, depth) in enumerate(face_lines(1, 1 - 2 * side)):
            if wanted(kind, index):
                y = ext_y - 1 - depth if side else depth
                for x in range(ext_x):
                    to_y[slot][line, x : x + 1, :] = line_of(kind, index, x, y)

    def pack_x(slot, side):
        full, ends = side_lines(1 - 2 * side)
        for line, (kind, index) in enumerate(full):
            if kind == "field" and wanted(kind, index):
                to_x[slot][line] = field_of(refs, kind, index, (ext_x - 1 if side else 0, every, every))
            elif kind == "pop" and wanted(kind, index):
                to_x[slot][line] = first[index, (ext_x - 1 if side else 0) + 2, pl.ds(8, ext_y), :]
            elif kind == "share" and shares is not None:
                to_x[slot][line] = shares[side, index]
        for spot, (index, depth, end) in enumerate(ends):
            if wanted("pop", index):
                x = ext_x - 1 - depth if side else depth
                to_x[slot][SIDE - 1, spot : spot + 1, :] = line_of("pop", index, x, ext_y - 1 if end else 0)

    def when_there(there, packet, act):
        pl.when(there)(act)
        if shares is None:

            @pl.when(jnp.logical_not(there))
            def _():
                packet[...] = jnp.zeros(packet.shape, jnp.float32)

    for slot_y in range(many_y):
        there_y = has_partner("gy", slot_y)
        when_there(there_y, to_y[slot_y], lambda: on_side(py, slot_y, functools.partial(pack_y, slot_y)))
        for slot_x in range(many_x):
            when_there(
                there_y & has_partner("gx", slot_x),
                to_xy[many_x * slot_y + slot_x],
                lambda: on_side(
                    py,
                    slot_y,
                    lambda side_y: on_side(px, slot_x, lambda side_x: pack_xy(slot_x, slot_y, side_x, side_y)),
                ),
            )
    for slot_x in range(many_x):
        when_there(
            has_partner("gx", slot_x), to_x[slot_x], lambda: on_side(px, slot_x, functools.partial(pack_x, slot_x))
        )


def is_flat(kind, index):
    return kind == "field" or VELOCITIES[index][2] == 0


def shift_kernel(slots, adj, den, vel, mask, first, *packets):
    many_x, many_y = slots
    _, ext_x, ext_y, _ = adj.shape
    for j in range(19):
        cz = VELOCITIES[j][2]
        for x, part in itertools.product(range(ext_x), range(ext_y // 8)):
            value = adj[j, x, pl.ds(8 * part, 8), :]
            first[j, 2 + x, pl.ds(8 + 8 * part, 8), :] = pltpu.roll(value, -cz % LANES, 1) if cz else value
    pack_lines((None, den, vel, mask), first, packets, many_x, many_y, is_flat, None)


def pack_xy_kernel(slots, den, vel, mask, near, *rest):
    many_x, many_y, many_z = slots
    count = many_x + many_y + many_x * many_y
    from_z, rest = rest[:many_z], rest[many_z + 1 + count :]
    z_set, first, packets, faces, shares = rest[0], rest[1], rest[2:-2], rest[-2], rest[-1]
    to_x, to_y, to_xy = packets[:many_x], packets[many_x : many_x + many_y], packets[many_x + many_y :]
    ext_x, ext_y = first.shape[1] - 4, near.shape[1]
    spot = lane_ids() % GROUP
    px, py, pz = parity_of("gx"), parity_of("gy"), parity_of("gz")

    z_set[OWN_LOW] = near[0]
    z_set[OWN_HIGH] = near[1]
    for tile in range(3):
        even = from_z[0][tile]
        odd = from_z[1][tile] if many_z > 1 else jnp.zeros_like(even)
        z_set[ABOVE + tile] = jnp.where(pz == 0, even, odd)
        z_set[BELOW + tile] = jnp.where(pz == 0, odd, even)

    for j in Z_UP + Z_DOWN:
        up = VELOCITIES[j][2] > 0
        group = (Z_UP if up else Z_DOWN).index(j)
        last = LANES - 1 if up else 0
        for part in range(ext_y // 8):
            halo = z_set[(ABOVE if up else BELOW) + 1, pl.ds(8 * part, 8), :]
            for x in range(ext_x):
                edge = pltpu.roll(halo, (last - 2 - GROUP * group - x) % LANES, 1)
                first[j, 2 + x, pl.ds(8 + 8 * part, 8), last : last + 1] = edge[:, last : last + 1]


    sub = lax.broadcasted_iota(jnp.int32, (8, LANES), 0)
    loaded = []
    for side, part in itertools.product(range(2), range(ext_y // 8)):
        toward, x = 1 - 2 * side, ext_x - 1 if side else 0
        pulled = []
        for j in range(19):
            cx, cy, _ = VELOCITIES[j]
            if cx == -toward:
                pulled.append(jnp.zeros((8, LANES), jnp.float32))
                continue
            value = first[j, x + 2 + cx, pl.ds(8 + 8 * part + cy, 8), :]
            if cy == -1 and part == 0:
                value = jnp.where(sub == 0, 0.0, value)
            if cy == 1 and part == ext_y // 8 - 1:
                value = jnp.where(sub == 7, 0.0, value)
            pulled.append(value)
        at = (x, pl.ds(8 * part, 8), slice(None))
        here = [den[(1, *at)], vel[(1, 0, *at)], vel[(1, 1, *at)], vel[(1, 2, *at)], mask[at] > 0]
        loaded.append((side, part, pulled, here))
    for side, part, pulled, (rho, ux, uy, uz, fluid) in loaded:
        wanted = pops(0, 1 - 2 * side)
        after, _ = collide(pulled, 1.0 / rho, rho, ux, uy, uz, None, wanted)
        for line, j in enumerate(wanted):
            shares[side, line, pl.ds(8 * part, 8), :] = jnp.where(fluid, after[j], 0.0)

    pack_lines((mask,), first, packets, many_x, many_y, lambda kind, index: not is_flat(kind, index), shares)

    for side in range(2):
        for part in range(ext_y // 8):
            rows = pl.ds(8 * part, 8)
            value = jnp.zeros((8, LANES), jnp.float32)
            for tile in range(Z_TILES):
                start = ext_x if side else 2
                moved = pltpu.roll(z_set[tile, rows, :], (2 * tile - start) % LANES, 1)
                value = jnp.where(spot // 2 == tile, moved, value)
            faces[side, rows, :] = value

    def add_xy(slot_x, slot_y, side_x, side_y):
        start = ext_y - 2 if side_y else 0
        to_xy[many_x * slot_y + slot_x][EDGE // 8, 0:2, :] = faces[side_x, start : start + 2, :]

    def add_y(slot, side):
        start = ext_y - 2 if side else 0
        for tile in range(Z_TILES):
            row = 2 * tile % 8
            to_y[slot][FACE + tile // 4, row : row + 2, :] = z_set[tile, start : start + 2, :]

    def add_x(slot, side):
        to_x[slot][SIDE] = faces[side]

    for slot_y in range(many_y):
        there_y = has_partner("gy", slot_y)
        pl.when(there_y)(lambda: on_side(py, slot_y, functools.partial(add_y, slot_y)))
        for slot_x in range(many_x):
            pl.when(there_y & has_partner("gx", slot_x))(
                lambda: on_side(
                    py,
                    slot_y,
                    lambda side_y: on_side(px, slot_x, lambda side_x: add_xy(slot_x, slot_y, side_x, side_y)),
                )
            )
    for slot_x in range(many_x):
        pl.when(has_partner("gx", slot_x))(lambda: on_side(px, slot_x, functools.partial(add_x, slot_x)))


def collide(pulled, inverse, rho, ux, uy, uz, fluid, wanted):
    total = {}
    diff = {}
    for j in range(1, 19, 2):
        total[j] = pulled[j] + pulled[j + 1]
        diff[j] = pulled[j] - pulled[j + 1]
    in_xy, in_xz, in_yz = total[7] + total[9], total[11] + total[13], total[15] + total[17]
    two_x, two_y, two_z = total[1] + total[1], total[3] + total[3], total[5] + total[5]
    count = (12.0 * pulled[0] + (two_x + two_y)) + (two_z + (in_xy + (in_xz + in_yz)))
    flow_x = (diff[1] + diff[1]) + ((diff[7] + diff[9]) + (diff[11] + diff[13]))
    flow_y = (diff[3] + diff[3]) + ((diff[7] - diff[9]) + (diff[15] + diff[17]))
    flow_z = (diff[5] + diff[5]) + ((diff[11] - diff[13]) + (diff[15] - diff[17]))
    xx, yy, zz = two_x + (in_xy + in_xz), two_y + (in_xy + in_yz), two_z + (in_xz + in_yz)
    xy, xz, yz = total[7] - total[9], total[11] - total[13], total[15] - total[17]
    push_x = xx * ux + xy * uy + xz * uz
    push_y = xy * ux + yy * uy + yz * uz
    push_z = xz * ux + yz * uy + zz * uz
    usq = ux * ux + uy * uy + uz * uz
    push = ux * push_x + uy * push_y + uz * push_z
    base = count * (OMEGA / 36.0 + (OMEGA / 24.0) * usq) - (OMEGA / 8.0) * push - ux * inverse
    along_x = (OMEGA / 12.0) * (flow_x + 3.0 * push_x - ux * count) + inverse
    along_y = (OMEGA / 12.0) * (flow_y + 3.0 * push_y - uy * count)
    along_z = (OMEGA / 12.0) * (flow_z + 3.0 * push_z - uz * count)
    parts = {
        1: along_x,
        3: along_y,
        5: along_z,
        7: along_x + along_y,
        9: along_x - along_y,
        11: along_x + along_z,
        13: along_x - along_z,
        15: along_y + along_z,
        17: along_y - along_z,
    }
    out = {}
    for j in wanted:
        if j == 0:
            shift = base
        elif j % 2:
            shift = base + parts[j]
        else:
            shift = base - parts[j - 1]
        out[j] = (1.0 - OMEGA) * pulled[j] + shift
        if fluid is not None:
            out[j] = jnp.where(fluid, out[j], pulled[OPPOSITE[j]])
    change = (-1.0 / 6.0) * rho * (flow_x * ux + flow_y * uy + flow_z * uz)
    return out, change if fluid is None else jnp.where(fluid, change, 0.0)


class Plane:
    def __init__(self, x, row):
        self.x, self.row = x, row

    def load(self, ref, lead, margin, cx=0, cy=0):
        return ref[lead, self.x + margin + cx, pl.ds(8 + self.row + cy, 8), :]

    def store(self, ref, lead, margin, value):
        ref[lead, self.x + margin, pl.ds(8 + self.row, 8), :] = value


class Rim:
    def __init__(self, x, ext_y):
        self.x, self.ext_y = x, ext_y

    def load(self, ref, lead, margin, cx=0, cy=0):
        at = self.x + margin + cx
        upper = ref[lead, at, pl.ds(8 + self.ext_y - 1 + cy, 8), :]
        lower = ref[lead, at, pl.ds(1 + cy, 8), :]
        return jnp.where(lax.broadcasted_iota(jnp.int32, (8, LANES), 0) < 4, upper, lower)

    def store(self, ref, lead, margin, value):
        at = self.x + margin
        ref[lead, at, pl.ds(8 + self.ext_y - 1, 2), :] = value[0:2]
        ref[lead, at, pl.ds(7, 2), :] = value[6:8]


def first_step(first, fields, second, change, tiles, outside=True, shares=None):
    loaded = [
        (
            [tile.load(first, j, 2, *VELOCITIES[j][:2]) for j in range(19)],
            [tile.load(fields, k, 1) for k in range(5)],
        )
        for tile in tiles
    ]
    done = [
        collide(pulled, 1.0 / rho, rho, ux, uy, uz, kind > 1.5, range(19))
        for pulled, (rho, ux, uy, uz, kind) in loaded
    ]
    for tile, (_, here), (after, gain) in zip(tiles, loaded, done):
        inside = here[KIND] > 0.5
        side = None if shares is None else {-1: 0, second.shape[1] - 2: 1}.get(tile.x)
        for j in range(19):
            value = after[j]
            if side is not None and VELOCITIES[j][0] == 2 * side - 1:
                value = value + shares[side, pops(0, 2 * side - 1).index(j), pl.ds(8 + tile.row, 8), :]
            if outside:
                value = jnp.where(inside, value, 0.0)
            cz = VELOCITIES[j][2]
            tile.store(second, j, 1, pltpu.roll(value, -cz % LANES, 1) if cz else value)
        tile.store(change, 0, 1, gain)


def inner_kernel(den, vel, mask, first, fields, second, change):
    refs = (None, den, vel, mask)
    ext_x, ext_y, _ = mask.shape
    every = slice(None)
    for k in range(5):
        fields[k, 1 : 1 + ext_x, pl.ds(8, ext_y), :] = field_of(refs, "field", k, (every, every, every))

    many = 3 if (ext_x - 2) % 3 == 0 else 1

    @pl.loop(0, (ext_x - 2) // many)
    def _(group):
        tiles = [Plane(many * group + at + 1, 1 + 8 * part) for at in range(many) for part in range(ext_y // 8)]
        first_step(first, fields, second, change, tiles, outside=False)


def put_row(first, fields, kind, index, x, y, value):
    row = y + 8
    if kind == "pop":
        first[index, x + 2, row : row + 1, :] = value
    else:
        fields[index, x + 1, row : row + 1, :] = value


def place_z(z_first, value, start, size, side, ext_x):
    rows = pl.ds(start, size)
    spot = lane_ids()[:size] % GROUP
    inside = spot >= 2 + ext_x if side else spot < 2
    for tile in range(Z_TILES):
        shift = (2 + ext_x if side else 0) - 2 * tile
        moved = pltpu.roll(value, shift % LANES, 1)[:size]
        z_first[tile, rows, :] = jnp.where(inside, moved, z_first[tile, rows, :])


def side_kernel(slots, z_set, *rest):
    many_x, many_y = slots
    from_x, from_y = rest[4 : 4 + many_x], rest[4 + many_x : 4 + many_x + many_y]
    first, fields, second, change, z_first, shares = rest[-6:]
    _, ext_y, _ = z_set.shape
    ext_x = change.shape[1] - 2
    inner = pl.ds(8, ext_y)
    put = functools.partial(put_row, first, fields)
    z_first[:, inner, :] = z_set[...]

    def place_y(slot, side):
        packet = from_y[slot]
        for line, (kind, index, depth) in enumerate(face_lines(1, 2 * side - 1)):
            y = ext_y + depth if side else -1 - depth
            for x in range(ext_x):
                put(kind, index, x, y, packet[line, x : x + 1, :])
        start = 8 + ext_y if side else 6
        for tile in range(Z_TILES):
            row = 2 * tile % 8
            z_first[tile, start : start + 2, :] = packet[FACE + tile // 4, row : row + 2, :]
        if many_y == 1:
            clear_y(1 - side)

    def clear_y(side):
        nothing = jnp.zeros((1, LANES), jnp.float32)
        for kind, index, depth in face_lines(1, 2 * side - 1):
            y = ext_y + depth if side else -1 - depth
            for x in range(-1, ext_x + 1):
                put(kind, index, x, y, nothing)
            if kind == "pop":
                put(kind, index, -2, y, nothing)
                put(kind, index, ext_x + 1, y, nothing)
        start = 8 + ext_y if side else 6
        for tile in range(Z_TILES):
            z_first[tile, start : start + 2, :] = jnp.zeros((2, LANES), jnp.float32)

    def place_x(slot, side):
        packet = from_x[slot]
        toward = 2 * side - 1
        near = ext_x if side else -1
        nothing = jnp.zeros((ext_y, LANES), jnp.float32)
        for j in pops(0, 0):
            first[j, near + 2, inner, :] = nothing
        for j in pops(0, toward):
            first[j, near + toward + 2, inner, :] = nothing
        fields[RHO, near + 1, inner, :] = jnp.full((ext_y, LANES), jnp.inf, jnp.float32)
        full, ends = side_lines(toward)
        for line, (kind, index) in enumerate(full):
            if kind == "pop":
                first[index, near + 2, inner, :] = packet[line]
            elif kind == "share":
                shares[side, index, inner, :] = packet[line]
            else:
                fields[index, near + 1, inner, :] = packet[line]
        for spot, (index, depth, end) in enumerate(ends):
            put("pop", index, near + toward * depth, ext_y - 1 if end else 0, packet[SIDE - 1, spot : spot + 1, :])
        for part in range(ext_y // 8):
            place_z(z_first, packet[SIDE, pl.ds(8 * part, 8), :], 8 + 8 * part, 8, side, ext_x)

    shares[:, :, pl.ds(0, 8), :] = jnp.zeros((2, 5, 8, LANES), jnp.float32)
    shares[:, :, pl.ds(8 + ext_y, 8), :] = jnp.zeros((2, 5, 8, LANES), jnp.float32)
    for slot_y in range(many_y):
        on_side(parity_of("gy"), slot_y, functools.partial(place_y, slot_y))
    for slot_x in range(many_x):
        on_side(parity_of("gx"), slot_x, functools.partial(place_x, slot_x))

    rims = range(7, ext_y - 8, 8)
    first_step(first, fields, second, change, [Plane(x, row) for x in (0, ext_x - 1) for row in rims], outside=False)
    first_step(first, fields, second, change, [Plane(x, row) for x in (-1, ext_x) for row in rims], shares=shares)

    many = 3 if (ext_x - 2) % 3 == 0 else 1

    @pl.loop(0, (ext_x - 2) // many)
    def _(group):
        first_step(first, fields, second, change, [Rim(many * group + at + 1, ext_y) for at in range(many)])


def last_kernel(slots, den, vel, mask, *rest):
    many_x, many_y = slots
    from_xy = rest[6 : 6 + many_x * many_y]
    out, sens, first, fields, second, change, z_first, shares, z_second, held, held_sens, sems = rest[-12:]
    ext_x, ext_y, _ = mask.shape
    lane = lane_ids()
    every = slice(None)
    px, py = parity_of("gx"), parity_of("gy")

    def place_xy(slot_x, slot_y, side_x, side_y):
        packet = from_xy[many_x * slot_y + slot_x]
        for line, (kind, index, far_x, far_y) in enumerate(edge_lines(2 * side_x - 1, 2 * side_y - 1)):
            x = ext_x + far_x if side_x else -1 - far_x
            y = ext_y + far_y if side_y else -1 - far_y
            put_row(first, fields, kind, index, x, y, packet[line // 8, line % 8 : line % 8 + 1, :])
        place_z(z_first, packet[EDGE // 8], 8 + ext_y if side_y else 6, 2, side_x, ext_x)

    for slot_x in range(many_x):
        for slot_y in range(many_y):
            on_side(
                py,
                slot_y,
                lambda side_y: on_side(px, slot_x, lambda side_x: place_xy(slot_x, slot_y, side_x, side_y)),
            )

    for pair in ((-1, 0), (ext_x - 1, ext_x)):
        tiles = [Plane(x, row) for x in pair for row in (-1, ext_y - 1)]
        first_step(first, fields, second, change, tiles, shares=shares)

    starts = [7 + 8 * part for part in range((ext_y + 2 + 7) // 8)]
    loaded = []
    for row in starts:

        def both(low_tile, high_tile, group, cx, cy):
            rows = pl.ds(row + cy, 8)
            low = pltpu.roll(z_first[low_tile, rows, :], (-GROUP * group - cx) % LANES, 1)
            high = pltpu.roll(z_first[high_tile, rows, :], (LANES // 2 - GROUP * group - cx) % LANES, 1)
            return jnp.where(lane < LANES // 2, low, high)

        pulled = []
        for j in range(19):
            cx, cy, cz = VELOCITIES[j]
            if cz == 0:
                tile, group = Z_PLACE[("pop", j)]
                pulled.append(both(BELOW + tile, ABOVE + tile, group, cx, cy))
            elif cz == 1:
                pulled.append(both(OWN_LOW, ABOVE + 2, Z_UP.index(j), cx, cy))
            else:
                pulled.append(both(BELOW + 2, OWN_HIGH, Z_DOWN.index(j), cx, cy))
        places = [Z_PLACE[("field", k)] for k in range(5)]
        loaded.append((pulled, [both(BELOW + tile, ABOVE + tile, group, 0, 0) for tile, group in places]))
    done = [
        collide(pulled, 1.0 / rho, rho, ux, uy, uz, kind > 1.5, Z_UP + Z_DOWN)[0]
        for pulled, (rho, ux, uy, uz, kind) in loaded
    ]
    for row, (_, here), after in zip(starts, loaded, done):
        for group in range(5):
            value = jnp.where(lane < LANES // 2, after[Z_DOWN[group]], after[Z_UP[group]])
            z_second[group, pl.ds(row, 8), :] = jnp.where(here[KIND] > 0.5, value, 0.0)

    def copies(x):
        return (
            pltpu.make_async_copy(held.at[:, x], out.at[:, x], sems.at[0, x]),
            pltpu.make_async_copy(held_sens.at[x], sens.at[x], sems.at[1, x]),
        )

    many = 4 if ext_x % 4 == 0 else 1

    @pl.loop(0, ext_x // many)
    def _(group):
        loaded = []
        planes = [many * group + at for at in range(many)]
        for x, part in itertools.product(planes, range(ext_y // 8)):
            row = 8 + 8 * part
            pulled = []
            for j in range(19):
                cx, cy, cz = VELOCITIES[j]
                rows = pl.ds(row + cy, 8)
                value = second[j, x + 1 + cx, rows, :]
                if cz == 1:
                    edge = z_second[Z_UP.index(j), rows, :]
                    edge = pltpu.roll(edge, LANES // 2 - 3 - cx - x, 1)
                    value = jnp.where(lane == LANES - 1, edge, value)
                elif cz == -1:
                    edge = z_second[Z_DOWN.index(j), rows, :]
                    edge = pltpu.roll(edge, LANES - 2 - cx - x, 1)
                    value = jnp.where(lane == 0, edge, value)
                pulled.append(value)
            at = (x, pl.ds(8 * part, 8), every)
            rho = den[(0, *at)]
            here = [1.0 / rho, rho, vel[(0, 0, *at)], vel[(0, 1, *at)], vel[(0, 2, *at)], mask[at] > 0]
            loaded.append((at, pulled, here, change[0, x + 1, pl.ds(row, 8), :]))
        done = [collide(pulled, *here, range(19)) for _, pulled, here, _ in loaded]
        for (at, _, _, before), (after, gain) in zip(loaded, done):
            for j in range(19):
                held[(j, *at)] = after[j]
            held_sens[at] = before + gain
        for x in planes:
            for copy in copies(x):
                copy.start()

    for x in range(ext_x):
        for copy in copies(x):
            copy.wait()


def shards(adjoint, density, velocity, pore_mask):
    ext_x, ext_y, ext_z = pore_mask.shape
    assert ext_z == LANES and ext_y % 8 == 0 and ext_x + 4 <= GROUP and ext_x == 8
    many_x = 2
    many_y, many_z = [1 if lax.axis_size(axis) == 2 else 2 for axis in ("gy", "gz")]
    vmem = pl.BlockSpec(memory_space=pltpu.VMEM)
    hbm = pl.BlockSpec(memory_space=pltpu.HBM)
    inputs = (adjoint, density, velocity, pore_mask)

    def array(*shape):
        return jax.ShapeDtypeStruct(shape, jnp.float32)

    def call(kernel, name, operands, shapes, limit, **more):
        more.setdefault("out_specs", [vmem] * len(shapes))
        more.setdefault("in_specs", [vmem] * len(operands))
        params = pltpu.CompilerParams(vmem_limit_bytes=limit * 1024 * 1024)
        return pl.pallas_call(kernel, out_shape=shapes, compiler_params=params, name=name, **more)(*operands)

    def partners(axis, slot):
        found = {}
        for at in range(slot, lax.axis_size(axis) - 1, 2):
            found[at], found[at + 1] = at + 1, at
        return found

    def ends(axis):
        last = lax.axis_size(axis) - 1
        return {0: last, last: 0}

    def swap(value, spares, *places):
        tables = {axis: partners(axis, slot) for axis, slot in places}
        axes = [axis for axis in ("gx", "gy", "gz") if axis in tables or axis in dict(spares)]
        sizes = [lax.axis_size(axis) for axis in axes]
        pairs = []
        for at in itertools.product(*[range(size) for size in sizes]):
            to = [tables.get(axis, {}).get(spot, spot) for axis, spot in zip(axes, at)]
            for spare, table in spares:
                if tuple(to) == at:
                    to = [table.get(spot, spot) if axis == spare else spot for axis, spot in zip(axes, at)]
            flat = []
            for spots in (at, to):
                index = 0
                for size, spot in zip(sizes, spots):
                    index = index * size + spot
                flat.append(index)
            pairs.append(tuple(flat))
        return lax.ppermute(value, tuple(axes), pairs)

    loaded = [jax.ShapeDtypeStruct(value.shape, value.dtype) for value in inputs]
    *held, near, a_z, b_z = (
        *call(
            functools.partial(pack_z_kernel, many_z),
            "pack_z",
            [pltpu.with_memory_space_constraint(value, pltpu.HBM) for value in inputs],
            loaded + [array(2, ext_y, LANES)] + [array(3, ext_y, LANES)] * many_z,
            8,
            in_specs=[hbm] * 4,
            scratch_shapes=[pltpu.SemaphoreType.DMA((7,))],
        ),
        *[None] * (2 - many_z),
    )
    from_z = [swap(value, [("gx", partners("gx", 0))], ("gz", slot)) for slot, value in enumerate((a_z, b_z)[:many_z])]

    rows = ext_y + 16
    adj, den, vel, mask = held
    shapes = (
        [array(19, ext_x + 4, rows, LANES)]
        + [array(SIDE + 1, ext_y, LANES)] * many_x
        + [array(FACE + 2, ext_x, LANES)] * many_y
        + [array(EDGE // 8 + 1, 8, LANES)] * (many_x * many_y)
    )
    shifted = call(
        functools.partial(shift_kernel, (many_x, many_y)),
        "shift",
        (adj, den, vel, mask),
        shapes,
        8,
        cost_estimate=pl.CostEstimate(flops=1_000_000, bytes_accessed=2_500_000, transcendentals=0),
    )
    z_set, first, *packets = call(
        functools.partial(pack_xy_kernel, (many_x, many_y, many_z)),
        "pack_xy",
        (den, vel, mask, near, *from_z, *shifted),
        [array(Z_TILES, ext_y, LANES)] + shapes,
        8,
        input_output_aliases={4 + many_z + at: 1 + at for at in range(len(shapes))},
        scratch_shapes=[
            pltpu.VMEM((2, ext_y, LANES), jnp.float32),
            pltpu.VMEM((2, 5, ext_y, LANES), jnp.float32),
        ],
    )
    to_x, to_y, to_xy = packets[:many_x], packets[many_x : many_x + many_y], packets[many_x + many_y :]
    from_xy = [
        swap(to_xy[many_x * slot_y + slot_x], [], ("gx", slot_x), ("gy", slot_y))
        for slot_y in range(many_y)
        for slot_x in range(many_x)
    ]
    from_y = [swap(value, [("gz", partners("gz", 0))], ("gy", slot)) for slot, value in enumerate(to_y)]
    spares = [("gx", ends("gx"))]
    from_x = [swap(value, spares, ("gx", slot)) for slot, value in enumerate(to_x)]

    fields, second, change = call(
        inner_kernel,
        "inner_step",
        (den, vel, mask, first),
        [array(5, ext_x + 2, rows, LANES), array(19, ext_x + 2, rows, LANES), array(1, ext_x + 2, rows, LANES)],
        8,
        cost_estimate=pl.CostEstimate(flops=40_000_000, bytes_accessed=8_000_000, transcendentals=0),
    )
    inout = (first, fields, second, change)
    inout = call(
        functools.partial(side_kernel, (many_x, many_y)),
        "side_step",
        (z_set, *inout, *from_x, *from_y),
        [array(*value.shape) for value in inout] + [array(Z_TILES, rows, LANES), array(2, 5, rows, LANES)],
        8,
        input_output_aliases={1 + at: at for at in range(4)},
        cost_estimate=pl.CostEstimate(flops=40_000_000, bytes_accessed=8_000_000, transcendentals=0),
    )
    return call(
        functools.partial(last_kernel, (many_x, many_y)),
        "last_steps",
        (den, vel, mask, *inout, *from_xy),
        [array(19, ext_x, ext_y, LANES), array(ext_x, ext_y, LANES)] + [array(*value.shape) for value in inout],
        8,
        out_specs=[hbm] * 2 + [vmem] * 6,
        input_output_aliases={3 + at: 2 + at for at in range(6)},
        scratch_shapes=[
            pltpu.VMEM((5, rows, LANES), jnp.float32),
            pltpu.VMEM((19, ext_x, ext_y, LANES), jnp.float32),
            pltpu.VMEM((ext_x, ext_y, LANES), jnp.float32),
            pltpu.SemaphoreType.DMA((2, ext_x)),
        ],
    )[:2]


def solution(mesh):
    placed = (
        P(None, "gx", "gy", "gz"),
        P(None, "gx", "gy", "gz"),
        P(None, None, "gx", "gy", "gz"),
        P("gx", "gy", "gz"),
    )

    def whole(*arrays):
        return tuple(shards(*arrays))

    return jax.shard_map(
        whole,
        mesh=mesh,
        in_specs=placed,
        out_specs=(P(None, "gx", "gy", "gz"), P("gx", "gy", "gz")),
        check_vma=False,
    )
```

```python
import functools
import itertools

import jax
import jax.numpy as jnp
from jax import lax
from jax.experimental import pallas as pl
from jax.experimental.pallas import tpu as pltpu
from jax.sharding import PartitionSpec as P

VELOCITIES = [
    (0, 0, 0),
    (1, 0, 0),
    (-1, 0, 0),
    (0, 1, 0),
    (0, -1, 0),
    (0, 0, 1),
    (0, 0, -1),
    (1, 1, 0),
    (-1, -1, 0),
    (1, -1, 0),
    (-1, 1, 0),
    (1, 0, 1),
    (-1, 0, -1),
    (1, 0, -1),
    (-1, 0, 1),
    (0, 1, 1),
    (0, -1, -1),
    (0, 1, -1),
    (0, -1, 1),
]
OPPOSITE = [0, 2, 1, 4, 3, 6, 5, 8, 7, 10, 9, 12, 11, 14, 13, 16, 15, 18, 17]
OMEGA = 1.25
LANES = 128
GROUP = 16


def pops(axis, sign):
    return [j for j in range(19) if VELOCITIES[j][axis] == sign]


def mirrored(j):
    cx, cy, cz = VELOCITIES[j]
    return VELOCITIES.index((cx, cy, -cz))


Z_FLAT = pops(2, 0)
Z_UP = pops(2, 1)
Z_DOWN = [mirrored(j) for j in Z_UP]
RHO, UX, UY, UZ, KIND = range(5)
Z_PLACE = {("pop", j): (0, g) for g, j in enumerate(Z_FLAT[:8])}
Z_PLACE[("pop", Z_FLAT[8])] = (1, 5)
Z_PLACE[("field", RHO)] = (1, 6)
Z_PLACE[("field", KIND)] = (1, 7)
Z_PLACE[("field", UX)] = (2, 5)
Z_PLACE[("field", UY)] = (2, 6)
Z_PLACE[("field", UZ)] = (2, 7)
BELOW, ABOVE, OWN_LOW, OWN_HIGH, Z_TILES = 0, 3, 6, 7, 8


def face_lines(axis, toward):
    near = pops(axis, 0) + pops(axis, toward)
    lines = [("pop", j, 0) for j in near] + [("field", k, 0) for k in range(5)]
    return lines + [("pop", j, 1) for j in pops(axis, toward)]


def edge_lines(toward_x, toward_y):
    lines = [("field", k, 0, 0) for k in range(5)]
    for j in range(19):
        cx, cy, _ = VELOCITIES[j]
        if cx not in (0, toward_x) or cy not in (0, toward_y):
            continue
        lines.append(("pop", j, 0, 0))
        if cx:
            lines.append(("pop", j, 1, 0))
        if cy:
            lines.append(("pop", j, 0, 1))
        if cx and cy:
            lines.append(("pop", j, 1, 1))
    return lines


FACE = 24
EDGE = 24
SIDE = 15


def side_lines(toward):
    full = [("pop", j) for j in pops(0, toward)] + [("share", p) for p in range(5)]
    full += [("field", k) for k in (UX, UY, UZ, KIND)]
    ends = []
    for end in range(2):
        for j in pops(1, 1 - 2 * end):
            cx = VELOCITIES[j][0]
            if cx in (0, toward):
                ends.append((j, abs(cx), end))
    return full, ends


def lane_ids():
    return lax.broadcasted_iota(jnp.int32, (8, LANES), 1)


def field_of(refs, kind, index, at):
    adj, den, vel, mask = refs
    if kind == "pop":
        return adj[(index, *at)]
    if index == RHO:
        return den[(1, *at)]
    if index == KIND:
        return (mask[at] + 1).astype(jnp.float32)
    return vel[(1, index - UX, *at)]


def parity_of(axis):
    return lax.rem(lax.axis_index(axis), 2)


def on_side(parity, slot, act):
    @pl.when(parity == slot)
    def _():
        act(1)

    @pl.when(parity != slot)
    def _():
        act(0)


def has_partner(axis, slot):
    at = lax.axis_index(axis)
    to = at + jnp.where(lax.rem(at, 2) == slot, 1, -1)
    return (to >= 0) & (to < lax.axis_size(axis))


def pack_z_kernel(slots, adj_in, den_in, vel_in, mask_in, adj, den, vel, mask, near, *rest):
    packets, sems = rest[:slots], rest[slots]
    refs = (adj, den, vel, mask)
    ext_x, ext_y, _ = mask.shape
    starts = range(0, 19, 5)
    loads = [
        pltpu.make_async_copy(adj_in.at[start : min(start + 5, 19)], adj.at[start : min(start + 5, 19)], sems.at[at])
        for at, start in enumerate(starts)
    ] + [
        pltpu.make_async_copy(source, target, sems.at[len(starts) + at])
        for at, (source, target) in enumerate([(den_in, den), (vel_in, vel), (mask_in, mask)])
    ]
    for load in loads:
        load.start()
    lane = lane_ids()
    parity = parity_of("gz")
    parts = range(ext_y // 8)
    zero = jnp.zeros((8, LANES), jnp.float32)
    lows, highs = [[zero] * 3 for _ in parts], [[zero] * 3 for _ in parts]
    far_low, far_high = [zero for _ in parts], [zero for _ in parts]

    def gather(kind, index):
        for x, part in itertools.product(range(ext_x), parts):
            value = field_of(refs, kind, index, (x, pl.ds(8 * part, 8), slice(None)))
            if kind == "pop" and VELOCITIES[index][2] == 1:
                spot = GROUP * Z_UP.index(index) + 2 + x
                moved = pltpu.roll(value, spot, 1)
                lows[part][1] = jnp.where(lane == spot, moved, lows[part][1])
                far_low[part] = jnp.where(lane == spot + 1, moved, far_low[part])
            elif kind == "pop" and VELOCITIES[index][2] == -1:
                spot = GROUP * Z_DOWN.index(index) + 2 + x
                moved = pltpu.roll(value, spot, 1)
                highs[part][1] = jnp.where(lane == spot - 1, moved, highs[part][1])
                far_high[part] = jnp.where(lane == spot - 2, moved, far_high[part])
            else:
                tile, group = Z_PLACE[(kind, index)]
                spot = GROUP * group + 2 + x
                moved = pltpu.roll(value, spot, 1)
                lows[part][tile] = jnp.where(lane == spot, moved, lows[part][tile])
                highs[part][tile] = jnp.where(lane == spot - 1, moved, highs[part][tile])

    for start, load in zip(starts, loads):
        load.wait()
        for j in range(start, min(start + 5, 19)):
            gather("pop", j)
    for load in loads[len(starts) :]:
        load.wait()
    for k in range(5):
        gather("field", k)
    for part in parts:
        rows = pl.ds(8 * part, 8)
        low = lows[part]
        high = [pltpu.roll(tile, 1, 1) for tile in highs[part]]
        low[2] = jnp.where(lane < 5 * GROUP, pltpu.roll(far_low[part], LANES - 1, 1), low[2])
        high[2] = jnp.where(lane < 5 * GROUP, pltpu.roll(far_high[part], 2, 1), high[2])
        near[0, rows, :] = low[1]
        near[1, rows, :] = high[1]
        for slot in range(slots):
            there = has_partner("gz", slot)
            for tile in range(3):
                value = jnp.where(parity == slot, high[tile], low[tile])
                packets[slot][tile, rows, :] = jnp.where(there, value, 0.0)


def pack_lines(refs, first, packets, many_x, many_y, wanted, shares):
    to_x, to_y = packets[:many_x], packets[many_x : many_x + many_y]
    to_xy = packets[many_x + many_y :]
    ext_x, ext_y, _ = refs[-1].shape
    every = slice(None)
    px, py = parity_of("gx"), parity_of("gy")

    def line_of(kind, index, x, y):
        if kind == "pop":
            return first[index, x + 2, y + 8 : y + 9, :]
        return field_of(refs, kind, index, (x, slice(y, y + 1), every))

    def pack_xy(slot_x, slot_y, side_x, side_y):
        packet = to_xy[many_x * slot_y + slot_x]
        for line, (kind, index, far_x, far_y) in enumerate(edge_lines(1 - 2 * side_x, 1 - 2 * side_y)):
            if wanted(kind, index):
                x = ext_x - 1 - far_x if side_x else far_x
                y = ext_y - 1 - far_y if side_y else far_y
                packet[line // 8, line % 8 : line % 8 + 1, :] = line_of(kind, index, x, y)

    def pack_y(slot, side):
        for line, (kind, index, depth) in enumerate(face_lines(1, 1 - 2 * side)):
            if wanted(kind, index):
                y = ext_y - 1 - depth if side else depth
                for x in range(ext_x):
                    to_y[slot][line, x : x + 1, :] = line_of(kind, index, x, y)

    def pack_x(slot, side):
        full, ends = side_lines(1 - 2 * side)
        for line, (kind, index) in enumerate(full):
            if kind == "field" and wanted(kind, index):
                to_x[slot][line] = field_of(refs, kind, index, (ext_x - 1 if side else 0, every, every))
            elif kind == "pop" and wanted(kind, index):
                to_x[slot][line] = first[index, (ext_x - 1 if side else 0) + 2, pl.ds(8, ext_y), :]
            elif kind == "share" and shares is not None:
                to_x[slot][line] = shares[side, index]
        for spot, (index, depth, end) in enumerate(ends):
            if wanted("pop", index):
                x = ext_x - 1 - depth if side else depth
                to_x[slot][SIDE - 1, spot : spot + 1, :] = line_of("pop", index, x, ext_y - 1 if end else 0)

    def when_there(there, packet, act):
        pl.when(there)(act)
        if shares is None:

            @pl.when(jnp.logical_not(there))
            def _():
                packet[...] = jnp.zeros(packet.shape, jnp.float32)

    for slot_y in range(many_y):
        there_y = has_partner("gy", slot_y)
        when_there(there_y, to_y[slot_y], lambda: on_side(py, slot_y, functools.partial(pack_y, slot_y)))
        for slot_x in range(many_x):
            when_there(
                there_y & has_partner("gx", slot_x),
                to_xy[many_x * slot_y + slot_x],
                lambda: on_side(
                    py,
                    slot_y,
                    lambda side_y: on_side(px, slot_x, lambda side_x: pack_xy(slot_x, slot_y, side_x, side_y)),
                ),
            )
    for slot_x in range(many_x):
        when_there(
            has_partner("gx", slot_x), to_x[slot_x], lambda: on_side(px, slot_x, functools.partial(pack_x, slot_x))
        )


def is_flat(kind, index):
    return kind == "field" or VELOCITIES[index][2] == 0


def shift_kernel(slots, adj, den, vel, mask, first, *packets):
    many_x, many_y = slots
    _, ext_x, ext_y, _ = adj.shape
    for j in range(19):
        cz = VELOCITIES[j][2]
        for x, part in itertools.product(range(ext_x), range(ext_y // 8)):
            value = adj[j, x, pl.ds(8 * part, 8), :]
            first[j, 2 + x, pl.ds(8 + 8 * part, 8), :] = pltpu.roll(value, -cz % LANES, 1) if cz else value
    pack_lines((None, den, vel, mask), first, packets, many_x, many_y, is_flat, None)


def pack_xy_kernel(slots, den, vel, mask, near, *rest):
    many_x, many_y, many_z = slots
    count = many_x + many_y + many_x * many_y
    from_z, rest = rest[:many_z], rest[many_z + 1 + count :]
    z_set, first, packets, faces, shares = rest[0], rest[1], rest[2:-2], rest[-2], rest[-1]
    to_x, to_y, to_xy = packets[:many_x], packets[many_x : many_x + many_y], packets[many_x + many_y :]
    ext_x, ext_y = first.shape[1] - 4, near.shape[1]
    spot = lane_ids() % GROUP
    px, py, pz = parity_of("gx"), parity_of("gy"), parity_of("gz")

    z_set[OWN_LOW] = near[0]
    z_set[OWN_HIGH] = near[1]
    for tile in range(3):
        even = from_z[0][tile]
        odd = from_z[1][tile] if many_z > 1 else jnp.zeros_like(even)
        z_set[ABOVE + tile] = jnp.where(pz == 0, even, odd)
        z_set[BELOW + tile] = jnp.where(pz == 0, odd, even)

    for j in Z_UP + Z_DOWN:
        up = VELOCITIES[j][2] > 0
        group = (Z_UP if up else Z_DOWN).index(j)
        last = LANES - 1 if up else 0
        for part in range(ext_y // 8):
            halo = z_set[(ABOVE if up else BELOW) + 1, pl.ds(8 * part, 8), :]
            for x in range(ext_x):
                edge = pltpu.roll(halo, (last - 2 - GROUP * group - x) % LANES, 1)
                first[j, 2 + x, pl.ds(8 + 8 * part, 8), last : last + 1] = edge[:, last : last + 1]


    sub = lax.broadcasted_iota(jnp.int32, (8, LANES), 0)
    loaded = []
    for side, part in itertools.product(range(2), range(ext_y // 8)):
        toward, x = 1 - 2 * side, ext_x - 1 if side else 0
        pulled = []
        for j in range(19):
            cx, cy, _ = VELOCITIES[j]
            if cx == -toward:
                pulled.append(jnp.zeros((8, LANES), jnp.float32))
                continue
            value = first[j, x + 2 + cx, pl.ds(8 + 8 * part + cy, 8), :]
            if cy == -1 and part == 0:
                value = jnp.where(sub == 0, 0.0, value)
            if cy == 1 and part == ext_y // 8 - 1:
                value = jnp.where(sub == 7, 0.0, value)
            pulled.append(value)
        at = (x, pl.ds(8 * part, 8), slice(None))
        here = [den[(1, *at)], vel[(1, 0, *at)], vel[(1, 1, *at)], vel[(1, 2, *at)], mask[at] > 0]
        loaded.append((side, part, pulled, here))
    for side, part, pulled, (rho, ux, uy, uz, fluid) in loaded:
        wanted = pops(0, 1 - 2 * side)
        after, _ = collide(pulled, 1.0 / rho, rho, ux, uy, uz, None, wanted)
        for line, j in enumerate(wanted):
            shares[side, line, pl.ds(8 * part, 8), :] = jnp.where(fluid, after[j], 0.0)

    pack_lines((mask,), first, packets, many_x, many_y, lambda kind, index: not is_flat(kind, index), shares)

    for side in range(2):
        for part in range(ext_y // 8):
            rows = pl.ds(8 * part, 8)
            value = jnp.zeros((8, LANES), jnp.float32)
            for tile in range(Z_TILES):
                start = ext_x if side else 2
                moved = pltpu.roll(z_set[tile, rows, :], (2 * tile - start) % LANES, 1)
                value = jnp.where(spot // 2 == tile, moved, value)
            faces[side, rows, :] = value

    def add_xy(slot_x, slot_y, side_x, side_y):
        start = ext_y - 2 if side_y else 0
        to_xy[many_x * slot_y + slot_x][EDGE // 8, 0:2, :] = faces[side_x, start : start + 2, :]

    def add_y(slot, side):
        start = ext_y - 2 if side else 0
        for tile in range(Z_TILES):
            row = 2 * tile % 8
            to_y[slot][FACE + tile // 4, row : row + 2, :] = z_set[tile, start : start + 2, :]

    def add_x(slot, side):
        to_x[slot][SIDE] = faces[side]

    for slot_y in range(many_y):
        there_y = has_partner("gy", slot_y)
        pl.when(there_y)(lambda: on_side(py, slot_y, functools.partial(add_y, slot_y)))
        for slot_x in range(many_x):
            pl.when(there_y & has_partner("gx", slot_x))(
                lambda: on_side(
                    py,
                    slot_y,
                    lambda side_y: on_side(px, slot_x, lambda side_x: add_xy(slot_x, slot_y, side_x, side_y)),
                )
            )
    for slot_x in range(many_x):
        pl.when(has_partner("gx", slot_x))(lambda: on_side(px, slot_x, functools.partial(add_x, slot_x)))


def collide(pulled, inverse, rho, ux, uy, uz, fluid, wanted):
    total = {}
    diff = {}
    for j in range(1, 19, 2):
        total[j] = pulled[j] + pulled[j + 1]
        diff[j] = pulled[j] - pulled[j + 1]
    in_xy, in_xz, in_yz = total[7] + total[9], total[11] + total[13], total[15] + total[17]
    two_x, two_y, two_z = total[1] + total[1], total[3] + total[3], total[5] + total[5]
    count = (12.0 * pulled[0] + (two_x + two_y)) + (two_z + (in_xy + (in_xz + in_yz)))
    flow_x = (diff[1] + diff[1]) + ((diff[7] + diff[9]) + (diff[11] + diff[13]))
    flow_y = (diff[3] + diff[3]) + ((diff[7] - diff[9]) + (diff[15] + diff[17]))
    flow_z = (diff[5] + diff[5]) + ((diff[11] - diff[13]) + (diff[15] - diff[17]))
    xx, yy, zz = two_x + (in_xy + in_xz), two_y + (in_xy + in_yz), two_z + (in_xz + in_yz)
    xy, xz, yz = total[7] - total[9], total[11] - total[13], total[15] - total[17]
    push_x = xx * ux + xy * uy + xz * uz
    push_y = xy * ux + yy * uy + yz * uz
    push_z = xz * ux + yz * uy + zz * uz
    usq = ux * ux + uy * uy + uz * uz
    push = ux * push_x + uy * push_y + uz * push_z
    base = count * (OMEGA / 36.0 + (OMEGA / 24.0) * usq) - (OMEGA / 8.0) * push - ux * inverse
    along_x = (OMEGA / 12.0) * (flow_x + 3.0 * push_x - ux * count) + inverse
    along_y = (OMEGA / 12.0) * (flow_y + 3.0 * push_y - uy * count)
    along_z = (OMEGA / 12.0) * (flow_z + 3.0 * push_z - uz * count)
    parts = {
        1: along_x,
        3: along_y,
        5: along_z,
        7: along_x + along_y,
        9: along_x - along_y,
        11: along_x + along_z,
        13: along_x - along_z,
        15: along_y + along_z,
        17: along_y - along_z,
    }
    out = {}
    for j in wanted:
        if j == 0:
            shift = base
        elif j % 2:
            shift = base + parts[j]
        else:
            shift = base - parts[j - 1]
        out[j] = (1.0 - OMEGA) * pulled[j] + shift
        if fluid is not None:
            out[j] = jnp.where(fluid, out[j], pulled[OPPOSITE[j]])
    change = (-1.0 / 6.0) * rho * (flow_x * ux + flow_y * uy + flow_z * uz)
    return out, change if fluid is None else jnp.where(fluid, change, 0.0)


class Plane:
    def __init__(self, x, row):
        self.x, self.row = x, row

    def load(self, ref, lead, margin, cx=0, cy=0):
        return ref[lead, self.x + margin + cx, pl.ds(8 + self.row + cy, 8), :]

    def store(self, ref, lead, margin, value):
        ref[lead, self.x + margin, pl.ds(8 + self.row, 8), :] = value


class Rim:
    def __init__(self, x, ext_y):
        self.x, self.ext_y = x, ext_y

    def load(self, ref, lead, margin, cx=0, cy=0):
        at = self.x + margin + cx
        upper = ref[lead, at, pl.ds(8 + self.ext_y - 1 + cy, 8), :]
        lower = ref[lead, at, pl.ds(1 + cy, 8), :]
        return jnp.where(lax.broadcasted_iota(jnp.int32, (8, LANES), 0) < 4, upper, lower)

    def store(self, ref, lead, margin, value):
        at = self.x + margin
        ref[lead, at, pl.ds(8 + self.ext_y - 1, 2), :] = value[0:2]
        ref[lead, at, pl.ds(7, 2), :] = value[6:8]


def first_step(first, fields, second, change, tiles, outside=True, shares=None):
    loaded = [
        (
            [tile.load(first, j, 2, *VELOCITIES[j][:2]) for j in range(19)],
            [tile.load(fields, k, 1) for k in range(5)],
        )
        for tile in tiles
    ]
    done = [
        collide(pulled, 1.0 / rho, rho, ux, uy, uz, kind > 1.5, range(19))
        for pulled, (rho, ux, uy, uz, kind) in loaded
    ]
    for tile, (_, here), (after, gain) in zip(tiles, loaded, done):
        inside = here[KIND] > 0.5
        side = None if shares is None else {-1: 0, second.shape[1] - 2: 1}.get(tile.x)
        for j in range(19):
            value = after[j]
            if side is not None and VELOCITIES[j][0] == 2 * side - 1:
                value = value + shares[side, pops(0, 2 * side - 1).index(j), pl.ds(8 + tile.row, 8), :]
            if outside:
                value = jnp.where(inside, value, 0.0)
            cz = VELOCITIES[j][2]
            tile.store(second, j, 1, pltpu.roll(value, -cz % LANES, 1) if cz else value)
        tile.store(change, 0, 1, gain)


def inner_kernel(den, vel, mask, first, fields, second, change):
    refs = (None, den, vel, mask)
    ext_x, ext_y, _ = mask.shape
    every = slice(None)
    for k in range(5):
        fields[k, 1 : 1 + ext_x, pl.ds(8, ext_y), :] = field_of(refs, "field", k, (every, every, every))

    many = 3 if (ext_x - 2) % 3 == 0 else 1

    @pl.loop(0, (ext_x - 2) // many)
    def _(group):
        tiles = [Plane(many * group + at + 1, 1 + 8 * part) for at in range(many) for part in range(ext_y // 8)]
        first_step(first, fields, second, change, tiles, outside=False)


def put_row(first, fields, kind, index, x, y, value):
    row = y + 8
    if kind == "pop":
        first[index, x + 2, row : row + 1, :] = value
    else:
        fields[index, x + 1, row : row + 1, :] = value


def place_z(z_first, value, start, size, side, ext_x):
    rows = pl.ds(start, size)
    spot = lane_ids()[:size] % GROUP
    inside = spot >= 2 + ext_x if side else spot < 2
    for tile in range(Z_TILES):
        shift = (2 + ext_x if side else 0) - 2 * tile
        moved = pltpu.roll(value, shift % LANES, 1)[:size]
        z_first[tile, rows, :] = jnp.where(inside, moved, z_first[tile, rows, :])


def side_kernel(slots, z_set, *rest):
    many_x, many_y = slots
    from_x, from_y = rest[4 : 4 + many_x], rest[4 + many_x : 4 + many_x + many_y]
    first, fields, second, change, z_first, shares = rest[-6:]
    _, ext_y, _ = z_set.shape
    ext_x = change.shape[1] - 2
    inner = pl.ds(8, ext_y)
    put = functools.partial(put_row, first, fields)
    z_first[:, inner, :] = z_set[...]

    def place_y(slot, side):
        packet = from_y[slot]
        for line, (kind, index, depth) in enumerate(face_lines(1, 2 * side - 1)):
            y = ext_y + depth if side else -1 - depth
            for x in range(ext_x):
                put(kind, index, x, y, packet[line, x : x + 1, :])
        start = 8 + ext_y if side else 6
        for tile in range(Z_TILES):
            row = 2 * tile % 8
            z_first[tile, start : start + 2, :] = packet[FACE + tile // 4, row : row + 2, :]
        if many_y == 1:
            clear_y(1 - side)

    def clear_y(side):
        nothing = jnp.zeros((1, LANES), jnp.float32)
        for kind, index, depth in face_lines(1, 2 * side - 1):
            y = ext_y + depth if side else -1 - depth
            for x in range(-1, ext_x + 1):
                put(kind, index, x, y, nothing)
            if kind == "pop":
                put(kind, index, -2, y, nothing)
                put(kind, index, ext_x + 1, y, nothing)
        start = 8 + ext_y if side else 6
        for tile in range(Z_TILES):
            z_first[tile, start : start + 2, :] = jnp.zeros((2, LANES), jnp.float32)

    def place_x(slot, side):
        packet = from_x[slot]
        toward = 2 * side - 1
        near = ext_x if side else -1
        nothing = jnp.zeros((ext_y, LANES), jnp.float32)
        for j in pops(0, 0):
            first[j, near + 2, inner, :] = nothing
        for j in pops(0, toward):
            first[j, near + toward + 2, inner, :] = nothing
        fields[RHO, near + 1, inner, :] = jnp.full((ext_y, LANES), jnp.inf, jnp.float32)
        full, ends = side_lines(toward)
        for line, (kind, index) in enumerate(full):
            if kind == "pop":
                first[index, near + 2, inner, :] = packet[line]
            elif kind == "share":
                shares[side, index, inner, :] = packet[line]
            else:
                fields[index, near + 1, inner, :] = packet[line]
        for spot, (index, depth, end) in enumerate(ends):
            put("pop", index, near + toward * depth, ext_y - 1 if end else 0, packet[SIDE - 1, spot : spot + 1, :])
        for part in range(ext_y // 8):
            place_z(z_first, packet[SIDE, pl.ds(8 * part, 8), :], 8 + 8 * part, 8, side, ext_x)

    shares[:, :, pl.ds(0, 8), :] = jnp.zeros((2, 5, 8, LANES), jnp.float32)
    shares[:, :, pl.ds(8 + ext_y, 8), :] = jnp.zeros((2, 5, 8, LANES), jnp.float32)
    for slot_y in range(many_y):
        on_side(parity_of("gy"), slot_y, functools.partial(place_y, slot_y))
    for slot_x in range(many_x):
        on_side(parity_of("gx"), slot_x, functools.partial(place_x, slot_x))

    rims = range(7, ext_y - 8, 8)
    first_step(first, fields, second, change, [Plane(x, row) for x in (0, ext_x - 1) for row in rims], outside=False)
    first_step(first, fields, second, change, [Plane(x, row) for x in (-1, ext_x) for row in rims], shares=shares)

    many = 3 if (ext_x - 2) % 3 == 0 else 1

    @pl.loop(0, (ext_x - 2) // many)
    def _(group):
        first_step(first, fields, second, change, [Rim(many * group + at + 1, ext_y) for at in range(many)])


def last_kernel(slots, den, vel, mask, *rest):
    many_x, many_y = slots
    from_xy = rest[6 : 6 + many_x * many_y]
    out, sens, first, fields, second, change, z_first, shares, z_second, held, held_sens, sems = rest[-12:]
    ext_x, ext_y, _ = mask.shape
    lane = lane_ids()
    every = slice(None)
    px, py = parity_of("gx"), parity_of("gy")

    def place_xy(slot_x, slot_y, side_x, side_y):
        packet = from_xy[many_x * slot_y + slot_x]
        for line, (kind, index, far_x, far_y) in enumerate(edge_lines(2 * side_x - 1, 2 * side_y - 1)):
            x = ext_x + far_x if side_x else -1 - far_x
            y = ext_y + far_y if side_y else -1 - far_y
            put_row(first, fields, kind, index, x, y, packet[line // 8, line % 8 : line % 8 + 1, :])
        place_z(z_first, packet[EDGE // 8], 8 + ext_y if side_y else 6, 2, side_x, ext_x)

    for slot_x in range(many_x):
        for slot_y in range(many_y):
            on_side(
                py,
                slot_y,
                lambda side_y: on_side(px, slot_x, lambda side_x: place_xy(slot_x, slot_y, side_x, side_y)),
            )

    for pair in ((-1, 0), (ext_x - 1, ext_x)):
        tiles = [Plane(x, row) for x in pair for row in (-1, ext_y - 1)]
        first_step(first, fields, second, change, tiles, shares=shares)

    starts = [7 + 8 * part for part in range((ext_y + 2 + 7) // 8)]
    loaded = []
    for row in starts:

        def both(low_tile, high_tile, group, cx, cy):
            rows = pl.ds(row + cy, 8)
            low = pltpu.roll(z_first[low_tile, rows, :], (-GROUP * group - cx) % LANES, 1)
            high = pltpu.roll(z_first[high_tile, rows, :], (LANES // 2 - GROUP * group - cx) % LANES, 1)
            return jnp.where(lane < LANES // 2, low, high)

        pulled = []
        for j in range(19):
            cx, cy, cz = VELOCITIES[j]
            if cz == 0:
                tile, group = Z_PLACE[("pop", j)]
                pulled.append(both(BELOW + tile, ABOVE + tile, group, cx, cy))
            elif cz == 1:
                pulled.append(both(OWN_LOW, ABOVE + 2, Z_UP.index(j), cx, cy))
            else:
                pulled.append(both(BELOW + 2, OWN_HIGH, Z_DOWN.index(j), cx, cy))
        places = [Z_PLACE[("field", k)] for k in range(5)]
        loaded.append((pulled, [both(BELOW + tile, ABOVE + tile, group, 0, 0) for tile, group in places]))
    done = [
        collide(pulled, 1.0 / rho, rho, ux, uy, uz, kind > 1.5, Z_UP + Z_DOWN)[0]
        for pulled, (rho, ux, uy, uz, kind) in loaded
    ]
    for row, (_, here), after in zip(starts, loaded, done):
        for group in range(5):
            value = jnp.where(lane < LANES // 2, after[Z_DOWN[group]], after[Z_UP[group]])
            z_second[group, pl.ds(row, 8), :] = jnp.where(here[KIND] > 0.5, value, 0.0)

    def copies(x):
        return (
            pltpu.make_async_copy(held.at[:, x], out.at[:, x], sems.at[0, x]),
            pltpu.make_async_copy(held_sens.at[x], sens.at[x], sems.at[1, x]),
        )

    many = 4 if ext_x % 4 == 0 else 1

    @pl.loop(0, ext_x // many)
    def _(group):
        loaded = []
        planes = [many * group + at for at in range(many)]
        for x, part in itertools.product(planes, range(ext_y // 8)):
            row = 8 + 8 * part
            pulled = []
            for j in range(19):
                cx, cy, cz = VELOCITIES[j]
                rows = pl.ds(row + cy, 8)
                value = second[j, x + 1 + cx, rows, :]
                if cz == 1:
                    edge = z_second[Z_UP.index(j), rows, :]
                    edge = pltpu.roll(edge, LANES // 2 - 3 - cx - x, 1)
                    value = jnp.where(lane == LANES - 1, edge, value)
                elif cz == -1:
                    edge = z_second[Z_DOWN.index(j), rows, :]
                    edge = pltpu.roll(edge, LANES - 2 - cx - x, 1)
                    value = jnp.where(lane == 0, edge, value)
                pulled.append(value)
            at = (x, pl.ds(8 * part, 8), every)
            rho = den[(0, *at)]
            here = [1.0 / rho, rho, vel[(0, 0, *at)], vel[(0, 1, *at)], vel[(0, 2, *at)], mask[at] > 0]
            loaded.append((at, pulled, here, change[0, x + 1, pl.ds(row, 8), :]))
        done = [collide(pulled, *here, range(19)) for _, pulled, here, _ in loaded]
        for (at, _, _, before), (after, gain) in zip(loaded, done):
            for j in range(19):
                held[(j, *at)] = after[j]
            held_sens[at] = before + gain
        for x in planes:
            for copy in copies(x):
                copy.start()

    for x in range(ext_x):
        for copy in copies(x):
            copy.wait()


def shards(adjoint, density, velocity, pore_mask):
    ext_x, ext_y, ext_z = pore_mask.shape
    assert ext_z == LANES and ext_y % 8 == 0 and ext_x + 4 <= GROUP and ext_x == 8
    many_x = 2
    many_y, many_z = [1 if lax.axis_size(axis) == 2 else 2 for axis in ("gy", "gz")]
    vmem = pl.BlockSpec(memory_space=pltpu.VMEM)
    hbm = pl.BlockSpec(memory_space=pltpu.HBM)
    inputs = (adjoint, density, velocity, pore_mask)

    def array(*shape):
        return jax.ShapeDtypeStruct(shape, jnp.float32)

    def call(kernel, name, operands, shapes, limit, **more):
        more.setdefault("out_specs", [vmem] * len(shapes))
        more.setdefault("in_specs", [vmem] * len(operands))
        params = pltpu.CompilerParams(vmem_limit_bytes=limit * 1024 * 1024)
        return pl.pallas_call(kernel, out_shape=shapes, compiler_params=params, name=name, **more)(*operands)

    def partners(axis, slot):
        found = {}
        for at in range(slot, lax.axis_size(axis) - 1, 2):
            found[at], found[at + 1] = at + 1, at
        return found

    def ends(axis):
        last = lax.axis_size(axis) - 1
        return {0: last, last: 0}

    def swap(value, spares, *places):
        tables = {axis: partners(axis, slot) for axis, slot in places}
        axes = [axis for axis in ("gx", "gy", "gz") if axis in tables or axis in dict(spares)]
        sizes = [lax.axis_size(axis) for axis in axes]
        pairs = []
        for at in itertools.product(*[range(size) for size in sizes]):
            to = [tables.get(axis, {}).get(spot, spot) for axis, spot in zip(axes, at)]
            for spare, table in spares:
                if tuple(to) == at:
                    to = [table.get(spot, spot) if axis == spare else spot for axis, spot in zip(axes, at)]
            flat = []
            for spots in (at, to):
                index = 0
                for size, spot in zip(sizes, spots):
                    index = index * size + spot
                flat.append(index)
            pairs.append(tuple(flat))
        return lax.ppermute(value, tuple(axes), pairs)

    loaded = [jax.ShapeDtypeStruct(value.shape, value.dtype) for value in inputs]
    *held, near, a_z, b_z = (
        *call(
            functools.partial(pack_z_kernel, many_z),
            "pack_z",
            [pltpu.with_memory_space_constraint(value, pltpu.HBM) for value in inputs],
            loaded + [array(2, ext_y, LANES)] + [array(3, ext_y, LANES)] * many_z,
            8,
            in_specs=[hbm] * 4,
            scratch_shapes=[pltpu.SemaphoreType.DMA((7,))],
        ),
        *[None] * (2 - many_z),
    )
    from_z = [swap(value, [("gx", partners("gx", 0))], ("gz", slot)) for slot, value in enumerate((a_z, b_z)[:many_z])]

    rows = ext_y + 16
    adj, den, vel, mask = held
    y_tiles = max(FACE + 2, (SIDE + 1) * ext_y // ext_x + 1)
    shapes = (
        [array(19, ext_x + 4, rows, LANES)]
        + [array(SIDE + 1, ext_y, LANES)] * many_x
        + [array(y_tiles, ext_x, LANES)] * many_y
        + [array(EDGE // 8 + 1, 8, LANES)] * (many_x * many_y)
    )
    shifted = call(
        functools.partial(shift_kernel, (many_x, many_y)),
        "shift",
        (adj, den, vel, mask),
        shapes,
        8,
        cost_estimate=pl.CostEstimate(flops=1_000_000, bytes_accessed=2_500_000, transcendentals=0),
    )
    z_set, first, *packets = call(
        functools.partial(pack_xy_kernel, (many_x, many_y, many_z)),
        "pack_xy",
        (den, vel, mask, near, *from_z, *shifted),
        [array(Z_TILES, ext_y, LANES)] + shapes,
        8,
        input_output_aliases={4 + many_z + at: 1 + at for at in range(len(shapes))},
        scratch_shapes=[
            pltpu.VMEM((2, ext_y, LANES), jnp.float32),
            pltpu.VMEM((2, 5, ext_y, LANES), jnp.float32),
        ],
    )
    to_x, to_y, to_xy = packets[:many_x], packets[many_x : many_x + many_y], packets[many_x + many_y :]
    from_xy = [
        swap(to_xy[many_x * slot_y + slot_x], [], ("gx", slot_x), ("gy", slot_y))
        for slot_y in range(many_y)
        for slot_x in range(many_x)
    ]
    from_y = [swap(value, [("gz", partners("gz", 0))], ("gy", slot)) for slot, value in enumerate(to_y)]
    spares = [("gy", partners("gy", 0))]
    from_x = [swap(value, spares, ("gx", slot)) for slot, value in enumerate(to_x)]

    fields, second, change = call(
        inner_kernel,
        "inner_step",
        (den, vel, mask, first),
        [array(5, ext_x + 2, rows, LANES), array(19, ext_x + 2, rows, LANES), array(1, ext_x + 2, rows, LANES)],
        8,
        cost_estimate=pl.CostEstimate(flops=40_000_000, bytes_accessed=8_000_000, transcendentals=0),
    )
    inout = (first, fields, second, change)
    inout = call(
        functools.partial(side_kernel, (many_x, many_y)),
        "side_step",
        (z_set, *inout, *from_x, *from_y),
        [array(*value.shape) for value in inout] + [array(Z_TILES, rows, LANES), array(2, 5, rows, LANES)],
        8,
        input_output_aliases={1 + at: at for at in range(4)},
        cost_estimate=pl.CostEstimate(flops=40_000_000, bytes_accessed=8_000_000, transcendentals=0),
    )
    return call(
        functools.partial(last_kernel, (many_x, many_y)),
        "last_steps",
        (den, vel, mask, *inout, *from_xy),
        [array(19, ext_x, ext_y, LANES), array(ext_x, ext_y, LANES)] + [array(*value.shape) for value in inout],
        8,
        out_specs=[hbm] * 2 + [vmem] * 6,
        input_output_aliases={3 + at: 2 + at for at in range(6)},
        scratch_shapes=[
            pltpu.VMEM((5, rows, LANES), jnp.float32),
            pltpu.VMEM((19, ext_x, ext_y, LANES), jnp.float32),
            pltpu.VMEM((ext_x, ext_y, LANES), jnp.float32),
            pltpu.SemaphoreType.DMA((2, ext_x)),
        ],
    )[:2]


def solution(mesh):
    placed = (
        P(None, "gx", "gy", "gz"),
        P(None, "gx", "gy", "gz"),
        P(None, None, "gx", "gy", "gz"),
        P("gx", "gy", "gz"),
    )

    def whole(*arrays):
        return tuple(shards(*arrays))

    return jax.shard_map(
        whole,
        mesh=mesh,
        in_specs=placed,
        out_specs=(P(None, "gx", "gy", "gz"), P("gx", "gy", "gz")),
        check_vma=False,
    )
```

```python
import functools
import itertools

import jax
import jax.numpy as jnp
from jax import lax
from jax.experimental import pallas as pl
from jax.experimental.pallas import tpu as pltpu
from jax.sharding import PartitionSpec as P

VELOCITIES = [
    (0, 0, 0),
    (1, 0, 0),
    (-1, 0, 0),
    (0, 1, 0),
    (0, -1, 0),
    (0, 0, 1),
    (0, 0, -1),
    (1, 1, 0),
    (-1, -1, 0),
    (1, -1, 0),
    (-1, 1, 0),
    (1, 0, 1),
    (-1, 0, -1),
    (1, 0, -1),
    (-1, 0, 1),
    (0, 1, 1),
    (0, -1, -1),
    (0, 1, -1),
    (0, -1, 1),
]
OPPOSITE = [0, 2, 1, 4, 3, 6, 5, 8, 7, 10, 9, 12, 11, 14, 13, 16, 15, 18, 17]
OMEGA = 1.25
LANES = 128
GROUP = 16


def pops(axis, sign):
    return [j for j in range(19) if VELOCITIES[j][axis] == sign]


def mirrored(j):
    cx, cy, cz = VELOCITIES[j]
    return VELOCITIES.index((cx, cy, -cz))


Z_FLAT = pops(2, 0)
Z_UP = pops(2, 1)
Z_DOWN = [mirrored(j) for j in Z_UP]
RHO, UX, UY, UZ, KIND = range(5)
Z_PLACE = {("pop", j): (0, g) for g, j in enumerate(Z_FLAT[:8])}
Z_PLACE[("pop", Z_FLAT[8])] = (1, 5)
Z_PLACE[("field", RHO)] = (1, 6)
Z_PLACE[("field", KIND)] = (1, 7)
Z_PLACE[("field", UX)] = (2, 5)
Z_PLACE[("field", UY)] = (2, 6)
Z_PLACE[("field", UZ)] = (2, 7)
BELOW, ABOVE, OWN_LOW, OWN_HIGH, Z_TILES = 0, 3, 6, 7, 8


def face_lines(axis, toward):
    near = pops(axis, 0) + pops(axis, toward)
    lines = [("pop", j, 0) for j in near] + [("field", k, 0) for k in range(5)]
    return lines + [("pop", j, 1) for j in pops(axis, toward)]


def edge_lines(toward_x, toward_y):
    lines = [("field", k, 0, 0) for k in range(5)]
    for j in range(19):
        cx, cy, _ = VELOCITIES[j]
        if cx not in (0, toward_x) or cy not in (0, toward_y):
            continue
        lines.append(("pop", j, 0, 0))
        if cx:
            lines.append(("pop", j, 1, 0))
        if cy:
            lines.append(("pop", j, 0, 1))
        if cx and cy:
            lines.append(("pop", j, 1, 1))
    return lines


FACE = 24
EDGE = 24
SIDE = 15


def side_lines(toward):
    full = [("pop", j) for j in pops(0, toward)] + [("share", p) for p in range(5)]
    full += [("field", k) for k in (UX, UY, UZ, KIND)]
    ends = []
    for end in range(2):
        for j in pops(1, 1 - 2 * end):
            cx = VELOCITIES[j][0]
            if cx in (0, toward):
                ends.append((j, abs(cx), end))
    return full, ends


def lane_ids():
    return lax.broadcasted_iota(jnp.int32, (8, LANES), 1)


def field_of(refs, kind, index, at):
    adj, den, vel, mask = refs
    if kind == "pop":
        return adj[(index, *at)]
    if index == RHO:
        return den[(1, *at)]
    if index == KIND:
        return (mask[at] + 1).astype(jnp.float32)
    return vel[(1, index - UX, *at)]


def parity_of(axis):
    return lax.rem(lax.axis_index(axis), 2)


def on_side(parity, slot, act):
    @pl.when(parity == slot)
    def _():
        act(1)

    @pl.when(parity != slot)
    def _():
        act(0)


def has_partner(axis, slot):
    at = lax.axis_index(axis)
    to = at + jnp.where(lax.rem(at, 2) == slot, 1, -1)
    return (to >= 0) & (to < lax.axis_size(axis))


def pack_z_kernel(slots, adj_in, den_in, vel_in, mask_in, adj, den, vel, mask, near, *rest):
    packets, sems = rest[:slots], rest[slots]
    refs = (adj, den, vel, mask)
    ext_x, ext_y, _ = mask.shape
    starts = range(0, 19, 5)
    loads = [
        pltpu.make_async_copy(adj_in.at[start : min(start + 5, 19)], adj.at[start : min(start + 5, 19)], sems.at[at])
        for at, start in enumerate(starts)
    ] + [
        pltpu.make_async_copy(source, target, sems.at[len(starts) + at])
        for at, (source, target) in enumerate([(den_in, den), (vel_in, vel), (mask_in, mask)])
    ]
    for load in loads:
        load.start()
    lane = lane_ids()
    parity = parity_of("gz")
    parts = range(ext_y // 8)
    zero = jnp.zeros((8, LANES), jnp.float32)
    lows, highs = [[zero] * 3 for _ in parts], [[zero] * 3 for _ in parts]
    far_low, far_high = [zero for _ in parts], [zero for _ in parts]

    def gather(kind, index):
        for x, part in itertools.product(range(ext_x), parts):
            value = field_of(refs, kind, index, (x, pl.ds(8 * part, 8), slice(None)))
            if kind == "pop" and VELOCITIES[index][2] == 1:
                spot = GROUP * Z_UP.index(index) + 2 + x
                moved = pltpu.roll(value, spot, 1)
                lows[part][1] = jnp.where(lane == spot, moved, lows[part][1])
                far_low[part] = jnp.where(lane == spot + 1, moved, far_low[part])
            elif kind == "pop" and VELOCITIES[index][2] == -1:
                spot = GROUP * Z_DOWN.index(index) + 2 + x
                moved = pltpu.roll(value, spot, 1)
                highs[part][1] = jnp.where(lane == spot - 1, moved, highs[part][1])
                far_high[part] = jnp.where(lane == spot - 2, moved, far_high[part])
            else:
                tile, group = Z_PLACE[(kind, index)]
                spot = GROUP * group + 2 + x
                moved = pltpu.roll(value, spot, 1)
                lows[part][tile] = jnp.where(lane == spot, moved, lows[part][tile])
                highs[part][tile] = jnp.where(lane == spot - 1, moved, highs[part][tile])

    for start, load in zip(starts, loads):
        load.wait()
        for j in range(start, min(start + 5, 19)):
            gather("pop", j)
    for load in loads[len(starts) :]:
        load.wait()
    for k in range(5):
        gather("field", k)
    for part in parts:
        rows = pl.ds(8 * part, 8)
        low = lows[part]
        high = [pltpu.roll(tile, 1, 1) for tile in highs[part]]
        low[2] = jnp.where(lane < 5 * GROUP, pltpu.roll(far_low[part], LANES - 1, 1), low[2])
        high[2] = jnp.where(lane < 5 * GROUP, pltpu.roll(far_high[part], 2, 1), high[2])
        near[0, rows, :] = low[1]
        near[1, rows, :] = high[1]
        for slot in range(slots):
            there = has_partner("gz", slot)
            for tile in range(3):
                value = jnp.where(parity == slot, high[tile], low[tile])
                packets[slot][tile, rows, :] = jnp.where(there, value, 0.0)


def pack_lines(refs, first, packets, many_x, many_y, wanted, shares):
    to_x, to_y = packets[:many_x], packets[many_x : many_x + many_y]
    to_xy = packets[many_x + many_y :]
    ext_x, ext_y, _ = refs[-1].shape
    every = slice(None)
    px, py = parity_of("gx"), parity_of("gy")

    def line_of(kind, index, x, y):
        if kind == "pop":
            return first[index, x + 2, y + 8 : y + 9, :]
        return field_of(refs, kind, index, (x, slice(y, y + 1), every))

    def pack_xy(slot_x, slot_y, side_x, side_y):
        packet = to_xy[many_x * slot_y + slot_x]
        for line, (kind, index, far_x, far_y) in enumerate(edge_lines(1 - 2 * side_x, 1 - 2 * side_y)):
            if wanted(kind, index):
                x = ext_x - 1 - far_x if side_x else far_x
                y = ext_y - 1 - far_y if side_y else far_y
                packet[line // 8, line % 8 : line % 8 + 1, :] = line_of(kind, index, x, y)

    def pack_y(slot, side):
        for line, (kind, index, depth) in enumerate(face_lines(1, 1 - 2 * side)):
            if wanted(kind, index):
                y = ext_y - 1 - depth if side else depth
                for x in range(ext_x):
                    to_y[slot][line, x : x + 1, :] = line_of(kind, index, x, y)

    def pack_x(slot, side):
        full, ends = side_lines(1 - 2 * side)
        for line, (kind, index) in enumerate(full):
            if kind == "field" and wanted(kind, index):
                to_x[slot][line] = field_of(refs, kind, index, (ext_x - 1 if side else 0, every, every))
            elif kind == "pop" and wanted(kind, index):
                to_x[slot][line] = first[index, (ext_x - 1 if side else 0) + 2, pl.ds(8, ext_y), :]
            elif kind == "share" and shares is not None:
                to_x[slot][line] = shares[side, index]
        for spot, (index, depth, end) in enumerate(ends):
            if wanted("pop", index):
                x = ext_x - 1 - depth if side else depth
                to_x[slot][SIDE - 1, spot : spot + 1, :] = line_of("pop", index, x, ext_y - 1 if end else 0)

    def when_there(there, packet, act):
        pl.when(there)(act)
        if shares is None:

            @pl.when(jnp.logical_not(there))
            def _():
                packet[...] = jnp.zeros(packet.shape, jnp.float32)

    for slot_y in range(many_y):
        there_y = has_partner("gy", slot_y)
        when_there(there_y, to_y[slot_y], lambda: on_side(py, slot_y, functools.partial(pack_y, slot_y)))
        for slot_x in range(many_x):
            when_there(
                there_y & has_partner("gx", slot_x),
                to_xy[many_x * slot_y + slot_x],
                lambda: on_side(
                    py,
                    slot_y,
                    lambda side_y: on_side(px, slot_x, lambda side_x: pack_xy(slot_x, slot_y, side_x, side_y)),
                ),
            )
    for slot_x in range(many_x):
        when_there(
            has_partner("gx", slot_x), to_x[slot_x], lambda: on_side(px, slot_x, functools.partial(pack_x, slot_x))
        )


def is_flat(kind, index):
    return kind == "field" or VELOCITIES[index][2] == 0


def shift_kernel(slots, adj, den, vel, mask, first, *packets):
    many_x, many_y = slots
    _, ext_x, ext_y, _ = adj.shape
    for j in range(19):
        cz = VELOCITIES[j][2]
        for x, part in itertools.product(range(ext_x), range(ext_y // 8)):
            value = adj[j, x, pl.ds(8 * part, 8), :]
            first[j, 2 + x, pl.ds(8 + 8 * part, 8), :] = pltpu.roll(value, -cz % LANES, 1) if cz else value
    pack_lines((None, den, vel, mask), first, packets, many_x, many_y, is_flat, None)


def pack_xy_kernel(slots, den, vel, mask, near, *rest):
    many_x, many_y, many_z = slots
    count = many_x + many_y + many_x * many_y
    from_z, rest = rest[:many_z], rest[many_z + 1 + count :]
    z_set, first, packets, faces, shares = rest[0], rest[1], rest[2:-2], rest[-2], rest[-1]
    to_x, to_y, to_xy = packets[:many_x], packets[many_x : many_x + many_y], packets[many_x + many_y :]
    ext_x, ext_y = first.shape[1] - 4, near.shape[1]
    spot = lane_ids() % GROUP
    px, py, pz = parity_of("gx"), parity_of("gy"), parity_of("gz")

    z_set[OWN_LOW] = near[0]
    z_set[OWN_HIGH] = near[1]
    for tile in range(3):
        even = from_z[0][tile]
        odd = from_z[1][tile] if many_z > 1 else jnp.zeros_like(even)
        z_set[ABOVE + tile] = jnp.where(pz == 0, even, odd)
        z_set[BELOW + tile] = jnp.where(pz == 0, odd, even)

    for j in Z_UP + Z_DOWN:
        up = VELOCITIES[j][2] > 0
        group = (Z_UP if up else Z_DOWN).index(j)
        last = LANES - 1 if up else 0
        for part in range(ext_y // 8):
            halo = z_set[(ABOVE if up else BELOW) + 1, pl.ds(8 * part, 8), :]
            for x in range(ext_x):
                edge = pltpu.roll(halo, (last - 2 - GROUP * group - x) % LANES, 1)
                first[j, 2 + x, pl.ds(8 + 8 * part, 8), last : last + 1] = edge[:, last : last + 1]


    sub = lax.broadcasted_iota(jnp.int32, (8, LANES), 0)
    loaded = []
    for side, part in itertools.product(range(2), range(ext_y // 8)):
        toward, x = 1 - 2 * side, ext_x - 1 if side else 0
        pulled = []
        for j in range(19):
            cx, cy, _ = VELOCITIES[j]
            if cx == -toward:
                pulled.append(jnp.zeros((8, LANES), jnp.float32))
                continue
            value = first[j, x + 2 + cx, pl.ds(8 + 8 * part + cy, 8), :]
            if cy == -1 and part == 0:
                value = jnp.where(sub == 0, 0.0, value)
            if cy == 1 and part == ext_y // 8 - 1:
                value = jnp.where(sub == 7, 0.0, value)
            pulled.append(value)
        at = (x, pl.ds(8 * part, 8), slice(None))
        here = [den[(1, *at)], vel[(1, 0, *at)], vel[(1, 1, *at)], vel[(1, 2, *at)], mask[at] > 0]
        loaded.append((side, part, pulled, here))
    for side, part, pulled, (rho, ux, uy, uz, fluid) in loaded:
        wanted = pops(0, 1 - 2 * side)
        after, _ = collide(pulled, 1.0 / rho, rho, ux, uy, uz, None, wanted)
        for line, j in enumerate(wanted):
            shares[side, line, pl.ds(8 * part, 8), :] = jnp.where(fluid, after[j], 0.0)

    pack_lines((mask,), first, packets, many_x, many_y, lambda kind, index: not is_flat(kind, index), shares)

    for side in range(2):
        for part in range(ext_y // 8):
            rows = pl.ds(8 * part, 8)
            value = jnp.zeros((8, LANES), jnp.float32)
            for tile in range(Z_TILES):
                start = ext_x if side else 2
                moved = pltpu.roll(z_set[tile, rows, :], (2 * tile - start) % LANES, 1)
                value = jnp.where(spot // 2 == tile, moved, value)
            faces[side, rows, :] = value

    def add_xy(slot_x, slot_y, side_x, side_y):
        start = ext_y - 2 if side_y else 0
        to_xy[many_x * slot_y + slot_x][EDGE // 8, 0:2, :] = faces[side_x, start : start + 2, :]

    def add_y(slot, side):
        start = ext_y - 2 if side else 0
        for tile in range(Z_TILES):
            row = 2 * tile % 8
            to_y[slot][FACE + tile // 4, row : row + 2, :] = z_set[tile, start : start + 2, :]

    def add_x(slot, side):
        to_x[slot][SIDE] = faces[side]

    for slot_y in range(many_y):
        there_y = has_partner("gy", slot_y)
        pl.when(there_y)(lambda: on_side(py, slot_y, functools.partial(add_y, slot_y)))
        for slot_x in range(many_x):
            pl.when(there_y & has_partner("gx", slot_x))(
                lambda: on_side(
                    py,
                    slot_y,
                    lambda side_y: on_side(px, slot_x, lambda side_x: add_xy(slot_x, slot_y, side_x, side_y)),
                )
            )
    for slot_x in range(many_x):
        pl.when(has_partner("gx", slot_x))(lambda: on_side(px, slot_x, functools.partial(add_x, slot_x)))


def collide(pulled, inverse, rho, ux, uy, uz, fluid, wanted):
    total = {}
    diff = {}
    for j in range(1, 19, 2):
        total[j] = pulled[j] + pulled[j + 1]
        diff[j] = pulled[j] - pulled[j + 1]
    in_xy, in_xz, in_yz = total[7] + total[9], total[11] + total[13], total[15] + total[17]
    two_x, two_y, two_z = total[1] + total[1], total[3] + total[3], total[5] + total[5]
    count = (12.0 * pulled[0] + (two_x + two_y)) + (two_z + (in_xy + (in_xz + in_yz)))
    flow_x = (diff[1] + diff[1]) + ((diff[7] + diff[9]) + (diff[11] + diff[13]))
    flow_y = (diff[3] + diff[3]) + ((diff[7] - diff[9]) + (diff[15] + diff[17]))
    flow_z = (diff[5] + diff[5]) + ((diff[11] - diff[13]) + (diff[15] - diff[17]))
    xx, yy, zz = two_x + (in_xy + in_xz), two_y + (in_xy + in_yz), two_z + (in_xz + in_yz)
    xy, xz, yz = total[7] - total[9], total[11] - total[13], total[15] - total[17]
    push_x = xx * ux + xy * uy + xz * uz
    push_y = xy * ux + yy * uy + yz * uz
    push_z = xz * ux + yz * uy + zz * uz
    usq = ux * ux + uy * uy + uz * uz
    push = ux * push_x + uy * push_y + uz * push_z
    base = count * (OMEGA / 36.0 + (OMEGA / 24.0) * usq) - (OMEGA / 8.0) * push - ux * inverse
    along_x = (OMEGA / 12.0) * (flow_x + 3.0 * push_x - ux * count) + inverse
    along_y = (OMEGA / 12.0) * (flow_y + 3.0 * push_y - uy * count)
    along_z = (OMEGA / 12.0) * (flow_z + 3.0 * push_z - uz * count)
    parts = {
        1: along_x,
        3: along_y,
        5: along_z,
        7: along_x + along_y,
        9: along_x - along_y,
        11: along_x + along_z,
        13: along_x - along_z,
        15: along_y + along_z,
        17: along_y - along_z,
    }
    out = {}
    for j in wanted:
        if j == 0:
            shift = base
        elif j % 2:
            shift = base + parts[j]
        else:
            shift = base - parts[j - 1]
        out[j] = (1.0 - OMEGA) * pulled[j] + shift
        if fluid is not None:
            out[j] = jnp.where(fluid, out[j], pulled[OPPOSITE[j]])
    change = (-1.0 / 6.0) * rho * (flow_x * ux + flow_y * uy + flow_z * uz)
    return out, change if fluid is None else jnp.where(fluid, change, 0.0)


class Plane:
    def __init__(self, x, row):
        self.x, self.row = x, row

    def load(self, ref, lead, margin, cx=0, cy=0):
        return ref[lead, self.x + margin + cx, pl.ds(8 + self.row + cy, 8), :]

    def store(self, ref, lead, margin, value):
        ref[lead, self.x + margin, pl.ds(8 + self.row, 8), :] = value


class Rim:
    def __init__(self, x, ext_y):
        self.x, self.ext_y = x, ext_y

    def load(self, ref, lead, margin, cx=0, cy=0):
        at = self.x + margin + cx
        upper = ref[lead, at, pl.ds(8 + self.ext_y - 1 + cy, 8), :]
        lower = ref[lead, at, pl.ds(1 + cy, 8), :]
        return jnp.where(lax.broadcasted_iota(jnp.int32, (8, LANES), 0) < 4, upper, lower)

    def store(self, ref, lead, margin, value):
        at = self.x + margin
        ref[lead, at, pl.ds(8 + self.ext_y - 1, 2), :] = value[0:2]
        ref[lead, at, pl.ds(7, 2), :] = value[6:8]


def first_step(first, fields, second, change, tiles, outside=True, shares=None):
    loaded = [
        (
            [tile.load(first, j, 2, *VELOCITIES[j][:2]) for j in range(19)],
            [tile.load(fields, k, 1) for k in range(5)],
        )
        for tile in tiles
    ]
    done = [
        collide(pulled, 1.0 / rho, rho, ux, uy, uz, kind > 1.5, range(19))
        for pulled, (rho, ux, uy, uz, kind) in loaded
    ]
    for tile, (_, here), (after, gain) in zip(tiles, loaded, done):
        inside = here[KIND] > 0.5
        side = None if shares is None else {-1: 0, second.shape[1] - 2: 1}.get(tile.x)
        for j in range(19):
            value = after[j]
            if side is not None and VELOCITIES[j][0] == 2 * side - 1:
                value = value + shares[side, pops(0, 2 * side - 1).index(j), pl.ds(8 + tile.row, 8), :]
            if outside:
                value = jnp.where(inside, value, 0.0)
            cz = VELOCITIES[j][2]
            tile.store(second, j, 1, pltpu.roll(value, -cz % LANES, 1) if cz else value)
        tile.store(change, 0, 1, gain)


def inner_kernel(den, vel, mask, first, fields, second, change):
    refs = (None, den, vel, mask)
    ext_x, ext_y, _ = mask.shape
    every = slice(None)
    for k in range(5):
        fields[k, 1 : 1 + ext_x, pl.ds(8, ext_y), :] = field_of(refs, "field", k, (every, every, every))

    many = 3 if (ext_x - 2) % 3 == 0 else 1

    @pl.loop(0, (ext_x - 2) // many)
    def _(group):
        tiles = [Plane(many * group + at + 1, 1 + 8 * part) for at in range(many) for part in range(ext_y // 8)]
        first_step(first, fields, second, change, tiles, outside=False)


def put_row(first, fields, kind, index, x, y, value):
    row = y + 8
    if kind == "pop":
        first[index, x + 2, row : row + 1, :] = value
    else:
        fields[index, x + 1, row : row + 1, :] = value


def place_z(z_first, value, start, size, side, ext_x):
    rows = pl.ds(start, size)
    spot = lane_ids()[:size] % GROUP
    inside = spot >= 2 + ext_x if side else spot < 2
    for tile in range(Z_TILES):
        shift = (2 + ext_x if side else 0) - 2 * tile
        moved = pltpu.roll(value, shift % LANES, 1)[:size]
        z_first[tile, rows, :] = jnp.where(inside, moved, z_first[tile, rows, :])


def side_kernel(slots, z_set, *rest):
    many_x, many_y = slots
    from_x, from_y = rest[4 : 4 + many_x], rest[4 + many_x : 4 + many_x + many_y]
    first, fields, second, change, z_first, shares = rest[-6:]
    _, ext_y, _ = z_set.shape
    ext_x = change.shape[1] - 2
    inner = pl.ds(8, ext_y)
    put = functools.partial(put_row, first, fields)
    z_first[:, inner, :] = z_set[...]

    def place_y(slot, side):
        packet = from_y[slot]
        for line, (kind, index, depth) in enumerate(face_lines(1, 2 * side - 1)):
            y = ext_y + depth if side else -1 - depth
            for x in range(ext_x):
                put(kind, index, x, y, packet[line, x : x + 1, :])
        start = 8 + ext_y if side else 6
        for tile in range(Z_TILES):
            row = 2 * tile % 8
            z_first[tile, start : start + 2, :] = packet[FACE + tile // 4, row : row + 2, :]
        if many_y == 1:
            clear_y(1 - side)

    def clear_y(side):
        nothing = jnp.zeros((1, LANES), jnp.float32)
        for kind, index, depth in face_lines(1, 2 * side - 1):
            y = ext_y + depth if side else -1 - depth
            for x in range(-1, ext_x + 1):
                put(kind, index, x, y, nothing)
            if kind == "pop":
                put(kind, index, -2, y, nothing)
                put(kind, index, ext_x + 1, y, nothing)
        start = 8 + ext_y if side else 6
        for tile in range(Z_TILES):
            z_first[tile, start : start + 2, :] = jnp.zeros((2, LANES), jnp.float32)

    def place_x(slot, side):
        packet = from_x[slot]
        toward = 2 * side - 1
        near = ext_x if side else -1
        nothing = jnp.zeros((ext_y, LANES), jnp.float32)
        for j in pops(0, 0):
            first[j, near + 2, inner, :] = nothing
        for j in pops(0, toward):
            first[j, near + toward + 2, inner, :] = nothing
        fields[RHO, near + 1, inner, :] = jnp.full((ext_y, LANES), jnp.inf, jnp.float32)
        full, ends = side_lines(toward)
        for line, (kind, index) in enumerate(full):
            if kind == "pop":
                first[index, near + 2, inner, :] = packet[line]
            elif kind == "share":
                shares[side, index, inner, :] = packet[line]
            else:
                fields[index, near + 1, inner, :] = packet[line]
        for spot, (index, depth, end) in enumerate(ends):
            put("pop", index, near + toward * depth, ext_y - 1 if end else 0, packet[SIDE - 1, spot : spot + 1, :])
        for part in range(ext_y // 8):
            place_z(z_first, packet[SIDE, pl.ds(8 * part, 8), :], 8 + 8 * part, 8, side, ext_x)

    shares[:, :, pl.ds(0, 8), :] = jnp.zeros((2, 5, 8, LANES), jnp.float32)
    shares[:, :, pl.ds(8 + ext_y, 8), :] = jnp.zeros((2, 5, 8, LANES), jnp.float32)
    for slot_y in range(many_y):
        on_side(parity_of("gy"), slot_y, functools.partial(place_y, slot_y))
    for slot_x in range(many_x):
        on_side(parity_of("gx"), slot_x, functools.partial(place_x, slot_x))

    rims = range(7, ext_y - 8, 8)
    first_step(first, fields, second, change, [Plane(x, row) for x in (0, ext_x - 1) for row in rims], outside=False)
    first_step(first, fields, second, change, [Plane(x, row) for x in (-1, ext_x) for row in rims], shares=shares)

    many = 3 if (ext_x - 2) % 3 == 0 else 1

    @pl.loop(0, (ext_x - 2) // many)
    def _(group):
        first_step(first, fields, second, change, [Rim(many * group + at + 1, ext_y) for at in range(many)])


def last_kernel(slots, den, vel, mask, *rest):
    many_x, many_y = slots
    from_xy = rest[6 : 6 + many_x * many_y]
    out, sens, first, fields, second, change, z_first, shares, z_second, held, held_sens, sems = rest[-12:]
    ext_x, ext_y, _ = mask.shape
    lane = lane_ids()
    every = slice(None)
    px, py = parity_of("gx"), parity_of("gy")

    def place_xy(slot_x, slot_y, side_x, side_y):
        packet = from_xy[many_x * slot_y + slot_x]
        for line, (kind, index, far_x, far_y) in enumerate(edge_lines(2 * side_x - 1, 2 * side_y - 1)):
            x = ext_x + far_x if side_x else -1 - far_x
            y = ext_y + far_y if side_y else -1 - far_y
            put_row(first, fields, kind, index, x, y, packet[line // 8, line % 8 : line % 8 + 1, :])
        place_z(z_first, packet[EDGE // 8], 8 + ext_y if side_y else 6, 2, side_x, ext_x)

    for slot_x in range(many_x):
        for slot_y in range(many_y):
            on_side(
                py,
                slot_y,
                lambda side_y: on_side(px, slot_x, lambda side_x: place_xy(slot_x, slot_y, side_x, side_y)),
            )

    for pair in ((-1, 0), (ext_x - 1, ext_x)):
        tiles = [Plane(x, row) for x in pair for row in (-1, ext_y - 1)]
        first_step(first, fields, second, change, tiles, shares=shares)

    starts = [7 + 8 * part for part in range((ext_y + 2 + 7) // 8)]
    loaded = []
    for row in starts:

        def both(low_tile, high_tile, group, cx, cy):
            rows = pl.ds(row + cy, 8)
            low = pltpu.roll(z_first[low_tile, rows, :], (-GROUP * group - cx) % LANES, 1)
            high = pltpu.roll(z_first[high_tile, rows, :], (LANES // 2 - GROUP * group - cx) % LANES, 1)
            return jnp.where(lane < LANES // 2, low, high)

        pulled = []
        for j in range(19):
            cx, cy, cz = VELOCITIES[j]
            if cz == 0:
                tile, group = Z_PLACE[("pop", j)]
                pulled.append(both(BELOW + tile, ABOVE + tile, group, cx, cy))
            elif cz == 1:
                pulled.append(both(OWN_LOW, ABOVE + 2, Z_UP.index(j), cx, cy))
            else:
                pulled.append(both(BELOW + 2, OWN_HIGH, Z_DOWN.index(j), cx, cy))
        places = [Z_PLACE[("field", k)] for k in range(5)]
        loaded.append((pulled, [both(BELOW + tile, ABOVE + tile, group, 0, 0) for tile, group in places]))
    done = [
        collide(pulled, 1.0 / rho, rho, ux, uy, uz, kind > 1.5, Z_UP + Z_DOWN)[0]
        for pulled, (rho, ux, uy, uz, kind) in loaded
    ]
    for row, (_, here), after in zip(starts, loaded, done):
        for group in range(5):
            value = jnp.where(lane < LANES // 2, after[Z_DOWN[group]], after[Z_UP[group]])
            z_second[group, pl.ds(row, 8), :] = jnp.where(here[KIND] > 0.5, value, 0.0)

    def copies(x):
        return (
            pltpu.make_async_copy(held.at[:, x], out.at[:, x], sems.at[0, x]),
            pltpu.make_async_copy(held_sens.at[x], sens.at[x], sems.at[1, x]),
        )

    many = 4 if ext_x % 4 == 0 else 1

    @pl.loop(0, ext_x // many)
    def _(group):
        loaded = []
        planes = [many * group + at for at in range(many)]
        for x, part in itertools.product(planes, range(ext_y // 8)):
            row = 8 + 8 * part
            pulled = []
            for j in range(19):
                cx, cy, cz = VELOCITIES[j]
                rows = pl.ds(row + cy, 8)
                value = second[j, x + 1 + cx, rows, :]
                if cz == 1:
                    edge = z_second[Z_UP.index(j), rows, :]
                    edge = pltpu.roll(edge, LANES // 2 - 3 - cx - x, 1)
                    value = jnp.where(lane == LANES - 1, edge, value)
                elif cz == -1:
                    edge = z_second[Z_DOWN.index(j), rows, :]
                    edge = pltpu.roll(edge, LANES - 2 - cx - x, 1)
                    value = jnp.where(lane == 0, edge, value)
                pulled.append(value)
            at = (x, pl.ds(8 * part, 8), every)
            rho = den[(0, *at)]
            here = [1.0 / rho, rho, vel[(0, 0, *at)], vel[(0, 1, *at)], vel[(0, 2, *at)], mask[at] > 0]
            loaded.append((at, pulled, here, change[0, x + 1, pl.ds(row, 8), :]))
        done = [collide(pulled, *here, range(19)) for _, pulled, here, _ in loaded]
        for (at, _, _, before), (after, gain) in zip(loaded, done):
            for j in range(19):
                held[(j, *at)] = after[j]
            held_sens[at] = before + gain
        for x in planes:
            for copy in copies(x):
                copy.start()

    for x in range(ext_x):
        for copy in copies(x):
            copy.wait()


def shards(adjoint, density, velocity, pore_mask):
    ext_x, ext_y, ext_z = pore_mask.shape
    assert ext_z == LANES and ext_y % 8 == 0 and ext_x + 4 <= GROUP and ext_x == 8
    many_x = 2
    many_y, many_z = [1 if lax.axis_size(axis) == 2 else 2 for axis in ("gy", "gz")]
    vmem = pl.BlockSpec(memory_space=pltpu.VMEM)
    hbm = pl.BlockSpec(memory_space=pltpu.HBM)
    inputs = (adjoint, density, velocity, pore_mask)

    def array(*shape):
        return jax.ShapeDtypeStruct(shape, jnp.float32)

    def call(kernel, name, operands, shapes, limit, **more):
        more.setdefault("out_specs", [vmem] * len(shapes))
        more.setdefault("in_specs", [vmem] * len(operands))
        params = pltpu.CompilerParams(vmem_limit_bytes=limit * 1024 * 1024)
        return pl.pallas_call(kernel, out_shape=shapes, compiler_params=params, name=name, **more)(*operands)

    def partners(axis, slot):
        found = {}
        for at in range(slot, lax.axis_size(axis) - 1, 2):
            found[at], found[at + 1] = at + 1, at
        return found

    def ends(axis):
        last = lax.axis_size(axis) - 1
        return {0: last, last: 0}

    def swap(value, spares, *places):
        tables = {axis: partners(axis, slot) for axis, slot in places}
        axes = [axis for axis in ("gx", "gy", "gz") if axis in tables or axis in dict(spares)]
        sizes = [lax.axis_size(axis) for axis in axes]
        pairs = []
        for at in itertools.product(*[range(size) for size in sizes]):
            to = [tables.get(axis, {}).get(spot, spot) for axis, spot in zip(axes, at)]
            for spare, table in spares:
                if tuple(to) == at:
                    to = [table.get(spot, spot) if axis == spare else spot for axis, spot in zip(axes, at)]
            flat = []
            for spots in (at, to):
                index = 0
                for size, spot in zip(sizes, spots):
                    index = index * size + spot
                flat.append(index)
            pairs.append(tuple(flat))
        return lax.ppermute(value, tuple(axes), pairs)

    loaded = [jax.ShapeDtypeStruct(value.shape, value.dtype) for value in inputs]
    *held, near, a_z, b_z = (
        *call(
            functools.partial(pack_z_kernel, many_z),
            "pack_z",
            [pltpu.with_memory_space_constraint(value, pltpu.HBM) for value in inputs],
            loaded + [array(2, ext_y, LANES)] + [array(3, ext_y, LANES)] * many_z,
            8,
            in_specs=[hbm] * 4,
            scratch_shapes=[pltpu.SemaphoreType.DMA((7,))],
        ),
        *[None] * (2 - many_z),
    )
    from_z = [swap(value, [("gx", partners("gx", 0))], ("gz", slot)) for slot, value in enumerate((a_z, b_z)[:many_z])]

    rows = ext_y + 16
    adj, den, vel, mask = held
    y_tiles = max(FACE + 2, (SIDE + 1) * ext_y // ext_x + 1)
    shapes = (
        [array(19, ext_x + 4, rows, LANES)]
        + [array(SIDE + 1, ext_y, LANES)] * many_x
        + [array(y_tiles, ext_x, LANES)] * many_y
        + [array(EDGE // 8 + 1, 8, LANES)] * (many_x * many_y)
    )
    shifted = call(
        functools.partial(shift_kernel, (many_x, many_y)),
        "shift",
        (adj, den, vel, mask),
        shapes,
        8,
        cost_estimate=pl.CostEstimate(flops=1_000_000, bytes_accessed=2_500_000, transcendentals=0),
    )
    z_set, first, *packets = call(
        functools.partial(pack_xy_kernel, (many_x, many_y, many_z)),
        "pack_xy",
        (den, vel, mask, near, *from_z, *shifted),
        [array(Z_TILES, ext_y, LANES)] + shapes,
        8,
        input_output_aliases={4 + many_z + at: 1 + at for at in range(len(shapes))},
        scratch_shapes=[
            pltpu.VMEM((2, ext_y, LANES), jnp.float32),
            pltpu.VMEM((2, 5, ext_y, LANES), jnp.float32),
        ],
    )
    to_x, to_y, to_xy = packets[:many_x], packets[many_x : many_x + many_y], packets[many_x + many_y :]
    from_xy = [
        swap(to_xy[many_x * slot_y + slot_x], [], ("gx", slot_x), ("gy", slot_y))
        for slot_y in range(many_y)
        for slot_x in range(many_x)
    ]
    from_y = [swap(value, [("gz", partners("gz", 0))], ("gy", slot)) for slot, value in enumerate(to_y)]
    spares = [("gx", ends("gx"))]
    from_x = [swap(value, spares, ("gx", slot)) for slot, value in enumerate(to_x)]

    fields, second, change = call(
        inner_kernel,
        "inner_step",
        (den, vel, mask, first),
        [array(5, ext_x + 2, rows, LANES), array(19, ext_x + 2, rows, LANES), array(1, ext_x + 2, rows, LANES)],
        8,
        cost_estimate=pl.CostEstimate(flops=40_000_000, bytes_accessed=8_000_000, transcendentals=0),
    )
    inout = (first, fields, second, change)
    inout = call(
        functools.partial(side_kernel, (many_x, many_y)),
        "side_step",
        (z_set, *inout, *from_x, *from_y),
        [array(*value.shape) for value in inout] + [array(Z_TILES, rows, LANES), array(2, 5, rows, LANES)],
        8,
        input_output_aliases={1 + at: at for at in range(4)},
        cost_estimate=pl.CostEstimate(flops=40_000_000, bytes_accessed=8_000_000, transcendentals=0),
    )
    return call(
        functools.partial(last_kernel, (many_x, many_y)),
        "last_steps",
        (den, vel, mask, *inout, *from_xy),
        [array(19, ext_x, ext_y, LANES), array(ext_x, ext_y, LANES)] + [array(*value.shape) for value in inout],
        8,
        out_specs=[hbm] * 2 + [vmem] * 6,
        input_output_aliases={3 + at: 2 + at for at in range(6)},
        scratch_shapes=[
            pltpu.VMEM((5, rows, LANES), jnp.float32),
            pltpu.VMEM((19, ext_x, ext_y, LANES), jnp.float32),
            pltpu.VMEM((ext_x, ext_y, LANES), jnp.float32),
            pltpu.SemaphoreType.DMA((2, ext_x)),
        ],
    )[:2]


def solution(mesh):
    placed = (
        P(None, "gx", "gy", "gz"),
        P(None, "gx", "gy", "gz"),
        P(None, None, "gx", "gy", "gz"),
        P("gx", "gy", "gz"),
    )

    def whole(*arrays):
        return tuple(shards(*arrays))

    return jax.shard_map(
        whole,
        mesh=mesh,
        in_specs=placed,
        out_specs=(P(None, "gx", "gy", "gz"), P("gx", "gy", "gz")),
        check_vma=False,
    )
```

```python
import functools
import itertools

import jax
import jax.numpy as jnp
from jax import lax
from jax.experimental import pallas as pl
from jax.experimental.pallas import tpu as pltpu
from jax.sharding import PartitionSpec as P

VELOCITIES = [
    (0, 0, 0),
    (1, 0, 0),
    (-1, 0, 0),
    (0, 1, 0),
    (0, -1, 0),
    (0, 0, 1),
    (0, 0, -1),
    (1, 1, 0),
    (-1, -1, 0),
    (1, -1, 0),
    (-1, 1, 0),
    (1, 0, 1),
    (-1, 0, -1),
    (1, 0, -1),
    (-1, 0, 1),
    (0, 1, 1),
    (0, -1, -1),
    (0, 1, -1),
    (0, -1, 1),
]
OPPOSITE = [0, 2, 1, 4, 3, 6, 5, 8, 7, 10, 9, 12, 11, 14, 13, 16, 15, 18, 17]
OMEGA = 1.25
LANES = 128
GROUP = 16


def pops(axis, sign):
    return [j for j in range(19) if VELOCITIES[j][axis] == sign]


def mirrored(j):
    cx, cy, cz = VELOCITIES[j]
    return VELOCITIES.index((cx, cy, -cz))


Z_FLAT = pops(2, 0)
Z_UP = pops(2, 1)
Z_DOWN = [mirrored(j) for j in Z_UP]
RHO, UX, UY, UZ, KIND = range(5)
Z_PLACE = {("pop", j): (0, g) for g, j in enumerate(Z_FLAT[:8])}
Z_PLACE[("pop", Z_FLAT[8])] = (1, 5)
Z_PLACE[("field", RHO)] = (1, 6)
Z_PLACE[("field", KIND)] = (1, 7)
Z_PLACE[("field", UX)] = (2, 5)
Z_PLACE[("field", UY)] = (2, 6)
Z_PLACE[("field", UZ)] = (2, 7)
BELOW, ABOVE, OWN_LOW, OWN_HIGH, Z_TILES = 0, 3, 6, 7, 8


def face_lines(axis, toward):
    near = pops(axis, 0) + pops(axis, toward)
    lines = [("pop", j, 0) for j in near] + [("field", k, 0) for k in range(5)]
    return lines + [("pop", j, 1) for j in pops(axis, toward)]


def edge_lines(toward_x, toward_y):
    lines = [("field", k, 0, 0) for k in range(5)]
    for j in range(19):
        cx, cy, _ = VELOCITIES[j]
        if cx not in (0, toward_x) or cy not in (0, toward_y):
            continue
        lines.append(("pop", j, 0, 0))
        if cx:
            lines.append(("pop", j, 1, 0))
        if cy:
            lines.append(("pop", j, 0, 1))
        if cx and cy:
            lines.append(("pop", j, 1, 1))
    return lines


FACE = 24
EDGE = 24
SIDE = 15


def side_lines(axis, toward):
    full = [("pop", j) for j in pops(axis, toward)] + [("share", p) for p in range(5)]
    full += [("field", k) for k in (UX, UY, UZ, KIND)]
    ends = []
    for end in range(2):
        for j in pops(1 - axis, 1 - 2 * end):
            across = VELOCITIES[j][axis]
            if across in (0, toward):
                ends.append((j, abs(across), end))
    return full, ends


def lane_ids():
    return lax.broadcasted_iota(jnp.int32, (8, LANES), 1)


def field_of(refs, kind, index, at):
    adj, den, vel, mask = refs
    if kind == "pop":
        return adj[(index, *at)]
    if index == RHO:
        return den[(1, *at)]
    if index == KIND:
        return (mask[at] + 1).astype(jnp.float32)
    return vel[(1, index - UX, *at)]


def parity_of(axis):
    return lax.rem(lax.axis_index(axis), 2)


def on_side(parity, slot, act):
    @pl.when(parity == slot)
    def _():
        act(1)

    @pl.when(parity != slot)
    def _():
        act(0)


def has_partner(axis, slot):
    at = lax.axis_index(axis)
    to = at + jnp.where(lax.rem(at, 2) == slot, 1, -1)
    return (to >= 0) & (to < lax.axis_size(axis))


def pack_z_kernel(slots, adj_in, den_in, vel_in, mask_in, adj, den, vel, mask, near, *rest):
    packets, sems = rest[:slots], rest[slots]
    refs = (adj, den, vel, mask)
    ext_x, ext_y, _ = mask.shape
    starts = range(0, 19, 5)
    loads = [
        pltpu.make_async_copy(adj_in.at[start : min(start + 5, 19)], adj.at[start : min(start + 5, 19)], sems.at[at])
        for at, start in enumerate(starts)
    ] + [
        pltpu.make_async_copy(source, target, sems.at[len(starts) + at])
        for at, (source, target) in enumerate([(den_in, den), (vel_in, vel), (mask_in, mask)])
    ]
    for load in loads:
        load.start()
    lane = lane_ids()
    parity = parity_of("gz")
    parts = range(ext_y // 8)
    zero = jnp.zeros((8, LANES), jnp.float32)
    lows, highs = [[zero] * 3 for _ in parts], [[zero] * 3 for _ in parts]
    far_low, far_high = [zero for _ in parts], [zero for _ in parts]

    def gather(kind, index):
        for x, part in itertools.product(range(ext_x), parts):
            value = field_of(refs, kind, index, (x, pl.ds(8 * part, 8), slice(None)))
            if kind == "pop" and VELOCITIES[index][2] == 1:
                spot = GROUP * Z_UP.index(index) + 2 + x
                moved = pltpu.roll(value, spot, 1)
                lows[part][1] = jnp.where(lane == spot, moved, lows[part][1])
                far_low[part] = jnp.where(lane == spot + 1, moved, far_low[part])
            elif kind == "pop" and VELOCITIES[index][2] == -1:
                spot = GROUP * Z_DOWN.index(index) + 2 + x
                moved = pltpu.roll(value, spot, 1)
                highs[part][1] = jnp.where(lane == spot - 1, moved, highs[part][1])
                far_high[part] = jnp.where(lane == spot - 2, moved, far_high[part])
            else:
                tile, group = Z_PLACE[(kind, index)]
                spot = GROUP * group + 2 + x
                moved = pltpu.roll(value, spot, 1)
                lows[part][tile] = jnp.where(lane == spot, moved, lows[part][tile])
                highs[part][tile] = jnp.where(lane == spot - 1, moved, highs[part][tile])

    for start, load in zip(starts, loads):
        load.wait()
        for j in range(start, min(start + 5, 19)):
            gather("pop", j)
    for load in loads[len(starts) :]:
        load.wait()
    for k in range(5):
        gather("field", k)
    for part in parts:
        rows = pl.ds(8 * part, 8)
        low = lows[part]
        high = [pltpu.roll(tile, 1, 1) for tile in highs[part]]
        low[2] = jnp.where(lane < 5 * GROUP, pltpu.roll(far_low[part], LANES - 1, 1), low[2])
        high[2] = jnp.where(lane < 5 * GROUP, pltpu.roll(far_high[part], 2, 1), high[2])
        near[0, rows, :] = low[1]
        near[1, rows, :] = high[1]
        for slot in range(slots):
            there = has_partner("gz", slot)
            for tile in range(3):
                value = jnp.where(parity == slot, high[tile], low[tile])
                packets[slot][tile, rows, :] = jnp.where(there, value, 0.0)


def pack_lines(refs, first, packets, many_x, many_y, wanted, shares):
    to_x, y_lines = packets[:many_x], packets[many_x : many_x + many_y]
    to_xy = packets[many_x + many_y :]
    ext_x, ext_y, _ = refs[-1].shape
    every = slice(None)
    px, py = parity_of("gx"), parity_of("gy")

    def line_of(kind, index, x, y):
        if kind == "pop":
            return first[index, x + 2, y + 8 : y + 9, :]
        return field_of(refs, kind, index, (x, slice(y, y + 1), every))

    def pack_xy(slot_x, slot_y, side_x, side_y):
        packet = to_xy[many_x * slot_y + slot_x]
        for line, (kind, index, far_x, far_y) in enumerate(edge_lines(1 - 2 * side_x, 1 - 2 * side_y)):
            if wanted(kind, index):
                x = ext_x - 1 - far_x if side_x else far_x
                y = ext_y - 1 - far_y if side_y else far_y
                packet[line // 8, line % 8 : line % 8 + 1, :] = line_of(kind, index, x, y)

    def pack_y(slot, side):
        for line, (kind, index, depth) in enumerate(face_lines(1, 1 - 2 * side)):
            if wanted(kind, index):
                y = ext_y - 1 - depth if side else depth
                for x in range(ext_x):
                    y_lines[slot][line, x : x + 1, :] = line_of(kind, index, x, y)

    def pack_x(slot, side):
        full, ends = side_lines(0, 1 - 2 * side)
        for line, (kind, index) in enumerate(full):
            if kind == "field" and wanted(kind, index):
                to_x[slot][line] = field_of(refs, kind, index, (ext_x - 1 if side else 0, every, every))
            elif kind == "pop" and wanted(kind, index):
                to_x[slot][line] = first[index, (ext_x - 1 if side else 0) + 2, pl.ds(8, ext_y), :]
            elif kind == "share" and shares is not None:
                to_x[slot][line] = shares[side, index]
        for spot, (index, depth, end) in enumerate(ends):
            if wanted("pop", index):
                x = ext_x - 1 - depth if side else depth
                to_x[slot][SIDE - 1, spot : spot + 1, :] = line_of("pop", index, x, ext_y - 1 if end else 0)

    def when_there(there, packet, act):
        pl.when(there)(act)
        if shares is None:

            @pl.when(jnp.logical_not(there))
            def _():
                packet[...] = jnp.zeros(packet.shape, jnp.float32)

    for slot_y in range(many_y):
        there_y = has_partner("gy", slot_y)
        when_there(there_y, y_lines[slot_y], lambda: on_side(py, slot_y, functools.partial(pack_y, slot_y)))
        for slot_x in range(many_x):
            when_there(
                there_y & has_partner("gx", slot_x),
                to_xy[many_x * slot_y + slot_x],
                lambda: on_side(
                    py,
                    slot_y,
                    lambda side_y: on_side(px, slot_x, lambda side_x: pack_xy(slot_x, slot_y, side_x, side_y)),
                ),
            )
    for slot_x in range(many_x):
        when_there(
            has_partner("gx", slot_x), to_x[slot_x], lambda: on_side(px, slot_x, functools.partial(pack_x, slot_x))
        )


def is_flat(kind, index):
    return kind == "field" or VELOCITIES[index][2] == 0


def shift_kernel(slots, adj, den, vel, mask, first, *packets):
    many_x, many_y = slots
    _, ext_x, ext_y, _ = adj.shape
    for j in range(19):
        cz = VELOCITIES[j][2]
        for x, part in itertools.product(range(ext_x), range(ext_y // 8)):
            value = adj[j, x, pl.ds(8 * part, 8), :]
            first[j, 2 + x, pl.ds(8 + 8 * part, 8), :] = pltpu.roll(value, -cz % LANES, 1) if cz else value
    pack_lines((None, den, vel, mask), first, packets, many_x, many_y, is_flat, None)


def pack_xy_kernel(slots, den, vel, mask, near, *rest):
    many_x, many_y, many_z = slots
    count = many_x + many_y + many_x * many_y
    from_z, rest = rest[:many_z], rest[many_z + 1 + count :]
    z_set, first, packets, faces, shares = rest[0], rest[1], rest[2 : 2 + count], rest[-2], rest[-1]
    to_x, y_lines, to_xy = packets[:many_x], packets[many_x : many_x + many_y], packets[many_x + many_y :]
    to_y = rest[2 + count : -2]
    ext_x, ext_y = first.shape[1] - 4, near.shape[1]
    spot = lane_ids() % GROUP
    px, py, pz = parity_of("gx"), parity_of("gy"), parity_of("gz")

    z_set[OWN_LOW] = near[0]
    z_set[OWN_HIGH] = near[1]
    for tile in range(3):
        even = from_z[0][tile]
        odd = from_z[1][tile] if many_z > 1 else jnp.zeros_like(even)
        z_set[ABOVE + tile] = jnp.where(pz == 0, even, odd)
        z_set[BELOW + tile] = jnp.where(pz == 0, odd, even)

    for j in Z_UP + Z_DOWN:
        up = VELOCITIES[j][2] > 0
        group = (Z_UP if up else Z_DOWN).index(j)
        last = LANES - 1 if up else 0
        for part in range(ext_y // 8):
            halo = z_set[(ABOVE if up else BELOW) + 1, pl.ds(8 * part, 8), :]
            for x in range(ext_x):
                edge = pltpu.roll(halo, (last - 2 - GROUP * group - x) % LANES, 1)
                first[j, 2 + x, pl.ds(8 + 8 * part, 8), last : last + 1] = edge[:, last : last + 1]


    sub = lax.broadcasted_iota(jnp.int32, (8, LANES), 0)
    loaded = []
    for side, part in itertools.product(range(2), range(ext_y // 8)):
        toward, x = 1 - 2 * side, ext_x - 1 if side else 0
        pulled = []
        for j in range(19):
            cx, cy, _ = VELOCITIES[j]
            if cx == -toward:
                pulled.append(jnp.zeros((8, LANES), jnp.float32))
                continue
            value = first[j, x + 2 + cx, pl.ds(8 + 8 * part + cy, 8), :]
            if cy == -1 and part == 0:
                value = jnp.where(sub == 0, 0.0, value)
            if cy == 1 and part == ext_y // 8 - 1:
                value = jnp.where(sub == 7, 0.0, value)
            pulled.append(value)
        at = (x, pl.ds(8 * part, 8), slice(None))
        here = [den[(1, *at)], vel[(1, 0, *at)], vel[(1, 1, *at)], vel[(1, 2, *at)], mask[at] > 0]
        loaded.append((side, part, pulled, here))
    for side, part, pulled, (rho, ux, uy, uz, fluid) in loaded:
        wanted = pops(0, 1 - 2 * side)
        after, _ = collide(pulled, 1.0 / rho, rho, ux, uy, uz, None, wanted)
        for line, j in enumerate(wanted):
            shares[side, line, pl.ds(8 * part, 8), :] = jnp.where(fluid, after[j], 0.0)

    pack_lines((mask,), first, packets, many_x, many_y, lambda kind, index: not is_flat(kind, index), shares)

    for side in range(2):
        for part in range(ext_y // 8):
            rows = pl.ds(8 * part, 8)
            value = jnp.zeros((8, LANES), jnp.float32)
            for tile in range(Z_TILES):
                start = ext_x if side else 2
                moved = pltpu.roll(z_set[tile, rows, :], (2 * tile - start) % LANES, 1)
                value = jnp.where(spot // 2 == tile, moved, value)
            faces[side, rows, :] = value

    def add_xy(slot_x, slot_y, side_x, side_y):
        start = ext_y - 2 if side_y else 0
        to_xy[many_x * slot_y + slot_x][EDGE // 8, 0:2, :] = faces[side_x, start : start + 2, :]

    def add_y(slot, side):
        toward = 1 - 2 * side
        lines = {name: line for line, name in enumerate(face_lines(1, toward))}
        pulled = []
        for j in range(19):
            cx, cy, _ = VELOCITIES[j]
            if cy == -toward:
                pulled.append(jnp.zeros((8, LANES), jnp.float32))
                continue
            value = y_lines[slot][lines[("pop", j, abs(cy))]]
            if cx:
                value = jnp.where(sub == (7 if cx > 0 else 0), 0.0, pltpu.roll(value, -cx % 8, 0))
            pulled.append(value)
        rho, ux, uy, uz, kind = [y_lines[slot][lines[("field", k, 0)]] for k in range(5)]
        after, _ = collide(pulled, 1.0 / rho, rho, ux, uy, uz, None, pops(1, toward))
        full, ends = side_lines(1, toward)
        for line, (what, index) in enumerate(full):
            if what == "share":
                to_y[slot][line] = jnp.where(kind > 1.5, after[pops(1, toward)[index]], 0.0)
            else:
                to_y[slot][line] = y_lines[slot][lines[(what, index, 0)]]
        for spot, (index, depth, end) in enumerate(ends):
            x = ext_x - 1 if end else 0
            to_y[slot][SIDE - 1, spot : spot + 1, :] = y_lines[slot][lines[("pop", index, depth)], x : x + 1, :]
        start = ext_y - 2 if side else 0
        for tile in range(Z_TILES):
            row = 2 * tile % 8
            to_y[slot][SIDE + tile // 4, row : row + 2, :] = z_set[tile, start : start + 2, :]

    def add_x(slot, side):
        to_x[slot][SIDE] = faces[side]

    for slot_y in range(many_y):
        there_y = has_partner("gy", slot_y)
        pl.when(there_y)(lambda: on_side(py, slot_y, functools.partial(add_y, slot_y)))

        @pl.when(jnp.logical_not(there_y))
        def _():
            to_y[slot_y][...] = jnp.zeros(to_y[slot_y].shape, jnp.float32)

        for slot_x in range(many_x):
            pl.when(there_y & has_partner("gx", slot_x))(
                lambda: on_side(
                    py,
                    slot_y,
                    lambda side_y: on_side(px, slot_x, lambda side_x: add_xy(slot_x, slot_y, side_x, side_y)),
                )
            )
    for slot_x in range(many_x):
        pl.when(has_partner("gx", slot_x))(lambda: on_side(px, slot_x, functools.partial(add_x, slot_x)))


def collide(pulled, inverse, rho, ux, uy, uz, fluid, wanted):
    total = {}
    diff = {}
    for j in range(1, 19, 2):
        total[j] = pulled[j] + pulled[j + 1]
        diff[j] = pulled[j] - pulled[j + 1]
    in_xy, in_xz, in_yz = total[7] + total[9], total[11] + total[13], total[15] + total[17]
    two_x, two_y, two_z = total[1] + total[1], total[3] + total[3], total[5] + total[5]
    count = (12.0 * pulled[0] + (two_x + two_y)) + (two_z + (in_xy + (in_xz + in_yz)))
    flow_x = (diff[1] + diff[1]) + ((diff[7] + diff[9]) + (diff[11] + diff[13]))
    flow_y = (diff[3] + diff[3]) + ((diff[7] - diff[9]) + (diff[15] + diff[17]))
    flow_z = (diff[5] + diff[5]) + ((diff[11] - diff[13]) + (diff[15] - diff[17]))
    xx, yy, zz = two_x + (in_xy + in_xz), two_y + (in_xy + in_yz), two_z + (in_xz + in_yz)
    xy, xz, yz = total[7] - total[9], total[11] - total[13], total[15] - total[17]
    push_x = xx * ux + xy * uy + xz * uz
    push_y = xy * ux + yy * uy + yz * uz
    push_z = xz * ux + yz * uy + zz * uz
    usq = ux * ux + uy * uy + uz * uz
    push = ux * push_x + uy * push_y + uz * push_z
    base = count * (OMEGA / 36.0 + (OMEGA / 24.0) * usq) - (OMEGA / 8.0) * push - ux * inverse
    along_x = (OMEGA / 12.0) * (flow_x + 3.0 * push_x - ux * count) + inverse
    along_y = (OMEGA / 12.0) * (flow_y + 3.0 * push_y - uy * count)
    along_z = (OMEGA / 12.0) * (flow_z + 3.0 * push_z - uz * count)
    parts = {
        1: along_x,
        3: along_y,
        5: along_z,
        7: along_x + along_y,
        9: along_x - along_y,
        11: along_x + along_z,
        13: along_x - along_z,
        15: along_y + along_z,
        17: along_y - along_z,
    }
    out = {}
    for j in wanted:
        if j == 0:
            shift = base
        elif j % 2:
            shift = base + parts[j]
        else:
            shift = base - parts[j - 1]
        out[j] = (1.0 - OMEGA) * pulled[j] + shift
        if fluid is not None:
            out[j] = jnp.where(fluid, out[j], pulled[OPPOSITE[j]])
    change = (-1.0 / 6.0) * rho * (flow_x * ux + flow_y * uy + flow_z * uz)
    return out, change if fluid is None else jnp.where(fluid, change, 0.0)


def only(value, row):
    return jnp.where(lax.broadcasted_iota(jnp.int32, (8, LANES), 0) == row, value, 0.0)


class Plane:
    def rim(self, shares, line, toward):
        if toward != (-1 if self.row < 0 else 1):
            return 0.0
        return only(shares[line, self.x, pl.ds(8 + self.row, 8), :], 0 if toward < 0 else 1)

    def __init__(self, x, row):
        self.x, self.row = x, row

    def load(self, ref, lead, margin, cx=0, cy=0):
        return ref[lead, self.x + margin + cx, pl.ds(8 + self.row + cy, 8), :]

    def store(self, ref, lead, margin, value):
        ref[lead, self.x + margin, pl.ds(8 + self.row, 8), :] = value


class Rim:
    def __init__(self, x, ext_y):
        self.x, self.ext_y = x, ext_y

    def rim(self, shares, line, toward):
        start = 1 if toward < 0 else 8 + self.ext_y - 1
        return only(shares[line, self.x, pl.ds(start, 8), :], 6 if toward < 0 else 1)

    def load(self, ref, lead, margin, cx=0, cy=0):
        at = self.x + margin + cx
        upper = ref[lead, at, pl.ds(8 + self.ext_y - 1 + cy, 8), :]
        lower = ref[lead, at, pl.ds(1 + cy, 8), :]
        return jnp.where(lax.broadcasted_iota(jnp.int32, (8, LANES), 0) < 4, upper, lower)

    def store(self, ref, lead, margin, value):
        at = self.x + margin
        ref[lead, at, pl.ds(8 + self.ext_y - 1, 2), :] = value[0:2]
        ref[lead, at, pl.ds(7, 2), :] = value[6:8]


def first_step(first, fields, second, change, tiles, outside=True, shares=None, y_shares=None):
    loaded = [
        (
            [tile.load(first, j, 2, *VELOCITIES[j][:2]) for j in range(19)],
            [tile.load(fields, k, 1) for k in range(5)],
        )
        for tile in tiles
    ]
    done = [
        collide(pulled, 1.0 / rho, rho, ux, uy, uz, kind > 1.5, range(19))
        for pulled, (rho, ux, uy, uz, kind) in loaded
    ]
    for tile, (_, here), (after, gain) in zip(tiles, loaded, done):
        inside = here[KIND] > 0.5
        side = None if shares is None else {-1: 0, second.shape[1] - 2: 1}.get(tile.x)
        for j in range(19):
            value = after[j]
            if side is not None and VELOCITIES[j][0] == 2 * side - 1:
                value = value + shares[side, pops(0, 2 * side - 1).index(j), pl.ds(8 + tile.row, 8), :]
            if side is None and y_shares is not None and VELOCITIES[j][1]:
                value = value + tile.rim(y_shares, pops(1, VELOCITIES[j][1]).index(j), VELOCITIES[j][1])
            if outside:
                value = jnp.where(inside, value, 0.0)
            cz = VELOCITIES[j][2]
            tile.store(second, j, 1, pltpu.roll(value, -cz % LANES, 1) if cz else value)
        tile.store(change, 0, 1, gain)


def inner_kernel(den, vel, mask, first, fields, second, change):
    refs = (None, den, vel, mask)
    ext_x, ext_y, _ = mask.shape
    every = slice(None)
    for k in range(5):
        fields[k, 1 : 1 + ext_x, pl.ds(8, ext_y), :] = field_of(refs, "field", k, (every, every, every))

    many = 3 if (ext_x - 2) % 3 == 0 else 1

    @pl.loop(0, (ext_x - 2) // many)
    def _(group):
        tiles = [Plane(many * group + at + 1, 1 + 8 * part) for at in range(many) for part in range(ext_y // 8)]
        first_step(first, fields, second, change, tiles, outside=False)


def put_row(first, fields, kind, index, x, y, value):
    row = y + 8
    if kind == "pop":
        first[index, x + 2, row : row + 1, :] = value
    else:
        fields[index, x + 1, row : row + 1, :] = value


def place_z(z_first, value, start, size, side, ext_x):
    rows = pl.ds(start, size)
    spot = lane_ids()[:size] % GROUP
    inside = spot >= 2 + ext_x if side else spot < 2
    for tile in range(Z_TILES):
        shift = (2 + ext_x if side else 0) - 2 * tile
        moved = pltpu.roll(value, shift % LANES, 1)[:size]
        z_first[tile, rows, :] = jnp.where(inside, moved, z_first[tile, rows, :])


def side_kernel(slots, z_set, *rest):
    many_x, many_y = slots
    from_x, from_y = rest[4 : 4 + many_x], rest[4 + many_x : 4 + many_x + many_y]
    first, fields, second, change, z_first, shares, y_shares = rest[-7:]
    _, ext_y, _ = z_set.shape
    ext_x = change.shape[1] - 2
    inner = pl.ds(8, ext_y)
    put = functools.partial(put_row, first, fields)
    z_first[:, inner, :] = z_set[...]

    def place_y(slot, side):
        packet = from_y[slot]
        toward = 2 * side - 1
        near = ext_y if side else -1
        nothing = jnp.zeros((1, LANES), jnp.float32)
        full, ends = side_lines(1, toward)
        for x in range(ext_x):
            for j in pops(1, 0):
                put("pop", j, x, near, nothing)
            for j in pops(1, toward):
                put("pop", j, x, near + toward, nothing)
            put("field", RHO, x, near, jnp.full((1, LANES), jnp.inf, jnp.float32))
            for line, (kind, index) in enumerate(full):
                if kind == "share":
                    y_shares[index, x, near + 8 : near + 9, :] = packet[line, x : x + 1, :]
                else:
                    put(kind, index, x, near, packet[line, x : x + 1, :])
        for spot, (index, depth, end) in enumerate(ends):
            put("pop", index, ext_x - 1 if end else 0, near + toward * depth, packet[SIDE - 1, spot : spot + 1, :])
        start = 8 + ext_y if side else 6
        for tile in range(Z_TILES):
            row = 2 * tile % 8
            z_first[tile, start : start + 2, :] = packet[SIDE + tile // 4, row : row + 2, :]
        if many_y == 1:
            clear_y(1 - side)

    def clear_y(side):
        nothing = jnp.zeros((1, LANES), jnp.float32)
        y = ext_y if side else -1
        for x in range(-2, ext_x + 2):
            for j in pops(1, 2 * side - 1):
                put("pop", j, x, y, nothing)
        for x in range(-1, ext_x + 1):
            put("field", KIND, x, y, nothing)
        start = 8 + ext_y if side else 6
        for tile in range(Z_TILES):
            z_first[tile, start : start + 2, :] = jnp.zeros((2, LANES), jnp.float32)

    def place_x(slot, side):
        packet = from_x[slot]
        toward = 2 * side - 1
        near = ext_x if side else -1
        nothing = jnp.zeros((ext_y, LANES), jnp.float32)
        for j in pops(0, 0):
            first[j, near + 2, inner, :] = nothing
        for j in pops(0, toward):
            first[j, near + toward + 2, inner, :] = nothing
        fields[RHO, near + 1, inner, :] = jnp.full((ext_y, LANES), jnp.inf, jnp.float32)
        full, ends = side_lines(0, toward)
        for line, (kind, index) in enumerate(full):
            if kind == "pop":
                first[index, near + 2, inner, :] = packet[line]
            elif kind == "share":
                shares[side, index, inner, :] = packet[line]
            else:
                fields[index, near + 1, inner, :] = packet[line]
        for spot, (index, depth, end) in enumerate(ends):
            put("pop", index, near + toward * depth, ext_y - 1 if end else 0, packet[SIDE - 1, spot : spot + 1, :])
        for part in range(ext_y // 8):
            place_z(z_first, packet[SIDE, pl.ds(8 * part, 8), :], 8 + 8 * part, 8, side, ext_x)

    shares[:, :, pl.ds(0, 8), :] = jnp.zeros((2, 5, 8, LANES), jnp.float32)
    shares[:, :, pl.ds(8 + ext_y, 8), :] = jnp.zeros((2, 5, 8, LANES), jnp.float32)
    for slot_y in range(many_y):
        on_side(parity_of("gy"), slot_y, functools.partial(place_y, slot_y))
    for slot_x in range(many_x):
        on_side(parity_of("gx"), slot_x, functools.partial(place_x, slot_x))

    rims = range(7, ext_y - 8, 8)
    first_step(first, fields, second, change, [Plane(x, row) for x in (0, ext_x - 1) for row in rims], outside=False)
    first_step(first, fields, second, change, [Plane(x, row) for x in (-1, ext_x) for row in rims], shares=shares)

    many = 3 if (ext_x - 2) % 3 == 0 else 1

    @pl.loop(0, (ext_x - 2) // many)
    def _(group):
        tiles = [Rim(many * group + at + 1, ext_y) for at in range(many)]
        first_step(first, fields, second, change, tiles, y_shares=y_shares)


def last_kernel(slots, den, vel, mask, *rest):
    many_x, many_y = slots
    from_xy = rest[7 : 7 + many_x * many_y]
    out, sens, first, fields, second, change, z_first, shares, y_shares = rest[-13:-4]
    z_second, held, held_sens, sems = rest[-4:]
    ext_x, ext_y, _ = mask.shape
    lane = lane_ids()
    every = slice(None)
    px, py = parity_of("gx"), parity_of("gy")

    def place_xy(slot_x, slot_y, side_x, side_y):
        packet = from_xy[many_x * slot_y + slot_x]
        for line, (kind, index, far_x, far_y) in enumerate(edge_lines(2 * side_x - 1, 2 * side_y - 1)):
            x = ext_x + far_x if side_x else -1 - far_x
            y = ext_y + far_y if side_y else -1 - far_y
            put_row(first, fields, kind, index, x, y, packet[line // 8, line % 8 : line % 8 + 1, :])
        place_z(z_first, packet[EDGE // 8], 8 + ext_y if side_y else 6, 2, side_x, ext_x)

    for slot_x in range(many_x):
        for slot_y in range(many_y):
            on_side(
                py,
                slot_y,
                lambda side_y: on_side(px, slot_x, lambda side_x: place_xy(slot_x, slot_y, side_x, side_y)),
            )

    for pair in ((-1, 0), (ext_x - 1, ext_x)):
        tiles = [Plane(x, row) for x in pair for row in (-1, ext_y - 1)]
        first_step(first, fields, second, change, tiles, shares=shares, y_shares=y_shares)

    starts = [7 + 8 * part for part in range((ext_y + 2 + 7) // 8)]
    loaded = []
    for row in starts:

        def both(low_tile, high_tile, group, cx, cy):
            rows = pl.ds(row + cy, 8)
            low = pltpu.roll(z_first[low_tile, rows, :], (-GROUP * group - cx) % LANES, 1)
            high = pltpu.roll(z_first[high_tile, rows, :], (LANES // 2 - GROUP * group - cx) % LANES, 1)
            return jnp.where(lane < LANES // 2, low, high)

        pulled = []
        for j in range(19):
            cx, cy, cz = VELOCITIES[j]
            if cz == 0:
                tile, group = Z_PLACE[("pop", j)]
                pulled.append(both(BELOW + tile, ABOVE + tile, group, cx, cy))
            elif cz == 1:
                pulled.append(both(OWN_LOW, ABOVE + 2, Z_UP.index(j), cx, cy))
            else:
                pulled.append(both(BELOW + 2, OWN_HIGH, Z_DOWN.index(j), cx, cy))
        places = [Z_PLACE[("field", k)] for k in range(5)]
        loaded.append((pulled, [both(BELOW + tile, ABOVE + tile, group, 0, 0) for tile, group in places]))
    done = [
        collide(pulled, 1.0 / rho, rho, ux, uy, uz, kind > 1.5, Z_UP + Z_DOWN)[0]
        for pulled, (rho, ux, uy, uz, kind) in loaded
    ]
    for row, (_, here), after in zip(starts, loaded, done):
        for group in range(5):
            value = jnp.where(lane < LANES // 2, after[Z_DOWN[group]], after[Z_UP[group]])
            z_second[group, pl.ds(row, 8), :] = jnp.where(here[KIND] > 0.5, value, 0.0)

    def copies(x):
        return (
            pltpu.make_async_copy(held.at[:, x], out.at[:, x], sems.at[0, x]),
            pltpu.make_async_copy(held_sens.at[x], sens.at[x], sems.at[1, x]),
        )

    many = 4 if ext_x % 4 == 0 else 1

    @pl.loop(0, ext_x // many)
    def _(group):
        loaded = []
        planes = [many * group + at for at in range(many)]
        for x, part in itertools.product(planes, range(ext_y // 8)):
            row = 8 + 8 * part
            pulled = []
            for j in range(19):
                cx, cy, cz = VELOCITIES[j]
                rows = pl.ds(row + cy, 8)
                value = second[j, x + 1 + cx, rows, :]
                if cz == 1:
                    edge = z_second[Z_UP.index(j), rows, :]
                    edge = pltpu.roll(edge, LANES // 2 - 3 - cx - x, 1)
                    value = jnp.where(lane == LANES - 1, edge, value)
                elif cz == -1:
                    edge = z_second[Z_DOWN.index(j), rows, :]
                    edge = pltpu.roll(edge, LANES - 2 - cx - x, 1)
                    value = jnp.where(lane == 0, edge, value)
                pulled.append(value)
            at = (x, pl.ds(8 * part, 8), every)
            rho = den[(0, *at)]
            here = [1.0 / rho, rho, vel[(0, 0, *at)], vel[(0, 1, *at)], vel[(0, 2, *at)], mask[at] > 0]
            loaded.append((at, pulled, here, change[0, x + 1, pl.ds(row, 8), :]))
        done = [collide(pulled, *here, range(19)) for _, pulled, here, _ in loaded]
        for (at, _, _, before), (after, gain) in zip(loaded, done):
            for j in range(19):
                held[(j, *at)] = after[j]
            held_sens[at] = before + gain
        for x in planes:
            for copy in copies(x):
                copy.start()

    for x in range(ext_x):
        for copy in copies(x):
            copy.wait()


def shards(adjoint, density, velocity, pore_mask):
    ext_x, ext_y, ext_z = pore_mask.shape
    assert ext_z == LANES and ext_y % 8 == 0 and ext_x + 4 <= GROUP and ext_x == 8
    many_x = 2
    many_y, many_z = [1 if lax.axis_size(axis) == 2 else 2 for axis in ("gy", "gz")]
    vmem = pl.BlockSpec(memory_space=pltpu.VMEM)
    hbm = pl.BlockSpec(memory_space=pltpu.HBM)
    inputs = (adjoint, density, velocity, pore_mask)

    def array(*shape):
        return jax.ShapeDtypeStruct(shape, jnp.float32)

    def call(kernel, name, operands, shapes, limit, **more):
        more.setdefault("out_specs", [vmem] * len(shapes))
        more.setdefault("in_specs", [vmem] * len(operands))
        params = pltpu.CompilerParams(vmem_limit_bytes=limit * 1024 * 1024)
        return pl.pallas_call(kernel, out_shape=shapes, compiler_params=params, name=name, **more)(*operands)

    def partners(axis, slot):
        found = {}
        for at in range(slot, lax.axis_size(axis) - 1, 2):
            found[at], found[at + 1] = at + 1, at
        return found

    def ends(axis):
        last = lax.axis_size(axis) - 1
        return {0: last, last: 0}

    def swap(value, spares, *places):
        tables = {axis: partners(axis, slot) for axis, slot in places}
        axes = [axis for axis in ("gx", "gy", "gz") if axis in tables or axis in dict(spares)]
        sizes = [lax.axis_size(axis) for axis in axes]
        pairs = []
        for at in itertools.product(*[range(size) for size in sizes]):
            to = [tables.get(axis, {}).get(spot, spot) for axis, spot in zip(axes, at)]
            for spare, table in spares:
                if tuple(to) == at:
                    to = [table.get(spot, spot) if axis == spare else spot for axis, spot in zip(axes, at)]
            flat = []
            for spots in (at, to):
                index = 0
                for size, spot in zip(sizes, spots):
                    index = index * size + spot
                flat.append(index)
            pairs.append(tuple(flat))
        return lax.ppermute(value, tuple(axes), pairs)

    loaded = [jax.ShapeDtypeStruct(value.shape, value.dtype) for value in inputs]
    *held, near, a_z, b_z = (
        *call(
            functools.partial(pack_z_kernel, many_z),
            "pack_z",
            [pltpu.with_memory_space_constraint(value, pltpu.HBM) for value in inputs],
            loaded + [array(2, ext_y, LANES)] + [array(3, ext_y, LANES)] * many_z,
            8,
            in_specs=[hbm] * 4,
            scratch_shapes=[pltpu.SemaphoreType.DMA((7,))],
        ),
        *[None] * (2 - many_z),
    )
    from_z = [swap(value, [("gx", partners("gx", 0))], ("gz", slot)) for slot, value in enumerate((a_z, b_z)[:many_z])]

    rows = ext_y + 16
    adj, den, vel, mask = held
    shapes = (
        [array(19, ext_x + 4, rows, LANES)]
        + [array(SIDE + 1, ext_y, LANES)] * many_x
        + [array(FACE, ext_x, LANES)] * many_y
        + [array(EDGE // 8 + 1, 8, LANES)] * (many_x * many_y)
    )
    shifted = call(
        functools.partial(shift_kernel, (many_x, many_y)),
        "shift",
        (adj, den, vel, mask),
        shapes,
        8,
        cost_estimate=pl.CostEstimate(flops=1_000_000, bytes_accessed=2_500_000, transcendentals=0),
    )
    z_set, first, *packets = call(
        functools.partial(pack_xy_kernel, (many_x, many_y, many_z)),
        "pack_xy",
        (den, vel, mask, near, *from_z, *shifted),
        [array(Z_TILES, ext_y, LANES)] + shapes + [array(SIDE + 2, ext_x, LANES)] * many_y,
        8,
        input_output_aliases={4 + many_z + at: 1 + at for at in range(len(shapes))},
        scratch_shapes=[
            pltpu.VMEM((2, ext_y, LANES), jnp.float32),
            pltpu.VMEM((2, 5, ext_y, LANES), jnp.float32),
        ],
    )
    to_x, to_xy, to_y = packets[:many_x], packets[many_x + many_y : -many_y], packets[-many_y:]
    from_xy = [
        swap(to_xy[many_x * slot_y + slot_x], [], ("gx", slot_x), ("gy", slot_y))
        for slot_y in range(many_y)
        for slot_x in range(many_x)
    ]
    from_y = [swap(value, [("gz", partners("gz", 0))], ("gy", slot)) for slot, value in enumerate(to_y)]
    spares = [("gy", partners("gy", 0))]
    from_x = [swap(value, spares, ("gx", slot)) for slot, value in enumerate(to_x)]

    fields, second, change = call(
        inner_kernel,
        "inner_step",
        (den, vel, mask, first),
        [array(5, ext_x + 2, rows, LANES), array(19, ext_x + 2, rows, LANES), array(1, ext_x + 2, rows, LANES)],
        8,
        cost_estimate=pl.CostEstimate(flops=40_000_000, bytes_accessed=8_000_000, transcendentals=0),
    )
    inout = (first, fields, second, change)
    inout = call(
        functools.partial(side_kernel, (many_x, many_y)),
        "side_step",
        (z_set, *inout, *from_x, *from_y),
        [array(*value.shape) for value in inout] + [array(Z_TILES, rows, LANES), array(2, 5, rows, LANES), array(5, ext_x, rows, LANES)],
        8,
        input_output_aliases={1 + at: at for at in range(4)},
        cost_estimate=pl.CostEstimate(flops=40_000_000, bytes_accessed=8_000_000, transcendentals=0),
    )
    return call(
        functools.partial(last_kernel, (many_x, many_y)),
        "last_steps",
        (den, vel, mask, *inout, *from_xy),
        [array(19, ext_x, ext_y, LANES), array(ext_x, ext_y, LANES)] + [array(*value.shape) for value in inout],
        8,
        out_specs=[hbm] * 2 + [vmem] * 7,
        input_output_aliases={3 + at: 2 + at for at in range(7)},
        scratch_shapes=[
            pltpu.VMEM((5, rows, LANES), jnp.float32),
            pltpu.VMEM((19, ext_x, ext_y, LANES), jnp.float32),
            pltpu.VMEM((ext_x, ext_y, LANES), jnp.float32),
            pltpu.SemaphoreType.DMA((2, ext_x)),
        ],
    )[:2]


def solution(mesh):
    placed = (
        P(None, "gx", "gy", "gz"),
        P(None, "gx", "gy", "gz"),
        P(None, None, "gx", "gy", "gz"),
        P("gx", "gy", "gz"),
    )

    def whole(*arrays):
        return tuple(shards(*arrays))

    return jax.shard_map(
        whole,
        mesh=mesh,
        in_specs=placed,
        out_specs=(P(None, "gx", "gy", "gz"), P("gx", "gy", "gz")),
        check_vma=False,
    )
```

```python
import functools
import itertools

import jax
import jax.numpy as jnp
from jax import lax
from jax.experimental import pallas as pl
from jax.experimental.pallas import tpu as pltpu
from jax.sharding import PartitionSpec as P

VELOCITIES = [
    (0, 0, 0),
    (1, 0, 0),
    (-1, 0, 0),
    (0, 1, 0),
    (0, -1, 0),
    (0, 0, 1),
    (0, 0, -1),
    (1, 1, 0),
    (-1, -1, 0),
    (1, -1, 0),
    (-1, 1, 0),
    (1, 0, 1),
    (-1, 0, -1),
    (1, 0, -1),
    (-1, 0, 1),
    (0, 1, 1),
    (0, -1, -1),
    (0, 1, -1),
    (0, -1, 1),
]
OPPOSITE = [0, 2, 1, 4, 3, 6, 5, 8, 7, 10, 9, 12, 11, 14, 13, 16, 15, 18, 17]
OMEGA = 1.25
LANES = 128
GROUP = 16


def pops(axis, sign):
    return [j for j in range(19) if VELOCITIES[j][axis] == sign]


def mirrored(j):
    cx, cy, cz = VELOCITIES[j]
    return VELOCITIES.index((cx, cy, -cz))


Z_FLAT = pops(2, 0)
Z_UP = pops(2, 1)
Z_DOWN = [mirrored(j) for j in Z_UP]
RHO, UX, UY, UZ, KIND = range(5)
Z_PLACE = {("pop", j): (0, g) for g, j in enumerate(Z_FLAT[:8])}
Z_PLACE[("pop", Z_FLAT[8])] = (1, 5)
Z_PLACE[("field", RHO)] = (1, 6)
Z_PLACE[("field", KIND)] = (1, 7)
Z_PLACE[("field", UX)] = (2, 5)
Z_PLACE[("field", UY)] = (2, 6)
Z_PLACE[("field", UZ)] = (2, 7)
BELOW, ABOVE, OWN_LOW, OWN_HIGH, Z_TILES = 0, 3, 6, 7, 8


def face_lines(axis, toward):
    near = pops(axis, 0) + pops(axis, toward)
    lines = [("pop", j, 0) for j in near] + [("field", k, 0) for k in range(5)]
    return lines + [("pop", j, 1) for j in pops(axis, toward)]


def edge_lines(toward_x, toward_y):
    lines = [("field", k, 0, 0) for k in range(5)]
    for j in range(19):
        cx, cy, _ = VELOCITIES[j]
        if cx not in (0, toward_x) or cy not in (0, toward_y):
            continue
        lines.append(("pop", j, 0, 0))
        if cx:
            lines.append(("pop", j, 1, 0))
        if cy:
            lines.append(("pop", j, 0, 1))
        if cx and cy:
            lines.append(("pop", j, 1, 1))
    return lines


FACE = 24
EDGE = 24
SIDE = 15


def side_lines(axis, toward):
    full = [("pop", j) for j in pops(axis, toward)] + [("share", p) for p in range(5)]
    full += [("field", k) for k in (UX, UY, UZ, KIND)]
    ends = []
    for end in range(2):
        for j in pops(1 - axis, 1 - 2 * end):
            across = VELOCITIES[j][axis]
            if across in (0, toward):
                ends.append((j, abs(across), end))
    return full, ends


def lane_ids():
    return lax.broadcasted_iota(jnp.int32, (8, LANES), 1)


def field_of(refs, kind, index, at):
    adj, den, vel, mask = refs
    if kind == "pop":
        return adj[(index, *at)]
    if index == RHO:
        return den[(1, *at)]
    if index == KIND:
        return (mask[at] + 1).astype(jnp.float32)
    return vel[(1, index - UX, *at)]


def parity_of(axis):
    return lax.rem(lax.axis_index(axis), 2)


def on_side(parity, slot, act):
    @pl.when(parity == slot)
    def _():
        act(1)

    @pl.when(parity != slot)
    def _():
        act(0)


def has_partner(axis, slot):
    at = lax.axis_index(axis)
    to = at + jnp.where(lax.rem(at, 2) == slot, 1, -1)
    return (to >= 0) & (to < lax.axis_size(axis))


def pack_z_kernel(slots, adj_in, den_in, vel_in, mask_in, adj, den, vel, mask, near, *rest):
    packets, sems = rest[:slots], rest[slots]
    refs = (adj, den, vel, mask)
    ext_x, ext_y, _ = mask.shape
    starts = range(0, 19, 5)
    loads = [
        pltpu.make_async_copy(adj_in.at[start : min(start + 5, 19)], adj.at[start : min(start + 5, 19)], sems.at[at])
        for at, start in enumerate(starts)
    ] + [
        pltpu.make_async_copy(source, target, sems.at[len(starts) + at])
        for at, (source, target) in enumerate([(den_in, den), (vel_in, vel), (mask_in, mask)])
    ]
    for load in loads:
        load.start()
    lane = lane_ids()
    parity = parity_of("gz")
    parts = range(ext_y // 8)
    zero = jnp.zeros((8, LANES), jnp.float32)
    lows, highs = [[zero] * 3 for _ in parts], [[zero] * 3 for _ in parts]
    far_low, far_high = [zero for _ in parts], [zero for _ in parts]

    def gather(kind, index):
        for x, part in itertools.product(range(ext_x), parts):
            value = field_of(refs, kind, index, (x, pl.ds(8 * part, 8), slice(None)))
            if kind == "pop" and VELOCITIES[index][2] == 1:
                spot = GROUP * Z_UP.index(index) + 2 + x
                moved = pltpu.roll(value, spot, 1)
                lows[part][1] = jnp.where(lane == spot, moved, lows[part][1])
                far_low[part] = jnp.where(lane == spot + 1, moved, far_low[part])
            elif kind == "pop" and VELOCITIES[index][2] == -1:
                spot = GROUP * Z_DOWN.index(index) + 2 + x
                moved = pltpu.roll(value, spot, 1)
                highs[part][1] = jnp.where(lane == spot - 1, moved, highs[part][1])
                far_high[part] = jnp.where(lane == spot - 2, moved, far_high[part])
            else:
                tile, group = Z_PLACE[(kind, index)]
                spot = GROUP * group + 2 + x
                moved = pltpu.roll(value, spot, 1)
                lows[part][tile] = jnp.where(lane == spot, moved, lows[part][tile])
                highs[part][tile] = jnp.where(lane == spot - 1, moved, highs[part][tile])

    for start, load in zip(starts, loads):
        load.wait()
        for j in range(start, min(start + 5, 19)):
            gather("pop", j)
    for load in loads[len(starts) :]:
        load.wait()
    for k in range(5):
        gather("field", k)
    for part in parts:
        rows = pl.ds(8 * part, 8)
        low = lows[part]
        high = [pltpu.roll(tile, 1, 1) for tile in highs[part]]
        low[2] = jnp.where(lane < 5 * GROUP, pltpu.roll(far_low[part], LANES - 1, 1), low[2])
        high[2] = jnp.where(lane < 5 * GROUP, pltpu.roll(far_high[part], 2, 1), high[2])
        near[0, rows, :] = low[1]
        near[1, rows, :] = high[1]
        for slot in range(slots):
            there = has_partner("gz", slot)
            for tile in range(3):
                value = jnp.where(parity == slot, high[tile], low[tile])
                packets[slot][tile, rows, :] = jnp.where(there, value, 0.0)


def pack_lines(refs, first, packets, many_x, many_y, wanted, shares):
    to_x, y_lines = packets[:many_x], packets[many_x : many_x + many_y]
    to_xy = packets[many_x + many_y :]
    ext_x, ext_y, _ = refs[-1].shape
    every = slice(None)
    px, py = parity_of("gx"), parity_of("gy")

    def line_of(kind, index, x, y):
        if kind == "pop":
            return first[index, x + 2, y + 8 : y + 9, :]
        return field_of(refs, kind, index, (x, slice(y, y + 1), every))

    def pack_xy(slot_x, slot_y, side_x, side_y):
        packet = to_xy[many_x * slot_y + slot_x]
        for line, (kind, index, far_x, far_y) in enumerate(edge_lines(1 - 2 * side_x, 1 - 2 * side_y)):
            if wanted(kind, index):
                x = ext_x - 1 - far_x if side_x else far_x
                y = ext_y - 1 - far_y if side_y else far_y
                packet[line // 8, line % 8 : line % 8 + 1, :] = line_of(kind, index, x, y)

    def pack_y(slot, side):
        for line, (kind, index, depth) in enumerate(face_lines(1, 1 - 2 * side)):
            if wanted(kind, index):
                y = ext_y - 1 - depth if side else depth
                for x in range(ext_x):
                    y_lines[slot][line, x : x + 1, :] = line_of(kind, index, x, y)

    def pack_x(slot, side):
        full, ends = side_lines(0, 1 - 2 * side)
        for line, (kind, index) in enumerate(full):
            if kind == "field" and wanted(kind, index):
                to_x[slot][line] = field_of(refs, kind, index, (ext_x - 1 if side else 0, every, every))
            elif kind == "pop" and wanted(kind, index):
                to_x[slot][line] = first[index, (ext_x - 1 if side else 0) + 2, pl.ds(8, ext_y), :]
            elif kind == "share" and shares is not None:
                to_x[slot][line] = shares[side, index]
        for spot, (index, depth, end) in enumerate(ends):
            if wanted("pop", index):
                x = ext_x - 1 - depth if side else depth
                to_x[slot][SIDE - 1, spot : spot + 1, :] = line_of("pop", index, x, ext_y - 1 if end else 0)

    def when_there(there, packet, act):
        pl.when(there)(act)
        if shares is None:

            @pl.when(jnp.logical_not(there))
            def _():
                packet[...] = jnp.zeros(packet.shape, jnp.float32)

    for slot_y in range(many_y):
        there_y = has_partner("gy", slot_y)
        when_there(there_y, y_lines[slot_y], lambda: on_side(py, slot_y, functools.partial(pack_y, slot_y)))
        for slot_x in range(many_x):
            when_there(
                there_y & has_partner("gx", slot_x),
                to_xy[many_x * slot_y + slot_x],
                lambda: on_side(
                    py,
                    slot_y,
                    lambda side_y: on_side(px, slot_x, lambda side_x: pack_xy(slot_x, slot_y, side_x, side_y)),
                ),
            )
    for slot_x in range(many_x):
        when_there(
            has_partner("gx", slot_x), to_x[slot_x], lambda: on_side(px, slot_x, functools.partial(pack_x, slot_x))
        )


def is_flat(kind, index):
    return kind == "field" or VELOCITIES[index][2] == 0


def shift_kernel(slots, adj, den, vel, mask, first, *packets):
    many_x, many_y = slots
    _, ext_x, ext_y, _ = adj.shape
    for j in range(19):
        cz = VELOCITIES[j][2]
        for x, part in itertools.product(range(ext_x), range(ext_y // 8)):
            value = adj[j, x, pl.ds(8 * part, 8), :]
            first[j, 2 + x, pl.ds(8 + 8 * part, 8), :] = pltpu.roll(value, -cz % LANES, 1) if cz else value
    pack_lines((None, den, vel, mask), first, packets, many_x, many_y, is_flat, None)


def pack_xy_kernel(slots, den, vel, mask, near, *rest):
    many_x, many_y, many_z = slots
    count = many_x + many_y + many_x * many_y
    from_z, rest = rest[:many_z], rest[many_z + 1 + count :]
    z_set, first, packets, faces, shares = rest[0], rest[1], rest[2 : 2 + count], rest[-2], rest[-1]
    to_x, y_lines, to_xy = packets[:many_x], packets[many_x : many_x + many_y], packets[many_x + many_y :]
    to_y = rest[2 + count : -2]
    ext_x, ext_y = first.shape[1] - 4, near.shape[1]
    spot = lane_ids() % GROUP
    px, py, pz = parity_of("gx"), parity_of("gy"), parity_of("gz")

    z_set[OWN_LOW] = near[0]
    z_set[OWN_HIGH] = near[1]
    for tile in range(3):
        even = from_z[0][tile]
        odd = from_z[1][tile] if many_z > 1 else jnp.zeros_like(even)
        z_set[ABOVE + tile] = jnp.where(pz == 0, even, odd)
        z_set[BELOW + tile] = jnp.where(pz == 0, odd, even)

    for j in Z_UP + Z_DOWN:
        up = VELOCITIES[j][2] > 0
        group = (Z_UP if up else Z_DOWN).index(j)
        last = LANES - 1 if up else 0
        for part in range(ext_y // 8):
            halo = z_set[(ABOVE if up else BELOW) + 1, pl.ds(8 * part, 8), :]
            for x in range(ext_x):
                edge = pltpu.roll(halo, (last - 2 - GROUP * group - x) % LANES, 1)
                first[j, 2 + x, pl.ds(8 + 8 * part, 8), last : last + 1] = edge[:, last : last + 1]


    sub = lax.broadcasted_iota(jnp.int32, (8, LANES), 0)
    loaded = []
    for side, part in itertools.product(range(2), range(ext_y // 8)):
        toward, x = 1 - 2 * side, ext_x - 1 if side else 0
        pulled = []
        for j in range(19):
            cx, cy, _ = VELOCITIES[j]
            if cx == -toward:
                pulled.append(jnp.zeros((8, LANES), jnp.float32))
                continue
            value = first[j, x + 2 + cx, pl.ds(8 + 8 * part + cy, 8), :]
            if cy == -1 and part == 0:
                value = jnp.where(sub == 0, 0.0, value)
            if cy == 1 and part == ext_y // 8 - 1:
                value = jnp.where(sub == 7, 0.0, value)
            pulled.append(value)
        at = (x, pl.ds(8 * part, 8), slice(None))
        here = [den[(1, *at)], vel[(1, 0, *at)], vel[(1, 1, *at)], vel[(1, 2, *at)], mask[at] > 0]
        loaded.append((side, part, pulled, here))
    for side, part, pulled, (rho, ux, uy, uz, fluid) in loaded:
        wanted = pops(0, 1 - 2 * side)
        after, _ = collide(pulled, 1.0 / rho, rho, ux, uy, uz, None, wanted)
        for line, j in enumerate(wanted):
            shares[side, line, pl.ds(8 * part, 8), :] = jnp.where(fluid, after[j], 0.0)

    pack_lines((mask,), first, packets, many_x, many_y, lambda kind, index: not is_flat(kind, index), shares)

    for side in range(2):
        for part in range(ext_y // 8):
            rows = pl.ds(8 * part, 8)
            value = jnp.zeros((8, LANES), jnp.float32)
            for tile in range(Z_TILES):
                start = ext_x if side else 2
                moved = pltpu.roll(z_set[tile, rows, :], (2 * tile - start) % LANES, 1)
                value = jnp.where(spot // 2 == tile, moved, value)
            faces[side, rows, :] = value

    def add_xy(slot_x, slot_y, side_x, side_y):
        start = ext_y - 2 if side_y else 0
        to_xy[many_x * slot_y + slot_x][EDGE // 8, 0:2, :] = faces[side_x, start : start + 2, :]

    def add_y(slot, side):
        toward = 1 - 2 * side
        lines = {name: line for line, name in enumerate(face_lines(1, toward))}
        pulled = []
        for j in range(19):
            cx, cy, _ = VELOCITIES[j]
            if cy == -toward:
                pulled.append(jnp.zeros((8, LANES), jnp.float32))
                continue
            value = y_lines[slot][lines[("pop", j, abs(cy))]]
            if cx:
                value = jnp.where(sub == (7 if cx > 0 else 0), 0.0, pltpu.roll(value, -cx % 8, 0))
            pulled.append(value)
        rho, ux, uy, uz, kind = [y_lines[slot][lines[("field", k, 0)]] for k in range(5)]
        after, _ = collide(pulled, 1.0 / rho, rho, ux, uy, uz, None, pops(1, toward))
        full, ends = side_lines(1, toward)
        for line, (what, index) in enumerate(full):
            if what == "share":
                to_y[slot][line] = jnp.where(kind > 1.5, after[pops(1, toward)[index]], 0.0)
            else:
                to_y[slot][line] = y_lines[slot][lines[(what, index, 0)]]
        for spot, (index, depth, end) in enumerate(ends):
            x = ext_x - 1 if end else 0
            to_y[slot][SIDE - 1, spot : spot + 1, :] = y_lines[slot][lines[("pop", index, depth)], x : x + 1, :]
        start = ext_y - 2 if side else 0
        for tile in range(Z_TILES):
            row = 2 * tile % 8
            to_y[slot][SIDE + tile // 4, row : row + 2, :] = z_set[tile, start : start + 2, :]

    def add_x(slot, side):
        to_x[slot][SIDE] = faces[side]

    for slot_y in range(many_y):
        there_y = has_partner("gy", slot_y)
        pl.when(there_y)(lambda: on_side(py, slot_y, functools.partial(add_y, slot_y)))

        @pl.when(jnp.logical_not(there_y))
        def _():
            to_y[slot_y][...] = jnp.zeros(to_y[slot_y].shape, jnp.float32)

        for slot_x in range(many_x):
            pl.when(there_y & has_partner("gx", slot_x))(
                lambda: on_side(
                    py,
                    slot_y,
                    lambda side_y: on_side(px, slot_x, lambda side_x: add_xy(slot_x, slot_y, side_x, side_y)),
                )
            )
    for slot_x in range(many_x):
        pl.when(has_partner("gx", slot_x))(lambda: on_side(px, slot_x, functools.partial(add_x, slot_x)))


def collide(pulled, inverse, rho, ux, uy, uz, fluid, wanted):
    total = {}
    diff = {}
    for j in range(1, 19, 2):
        total[j] = pulled[j] + pulled[j + 1]
        diff[j] = pulled[j] - pulled[j + 1]
    in_xy, in_xz, in_yz = total[7] + total[9], total[11] + total[13], total[15] + total[17]
    two_x, two_y, two_z = total[1] + total[1], total[3] + total[3], total[5] + total[5]
    count = (12.0 * pulled[0] + (two_x + two_y)) + (two_z + (in_xy + (in_xz + in_yz)))
    flow_x = (diff[1] + diff[1]) + ((diff[7] + diff[9]) + (diff[11] + diff[13]))
    flow_y = (diff[3] + diff[3]) + ((diff[7] - diff[9]) + (diff[15] + diff[17]))
    flow_z = (diff[5] + diff[5]) + ((diff[11] - diff[13]) + (diff[15] - diff[17]))
    xx, yy, zz = two_x + (in_xy + in_xz), two_y + (in_xy + in_yz), two_z + (in_xz + in_yz)
    xy, xz, yz = total[7] - total[9], total[11] - total[13], total[15] - total[17]
    push_x = xx * ux + xy * uy + xz * uz
    push_y = xy * ux + yy * uy + yz * uz
    push_z = xz * ux + yz * uy + zz * uz
    usq = ux * ux + uy * uy + uz * uz
    push = ux * push_x + uy * push_y + uz * push_z
    base = count * (OMEGA / 36.0 + (OMEGA / 24.0) * usq) - (OMEGA / 8.0) * push - ux * inverse
    along_x = (OMEGA / 12.0) * (flow_x + 3.0 * push_x - ux * count) + inverse
    along_y = (OMEGA / 12.0) * (flow_y + 3.0 * push_y - uy * count)
    along_z = (OMEGA / 12.0) * (flow_z + 3.0 * push_z - uz * count)
    parts = {
        1: along_x,
        3: along_y,
        5: along_z,
        7: along_x + along_y,
        9: along_x - along_y,
        11: along_x + along_z,
        13: along_x - along_z,
        15: along_y + along_z,
        17: along_y - along_z,
    }
    out = {}
    for j in wanted:
        if j == 0:
            shift = base
        elif j % 2:
            shift = base + parts[j]
        else:
            shift = base - parts[j - 1]
        out[j] = (1.0 - OMEGA) * pulled[j] + shift
        if fluid is not None:
            out[j] = jnp.where(fluid, out[j], pulled[OPPOSITE[j]])
    change = (-1.0 / 6.0) * rho * (flow_x * ux + flow_y * uy + flow_z * uz)
    return out, change if fluid is None else jnp.where(fluid, change, 0.0)


def only(value, row):
    return jnp.where(lax.broadcasted_iota(jnp.int32, (8, LANES), 0) == row, value, 0.0)


class Plane:
    def rim(self, shares, line, toward):
        if toward != (-1 if self.row < 0 else 1):
            return 0.0
        return only(shares[line, self.x, pl.ds(8 + self.row, 8), :], 0 if toward < 0 else 1)

    def __init__(self, x, row):
        self.x, self.row = x, row

    def load(self, ref, lead, margin, cx=0, cy=0):
        return ref[lead, self.x + margin + cx, pl.ds(8 + self.row + cy, 8), :]

    def store(self, ref, lead, margin, value):
        ref[lead, self.x + margin, pl.ds(8 + self.row, 8), :] = value


class Rim:
    def __init__(self, x, ext_y):
        self.x, self.ext_y = x, ext_y

    def rim(self, shares, line, toward):
        start = 1 if toward < 0 else 8 + self.ext_y - 1
        return only(shares[line, self.x, pl.ds(start, 8), :], 6 if toward < 0 else 1)

    def load(self, ref, lead, margin, cx=0, cy=0):
        at = self.x + margin + cx
        upper = ref[lead, at, pl.ds(8 + self.ext_y - 1 + cy, 8), :]
        lower = ref[lead, at, pl.ds(1 + cy, 8), :]
        return jnp.where(lax.broadcasted_iota(jnp.int32, (8, LANES), 0) < 4, upper, lower)

    def store(self, ref, lead, margin, value):
        at = self.x + margin
        ref[lead, at, pl.ds(8 + self.ext_y - 1, 2), :] = value[0:2]
        ref[lead, at, pl.ds(7, 2), :] = value[6:8]


def first_step(first, fields, second, change, tiles, outside=True, shares=None, y_shares=None):
    loaded = [
        (
            [tile.load(first, j, 2, *VELOCITIES[j][:2]) for j in range(19)],
            [tile.load(fields, k, 1) for k in range(5)],
        )
        for tile in tiles
    ]
    done = [
        collide(pulled, 1.0 / rho, rho, ux, uy, uz, kind > 1.5, range(19))
        for pulled, (rho, ux, uy, uz, kind) in loaded
    ]
    for tile, (_, here), (after, gain) in zip(tiles, loaded, done):
        inside = here[KIND] > 0.5
        side = None if shares is None else {-1: 0, second.shape[1] - 2: 1}.get(tile.x)
        for j in range(19):
            value = after[j]
            if side is not None and VELOCITIES[j][0] == 2 * side - 1:
                value = value + shares[side, pops(0, 2 * side - 1).index(j), pl.ds(8 + tile.row, 8), :]
            if side is None and y_shares is not None and VELOCITIES[j][1]:
                value = value + tile.rim(y_shares, pops(1, VELOCITIES[j][1]).index(j), VELOCITIES[j][1])
            if outside:
                value = jnp.where(inside, value, 0.0)
            cz = VELOCITIES[j][2]
            tile.store(second, j, 1, pltpu.roll(value, -cz % LANES, 1) if cz else value)
        tile.store(change, 0, 1, gain)


def inner_kernel(den, vel, mask, first, fields, second, change):
    refs = (None, den, vel, mask)
    ext_x, ext_y, _ = mask.shape
    every = slice(None)
    for k in range(5):
        fields[k, 1 : 1 + ext_x, pl.ds(8, ext_y), :] = field_of(refs, "field", k, (every, every, every))

    many = 3 if (ext_x - 2) % 3 == 0 else 1

    @pl.loop(0, (ext_x - 2) // many)
    def _(group):
        tiles = [Plane(many * group + at + 1, 1 + 8 * part) for at in range(many) for part in range(ext_y // 8)]
        first_step(first, fields, second, change, tiles, outside=False)


def put_row(first, fields, kind, index, x, y, value):
    row = y + 8
    if kind == "pop":
        first[index, x + 2, row : row + 1, :] = value
    else:
        fields[index, x + 1, row : row + 1, :] = value


def place_z(z_first, value, start, size, side, ext_x):
    rows = pl.ds(start, size)
    spot = lane_ids()[:size] % GROUP
    inside = spot >= 2 + ext_x if side else spot < 2
    for tile in range(Z_TILES):
        shift = (2 + ext_x if side else 0) - 2 * tile
        moved = pltpu.roll(value, shift % LANES, 1)[:size]
        z_first[tile, rows, :] = jnp.where(inside, moved, z_first[tile, rows, :])


def side_kernel(slots, z_set, *rest):
    many_x, many_y = slots
    from_x, from_y = rest[4 : 4 + many_x], rest[4 + many_x : 4 + many_x + many_y]
    first, fields, second, change, z_first, shares, y_shares = rest[-7:]
    _, ext_y, _ = z_set.shape
    ext_x = change.shape[1] - 2
    inner = pl.ds(8, ext_y)
    put = functools.partial(put_row, first, fields)
    z_first[:, inner, :] = z_set[...]

    def place_y(slot, side):
        packet = from_y[slot]
        toward = 2 * side - 1
        near = ext_y if side else -1
        nothing = jnp.zeros((1, LANES), jnp.float32)
        full, ends = side_lines(1, toward)
        for x in range(ext_x):
            for j in pops(1, 0):
                put("pop", j, x, near, nothing)
            for j in pops(1, toward):
                put("pop", j, x, near + toward, nothing)
            put("field", RHO, x, near, jnp.full((1, LANES), jnp.inf, jnp.float32))
            for line, (kind, index) in enumerate(full):
                if kind == "share":
                    y_shares[index, x, near + 8 : near + 9, :] = packet[line, x : x + 1, :]
                else:
                    put(kind, index, x, near, packet[line, x : x + 1, :])
        for spot, (index, depth, end) in enumerate(ends):
            put("pop", index, ext_x - 1 if end else 0, near + toward * depth, packet[SIDE - 1, spot : spot + 1, :])
        start = 8 + ext_y if side else 6
        for tile in range(Z_TILES):
            row = 2 * tile % 8
            z_first[tile, start : start + 2, :] = packet[SIDE + tile // 4, row : row + 2, :]
        if many_y == 1:
            clear_y(1 - side)

    def clear_y(side):
        nothing = jnp.zeros((1, LANES), jnp.float32)
        y = ext_y if side else -1
        for x in range(-2, ext_x + 2):
            for j in pops(1, 2 * side - 1):
                put("pop", j, x, y, nothing)
        for x in range(-1, ext_x + 1):
            put("field", KIND, x, y, nothing)
        start = 8 + ext_y if side else 6
        for tile in range(Z_TILES):
            z_first[tile, start : start + 2, :] = jnp.zeros((2, LANES), jnp.float32)

    def place_x(slot, side):
        packet = from_x[slot]
        toward = 2 * side - 1
        near = ext_x if side else -1
        nothing = jnp.zeros((ext_y, LANES), jnp.float32)
        for j in pops(0, 0):
            first[j, near + 2, inner, :] = nothing
        for j in pops(0, toward):
            first[j, near + toward + 2, inner, :] = nothing
        fields[RHO, near + 1, inner, :] = jnp.full((ext_y, LANES), jnp.inf, jnp.float32)
        full, ends = side_lines(0, toward)
        for line, (kind, index) in enumerate(full):
            if kind == "pop":
                first[index, near + 2, inner, :] = packet[line]
            elif kind == "share":
                shares[side, index, inner, :] = packet[line]
            else:
                fields[index, near + 1, inner, :] = packet[line]
        for spot, (index, depth, end) in enumerate(ends):
            put("pop", index, near + toward * depth, ext_y - 1 if end else 0, packet[SIDE - 1, spot : spot + 1, :])
        for part in range(ext_y // 8):
            place_z(z_first, packet[SIDE, pl.ds(8 * part, 8), :], 8 + 8 * part, 8, side, ext_x)

    shares[:, :, pl.ds(0, 8), :] = jnp.zeros((2, 5, 8, LANES), jnp.float32)
    shares[:, :, pl.ds(8 + ext_y, 8), :] = jnp.zeros((2, 5, 8, LANES), jnp.float32)
    for slot_y in range(many_y):
        on_side(parity_of("gy"), slot_y, functools.partial(place_y, slot_y))
    for slot_x in range(many_x):
        on_side(parity_of("gx"), slot_x, functools.partial(place_x, slot_x))

    rims = range(7, ext_y - 8, 8)
    first_step(first, fields, second, change, [Plane(x, row) for x in (0, ext_x - 1) for row in rims], outside=False)
    first_step(first, fields, second, change, [Plane(x, row) for x in (-1, ext_x) for row in rims], shares=shares)

    many = 3 if (ext_x - 2) % 3 == 0 else 1

    @pl.loop(0, (ext_x - 2) // many)
    def _(group):
        tiles = [Rim(many * group + at + 1, ext_y) for at in range(many)]
        first_step(first, fields, second, change, tiles, y_shares=y_shares)


def last_kernel(slots, den, vel, mask, *rest):
    many_x, many_y = slots
    from_xy = rest[7 : 7 + many_x * many_y]
    out, sens, first, fields, second, change, z_first, shares, y_shares = rest[-13:-4]
    z_second, held, held_sens, sems = rest[-4:]
    ext_x, ext_y, _ = mask.shape
    lane = lane_ids()
    every = slice(None)
    px, py = parity_of("gx"), parity_of("gy")

    def place_xy(slot_x, slot_y, side_x, side_y):
        packet = from_xy[many_x * slot_y + slot_x]
        for line, (kind, index, far_x, far_y) in enumerate(edge_lines(2 * side_x - 1, 2 * side_y - 1)):
            x = ext_x + far_x if side_x else -1 - far_x
            y = ext_y + far_y if side_y else -1 - far_y
            put_row(first, fields, kind, index, x, y, packet[line // 8, line % 8 : line % 8 + 1, :])
        place_z(z_first, packet[EDGE // 8], 8 + ext_y if side_y else 6, 2, side_x, ext_x)

    for slot_x in range(many_x):
        for slot_y in range(many_y):
            on_side(
                py,
                slot_y,
                lambda side_y: on_side(px, slot_x, lambda side_x: place_xy(slot_x, slot_y, side_x, side_y)),
            )

    for pair in ((-1, 0), (ext_x - 1, ext_x)):
        tiles = [Plane(x, row) for x in pair for row in (-1, ext_y - 1)]
        first_step(first, fields, second, change, tiles, shares=shares, y_shares=y_shares)

    starts = [7 + 8 * part for part in range((ext_y + 2 + 7) // 8)]
    loaded = []
    for row in starts:

        def both(low_tile, high_tile, group, cx, cy):
            rows = pl.ds(row + cy, 8)
            low = pltpu.roll(z_first[low_tile, rows, :], (-GROUP * group - cx) % LANES, 1)
            high = pltpu.roll(z_first[high_tile, rows, :], (LANES // 2 - GROUP * group - cx) % LANES, 1)
            return jnp.where(lane < LANES // 2, low, high)

        pulled = []
        for j in range(19):
            cx, cy, cz = VELOCITIES[j]
            if cz == 0:
                tile, group = Z_PLACE[("pop", j)]
                pulled.append(both(BELOW + tile, ABOVE + tile, group, cx, cy))
            elif cz == 1:
                pulled.append(both(OWN_LOW, ABOVE + 2, Z_UP.index(j), cx, cy))
            else:
                pulled.append(both(BELOW + 2, OWN_HIGH, Z_DOWN.index(j), cx, cy))
        places = [Z_PLACE[("field", k)] for k in range(5)]
        loaded.append((pulled, [both(BELOW + tile, ABOVE + tile, group, 0, 0) for tile, group in places]))
    done = [
        collide(pulled, 1.0 / rho, rho, ux, uy, uz, kind > 1.5, Z_UP + Z_DOWN)[0]
        for pulled, (rho, ux, uy, uz, kind) in loaded
    ]
    for row, (_, here), after in zip(starts, loaded, done):
        for group in range(5):
            value = jnp.where(lane < LANES // 2, after[Z_DOWN[group]], after[Z_UP[group]])
            z_second[group, pl.ds(row, 8), :] = jnp.where(here[KIND] > 0.5, value, 0.0)

    def copies(x):
        return (
            pltpu.make_async_copy(held.at[:, x], out.at[:, x], sems.at[0, x]),
            pltpu.make_async_copy(held_sens.at[x], sens.at[x], sems.at[1, x]),
        )

    many = 4 if ext_x % 4 == 0 else 1

    @pl.loop(0, ext_x // many)
    def _(group):
        loaded = []
        planes = [many * group + at for at in range(many)]
        for x, part in itertools.product(planes, range(ext_y // 8)):
            row = 8 + 8 * part
            pulled = []
            for j in range(19):
                cx, cy, cz = VELOCITIES[j]
                rows = pl.ds(row + cy, 8)
                value = second[j, x + 1 + cx, rows, :]
                if cz == 1:
                    edge = z_second[Z_UP.index(j), rows, :]
                    edge = pltpu.roll(edge, LANES // 2 - 3 - cx - x, 1)
                    value = jnp.where(lane == LANES - 1, edge, value)
                elif cz == -1:
                    edge = z_second[Z_DOWN.index(j), rows, :]
                    edge = pltpu.roll(edge, LANES - 2 - cx - x, 1)
                    value = jnp.where(lane == 0, edge, value)
                pulled.append(value)
            at = (x, pl.ds(8 * part, 8), every)
            rho = den[(0, *at)]
            here = [1.0 / rho, rho, vel[(0, 0, *at)], vel[(0, 1, *at)], vel[(0, 2, *at)], mask[at] > 0]
            loaded.append((at, pulled, here, change[0, x + 1, pl.ds(row, 8), :]))
        done = [collide(pulled, *here, range(19)) for _, pulled, here, _ in loaded]
        for (at, _, _, before), (after, gain) in zip(loaded, done):
            for j in range(19):
                held[(j, *at)] = after[j]
            held_sens[at] = before + gain
        for x in planes:
            for copy in copies(x):
                copy.start()

    for x in range(ext_x):
        for copy in copies(x):
            copy.wait()


def shards(adjoint, density, velocity, pore_mask):
    ext_x, ext_y, ext_z = pore_mask.shape
    assert ext_z == LANES and ext_y % 8 == 0 and ext_x + 4 <= GROUP and ext_x == 8
    many_x = 2
    many_y, many_z = [1 if lax.axis_size(axis) == 2 else 2 for axis in ("gy", "gz")]
    vmem = pl.BlockSpec(memory_space=pltpu.VMEM)
    hbm = pl.BlockSpec(memory_space=pltpu.HBM)
    inputs = (adjoint, density, velocity, pore_mask)

    def array(*shape):
        return jax.ShapeDtypeStruct(shape, jnp.float32)

    def call(kernel, name, operands, shapes, limit, **more):
        more.setdefault("out_specs", [vmem] * len(shapes))
        more.setdefault("in_specs", [vmem] * len(operands))
        params = pltpu.CompilerParams(vmem_limit_bytes=limit * 1024 * 1024)
        return pl.pallas_call(kernel, out_shape=shapes, compiler_params=params, name=name, **more)(*operands)

    def partners(axis, slot):
        found = {}
        for at in range(slot, lax.axis_size(axis) - 1, 2):
            found[at], found[at + 1] = at + 1, at
        return found

    def ends(axis):
        last = lax.axis_size(axis) - 1
        return {0: last, last: 0}

    def swap(value, spares, *places):
        tables = {axis: partners(axis, slot) for axis, slot in places}
        axes = [axis for axis in ("gx", "gy", "gz") if axis in tables or axis in dict(spares)]
        sizes = [lax.axis_size(axis) for axis in axes]
        pairs = []
        for at in itertools.product(*[range(size) for size in sizes]):
            to = [tables.get(axis, {}).get(spot, spot) for axis, spot in zip(axes, at)]
            for spare, table in spares:
                if tuple(to) == at:
                    to = [table.get(spot, spot) if axis == spare else spot for axis, spot in zip(axes, at)]
            flat = []
            for spots in (at, to):
                index = 0
                for size, spot in zip(sizes, spots):
                    index = index * size + spot
                flat.append(index)
            pairs.append(tuple(flat))
        return lax.ppermute(value, tuple(axes), pairs)

    loaded = [jax.ShapeDtypeStruct(value.shape, value.dtype) for value in inputs]
    *held, near, a_z, b_z = (
        *call(
            functools.partial(pack_z_kernel, many_z),
            "pack_z",
            [pltpu.with_memory_space_constraint(value, pltpu.HBM) for value in inputs],
            loaded + [array(2, ext_y, LANES)] + [array(3, ext_y, LANES)] * many_z,
            8,
            in_specs=[hbm] * 4,
            scratch_shapes=[pltpu.SemaphoreType.DMA((7,))],
        ),
        *[None] * (2 - many_z),
    )
    from_z = [swap(value, [("gx", partners("gx", 0))], ("gz", slot)) for slot, value in enumerate((a_z, b_z)[:many_z])]

    rows = ext_y + 16
    adj, den, vel, mask = held
    shapes = (
        [array(19, ext_x + 4, rows, LANES)]
        + [array(SIDE + 1, ext_y, LANES)] * many_x
        + [array(FACE, ext_x, LANES)] * many_y
        + [array(EDGE // 8 + 1, 8, LANES)] * (many_x * many_y)
    )
    shifted = call(
        functools.partial(shift_kernel, (many_x, many_y)),
        "shift",
        (adj, den, vel, mask),
        shapes,
        8,
        cost_estimate=pl.CostEstimate(flops=1_000_000, bytes_accessed=2_500_000, transcendentals=0),
    )
    z_set, first, *packets = call(
        functools.partial(pack_xy_kernel, (many_x, many_y, many_z)),
        "pack_xy",
        (den, vel, mask, near, *from_z, *shifted),
        [array(Z_TILES, ext_y, LANES)] + shapes + [array(SIDE + 2, ext_x, LANES)] * many_y,
        8,
        input_output_aliases={4 + many_z + at: 1 + at for at in range(len(shapes))},
        scratch_shapes=[
            pltpu.VMEM((2, ext_y, LANES), jnp.float32),
            pltpu.VMEM((2, 5, ext_y, LANES), jnp.float32),
        ],
    )
    to_x, to_xy, to_y = packets[:many_x], packets[many_x + many_y : -many_y], packets[-many_y:]
    from_xy = [
        swap(to_xy[many_x * slot_y + slot_x], [], ("gx", slot_x), ("gy", slot_y))
        for slot_y in range(many_y)
        for slot_x in range(many_x)
    ]
    from_y = [swap(value, [("gz", partners("gz", 0))], ("gy", slot)) for slot, value in enumerate(to_y)]
    spares = [("gx", ends("gx"))]
    if lax.axis_size("gz") > 2:
        top = lax.axis_size("gz") - 1
        spares = [("gz", {top - 1: top, top: top - 1})] + spares
    from_x = [swap(value, spares, ("gx", slot)) for slot, value in enumerate(to_x)]

    fields, second, change = call(
        inner_kernel,
        "inner_step",
        (den, vel, mask, first),
        [array(5, ext_x + 2, rows, LANES), array(19, ext_x + 2, rows, LANES), array(1, ext_x + 2, rows, LANES)],
        8,
        cost_estimate=pl.CostEstimate(flops=40_000_000, bytes_accessed=8_000_000, transcendentals=0),
    )
    inout = (first, fields, second, change)
    inout = call(
        functools.partial(side_kernel, (many_x, many_y)),
        "side_step",
        (z_set, *inout, *from_x, *from_y),
        [array(*value.shape) for value in inout] + [array(Z_TILES, rows, LANES), array(2, 5, rows, LANES), array(5, ext_x, rows, LANES)],
        8,
        input_output_aliases={1 + at: at for at in range(4)},
        cost_estimate=pl.CostEstimate(flops=40_000_000, bytes_accessed=8_000_000, transcendentals=0),
    )
    return call(
        functools.partial(last_kernel, (many_x, many_y)),
        "last_steps",
        (den, vel, mask, *inout, *from_xy),
        [array(19, ext_x, ext_y, LANES), array(ext_x, ext_y, LANES)] + [array(*value.shape) for value in inout],
        8,
        out_specs=[hbm] * 2 + [vmem] * 7,
        input_output_aliases={3 + at: 2 + at for at in range(7)},
        scratch_shapes=[
            pltpu.VMEM((5, rows, LANES), jnp.float32),
            pltpu.VMEM((19, ext_x, ext_y, LANES), jnp.float32),
            pltpu.VMEM((ext_x, ext_y, LANES), jnp.float32),
            pltpu.SemaphoreType.DMA((2, ext_x)),
        ],
    )[:2]


def solution(mesh):
    placed = (
        P(None, "gx", "gy", "gz"),
        P(None, "gx", "gy", "gz"),
        P(None, None, "gx", "gy", "gz"),
        P("gx", "gy", "gz"),
    )

    def whole(*arrays):
        return tuple(shards(*arrays))

    return jax.shard_map(
        whole,
        mesh=mesh,
        in_specs=placed,
        out_specs=(P(None, "gx", "gy", "gz"), P("gx", "gy", "gz")),
        check_vma=False,
    )
```

```python
import functools
import itertools

import jax
import jax.numpy as jnp
from jax import lax
from jax.experimental import pallas as pl
from jax.experimental.pallas import tpu as pltpu
from jax.sharding import PartitionSpec as P

VELOCITIES = [
    (0, 0, 0),
    (1, 0, 0),
    (-1, 0, 0),
    (0, 1, 0),
    (0, -1, 0),
    (0, 0, 1),
    (0, 0, -1),
    (1, 1, 0),
    (-1, -1, 0),
    (1, -1, 0),
    (-1, 1, 0),
    (1, 0, 1),
    (-1, 0, -1),
    (1, 0, -1),
    (-1, 0, 1),
    (0, 1, 1),
    (0, -1, -1),
    (0, 1, -1),
    (0, -1, 1),
]
OPPOSITE = [0, 2, 1, 4, 3, 6, 5, 8, 7, 10, 9, 12, 11, 14, 13, 16, 15, 18, 17]
OMEGA = 1.25
LANES = 128
GROUP = 16


def pops(axis, sign):
    return [j for j in range(19) if VELOCITIES[j][axis] == sign]


def mirrored(j):
    cx, cy, cz = VELOCITIES[j]
    return VELOCITIES.index((cx, cy, -cz))


Z_FLAT = pops(2, 0)
Z_UP = pops(2, 1)
Z_DOWN = [mirrored(j) for j in Z_UP]
RHO, UX, UY, UZ, KIND = range(5)
Z_PLACE = {("pop", j): (0, g) for g, j in enumerate(Z_FLAT[:8])}
Z_PLACE[("pop", Z_FLAT[8])] = (1, 5)
Z_PLACE[("field", RHO)] = (1, 6)
Z_PLACE[("field", KIND)] = (1, 7)
Z_PLACE[("field", UX)] = (2, 5)
Z_PLACE[("field", UY)] = (2, 6)
Z_PLACE[("field", UZ)] = (2, 7)
BELOW, ABOVE, OWN_LOW, OWN_HIGH, Z_TILES = 0, 3, 6, 7, 8


def face_lines(axis, toward):
    near = pops(axis, 0) + pops(axis, toward)
    lines = [("pop", j, 0) for j in near] + [("field", k, 0) for k in range(5)]
    return lines + [("pop", j, 1) for j in pops(axis, toward)]


def edge_lines(toward_x, toward_y):
    lines = [("field", k, 0, 0) for k in range(5)]
    for j in range(19):
        cx, cy, _ = VELOCITIES[j]
        if cx not in (0, toward_x) or cy not in (0, toward_y):
            continue
        lines.append(("pop", j, 0, 0))
        if cx:
            lines.append(("pop", j, 1, 0))
        if cy:
            lines.append(("pop", j, 0, 1))
        if cx and cy:
            lines.append(("pop", j, 1, 1))
    return lines


FACE = 24
EDGE = 24
SIDE = 15


def side_lines(axis, toward):
    full = [("pop", j) for j in pops(axis, toward)] + [("share", p) for p in range(5)]
    full += [("field", k) for k in (UX, UY, UZ, KIND)]
    ends = []
    for end in range(2):
        for j in pops(1 - axis, 1 - 2 * end):
            across = VELOCITIES[j][axis]
            if across in (0, toward):
                ends.append((j, abs(across), end))
    return full, ends


def lane_ids():
    return lax.broadcasted_iota(jnp.int32, (8, LANES), 1)


def field_of(refs, kind, index, at):
    adj, den, vel, mask = refs
    if kind == "pop":
        return adj[(index, *at)]
    if index == RHO:
        return den[(1, *at)]
    if index == KIND:
        return (mask[at] + 1).astype(jnp.float32)
    return vel[(1, index - UX, *at)]


def parity_of(axis):
    return lax.rem(lax.axis_index(axis), 2)


def on_side(parity, slot, act):
    @pl.when(parity == slot)
    def _():
        act(1)

    @pl.when(parity != slot)
    def _():
        act(0)


def has_partner(axis, slot):
    at = lax.axis_index(axis)
    to = at + jnp.where(lax.rem(at, 2) == slot, 1, -1)
    return (to >= 0) & (to < lax.axis_size(axis))


def pack_z_kernel(slots, adj_in, den_in, vel_in, mask_in, adj, den, vel, mask, near, *rest):
    packets, sems = rest[:slots], rest[slots]
    refs = (adj, den, vel, mask)
    ext_x, ext_y, _ = mask.shape
    starts = range(0, 19, 5)
    loads = [
        pltpu.make_async_copy(adj_in.at[start : min(start + 5, 19)], adj.at[start : min(start + 5, 19)], sems.at[at])
        for at, start in enumerate(starts)
    ] + [
        pltpu.make_async_copy(source, target, sems.at[len(starts) + at])
        for at, (source, target) in enumerate([(den_in, den), (vel_in, vel), (mask_in, mask)])
    ]
    for load in loads:
        load.start()
    lane = lane_ids()
    parity = parity_of("gz")
    parts = range(ext_y // 8)
    zero = jnp.zeros((8, LANES), jnp.float32)
    lows, highs = [[zero] * 3 for _ in parts], [[zero] * 3 for _ in parts]
    far_low, far_high = [zero for _ in parts], [zero for _ in parts]

    def gather(kind, index):
        for x, part in itertools.product(range(ext_x), parts):
            value = field_of(refs, kind, index, (x, pl.ds(8 * part, 8), slice(None)))
            if kind == "pop" and VELOCITIES[index][2] == 1:
                spot = GROUP * Z_UP.index(index) + 2 + x
                moved = pltpu.roll(value, spot, 1)
                lows[part][1] = jnp.where(lane == spot, moved, lows[part][1])
                far_low[part] = jnp.where(lane == spot + 1, moved, far_low[part])
            elif kind == "pop" and VELOCITIES[index][2] == -1:
                spot = GROUP * Z_DOWN.index(index) + 2 + x
                moved = pltpu.roll(value, spot, 1)
                highs[part][1] = jnp.where(lane == spot - 1, moved, highs[part][1])
                far_high[part] = jnp.where(lane == spot - 2, moved, far_high[part])
            else:
                tile, group = Z_PLACE[(kind, index)]
                spot = GROUP * group + 2 + x
                moved = pltpu.roll(value, spot, 1)
                lows[part][tile] = jnp.where(lane == spot, moved, lows[part][tile])
                highs[part][tile] = jnp.where(lane == spot - 1, moved, highs[part][tile])

    for start, load in zip(starts, loads):
        load.wait()
        for j in range(start, min(start + 5, 19)):
            gather("pop", j)
    for load in loads[len(starts) :]:
        load.wait()
    for k in range(5):
        gather("field", k)
    for part in parts:
        rows = pl.ds(8 * part, 8)
        low = lows[part]
        high = [pltpu.roll(tile, 1, 1) for tile in highs[part]]
        low[2] = jnp.where(lane < 5 * GROUP, pltpu.roll(far_low[part], LANES - 1, 1), low[2])
        high[2] = jnp.where(lane < 5 * GROUP, pltpu.roll(far_high[part], 2, 1), high[2])
        near[0, rows, :] = low[1]
        near[1, rows, :] = high[1]
        for slot in range(slots):
            there = has_partner("gz", slot)
            for tile in range(3):
                value = jnp.where(parity == slot, high[tile], low[tile])
                packets[slot][tile, rows, :] = jnp.where(there, value, 0.0)


def pack_lines(refs, first, packets, many_x, many_y, wanted, shares):
    to_x, y_lines = packets[:many_x], packets[many_x : many_x + many_y]
    to_xy = packets[many_x + many_y :]
    ext_x, ext_y, _ = refs[-1].shape
    every = slice(None)
    px, py = parity_of("gx"), parity_of("gy")

    def line_of(kind, index, x, y):
        if kind == "pop":
            return first[index, x + 2, y + 8 : y + 9, :]
        return field_of(refs, kind, index, (x, slice(y, y + 1), every))

    def pack_xy(slot_x, slot_y, side_x, side_y):
        packet = to_xy[many_x * slot_y + slot_x]
        for line, (kind, index, far_x, far_y) in enumerate(edge_lines(1 - 2 * side_x, 1 - 2 * side_y)):
            if wanted(kind, index):
                x = ext_x - 1 - far_x if side_x else far_x
                y = ext_y - 1 - far_y if side_y else far_y
                packet[line // 8, line % 8 : line % 8 + 1, :] = line_of(kind, index, x, y)

    def pack_y(slot, side):
        for line, (kind, index, depth) in enumerate(face_lines(1, 1 - 2 * side)):
            if wanted(kind, index):
                y = ext_y - 1 - depth if side else depth
                for x in range(ext_x):
                    y_lines[slot][line, x : x + 1, :] = line_of(kind, index, x, y)

    def pack_x(slot, side):
        full, ends = side_lines(0, 1 - 2 * side)
        for line, (kind, index) in enumerate(full):
            if kind == "field" and wanted(kind, index):
                to_x[slot][line] = field_of(refs, kind, index, (ext_x - 1 if side else 0, every, every))
            elif kind == "pop" and wanted(kind, index):
                to_x[slot][line] = first[index, (ext_x - 1 if side else 0) + 2, pl.ds(8, ext_y), :]
            elif kind == "share" and shares is not None:
                to_x[slot][line] = shares[side, index]
        for spot, (index, depth, end) in enumerate(ends):
            if wanted("pop", index):
                x = ext_x - 1 - depth if side else depth
                to_x[slot][SIDE - 1, spot : spot + 1, :] = line_of("pop", index, x, ext_y - 1 if end else 0)

    def when_there(there, packet, act):
        pl.when(there)(act)
        if shares is None:

            @pl.when(jnp.logical_not(there))
            def _():
                packet[...] = jnp.zeros(packet.shape, jnp.float32)

    for slot_y in range(many_y):
        there_y = has_partner("gy", slot_y)
        when_there(there_y, y_lines[slot_y], lambda: on_side(py, slot_y, functools.partial(pack_y, slot_y)))
        for slot_x in range(many_x):
            when_there(
                there_y & has_partner("gx", slot_x),
                to_xy[many_x * slot_y + slot_x],
                lambda: on_side(
                    py,
                    slot_y,
                    lambda side_y: on_side(px, slot_x, lambda side_x: pack_xy(slot_x, slot_y, side_x, side_y)),
                ),
            )
    for slot_x in range(many_x):
        when_there(
            has_partner("gx", slot_x), to_x[slot_x], lambda: on_side(px, slot_x, functools.partial(pack_x, slot_x))
        )


def is_flat(kind, index):
    return kind == "field" or VELOCITIES[index][2] == 0


def shift_kernel(slots, adj, den, vel, mask, first, *packets):
    many_x, many_y = slots
    _, ext_x, ext_y, _ = adj.shape
    for j in range(19):
        cz = VELOCITIES[j][2]
        for x, part in itertools.product(range(ext_x), range(ext_y // 8)):
            value = adj[j, x, pl.ds(8 * part, 8), :]
            first[j, 2 + x, pl.ds(8 + 8 * part, 8), :] = pltpu.roll(value, -cz % LANES, 1) if cz else value
    pack_lines((None, den, vel, mask), first, packets, many_x, many_y, is_flat, None)


def pack_xy_kernel(slots, den, vel, mask, near, *rest):
    many_x, many_y, many_z = slots
    count = many_x + many_y + many_x * many_y
    from_z, rest = rest[:many_z], rest[many_z + 1 + count :]
    z_set, first, packets, faces, shares = rest[0], rest[1], rest[2 : 2 + count], rest[-2], rest[-1]
    to_x, y_lines, to_xy = packets[:many_x], packets[many_x : many_x + many_y], packets[many_x + many_y :]
    to_y = rest[2 + count : -2]
    ext_x, ext_y = first.shape[1] - 4, near.shape[1]
    spot = lane_ids() % GROUP
    px, py, pz = parity_of("gx"), parity_of("gy"), parity_of("gz")

    z_set[OWN_LOW] = near[0]
    z_set[OWN_HIGH] = near[1]
    for tile in range(3):
        even = from_z[0][tile]
        odd = from_z[1][tile] if many_z > 1 else jnp.zeros_like(even)
        z_set[ABOVE + tile] = jnp.where(pz == 0, even, odd)
        z_set[BELOW + tile] = jnp.where(pz == 0, odd, even)

    for j in Z_UP + Z_DOWN:
        up = VELOCITIES[j][2] > 0
        group = (Z_UP if up else Z_DOWN).index(j)
        last = LANES - 1 if up else 0
        for part in range(ext_y // 8):
            halo = z_set[(ABOVE if up else BELOW) + 1, pl.ds(8 * part, 8), :]
            for x in range(ext_x):
                edge = pltpu.roll(halo, (last - 2 - GROUP * group - x) % LANES, 1)
                first[j, 2 + x, pl.ds(8 + 8 * part, 8), last : last + 1] = edge[:, last : last + 1]


    sub = lax.broadcasted_iota(jnp.int32, (8, LANES), 0)
    loaded = []
    for side, part in itertools.product(range(2), range(ext_y // 8)):
        toward, x = 1 - 2 * side, ext_x - 1 if side else 0
        pulled = []
        for j in range(19):
            cx, cy, _ = VELOCITIES[j]
            if cx == -toward:
                pulled.append(jnp.zeros((8, LANES), jnp.float32))
                continue
            value = first[j, x + 2 + cx, pl.ds(8 + 8 * part + cy, 8), :]
            if cy == -1 and part == 0:
                value = jnp.where(sub == 0, 0.0, value)
            if cy == 1 and part == ext_y // 8 - 1:
                value = jnp.where(sub == 7, 0.0, value)
            pulled.append(value)
        at = (x, pl.ds(8 * part, 8), slice(None))
        here = [den[(1, *at)], vel[(1, 0, *at)], vel[(1, 1, *at)], vel[(1, 2, *at)], mask[at] > 0]
        loaded.append((side, part, pulled, here))
    for side, part, pulled, (rho, ux, uy, uz, fluid) in loaded:
        wanted = pops(0, 1 - 2 * side)
        after, _ = collide(pulled, 1.0 / rho, rho, ux, uy, uz, None, wanted)
        for line, j in enumerate(wanted):
            shares[side, line, pl.ds(8 * part, 8), :] = jnp.where(fluid, after[j], 0.0)

    pack_lines((mask,), first, packets, many_x, many_y, lambda kind, index: not is_flat(kind, index), shares)

    for side in range(2):
        for part in range(ext_y // 8):
            rows = pl.ds(8 * part, 8)
            value = jnp.zeros((8, LANES), jnp.float32)
            for tile in range(Z_TILES):
                start = ext_x if side else 2
                moved = pltpu.roll(z_set[tile, rows, :], (2 * tile - start) % LANES, 1)
                value = jnp.where(spot // 2 == tile, moved, value)
            faces[side, rows, :] = value

    def add_xy(slot_x, slot_y, side_x, side_y):
        start = ext_y - 2 if side_y else 0
        to_xy[many_x * slot_y + slot_x][EDGE // 8, 0:2, :] = faces[side_x, start : start + 2, :]

    def add_y(slot, side):
        toward = 1 - 2 * side
        lines = {name: line for line, name in enumerate(face_lines(1, toward))}
        pulled = []
        for j in range(19):
            cx, cy, _ = VELOCITIES[j]
            if cy == -toward:
                pulled.append(jnp.zeros((8, LANES), jnp.float32))
                continue
            value = y_lines[slot][lines[("pop", j, abs(cy))]]
            if cx:
                value = jnp.where(sub == (7 if cx > 0 else 0), 0.0, pltpu.roll(value, -cx % 8, 0))
            pulled.append(value)
        rho, ux, uy, uz, kind = [y_lines[slot][lines[("field", k, 0)]] for k in range(5)]
        after, _ = collide(pulled, 1.0 / rho, rho, ux, uy, uz, None, pops(1, toward))
        full, ends = side_lines(1, toward)
        for line, (what, index) in enumerate(full):
            if what == "share":
                to_y[slot][line] = jnp.where(kind > 1.5, after[pops(1, toward)[index]], 0.0)
            else:
                to_y[slot][line] = y_lines[slot][lines[(what, index, 0)]]
        for spot, (index, depth, end) in enumerate(ends):
            x = ext_x - 1 if end else 0
            to_y[slot][SIDE - 1, spot : spot + 1, :] = y_lines[slot][lines[("pop", index, depth)], x : x + 1, :]
        start = ext_y - 2 if side else 0
        for tile in range(Z_TILES):
            row = 2 * tile % 8
            to_y[slot][SIDE + tile // 4, row : row + 2, :] = z_set[tile, start : start + 2, :]

    def add_x(slot, side):
        to_x[slot][SIDE] = faces[side]

    for slot_y in range(many_y):
        there_y = has_partner("gy", slot_y)
        pl.when(there_y)(lambda: on_side(py, slot_y, functools.partial(add_y, slot_y)))

        @pl.when(jnp.logical_not(there_y))
        def _():
            to_y[slot_y][...] = jnp.zeros(to_y[slot_y].shape, jnp.float32)

        for slot_x in range(many_x):
            pl.when(there_y & has_partner("gx", slot_x))(
                lambda: on_side(
                    py,
                    slot_y,
                    lambda side_y: on_side(px, slot_x, lambda side_x: add_xy(slot_x, slot_y, side_x, side_y)),
                )
            )
    for slot_x in range(many_x):
        pl.when(has_partner("gx", slot_x))(lambda: on_side(px, slot_x, functools.partial(add_x, slot_x)))


def collide(pulled, inverse, rho, ux, uy, uz, fluid, wanted):
    total = {}
    diff = {}
    for j in range(1, 19, 2):
        total[j] = pulled[j] + pulled[j + 1]
        diff[j] = pulled[j] - pulled[j + 1]
    in_xy, in_xz, in_yz = total[7] + total[9], total[11] + total[13], total[15] + total[17]
    two_x, two_y, two_z = total[1] + total[1], total[3] + total[3], total[5] + total[5]
    count = (12.0 * pulled[0] + (two_x + two_y)) + (two_z + (in_xy + (in_xz + in_yz)))
    flow_x = (diff[1] + diff[1]) + ((diff[7] + diff[9]) + (diff[11] + diff[13]))
    flow_y = (diff[3] + diff[3]) + ((diff[7] - diff[9]) + (diff[15] + diff[17]))
    flow_z = (diff[5] + diff[5]) + ((diff[11] - diff[13]) + (diff[15] - diff[17]))
    xx, yy, zz = two_x + (in_xy + in_xz), two_y + (in_xy + in_yz), two_z + (in_xz + in_yz)
    xy, xz, yz = total[7] - total[9], total[11] - total[13], total[15] - total[17]
    push_x = xx * ux + xy * uy + xz * uz
    push_y = xy * ux + yy * uy + yz * uz
    push_z = xz * ux + yz * uy + zz * uz
    usq = ux * ux + uy * uy + uz * uz
    push = ux * push_x + uy * push_y + uz * push_z
    base = count * (OMEGA / 36.0 + (OMEGA / 24.0) * usq) - (OMEGA / 8.0) * push - ux * inverse
    along_x = (OMEGA / 12.0) * (flow_x + 3.0 * push_x - ux * count) + inverse
    along_y = (OMEGA / 12.0) * (flow_y + 3.0 * push_y - uy * count)
    along_z = (OMEGA / 12.0) * (flow_z + 3.0 * push_z - uz * count)
    parts = {
        1: along_x,
        3: along_y,
        5: along_z,
        7: along_x + along_y,
        9: along_x - along_y,
        11: along_x + along_z,
        13: along_x - along_z,
        15: along_y + along_z,
        17: along_y - along_z,
    }
    out = {}
    for j in wanted:
        if j == 0:
            shift = base
        elif j % 2:
            shift = base + parts[j]
        else:
            shift = base - parts[j - 1]
        out[j] = (1.0 - OMEGA) * pulled[j] + shift
        if fluid is not None:
            out[j] = jnp.where(fluid, out[j], pulled[OPPOSITE[j]])
    change = (-1.0 / 6.0) * rho * (flow_x * ux + flow_y * uy + flow_z * uz)
    return out, change if fluid is None else jnp.where(fluid, change, 0.0)


def only(value, row):
    return jnp.where(lax.broadcasted_iota(jnp.int32, (8, LANES), 0) == row, value, 0.0)


class Plane:
    def across(self, shares, side, line):
        return shares[side, line, pl.ds(8 + self.row, 8), :]

    def rim(self, shares, line, toward):
        if toward != (-1 if self.row < 0 else 1):
            return 0.0
        return only(shares[line, self.x, pl.ds(8 + self.row, 8), :], 0 if toward < 0 else 1)

    def __init__(self, x, row):
        self.x, self.row = x, row

    def load(self, ref, lead, margin, cx=0, cy=0):
        return ref[lead, self.x + margin + cx, pl.ds(8 + self.row + cy, 8), :]

    def store(self, ref, lead, margin, value):
        ref[lead, self.x + margin, pl.ds(8 + self.row, 8), :] = value


class Rim:
    def __init__(self, x, ext_y):
        self.x, self.ext_y = x, ext_y

    def across(self, shares, side, line):
        upper, lower = shares[side, line, pl.ds(8 + self.ext_y - 1, 8), :], shares[side, line, pl.ds(1, 8), :]
        return jnp.where(lax.broadcasted_iota(jnp.int32, (8, LANES), 0) < 4, upper, lower)

    def rim(self, shares, line, toward):
        start = 1 if toward < 0 else 8 + self.ext_y - 1
        return only(shares[line, self.x, pl.ds(start, 8), :], 6 if toward < 0 else 1)

    def load(self, ref, lead, margin, cx=0, cy=0):
        at = self.x + margin + cx
        upper = ref[lead, at, pl.ds(8 + self.ext_y - 1 + cy, 8), :]
        lower = ref[lead, at, pl.ds(1 + cy, 8), :]
        return jnp.where(lax.broadcasted_iota(jnp.int32, (8, LANES), 0) < 4, upper, lower)

    def store(self, ref, lead, margin, value):
        at = self.x + margin
        ref[lead, at, pl.ds(8 + self.ext_y - 1, 2), :] = value[0:2]
        ref[lead, at, pl.ds(7, 2), :] = value[6:8]


def first_step(first, fields, second, change, tiles, outside=True, shares=None, y_shares=None):
    loaded = [
        (
            [tile.load(first, j, 2, *VELOCITIES[j][:2]) for j in range(19)],
            [tile.load(fields, k, 1) for k in range(5)],
        )
        for tile in tiles
    ]
    done = [
        collide(pulled, 1.0 / rho, rho, ux, uy, uz, kind > 1.5, range(19))
        for pulled, (rho, ux, uy, uz, kind) in loaded
    ]
    for tile, (_, here), (after, gain) in zip(tiles, loaded, done):
        inside = here[KIND] > 0.5
        side = None if shares is None else {-1: 0, second.shape[1] - 2: 1}.get(tile.x)
        for j in range(19):
            value = after[j]
            if side is not None and VELOCITIES[j][0] == 2 * side - 1:
                value = value + tile.across(shares, side, pops(0, 2 * side - 1).index(j))
            if side is None and y_shares is not None and VELOCITIES[j][1]:
                value = value + tile.rim(y_shares, pops(1, VELOCITIES[j][1]).index(j), VELOCITIES[j][1])
            if outside:
                value = jnp.where(inside, value, 0.0)
            cz = VELOCITIES[j][2]
            tile.store(second, j, 1, pltpu.roll(value, -cz % LANES, 1) if cz else value)
        tile.store(change, 0, 1, gain)


def inner_kernel(den, vel, mask, first, fields, second, change):
    refs = (None, den, vel, mask)
    ext_x, ext_y, _ = mask.shape
    every = slice(None)
    for k in range(5):
        fields[k, 1 : 1 + ext_x, pl.ds(8, ext_y), :] = field_of(refs, "field", k, (every, every, every))

    many = 3 if (ext_x - 2) % 3 == 0 else 1

    @pl.loop(0, (ext_x - 2) // many)
    def _(group):
        tiles = [Plane(many * group + at + 1, 1 + 8 * part) for at in range(many) for part in range(ext_y // 8)]
        first_step(first, fields, second, change, tiles, outside=False)


def put_row(first, fields, kind, index, x, y, value):
    row = y + 8
    if kind == "pop":
        first[index, x + 2, row : row + 1, :] = value
    else:
        fields[index, x + 1, row : row + 1, :] = value


def place_z(z_first, value, start, size, side, ext_x):
    rows = pl.ds(start, size)
    spot = lane_ids()[:size] % GROUP
    inside = spot >= 2 + ext_x if side else spot < 2
    for tile in range(Z_TILES):
        shift = (2 + ext_x if side else 0) - 2 * tile
        moved = pltpu.roll(value, shift % LANES, 1)[:size]
        z_first[tile, rows, :] = jnp.where(inside, moved, z_first[tile, rows, :])


def z_step(z_first, z_second, starts):
    lane = lane_ids()
    loaded = []
    for row in starts:

        def both(low_tile, high_tile, group, cx, cy):
            rows = pl.ds(8 + row + cy, 8)
            low = pltpu.roll(z_first[low_tile, rows, :], (-GROUP * group - cx) % LANES, 1)
            high = pltpu.roll(z_first[high_tile, rows, :], (LANES // 2 - GROUP * group - cx) % LANES, 1)
            return jnp.where(lane < LANES // 2, low, high)

        pulled = []
        for j in range(19):
            cx, cy, cz = VELOCITIES[j]
            if cz == 0:
                tile, group = Z_PLACE[("pop", j)]
                pulled.append(both(BELOW + tile, ABOVE + tile, group, cx, cy))
            elif cz == 1:
                pulled.append(both(OWN_LOW, ABOVE + 2, Z_UP.index(j), cx, cy))
            else:
                pulled.append(both(BELOW + 2, OWN_HIGH, Z_DOWN.index(j), cx, cy))
        places = [Z_PLACE[("field", k)] for k in range(5)]
        loaded.append((pulled, [both(BELOW + tile, ABOVE + tile, group, 0, 0) for tile, group in places]))
    done = [
        collide(pulled, 1.0 / rho, rho, ux, uy, uz, kind > 1.5, Z_UP + Z_DOWN)[0]
        for pulled, (rho, ux, uy, uz, kind) in loaded
    ]
    for row, (_, here), after in zip(starts, loaded, done):
        for group in range(5):
            value = jnp.where(lane < LANES // 2, after[Z_DOWN[group]], after[Z_UP[group]])
            z_second[group, pl.ds(8 + row, 8), :] = jnp.where(here[KIND] > 0.5, value, 0.0)


def side_kernel(slots, z_set, *rest):
    many_x, many_y = slots
    from_x, from_y = rest[4 : 4 + many_x], rest[4 + many_x : 4 + many_x + many_y]
    first, fields, second, change, z_first, z_second, shares, y_shares = rest[-8:]
    _, ext_y, _ = z_set.shape
    ext_x = change.shape[1] - 2
    inner = pl.ds(8, ext_y)
    put = functools.partial(put_row, first, fields)
    z_first[:, inner, :] = z_set[...]

    def place_y(slot, side):
        packet = from_y[slot]
        toward = 2 * side - 1
        near = ext_y if side else -1
        nothing = jnp.zeros((1, LANES), jnp.float32)
        full, ends = side_lines(1, toward)
        for x in range(ext_x):
            for j in pops(1, 0):
                put("pop", j, x, near, nothing)
            for j in pops(1, toward):
                put("pop", j, x, near + toward, nothing)
            put("field", RHO, x, near, jnp.full((1, LANES), jnp.inf, jnp.float32))
            for line, (kind, index) in enumerate(full):
                if kind == "share":
                    y_shares[index, x, near + 8 : near + 9, :] = packet[line, x : x + 1, :]
                else:
                    put(kind, index, x, near, packet[line, x : x + 1, :])
        for spot, (index, depth, end) in enumerate(ends):
            put("pop", index, ext_x - 1 if end else 0, near + toward * depth, packet[SIDE - 1, spot : spot + 1, :])
        start = 8 + ext_y if side else 6
        for tile in range(Z_TILES):
            row = 2 * tile % 8
            z_first[tile, start : start + 2, :] = packet[SIDE + tile // 4, row : row + 2, :]
        if many_y == 1:
            clear_y(1 - side)

    def clear_y(side):
        nothing = jnp.zeros((1, LANES), jnp.float32)
        y = ext_y if side else -1
        for x in range(-2, ext_x + 2):
            for j in pops(1, 2 * side - 1):
                put("pop", j, x, y, nothing)
        for x in range(-1, ext_x + 1):
            put("field", KIND, x, y, nothing)
        start = 8 + ext_y if side else 6
        for tile in range(Z_TILES):
            z_first[tile, start : start + 2, :] = jnp.zeros((2, LANES), jnp.float32)

    def place_x(slot, side):
        packet = from_x[slot]
        toward = 2 * side - 1
        near = ext_x if side else -1
        nothing = jnp.zeros((ext_y, LANES), jnp.float32)
        for j in pops(0, 0):
            first[j, near + 2, inner, :] = nothing
        for j in pops(0, toward):
            first[j, near + toward + 2, inner, :] = nothing
        fields[RHO, near + 1, inner, :] = jnp.full((ext_y, LANES), jnp.inf, jnp.float32)
        full, ends = side_lines(0, toward)
        for line, (kind, index) in enumerate(full):
            if kind == "pop":
                first[index, near + 2, inner, :] = packet[line]
            elif kind == "share":
                shares[side, index, inner, :] = packet[line]
            else:
                fields[index, near + 1, inner, :] = packet[line]
        for spot, (index, depth, end) in enumerate(ends):
            put("pop", index, near + toward * depth, ext_y - 1 if end else 0, packet[SIDE - 1, spot : spot + 1, :])
        for part in range(ext_y // 8):
            place_z(z_first, packet[SIDE, pl.ds(8 * part, 8), :], 8 + 8 * part, 8, side, ext_x)

    shares[:, :, pl.ds(0, 8), :] = jnp.zeros((2, 5, 8, LANES), jnp.float32)
    shares[:, :, pl.ds(8 + ext_y, 8), :] = jnp.zeros((2, 5, 8, LANES), jnp.float32)
    for slot_y in range(many_y):
        on_side(parity_of("gy"), slot_y, functools.partial(place_y, slot_y))
    for slot_x in range(many_x):
        on_side(parity_of("gx"), slot_x, functools.partial(place_x, slot_x))

    starts = range(1, ext_y, 8)
    first_step(first, fields, second, change, [Plane(x, row) for x in (0, ext_x - 1) for row in starts], outside=False)
    first_step(first, fields, second, change, [Plane(x, row) for x in (-1, ext_x) for row in starts], shares=shares)
    z_step(z_first, z_second, range(7, ext_y - 8, 8))
    many = 3 if (ext_x - 2) % 3 == 0 else 1

    @pl.loop(0, (ext_x - 2) // many)
    def _(group):
        tiles = [Rim(many * group + at + 1, ext_y) for at in range(many)]
        first_step(first, fields, second, change, tiles, y_shares=y_shares)


def last_kernel(slots, den, vel, mask, *rest):
    many_x, many_y = slots
    from_xy = rest[8 : 8 + many_x * many_y]
    out, sens, first, fields, second, change, z_first, z_second, shares, y_shares = rest[-13:-3]
    held, held_sens, sems = rest[-3:]
    ext_x, ext_y, _ = mask.shape
    lane = lane_ids()
    every = slice(None)
    px, py = parity_of("gx"), parity_of("gy")

    def place_xy(slot_x, slot_y, side_x, side_y):
        packet = from_xy[many_x * slot_y + slot_x]
        for line, (kind, index, far_x, far_y) in enumerate(edge_lines(2 * side_x - 1, 2 * side_y - 1)):
            x = ext_x + far_x if side_x else -1 - far_x
            y = ext_y + far_y if side_y else -1 - far_y
            put_row(first, fields, kind, index, x, y, packet[line // 8, line % 8 : line % 8 + 1, :])
        place_z(z_first, packet[EDGE // 8], 8 + ext_y if side_y else 6, 2, side_x, ext_x)

    for slot_x in range(many_x):
        for slot_y in range(many_y):
            on_side(
                py,
                slot_y,
                lambda side_y: on_side(px, slot_x, lambda side_x: place_xy(slot_x, slot_y, side_x, side_y)),
            )

    for pair in ((-1, 0), (ext_x - 1, ext_x)):
        tiles = [Rim(x, ext_y) for x in pair]
        first_step(first, fields, second, change, tiles, shares=shares, y_shares=y_shares)

    z_step(z_first, z_second, (-1, ext_y - 1))

    def copies(x):
        return (
            pltpu.make_async_copy(held.at[:, x], out.at[:, x], sems.at[0, x]),
            pltpu.make_async_copy(held_sens.at[x], sens.at[x], sems.at[1, x]),
        )

    def second_step(planes):
        loaded = []
        for x, part in itertools.product(planes, range(ext_y // 8)):
            row = 8 + 8 * part
            pulled = []
            for j in range(19):
                cx, cy, cz = VELOCITIES[j]
                rows = pl.ds(row + cy, 8)
                value = second[j, x + 1 + cx, rows, :]
                if cz == 1:
                    edge = z_second[Z_UP.index(j), rows, :]
                    edge = pltpu.roll(edge, LANES // 2 - 3 - cx - x, 1)
                    value = jnp.where(lane == LANES - 1, edge, value)
                elif cz == -1:
                    edge = z_second[Z_DOWN.index(j), rows, :]
                    edge = pltpu.roll(edge, LANES - 2 - cx - x, 1)
                    value = jnp.where(lane == 0, edge, value)
                pulled.append(value)
            at = (x, pl.ds(8 * part, 8), every)
            rho = den[(0, *at)]
            here = [1.0 / rho, rho, vel[(0, 0, *at)], vel[(0, 1, *at)], vel[(0, 2, *at)], mask[at] > 0]
            loaded.append((at, pulled, here, change[0, x + 1, pl.ds(row, 8), :]))
        done = [collide(pulled, *here, range(19)) for _, pulled, here, _ in loaded]
        for (at, _, _, before), (after, gain) in zip(loaded, done):
            for j in range(19):
                held[(j, *at)] = after[j]
            held_sens[at] = before + gain
        for x in planes:
            for copy in copies(x):
                copy.start()

    second_step(range(ext_x // 2))

    @pl.loop(ext_x // 4, ext_x // 2)
    def _(pair):
        second_step([2 * pair, 2 * pair + 1])

    for x in range(ext_x):
        for copy in copies(x):
            copy.wait()


def shards(adjoint, density, velocity, pore_mask):
    ext_x, ext_y, ext_z = pore_mask.shape
    assert ext_z == LANES and ext_y % 8 == 0 and ext_x + 4 <= GROUP and ext_x == 8
    many_x = 2
    many_y, many_z = [1 if lax.axis_size(axis) == 2 else 2 for axis in ("gy", "gz")]
    vmem = pl.BlockSpec(memory_space=pltpu.VMEM)
    hbm = pl.BlockSpec(memory_space=pltpu.HBM)
    inputs = (adjoint, density, velocity, pore_mask)

    def array(*shape):
        return jax.ShapeDtypeStruct(shape, jnp.float32)

    def call(kernel, name, operands, shapes, limit, **more):
        more.setdefault("out_specs", [vmem] * len(shapes))
        more.setdefault("in_specs", [vmem] * len(operands))
        params = pltpu.CompilerParams(vmem_limit_bytes=limit * 1024 * 1024)
        return pl.pallas_call(kernel, out_shape=shapes, compiler_params=params, name=name, **more)(*operands)

    def partners(axis, slot):
        found = {}
        for at in range(slot, lax.axis_size(axis) - 1, 2):
            found[at], found[at + 1] = at + 1, at
        return found

    def ends(axis):
        last = lax.axis_size(axis) - 1
        return {0: last, last: 0}

    def swap(value, spares, *places):
        tables = {axis: partners(axis, slot) for axis, slot in places}
        axes = [axis for axis in ("gx", "gy", "gz") if axis in tables or axis in dict(spares)]
        sizes = [lax.axis_size(axis) for axis in axes]
        pairs = []
        for at in itertools.product(*[range(size) for size in sizes]):
            to = [tables.get(axis, {}).get(spot, spot) for axis, spot in zip(axes, at)]
            for spare, table in spares:
                if tuple(to) == at:
                    to = [table.get(spot, spot) if axis == spare else spot for axis, spot in zip(axes, at)]
            flat = []
            for spots in (at, to):
                index = 0
                for size, spot in zip(sizes, spots):
                    index = index * size + spot
                flat.append(index)
            pairs.append(tuple(flat))
        return lax.ppermute(value, tuple(axes), pairs)

    loaded = [jax.ShapeDtypeStruct(value.shape, value.dtype) for value in inputs]
    *held, near, a_z, b_z = (
        *call(
            functools.partial(pack_z_kernel, many_z),
            "pack_z",
            [pltpu.with_memory_space_constraint(value, pltpu.HBM) for value in inputs],
            loaded + [array(2, ext_y, LANES)] + [array(3, ext_y, LANES)] * many_z,
            8,
            in_specs=[hbm] * 4,
            scratch_shapes=[pltpu.SemaphoreType.DMA((7,))],
        ),
        *[None] * (2 - many_z),
    )
    from_z = [swap(value, [("gx", partners("gx", 0))], ("gz", slot)) for slot, value in enumerate((a_z, b_z)[:many_z])]

    rows = ext_y + 16
    adj, den, vel, mask = held
    shapes = (
        [array(19, ext_x + 4, rows, LANES)]
        + [array(SIDE + 1, ext_y, LANES)] * many_x
        + [array(FACE, ext_x, LANES)] * many_y
        + [array(EDGE // 8 + 1, 8, LANES)] * (many_x * many_y)
    )
    shifted = call(
        functools.partial(shift_kernel, (many_x, many_y)),
        "shift",
        (adj, den, vel, mask),
        shapes,
        8,
        cost_estimate=pl.CostEstimate(flops=1_000_000, bytes_accessed=2_500_000, transcendentals=0),
    )
    z_set, first, *packets = call(
        functools.partial(pack_xy_kernel, (many_x, many_y, many_z)),
        "pack_xy",
        (den, vel, mask, near, *from_z, *shifted),
        [array(Z_TILES, ext_y, LANES)] + shapes + [array(SIDE + 2, ext_x, LANES)] * many_y,
        8,
        input_output_aliases={4 + many_z + at: 1 + at for at in range(len(shapes))},
        scratch_shapes=[
            pltpu.VMEM((2, ext_y, LANES), jnp.float32),
            pltpu.VMEM((2, 5, ext_y, LANES), jnp.float32),
        ],
    )
    to_x, to_xy, to_y = packets[:many_x], packets[many_x + many_y : -many_y], packets[-many_y:]
    from_xy = [
        swap(to_xy[many_x * slot_y + slot_x], [], ("gx", slot_x), ("gy", slot_y))
        for slot_y in range(many_y)
        for slot_x in range(many_x)
    ]
    from_y = [swap(value, [("gz", partners("gz", 0))], ("gy", slot)) for slot, value in enumerate(to_y)]
    spares = [("gx", ends("gx"))]
    if lax.axis_size("gz") > 2:
        top = lax.axis_size("gz") - 1
        spares = [("gz", {top - 1: top, top: top - 1})] + spares
    from_x = [swap(value, spares, ("gx", slot)) for slot, value in enumerate(to_x)]

    fields, second, change = call(
        inner_kernel,
        "inner_step",
        (den, vel, mask, first),
        [array(5, ext_x + 2, rows, LANES), array(19, ext_x + 2, rows, LANES), array(1, ext_x + 2, rows, LANES)],
        8,
        cost_estimate=pl.CostEstimate(flops=40_000_000, bytes_accessed=8_000_000, transcendentals=0),
    )
    inout = (first, fields, second, change)
    inout = call(
        functools.partial(side_kernel, (many_x, many_y)),
        "side_step",
        (z_set, *inout, *from_x, *from_y),
        [array(*value.shape) for value in inout] + [array(Z_TILES, rows, LANES), array(5, rows, LANES), array(2, 5, rows, LANES), array(5, ext_x, rows, LANES)],
        8,
        input_output_aliases={1 + at: at for at in range(4)},
        cost_estimate=pl.CostEstimate(flops=40_000_000, bytes_accessed=8_000_000, transcendentals=0),
    )
    return call(
        functools.partial(last_kernel, (many_x, many_y)),
        "last_steps",
        (den, vel, mask, *inout, *from_xy),
        [array(19, ext_x, ext_y, LANES), array(ext_x, ext_y, LANES)] + [array(*value.shape) for value in inout],
        8,
        out_specs=[hbm] * 2 + [vmem] * 8,
        input_output_aliases={3 + at: 2 + at for at in range(8)},
        scratch_shapes=[
            pltpu.VMEM((19, ext_x, ext_y, LANES), jnp.float32),
            pltpu.VMEM((ext_x, ext_y, LANES), jnp.float32),
            pltpu.SemaphoreType.DMA((2, ext_x)),
        ],
    )[:2]


def solution(mesh):
    placed = (
        P(None, "gx", "gy", "gz"),
        P(None, "gx", "gy", "gz"),
        P(None, None, "gx", "gy", "gz"),
        P("gx", "gy", "gz"),
    )

    def whole(*arrays):
        return tuple(shards(*arrays))

    return jax.shard_map(
        whole,
        mesh=mesh,
        in_specs=placed,
        out_specs=(P(None, "gx", "gy", "gz"), P("gx", "gy", "gz")),
        check_vma=False,
    )
```

```python
import functools
import itertools

import jax
import jax.numpy as jnp
from jax import lax
from jax.experimental import pallas as pl
from jax.experimental.pallas import tpu as pltpu
from jax.sharding import PartitionSpec as P

VELOCITIES = [
    (0, 0, 0),
    (1, 0, 0),
    (-1, 0, 0),
    (0, 1, 0),
    (0, -1, 0),
    (0, 0, 1),
    (0, 0, -1),
    (1, 1, 0),
    (-1, -1, 0),
    (1, -1, 0),
    (-1, 1, 0),
    (1, 0, 1),
    (-1, 0, -1),
    (1, 0, -1),
    (-1, 0, 1),
    (0, 1, 1),
    (0, -1, -1),
    (0, 1, -1),
    (0, -1, 1),
]
OPPOSITE = [0, 2, 1, 4, 3, 6, 5, 8, 7, 10, 9, 12, 11, 14, 13, 16, 15, 18, 17]
OMEGA = 1.25
LANES = 128
GROUP = 16


def pops(axis, sign):
    return [j for j in range(19) if VELOCITIES[j][axis] == sign]


def mirrored(j):
    cx, cy, cz = VELOCITIES[j]
    return VELOCITIES.index((cx, cy, -cz))


Z_FLAT = pops(2, 0)
Z_UP = pops(2, 1)
Z_DOWN = [mirrored(j) for j in Z_UP]
RHO, UX, UY, UZ, KIND = range(5)
Z_PLACE = {("pop", j): (0, g) for g, j in enumerate(Z_FLAT[:8])}
Z_PLACE[("pop", Z_FLAT[8])] = (1, 5)
Z_PLACE[("field", RHO)] = (1, 6)
Z_PLACE[("field", KIND)] = (1, 7)
Z_PLACE[("field", UX)] = (2, 5)
Z_PLACE[("field", UY)] = (2, 6)
Z_PLACE[("field", UZ)] = (2, 7)
BELOW, ABOVE, OWN_LOW, OWN_HIGH, Z_TILES = 0, 3, 6, 7, 8


def face_lines(axis, toward):
    near = pops(axis, 0) + pops(axis, toward)
    lines = [("pop", j, 0) for j in near] + [("field", k, 0) for k in range(5)]
    return lines + [("pop", j, 1) for j in pops(axis, toward)]


def edge_lines(toward_x, toward_y):
    lines = [("field", k, 0, 0) for k in range(5)]
    for j in range(19):
        cx, cy, _ = VELOCITIES[j]
        if cx not in (0, toward_x) or cy not in (0, toward_y):
            continue
        lines.append(("pop", j, 0, 0))
        if cx:
            lines.append(("pop", j, 1, 0))
        if cy:
            lines.append(("pop", j, 0, 1))
        if cx and cy:
            lines.append(("pop", j, 1, 1))
    return lines


FACE = 24
EDGE = 24
SIDE = 15


def side_lines(axis, toward):
    full = [("pop", j) for j in pops(axis, toward)] + [("share", p) for p in range(5)]
    full += [("field", k) for k in (UX, UY, UZ, KIND)]
    ends = []
    for end in range(2):
        for j in pops(1 - axis, 1 - 2 * end):
            across = VELOCITIES[j][axis]
            if across in (0, toward):
                ends.append((j, abs(across), end))
    return full, ends


def lane_ids():
    return lax.broadcasted_iota(jnp.int32, (8, LANES), 1)


def field_of(refs, kind, index, at):
    adj, den, vel, mask = refs
    if kind == "pop":
        return adj[(index, *at)]
    if index == RHO:
        return den[(1, *at)]
    if index == KIND:
        return (mask[at] + 1).astype(jnp.float32)
    return vel[(1, index - UX, *at)]


def parity_of(axis):
    return lax.rem(lax.axis_index(axis), 2)


def on_side(parity, slot, act):
    @pl.when(parity == slot)
    def _():
        act(1)

    @pl.when(parity != slot)
    def _():
        act(0)


def has_partner(axis, slot):
    at = lax.axis_index(axis)
    to = at + jnp.where(lax.rem(at, 2) == slot, 1, -1)
    return (to >= 0) & (to < lax.axis_size(axis))


def pack_z_kernel(slots, adj_in, den_in, vel_in, mask_in, adj, den, vel, mask, near, *rest):
    packets, sems = rest[:slots], rest[slots]
    refs = (adj, den, vel, mask)
    ext_x, ext_y, _ = mask.shape
    starts = range(0, 19, 5)
    loads = [
        pltpu.make_async_copy(adj_in.at[start : min(start + 5, 19)], adj.at[start : min(start + 5, 19)], sems.at[at])
        for at, start in enumerate(starts)
    ] + [
        pltpu.make_async_copy(source, target, sems.at[len(starts) + at])
        for at, (source, target) in enumerate([(den_in, den), (vel_in, vel), (mask_in, mask)])
    ]
    for load in loads:
        load.start()
    lane = lane_ids()
    parity = parity_of("gz")
    parts = range(ext_y // 8)
    zero = jnp.zeros((8, LANES), jnp.float32)
    lows, highs = [[zero] * 3 for _ in parts], [[zero] * 3 for _ in parts]
    far_low, far_high = [zero for _ in parts], [zero for _ in parts]

    def gather(kind, index):
        for x, part in itertools.product(range(ext_x), parts):
            value = field_of(refs, kind, index, (x, pl.ds(8 * part, 8), slice(None)))
            if kind == "pop" and VELOCITIES[index][2] == 1:
                spot = GROUP * Z_UP.index(index) + 2 + x
                moved = pltpu.roll(value, spot, 1)
                lows[part][1] = jnp.where(lane == spot, moved, lows[part][1])
                far_low[part] = jnp.where(lane == spot + 1, moved, far_low[part])
            elif kind == "pop" and VELOCITIES[index][2] == -1:
                spot = GROUP * Z_DOWN.index(index) + 2 + x
                moved = pltpu.roll(value, spot, 1)
                highs[part][1] = jnp.where(lane == spot - 1, moved, highs[part][1])
                far_high[part] = jnp.where(lane == spot - 2, moved, far_high[part])
            else:
                tile, group = Z_PLACE[(kind, index)]
                spot = GROUP * group + 2 + x
                moved = pltpu.roll(value, spot, 1)
                lows[part][tile] = jnp.where(lane == spot, moved, lows[part][tile])
                highs[part][tile] = jnp.where(lane == spot - 1, moved, highs[part][tile])

    for start, load in zip(starts, loads):
        load.wait()
        for j in range(start, min(start + 5, 19)):
            gather("pop", j)
    for load in loads[len(starts) :]:
        load.wait()
    for k in range(5):
        gather("field", k)
    for part in parts:
        rows = pl.ds(8 * part, 8)
        low = lows[part]
        high = [pltpu.roll(tile, 1, 1) for tile in highs[part]]
        low[2] = jnp.where(lane < 5 * GROUP, pltpu.roll(far_low[part], LANES - 1, 1), low[2])
        high[2] = jnp.where(lane < 5 * GROUP, pltpu.roll(far_high[part], 2, 1), high[2])
        near[0, rows, :] = low[1]
        near[1, rows, :] = high[1]
        for slot in range(slots):
            there = has_partner("gz", slot)
            for tile in range(3):
                value = jnp.where(parity == slot, high[tile], low[tile])
                packets[slot][tile, rows, :] = jnp.where(there, value, 0.0)


def pack_lines(refs, first, packets, many_x, many_y, wanted, shares):
    to_x, y_lines = packets[:many_x], packets[many_x : many_x + many_y]
    to_xy = packets[many_x + many_y :]
    ext_x, ext_y, _ = refs[-1].shape
    every = slice(None)
    px, py = parity_of("gx"), parity_of("gy")

    def line_of(kind, index, x, y):
        if kind == "pop":
            return first[index, x + 2, y + 8 : y + 9, :]
        return field_of(refs, kind, index, (x, slice(y, y + 1), every))

    def pack_xy(slot_x, slot_y, side_x, side_y):
        packet = to_xy[many_x * slot_y + slot_x]
        for line, (kind, index, far_x, far_y) in enumerate(edge_lines(1 - 2 * side_x, 1 - 2 * side_y)):
            if wanted(kind, index):
                x = ext_x - 1 - far_x if side_x else far_x
                y = ext_y - 1 - far_y if side_y else far_y
                packet[line // 8, line % 8 : line % 8 + 1, :] = line_of(kind, index, x, y)

    def pack_y(slot, side):
        for line, (kind, index, depth) in enumerate(face_lines(1, 1 - 2 * side)):
            if wanted(kind, index):
                y = ext_y - 1 - depth if side else depth
                for x in range(ext_x):
                    y_lines[slot][line, x : x + 1, :] = line_of(kind, index, x, y)

    def pack_x(slot, side):
        full, ends = side_lines(0, 1 - 2 * side)
        for line, (kind, index) in enumerate(full):
            if kind == "field" and wanted(kind, index):
                to_x[slot][line] = field_of(refs, kind, index, (ext_x - 1 if side else 0, every, every))
            elif kind == "pop" and wanted(kind, index):
                to_x[slot][line] = first[index, (ext_x - 1 if side else 0) + 2, pl.ds(8, ext_y), :]
            elif kind == "share" and shares is not None:
                to_x[slot][line] = shares[side, index]
        for spot, (index, depth, end) in enumerate(ends):
            if wanted("pop", index):
                x = ext_x - 1 - depth if side else depth
                to_x[slot][SIDE - 1, spot : spot + 1, :] = line_of("pop", index, x, ext_y - 1 if end else 0)

    def when_there(there, packet, act):
        pl.when(there)(act)
        if shares is None:

            @pl.when(jnp.logical_not(there))
            def _():
                packet[...] = jnp.zeros(packet.shape, jnp.float32)

    for slot_y in range(many_y):
        there_y = has_partner("gy", slot_y)
        when_there(there_y, y_lines[slot_y], lambda: on_side(py, slot_y, functools.partial(pack_y, slot_y)))
        for slot_x in range(many_x):
            when_there(
                there_y & has_partner("gx", slot_x),
                to_xy[many_x * slot_y + slot_x],
                lambda: on_side(
                    py,
                    slot_y,
                    lambda side_y: on_side(px, slot_x, lambda side_x: pack_xy(slot_x, slot_y, side_x, side_y)),
                ),
            )
    for slot_x in range(many_x):
        when_there(
            has_partner("gx", slot_x), to_x[slot_x], lambda: on_side(px, slot_x, functools.partial(pack_x, slot_x))
        )


def is_flat(kind, index):
    return kind == "field" or VELOCITIES[index][2] == 0


def shift_kernel(slots, adj, den, vel, mask, first, *packets):
    many_x, many_y = slots
    _, ext_x, ext_y, _ = adj.shape
    for j in range(19):
        cz = VELOCITIES[j][2]
        for x, part in itertools.product(range(ext_x), range(ext_y // 8)):
            value = adj[j, x, pl.ds(8 * part, 8), :]
            first[j, 2 + x, pl.ds(8 + 8 * part, 8), :] = pltpu.roll(value, -cz % LANES, 1) if cz else value
    pack_lines((None, den, vel, mask), first, packets, many_x, many_y, is_flat, None)


def pack_xy_kernel(slots, den, vel, mask, near, *rest):
    many_x, many_y, many_z = slots
    count = many_x + many_y + many_x * many_y
    from_z, rest = rest[:many_z], rest[many_z + 1 + count :]
    z_set, first, packets, faces, shares = rest[0], rest[1], rest[2 : 2 + count], rest[-2], rest[-1]
    to_x, y_lines, to_xy = packets[:many_x], packets[many_x : many_x + many_y], packets[many_x + many_y :]
    to_y = rest[2 + count : -2]
    ext_x, ext_y = first.shape[1] - 4, near.shape[1]
    spot = lane_ids() % GROUP
    px, py, pz = parity_of("gx"), parity_of("gy"), parity_of("gz")

    z_set[OWN_LOW] = near[0]
    z_set[OWN_HIGH] = near[1]
    for tile in range(3):
        even = from_z[0][tile]
        odd = from_z[1][tile] if many_z > 1 else jnp.zeros_like(even)
        z_set[ABOVE + tile] = jnp.where(pz == 0, even, odd)
        z_set[BELOW + tile] = jnp.where(pz == 0, odd, even)

    for j in Z_UP + Z_DOWN:
        up = VELOCITIES[j][2] > 0
        group = (Z_UP if up else Z_DOWN).index(j)
        last = LANES - 1 if up else 0
        for part in range(ext_y // 8):
            halo = z_set[(ABOVE if up else BELOW) + 1, pl.ds(8 * part, 8), :]
            for x in range(ext_x):
                edge = pltpu.roll(halo, (last - 2 - GROUP * group - x) % LANES, 1)
                first[j, 2 + x, pl.ds(8 + 8 * part, 8), last : last + 1] = edge[:, last : last + 1]


    sub = lax.broadcasted_iota(jnp.int32, (8, LANES), 0)
    loaded = []
    for side, part in itertools.product(range(2), range(ext_y // 8)):
        toward, x = 1 - 2 * side, ext_x - 1 if side else 0
        pulled = []
        for j in range(19):
            cx, cy, _ = VELOCITIES[j]
            if cx == -toward:
                pulled.append(jnp.zeros((8, LANES), jnp.float32))
                continue
            value = first[j, x + 2 + cx, pl.ds(8 + 8 * part + cy, 8), :]
            if cy == -1 and part == 0:
                value = jnp.where(sub == 0, 0.0, value)
            if cy == 1 and part == ext_y // 8 - 1:
                value = jnp.where(sub == 7, 0.0, value)
            pulled.append(value)
        at = (x, pl.ds(8 * part, 8), slice(None))
        here = [den[(1, *at)], vel[(1, 0, *at)], vel[(1, 1, *at)], vel[(1, 2, *at)], mask[at] > 0]
        loaded.append((side, part, pulled, here))
    for side, part, pulled, (rho, ux, uy, uz, fluid) in loaded:
        wanted = pops(0, 1 - 2 * side)
        after, _ = collide(pulled, 1.0 / rho, rho, ux, uy, uz, None, wanted)
        for line, j in enumerate(wanted):
            shares[side, line, pl.ds(8 * part, 8), :] = jnp.where(fluid, after[j], 0.0)

    pack_lines((mask,), first, packets, many_x, many_y, lambda kind, index: not is_flat(kind, index), shares)

    for side in range(2):
        for part in range(ext_y // 8):
            rows = pl.ds(8 * part, 8)
            value = jnp.zeros((8, LANES), jnp.float32)
            for tile in range(Z_TILES):
                start = ext_x if side else 2
                moved = pltpu.roll(z_set[tile, rows, :], (2 * tile - start) % LANES, 1)
                value = jnp.where(spot // 2 == tile, moved, value)
            faces[side, rows, :] = value

    def add_xy(slot_x, slot_y, side_x, side_y):
        start = ext_y - 2 if side_y else 0
        to_xy[many_x * slot_y + slot_x][EDGE // 8, 0:2, :] = faces[side_x, start : start + 2, :]

    def add_y(slot, side):
        toward = 1 - 2 * side
        lines = {name: line for line, name in enumerate(face_lines(1, toward))}
        pulled = []
        for j in range(19):
            cx, cy, _ = VELOCITIES[j]
            if cy == -toward:
                pulled.append(jnp.zeros((8, LANES), jnp.float32))
                continue
            value = y_lines[slot][lines[("pop", j, abs(cy))]]
            if cx:
                value = jnp.where(sub == (7 if cx > 0 else 0), 0.0, pltpu.roll(value, -cx % 8, 0))
            pulled.append(value)
        rho, ux, uy, uz, kind = [y_lines[slot][lines[("field", k, 0)]] for k in range(5)]
        after, _ = collide(pulled, 1.0 / rho, rho, ux, uy, uz, None, pops(1, toward))
        full, ends = side_lines(1, toward)
        for line, (what, index) in enumerate(full):
            if what == "share":
                to_y[slot][line] = jnp.where(kind > 1.5, after[pops(1, toward)[index]], 0.0)
            else:
                to_y[slot][line] = y_lines[slot][lines[(what, index, 0)]]
        for spot, (index, depth, end) in enumerate(ends):
            x = ext_x - 1 if end else 0
            to_y[slot][SIDE - 1, spot : spot + 1, :] = y_lines[slot][lines[("pop", index, depth)], x : x + 1, :]
        start = ext_y - 2 if side else 0
        for tile in range(Z_TILES):
            row = 2 * tile % 8
            to_y[slot][SIDE + tile // 4, row : row + 2, :] = z_set[tile, start : start + 2, :]

    def add_x(slot, side):
        to_x[slot][SIDE] = faces[side]

    for slot_y in range(many_y):
        there_y = has_partner("gy", slot_y)
        pl.when(there_y)(lambda: on_side(py, slot_y, functools.partial(add_y, slot_y)))

        @pl.when(jnp.logical_not(there_y))
        def _():
            to_y[slot_y][...] = jnp.zeros(to_y[slot_y].shape, jnp.float32)

        for slot_x in range(many_x):
            pl.when(there_y & has_partner("gx", slot_x))(
                lambda: on_side(
                    py,
                    slot_y,
                    lambda side_y: on_side(px, slot_x, lambda side_x: add_xy(slot_x, slot_y, side_x, side_y)),
                )
            )
    for slot_x in range(many_x):
        pl.when(has_partner("gx", slot_x))(lambda: on_side(px, slot_x, functools.partial(add_x, slot_x)))


def collide(pulled, inverse, rho, ux, uy, uz, fluid, wanted):
    total = {}
    diff = {}
    for j in range(1, 19, 2):
        total[j] = pulled[j] + pulled[j + 1]
        diff[j] = pulled[j] - pulled[j + 1]
    in_xy, in_xz, in_yz = total[7] + total[9], total[11] + total[13], total[15] + total[17]
    two_x, two_y, two_z = total[1] + total[1], total[3] + total[3], total[5] + total[5]
    count = (12.0 * pulled[0] + (two_x + two_y)) + (two_z + (in_xy + (in_xz + in_yz)))
    flow_x = (diff[1] + diff[1]) + ((diff[7] + diff[9]) + (diff[11] + diff[13]))
    flow_y = (diff[3] + diff[3]) + ((diff[7] - diff[9]) + (diff[15] + diff[17]))
    flow_z = (diff[5] + diff[5]) + ((diff[11] - diff[13]) + (diff[15] - diff[17]))
    xx, yy, zz = two_x + (in_xy + in_xz), two_y + (in_xy + in_yz), two_z + (in_xz + in_yz)
    xy, xz, yz = total[7] - total[9], total[11] - total[13], total[15] - total[17]
    push_x = xx * ux + xy * uy + xz * uz
    push_y = xy * ux + yy * uy + yz * uz
    push_z = xz * ux + yz * uy + zz * uz
    usq = ux * ux + uy * uy + uz * uz
    push = ux * push_x + uy * push_y + uz * push_z
    base = count * (OMEGA / 36.0 + (OMEGA / 24.0) * usq) - (OMEGA / 8.0) * push - ux * inverse
    along_x = (OMEGA / 12.0) * (flow_x + 3.0 * push_x - ux * count) + inverse
    along_y = (OMEGA / 12.0) * (flow_y + 3.0 * push_y - uy * count)
    along_z = (OMEGA / 12.0) * (flow_z + 3.0 * push_z - uz * count)
    parts = {
        1: along_x,
        3: along_y,
        5: along_z,
        7: along_x + along_y,
        9: along_x - along_y,
        11: along_x + along_z,
        13: along_x - along_z,
        15: along_y + along_z,
        17: along_y - along_z,
    }
    out = {}
    for j in wanted:
        if j == 0:
            shift = base
        elif j % 2:
            shift = base + parts[j]
        else:
            shift = base - parts[j - 1]
        out[j] = (1.0 - OMEGA) * pulled[j] + shift
        if fluid is not None:
            out[j] = jnp.where(fluid, out[j], pulled[OPPOSITE[j]])
    change = (-1.0 / 6.0) * rho * (flow_x * ux + flow_y * uy + flow_z * uz)
    return out, change if fluid is None else jnp.where(fluid, change, 0.0)


def only(value, row):
    return jnp.where(lax.broadcasted_iota(jnp.int32, (8, LANES), 0) == row, value, 0.0)


class Plane:
    def across(self, shares, side, line):
        return shares[side, line, pl.ds(8 + self.row, 8), :]

    def rim(self, shares, line, toward):
        if toward != (-1 if self.row < 0 else 1):
            return 0.0
        return only(shares[line, self.x, pl.ds(8 + self.row, 8), :], 0 if toward < 0 else 1)

    def __init__(self, x, row):
        self.x, self.row = x, row

    def load(self, ref, lead, margin, cx=0, cy=0):
        return ref[lead, self.x + margin + cx, pl.ds(8 + self.row + cy, 8), :]

    def store(self, ref, lead, margin, value):
        ref[lead, self.x + margin, pl.ds(8 + self.row, 8), :] = value


class Rim:
    def __init__(self, x, ext_y):
        self.x, self.ext_y = x, ext_y

    def across(self, shares, side, line):
        upper, lower = shares[side, line, pl.ds(8 + self.ext_y - 1, 8), :], shares[side, line, pl.ds(1, 8), :]
        return jnp.where(lax.broadcasted_iota(jnp.int32, (8, LANES), 0) < 4, upper, lower)

    def rim(self, shares, line, toward):
        start = 1 if toward < 0 else 8 + self.ext_y - 1
        return only(shares[line, self.x, pl.ds(start, 8), :], 6 if toward < 0 else 1)

    def load(self, ref, lead, margin, cx=0, cy=0):
        at = self.x + margin + cx
        upper = ref[lead, at, pl.ds(8 + self.ext_y - 1 + cy, 8), :]
        lower = ref[lead, at, pl.ds(1 + cy, 8), :]
        return jnp.where(lax.broadcasted_iota(jnp.int32, (8, LANES), 0) < 4, upper, lower)

    def store(self, ref, lead, margin, value):
        at = self.x + margin
        ref[lead, at, pl.ds(8 + self.ext_y - 1, 2), :] = value[0:2]
        ref[lead, at, pl.ds(7, 2), :] = value[6:8]


def first_step(first, fields, second, change, tiles, outside=True, shares=None, y_shares=None):
    loaded = [
        (
            [tile.load(first, j, 2, *VELOCITIES[j][:2]) for j in range(19)],
            [tile.load(fields, k, 1) for k in range(5)],
        )
        for tile in tiles
    ]
    done = [
        collide(pulled, 1.0 / rho, rho, ux, uy, uz, kind > 1.5, range(19))
        for pulled, (rho, ux, uy, uz, kind) in loaded
    ]
    for tile, (_, here), (after, gain) in zip(tiles, loaded, done):
        inside = here[KIND] > 0.5
        side = None if shares is None else {-1: 0, second.shape[1] - 2: 1}.get(tile.x)
        for j in range(19):
            value = after[j]
            if side is not None and VELOCITIES[j][0] == 2 * side - 1:
                value = value + tile.across(shares, side, pops(0, 2 * side - 1).index(j))
            if side is None and y_shares is not None and VELOCITIES[j][1]:
                value = value + tile.rim(y_shares, pops(1, VELOCITIES[j][1]).index(j), VELOCITIES[j][1])
            if outside:
                value = jnp.where(inside, value, 0.0)
            cz = VELOCITIES[j][2]
            tile.store(second, j, 1, pltpu.roll(value, -cz % LANES, 1) if cz else value)
        tile.store(change, 0, 1, gain)


def inner_kernel(den, vel, mask, first, fields, second, change):
    refs = (None, den, vel, mask)
    ext_x, ext_y, _ = mask.shape
    every = slice(None)
    for k in range(5):
        fields[k, 1 : 1 + ext_x, pl.ds(8, ext_y), :] = field_of(refs, "field", k, (every, every, every))

    many = 3 if (ext_x - 2) % 3 == 0 else 1

    @pl.loop(0, (ext_x - 2) // many)
    def _(group):
        tiles = [Plane(many * group + at + 1, 1 + 8 * part) for at in range(many) for part in range(ext_y // 8)]
        first_step(first, fields, second, change, tiles, outside=False)


def put_row(first, fields, kind, index, x, y, value):
    row = y + 8
    if kind == "pop":
        first[index, x + 2, row : row + 1, :] = value
    else:
        fields[index, x + 1, row : row + 1, :] = value


def place_z(z_first, value, start, size, side, ext_x):
    rows = pl.ds(start, size)
    spot = lane_ids()[:size] % GROUP
    inside = spot >= 2 + ext_x if side else spot < 2
    for tile in range(Z_TILES):
        shift = (2 + ext_x if side else 0) - 2 * tile
        moved = pltpu.roll(value, shift % LANES, 1)[:size]
        z_first[tile, rows, :] = jnp.where(inside, moved, z_first[tile, rows, :])


def z_step(z_first, z_second, starts):
    lane = lane_ids()
    loaded = []
    for row in starts:

        def both(low_tile, high_tile, group, cx, cy):
            rows = pl.ds(8 + row + cy, 8)
            low = pltpu.roll(z_first[low_tile, rows, :], (-GROUP * group - cx) % LANES, 1)
            high = pltpu.roll(z_first[high_tile, rows, :], (LANES // 2 - GROUP * group - cx) % LANES, 1)
            return jnp.where(lane < LANES // 2, low, high)

        pulled = []
        for j in range(19):
            cx, cy, cz = VELOCITIES[j]
            if cz == 0:
                tile, group = Z_PLACE[("pop", j)]
                pulled.append(both(BELOW + tile, ABOVE + tile, group, cx, cy))
            elif cz == 1:
                pulled.append(both(OWN_LOW, ABOVE + 2, Z_UP.index(j), cx, cy))
            else:
                pulled.append(both(BELOW + 2, OWN_HIGH, Z_DOWN.index(j), cx, cy))
        places = [Z_PLACE[("field", k)] for k in range(5)]
        loaded.append((pulled, [both(BELOW + tile, ABOVE + tile, group, 0, 0) for tile, group in places]))
    done = [
        collide(pulled, 1.0 / rho, rho, ux, uy, uz, kind > 1.5, Z_UP + Z_DOWN)[0]
        for pulled, (rho, ux, uy, uz, kind) in loaded
    ]
    for row, (_, here), after in zip(starts, loaded, done):
        for group in range(5):
            value = jnp.where(lane < LANES // 2, after[Z_DOWN[group]], after[Z_UP[group]])
            z_second[group, pl.ds(8 + row, 8), :] = jnp.where(here[KIND] > 0.5, value, 0.0)


def second_step(refs, second, z_second, change, held, held_sens, planes):
    den, vel, mask = refs
    _, ext_y, _ = mask.shape
    lane = lane_ids()
    every = slice(None)
    loaded = []
    for x, part in itertools.product(planes, range(ext_y // 8)):
        row = 8 + 8 * part
        pulled = []
        for j in range(19):
            cx, cy, cz = VELOCITIES[j]
            rows = pl.ds(row + cy, 8)
            value = second[j, x + 1 + cx, rows, :]
            if cz == 1:
                edge = z_second[Z_UP.index(j), rows, :]
                edge = pltpu.roll(edge, LANES // 2 - 3 - cx - x, 1)
                value = jnp.where(lane == LANES - 1, edge, value)
            elif cz == -1:
                edge = z_second[Z_DOWN.index(j), rows, :]
                edge = pltpu.roll(edge, LANES - 2 - cx - x, 1)
                value = jnp.where(lane == 0, edge, value)
            pulled.append(value)
        at = (x, pl.ds(8 * part, 8), every)
        rho = den[(0, *at)]
        here = [1.0 / rho, rho, vel[(0, 0, *at)], vel[(0, 1, *at)], vel[(0, 2, *at)], mask[at] > 0]
        loaded.append((at, pulled, here, change[0, x + 1, pl.ds(row, 8), :]))
    done = [collide(pulled, *here, range(19)) for _, pulled, here, _ in loaded]
    for (at, _, _, before), (after, gain) in zip(loaded, done):
        for j in range(19):
            held[(j, *at)] = after[j]
        held_sens[at] = before + gain


def side_kernel(slots, den, vel, mask, z_set, *rest):
    many_x, many_y = slots
    from_x, from_y = rest[4 : 4 + many_x], rest[4 + many_x : 4 + many_x + many_y]
    first, fields, second, change, z_first, z_second, shares, y_shares, held, held_sens = rest[-10:]
    _, ext_y, _ = z_set.shape
    ext_x = change.shape[1] - 2
    inner = pl.ds(8, ext_y)
    put = functools.partial(put_row, first, fields)
    z_first[:, inner, :] = z_set[...]

    def place_y(slot, side):
        packet = from_y[slot]
        toward = 2 * side - 1
        near = ext_y if side else -1
        nothing = jnp.zeros((1, LANES), jnp.float32)
        full, ends = side_lines(1, toward)
        for x in range(ext_x):
            for j in pops(1, 0):
                put("pop", j, x, near, nothing)
            for j in pops(1, toward):
                put("pop", j, x, near + toward, nothing)
            put("field", RHO, x, near, jnp.full((1, LANES), jnp.inf, jnp.float32))
            for line, (kind, index) in enumerate(full):
                if kind == "share":
                    y_shares[index, x, near + 8 : near + 9, :] = packet[line, x : x + 1, :]
                else:
                    put(kind, index, x, near, packet[line, x : x + 1, :])
        for spot, (index, depth, end) in enumerate(ends):
            put("pop", index, ext_x - 1 if end else 0, near + toward * depth, packet[SIDE - 1, spot : spot + 1, :])
        start = 8 + ext_y if side else 6
        for tile in range(Z_TILES):
            row = 2 * tile % 8
            z_first[tile, start : start + 2, :] = packet[SIDE + tile // 4, row : row + 2, :]
        if many_y == 1:
            clear_y(1 - side)

    def clear_y(side):
        nothing = jnp.zeros((1, LANES), jnp.float32)
        y = ext_y if side else -1
        for x in range(-2, ext_x + 2):
            for j in pops(1, 2 * side - 1):
                put("pop", j, x, y, nothing)
        for x in range(-1, ext_x + 1):
            put("field", KIND, x, y, nothing)
        start = 8 + ext_y if side else 6
        for tile in range(Z_TILES):
            z_first[tile, start : start + 2, :] = jnp.zeros((2, LANES), jnp.float32)

    def place_x(slot, side):
        packet = from_x[slot]
        toward = 2 * side - 1
        near = ext_x if side else -1
        nothing = jnp.zeros((ext_y, LANES), jnp.float32)
        for j in pops(0, 0):
            first[j, near + 2, inner, :] = nothing
        for j in pops(0, toward):
            first[j, near + toward + 2, inner, :] = nothing
        fields[RHO, near + 1, inner, :] = jnp.full((ext_y, LANES), jnp.inf, jnp.float32)
        full, ends = side_lines(0, toward)
        for line, (kind, index) in enumerate(full):
            if kind == "pop":
                first[index, near + 2, inner, :] = packet[line]
            elif kind == "share":
                shares[side, index, inner, :] = packet[line]
            else:
                fields[index, near + 1, inner, :] = packet[line]
        for spot, (index, depth, end) in enumerate(ends):
            put("pop", index, near + toward * depth, ext_y - 1 if end else 0, packet[SIDE - 1, spot : spot + 1, :])
        for part in range(ext_y // 8):
            place_z(z_first, packet[SIDE, pl.ds(8 * part, 8), :], 8 + 8 * part, 8, side, ext_x)

    shares[:, :, pl.ds(0, 8), :] = jnp.zeros((2, 5, 8, LANES), jnp.float32)
    shares[:, :, pl.ds(8 + ext_y, 8), :] = jnp.zeros((2, 5, 8, LANES), jnp.float32)
    for slot_y in range(many_y):
        on_side(parity_of("gy"), slot_y, functools.partial(place_y, slot_y))
    for slot_x in range(many_x):
        on_side(parity_of("gx"), slot_x, functools.partial(place_x, slot_x))

    starts = range(1, ext_y, 8)
    first_step(first, fields, second, change, [Plane(x, row) for x in (0, ext_x - 1) for row in starts], outside=False)
    first_step(first, fields, second, change, [Plane(x, row) for x in (-1, ext_x) for row in starts], shares=shares)
    z_step(z_first, z_second, range(7, ext_y - 8, 8))
    many = 3 if (ext_x - 2) % 3 == 0 else 1

    @pl.loop(0, (ext_x - 2) // many)
    def _(group):
        tiles = [Rim(many * group + at + 1, ext_y) for at in range(many)]
        first_step(first, fields, second, change, tiles, y_shares=y_shares)

    z_step(z_first, z_second, (-1, ext_y - 1))
    second_step((den, vel, mask), second, z_second, change, held, held_sens, range(2, ext_x - 2))


def last_kernel(slots, den, vel, mask, *rest):
    many_x, many_y = slots
    from_xy = rest[10 : 10 + many_x * many_y]
    out, sens, first, fields, second, change, z_first, z_second, shares, y_shares, held, held_sens, sems = rest[-13:]
    ext_x, ext_y, _ = mask.shape
    lane = lane_ids()
    every = slice(None)
    px, py = parity_of("gx"), parity_of("gy")

    def copies(x):
        return (
            pltpu.make_async_copy(held.at[:, x], out.at[:, x], sems.at[0, x]),
            pltpu.make_async_copy(held_sens.at[x], sens.at[x], sems.at[1, x]),
        )

    for x in range(2, ext_x - 2):
        for copy in copies(x):
            copy.start()

    def place_xy(slot_x, slot_y, side_x, side_y):
        packet = from_xy[many_x * slot_y + slot_x]
        for line, (kind, index, far_x, far_y) in enumerate(edge_lines(2 * side_x - 1, 2 * side_y - 1)):
            x = ext_x + far_x if side_x else -1 - far_x
            y = ext_y + far_y if side_y else -1 - far_y
            put_row(first, fields, kind, index, x, y, packet[line // 8, line % 8 : line % 8 + 1, :])
        place_z(z_first, packet[EDGE // 8], 8 + ext_y if side_y else 6, 2, side_x, ext_x)

    for slot_x in range(many_x):
        for slot_y in range(many_y):
            on_side(
                py,
                slot_y,
                lambda side_y: on_side(px, slot_x, lambda side_x: place_xy(slot_x, slot_y, side_x, side_y)),
            )

    for pair in ((-1, 0), (ext_x - 1, ext_x)):
        tiles = [Rim(x, ext_y) for x in pair]
        first_step(first, fields, second, change, tiles, shares=shares, y_shares=y_shares)

    z_step(z_first, z_second, (-1, ext_y - 1))

    planes = [0, 1, ext_x - 2, ext_x - 1]
    for pair in (planes[:2], planes[2:]):
        second_step((den, vel, mask), second, z_second, change, held, held_sens, pair)
        for x in pair:
            for copy in copies(x):
                copy.start()

    for x in range(ext_x):
        for copy in copies(x):
            copy.wait()


def shards(adjoint, density, velocity, pore_mask):
    ext_x, ext_y, ext_z = pore_mask.shape
    assert ext_z == LANES and ext_y % 8 == 0 and ext_x + 4 <= GROUP and ext_x == 8
    many_x = 2
    many_y, many_z = [1 if lax.axis_size(axis) == 2 else 2 for axis in ("gy", "gz")]
    vmem = pl.BlockSpec(memory_space=pltpu.VMEM)
    hbm = pl.BlockSpec(memory_space=pltpu.HBM)
    inputs = (adjoint, density, velocity, pore_mask)

    def array(*shape):
        return jax.ShapeDtypeStruct(shape, jnp.float32)

    def call(kernel, name, operands, shapes, limit, **more):
        more.setdefault("out_specs", [vmem] * len(shapes))
        more.setdefault("in_specs", [vmem] * len(operands))
        params = pltpu.CompilerParams(vmem_limit_bytes=limit * 1024 * 1024)
        return pl.pallas_call(kernel, out_shape=shapes, compiler_params=params, name=name, **more)(*operands)

    def partners(axis, slot):
        found = {}
        for at in range(slot, lax.axis_size(axis) - 1, 2):
            found[at], found[at + 1] = at + 1, at
        return found

    def ends(axis):
        last = lax.axis_size(axis) - 1
        return {0: last, last: 0}

    def swap(value, spares, *places):
        tables = {axis: partners(axis, slot) for axis, slot in places}
        axes = [axis for axis in ("gx", "gy", "gz") if axis in tables or axis in dict(spares)]
        sizes = [lax.axis_size(axis) for axis in axes]
        pairs = []
        for at in itertools.product(*[range(size) for size in sizes]):
            to = [tables.get(axis, {}).get(spot, spot) for axis, spot in zip(axes, at)]
            for spare, table in spares:
                if tuple(to) == at:
                    to = [table.get(spot, spot) if axis == spare else spot for axis, spot in zip(axes, at)]
            flat = []
            for spots in (at, to):
                index = 0
                for size, spot in zip(sizes, spots):
                    index = index * size + spot
                flat.append(index)
            pairs.append(tuple(flat))
        return lax.ppermute(value, tuple(axes), pairs)

    loaded = [jax.ShapeDtypeStruct(value.shape, value.dtype) for value in inputs]
    *held, near, a_z, b_z = (
        *call(
            functools.partial(pack_z_kernel, many_z),
            "pack_z",
            [pltpu.with_memory_space_constraint(value, pltpu.HBM) for value in inputs],
            loaded + [array(2, ext_y, LANES)] + [array(3, ext_y, LANES)] * many_z,
            8,
            in_specs=[hbm] * 4,
            scratch_shapes=[pltpu.SemaphoreType.DMA((7,))],
        ),
        *[None] * (2 - many_z),
    )
    from_z = [swap(value, [("gx", partners("gx", 0))], ("gz", slot)) for slot, value in enumerate((a_z, b_z)[:many_z])]

    rows = ext_y + 16
    adj, den, vel, mask = held
    shapes = (
        [array(19, ext_x + 4, rows, LANES)]
        + [array(SIDE + 1, ext_y, LANES)] * many_x
        + [array(FACE, ext_x, LANES)] * many_y
        + [array(EDGE // 8 + 1, 8, LANES)] * (many_x * many_y)
    )
    shifted = call(
        functools.partial(shift_kernel, (many_x, many_y)),
        "shift",
        (adj, den, vel, mask),
        shapes,
        8,
        cost_estimate=pl.CostEstimate(flops=1_000_000, bytes_accessed=2_500_000, transcendentals=0),
    )
    z_set, first, *packets = call(
        functools.partial(pack_xy_kernel, (many_x, many_y, many_z)),
        "pack_xy",
        (den, vel, mask, near, *from_z, *shifted),
        [array(Z_TILES, ext_y, LANES)] + shapes + [array(SIDE + 2, ext_x, LANES)] * many_y,
        8,
        input_output_aliases={4 + many_z + at: 1 + at for at in range(len(shapes))},
        scratch_shapes=[
            pltpu.VMEM((2, ext_y, LANES), jnp.float32),
            pltpu.VMEM((2, 5, ext_y, LANES), jnp.float32),
        ],
    )
    to_x, to_xy, to_y = packets[:many_x], packets[many_x + many_y : -many_y], packets[-many_y:]
    from_xy = [
        swap(to_xy[many_x * slot_y + slot_x], [], ("gx", slot_x), ("gy", slot_y))
        for slot_y in range(many_y)
        for slot_x in range(many_x)
    ]
    from_y = [swap(value, [("gz", partners("gz", 0))], ("gy", slot)) for slot, value in enumerate(to_y)]
    spares = [("gx", ends("gx"))]
    if lax.axis_size("gz") > 2:
        top = lax.axis_size("gz") - 1
        spares = [("gz", {top - 1: top, top: top - 1})] + spares
    from_x = [swap(value, spares, ("gx", slot)) for slot, value in enumerate(to_x)]

    fields, second, change = call(
        inner_kernel,
        "inner_step",
        (den, vel, mask, first),
        [array(5, ext_x + 2, rows, LANES), array(19, ext_x + 2, rows, LANES), array(1, ext_x + 2, rows, LANES)],
        8,
        cost_estimate=pl.CostEstimate(flops=40_000_000, bytes_accessed=8_000_000, transcendentals=0),
    )
    inout = (first, fields, second, change)
    inout = call(
        functools.partial(side_kernel, (many_x, many_y)),
        "side_step",
        (den, vel, mask, z_set, *inout, *from_x, *from_y),
        [array(*value.shape) for value in inout] + [array(Z_TILES, rows, LANES), array(5, rows, LANES), array(2, 5, rows, LANES), array(5, ext_x, rows, LANES)]
        + [array(19, ext_x, ext_y, LANES), array(ext_x, ext_y, LANES)],
        8,
        input_output_aliases={4 + at: at for at in range(4)},
        cost_estimate=pl.CostEstimate(flops=40_000_000, bytes_accessed=8_000_000, transcendentals=0),
    )
    return call(
        functools.partial(last_kernel, (many_x, many_y)),
        "last_steps",
        (den, vel, mask, *inout, *from_xy),
        [array(19, ext_x, ext_y, LANES), array(ext_x, ext_y, LANES)] + [array(*value.shape) for value in inout],
        8,
        out_specs=[hbm] * 2 + [vmem] * 10,
        input_output_aliases={3 + at: 2 + at for at in range(10)},
        scratch_shapes=[pltpu.SemaphoreType.DMA((2, ext_x))],
    )[:2]


def solution(mesh):
    placed = (
        P(None, "gx", "gy", "gz"),
        P(None, "gx", "gy", "gz"),
        P(None, None, "gx", "gy", "gz"),
        P("gx", "gy", "gz"),
    )

    def whole(*arrays):
        return tuple(shards(*arrays))

    return jax.shard_map(
        whole,
        mesh=mesh,
        in_specs=placed,
        out_specs=(P(None, "gx", "gy", "gz"), P("gx", "gy", "gz")),
        check_vma=False,
    )
```

```python
import functools
import itertools

import jax
import jax.numpy as jnp
from jax import lax
from jax.experimental import pallas as pl
from jax.experimental.pallas import tpu as pltpu
from jax.sharding import PartitionSpec as P

VELOCITIES = [
    (0, 0, 0),
    (1, 0, 0),
    (-1, 0, 0),
    (0, 1, 0),
    (0, -1, 0),
    (0, 0, 1),
    (0, 0, -1),
    (1, 1, 0),
    (-1, -1, 0),
    (1, -1, 0),
    (-1, 1, 0),
    (1, 0, 1),
    (-1, 0, -1),
    (1, 0, -1),
    (-1, 0, 1),
    (0, 1, 1),
    (0, -1, -1),
    (0, 1, -1),
    (0, -1, 1),
]
OPPOSITE = [0, 2, 1, 4, 3, 6, 5, 8, 7, 10, 9, 12, 11, 14, 13, 16, 15, 18, 17]
OMEGA = 1.25
LANES = 128
GROUP = 16


def pops(axis, sign):
    return [j for j in range(19) if VELOCITIES[j][axis] == sign]


def mirrored(j):
    cx, cy, cz = VELOCITIES[j]
    return VELOCITIES.index((cx, cy, -cz))


Z_FLAT = pops(2, 0)
Z_UP = pops(2, 1)
Z_DOWN = [mirrored(j) for j in Z_UP]
RHO, UX, UY, UZ, KIND = range(5)
Z_PLACE = {("pop", j): (0, g) for g, j in enumerate(Z_FLAT[:8])}
Z_PLACE[("pop", Z_FLAT[8])] = (1, 5)
Z_PLACE[("field", RHO)] = (1, 6)
Z_PLACE[("field", KIND)] = (1, 7)
Z_PLACE[("field", UX)] = (2, 5)
Z_PLACE[("field", UY)] = (2, 6)
Z_PLACE[("field", UZ)] = (2, 7)
BELOW, ABOVE, OWN_LOW, OWN_HIGH, Z_TILES = 0, 3, 6, 7, 8


def face_lines(axis, toward):
    near = pops(axis, 0) + pops(axis, toward)
    lines = [("pop", j, 0) for j in near] + [("field", k, 0) for k in range(5)]
    return lines + [("pop", j, 1) for j in pops(axis, toward)]


def edge_lines(toward_x, toward_y):
    lines = [("field", k, 0, 0) for k in range(5)]
    for j in range(19):
        cx, cy, _ = VELOCITIES[j]
        if cx not in (0, toward_x) or cy not in (0, toward_y):
            continue
        lines.append(("pop", j, 0, 0))
        if cx:
            lines.append(("pop", j, 1, 0))
        if cy:
            lines.append(("pop", j, 0, 1))
        if cx and cy:
            lines.append(("pop", j, 1, 1))
    return lines


FACE = 24
EDGE = 24
SIDE = 15


def side_lines(axis, toward):
    full = [("pop", j) for j in pops(axis, toward)] + [("share", p) for p in range(5)]
    full += [("field", k) for k in (UX, UY, UZ, KIND)]
    ends = []
    for end in range(2):
        for j in pops(1 - axis, 1 - 2 * end):
            across = VELOCITIES[j][axis]
            if across in (0, toward):
                ends.append((j, abs(across), end))
    return full, ends


def lane_ids():
    return lax.broadcasted_iota(jnp.int32, (8, LANES), 1)


def field_of(refs, kind, index, at):
    adj, den, vel, mask = refs
    if kind == "pop":
        return adj[(index, *at)]
    if index == RHO:
        return den[(1, *at)]
    if index == KIND:
        return (mask[at] + 1).astype(jnp.float32)
    return vel[(1, index - UX, *at)]


def parity_of(axis):
    return lax.rem(lax.axis_index(axis), 2)


def on_side(parity, slot, act):
    @pl.when(parity == slot)
    def _():
        act(1)

    @pl.when(parity != slot)
    def _():
        act(0)


def has_partner(axis, slot):
    at = lax.axis_index(axis)
    to = at + jnp.where(lax.rem(at, 2) == slot, 1, -1)
    return (to >= 0) & (to < lax.axis_size(axis))


def pack_z_kernel(slots, adj_in, den_in, vel_in, mask_in, adj, den, vel, mask, near, *rest):
    packets, sems = rest[:slots], rest[slots]
    refs = (adj, den, vel, mask)
    ext_x, ext_y, _ = mask.shape
    starts = range(0, 19, 5)
    loads = [
        pltpu.make_async_copy(adj_in.at[start : min(start + 5, 19)], adj.at[start : min(start + 5, 19)], sems.at[at])
        for at, start in enumerate(starts)
    ] + [
        pltpu.make_async_copy(source, target, sems.at[len(starts) + at])
        for at, (source, target) in enumerate([(den_in, den), (vel_in, vel), (mask_in, mask)])
    ]
    for load in loads:
        load.start()
    lane = lane_ids()
    parity = parity_of("gz")
    parts = range(ext_y // 8)
    zero = jnp.zeros((8, LANES), jnp.float32)
    lows, highs = [[zero] * 3 for _ in parts], [[zero] * 3 for _ in parts]
    far_low, far_high = [zero for _ in parts], [zero for _ in parts]

    def gather(kind, index):
        for x, part in itertools.product(range(ext_x), parts):
            value = field_of(refs, kind, index, (x, pl.ds(8 * part, 8), slice(None)))
            if kind == "pop" and VELOCITIES[index][2] == 1:
                spot = GROUP * Z_UP.index(index) + 2 + x
                moved = pltpu.roll(value, spot, 1)
                lows[part][1] = jnp.where(lane == spot, moved, lows[part][1])
                far_low[part] = jnp.where(lane == spot + 1, moved, far_low[part])
            elif kind == "pop" and VELOCITIES[index][2] == -1:
                spot = GROUP * Z_DOWN.index(index) + 2 + x
                moved = pltpu.roll(value, spot, 1)
                highs[part][1] = jnp.where(lane == spot - 1, moved, highs[part][1])
                far_high[part] = jnp.where(lane == spot - 2, moved, far_high[part])
            else:
                tile, group = Z_PLACE[(kind, index)]
                spot = GROUP * group + 2 + x
                moved = pltpu.roll(value, spot, 1)
                lows[part][tile] = jnp.where(lane == spot, moved, lows[part][tile])
                highs[part][tile] = jnp.where(lane == spot - 1, moved, highs[part][tile])

    for start, load in zip(starts, loads):
        load.wait()
        for j in range(start, min(start + 5, 19)):
            gather("pop", j)
    for load in loads[len(starts) :]:
        load.wait()
    for k in range(5):
        gather("field", k)
    for part in parts:
        rows = pl.ds(8 * part, 8)
        low = lows[part]
        high = [pltpu.roll(tile, 1, 1) for tile in highs[part]]
        low[2] = jnp.where(lane < 5 * GROUP, pltpu.roll(far_low[part], LANES - 1, 1), low[2])
        high[2] = jnp.where(lane < 5 * GROUP, pltpu.roll(far_high[part], 2, 1), high[2])
        near[0, rows, :] = low[1]
        near[1, rows, :] = high[1]
        for slot in range(slots):
            there = has_partner("gz", slot)
            sent = [jnp.where(there, jnp.where(parity == slot, up, down), 0.0) for up, down in zip(high, low)]
            mine = (lane + (GROUP - 2)) % GROUP < GROUP // 2
            packets[slot][0, rows, :] = jnp.where(mine, sent[0], pltpu.roll(sent[1], GROUP // 2, 1))
            packets[slot][1, rows, :] = sent[2]


def pack_lines(refs, first, packets, many_x, many_y, wanted, shares):
    to_x, y_lines = packets[:many_x], packets[many_x : many_x + many_y]
    to_xy = packets[many_x + many_y :]
    ext_x, ext_y, _ = refs[-1].shape
    every = slice(None)
    px, py = parity_of("gx"), parity_of("gy")

    def line_of(kind, index, x, y):
        if kind == "pop":
            return first[index, x + 2, y + 8 : y + 9, :]
        return field_of(refs, kind, index, (x, slice(y, y + 1), every))

    def pack_xy(slot_x, slot_y, side_x, side_y):
        packet = to_xy[many_x * slot_y + slot_x]
        for line, (kind, index, far_x, far_y) in enumerate(edge_lines(1 - 2 * side_x, 1 - 2 * side_y)):
            if wanted(kind, index):
                x = ext_x - 1 - far_x if side_x else far_x
                y = ext_y - 1 - far_y if side_y else far_y
                packet[line // 8, line % 8 : line % 8 + 1, :] = line_of(kind, index, x, y)

    def pack_y(slot, side):
        for line, (kind, index, depth) in enumerate(face_lines(1, 1 - 2 * side)):
            if wanted(kind, index):
                y = ext_y - 1 - depth if side else depth
                for x in range(ext_x):
                    y_lines[slot][line, x : x + 1, :] = line_of(kind, index, x, y)

    def pack_x(slot, side):
        full, ends = side_lines(0, 1 - 2 * side)
        for line, (kind, index) in enumerate(full):
            if kind == "field" and wanted(kind, index):
                to_x[slot][line] = field_of(refs, kind, index, (ext_x - 1 if side else 0, every, every))
            elif kind == "pop" and wanted(kind, index):
                to_x[slot][line] = first[index, (ext_x - 1 if side else 0) + 2, pl.ds(8, ext_y), :]
            elif kind == "share" and shares is not None:
                to_x[slot][line] = shares[side, index]
        for spot, (index, depth, end) in enumerate(ends):
            if wanted("pop", index):
                x = ext_x - 1 - depth if side else depth
                to_x[slot][SIDE - 1, spot : spot + 1, :] = line_of("pop", index, x, ext_y - 1 if end else 0)

    def when_there(there, packet, act):
        pl.when(there)(act)
        if shares is None:

            @pl.when(jnp.logical_not(there))
            def _():
                packet[...] = jnp.zeros(packet.shape, jnp.float32)

    for slot_y in range(many_y):
        there_y = has_partner("gy", slot_y)
        when_there(there_y, y_lines[slot_y], lambda: on_side(py, slot_y, functools.partial(pack_y, slot_y)))
        for slot_x in range(many_x):
            when_there(
                there_y & has_partner("gx", slot_x),
                to_xy[many_x * slot_y + slot_x],
                lambda: on_side(
                    py,
                    slot_y,
                    lambda side_y: on_side(px, slot_x, lambda side_x: pack_xy(slot_x, slot_y, side_x, side_y)),
                ),
            )
    for slot_x in range(many_x):
        when_there(
            has_partner("gx", slot_x), to_x[slot_x], lambda: on_side(px, slot_x, functools.partial(pack_x, slot_x))
        )


def is_flat(kind, index):
    return kind == "field" or VELOCITIES[index][2] == 0


def shift_kernel(slots, adj, den, vel, mask, first, *packets):
    many_x, many_y = slots
    _, ext_x, ext_y, _ = adj.shape
    for j in range(19):
        cz = VELOCITIES[j][2]
        for x, part in itertools.product(range(ext_x), range(ext_y // 8)):
            value = adj[j, x, pl.ds(8 * part, 8), :]
            first[j, 2 + x, pl.ds(8 + 8 * part, 8), :] = pltpu.roll(value, -cz % LANES, 1) if cz else value
    pack_lines((None, den, vel, mask), first, packets, many_x, many_y, is_flat, None)


def pack_xy_kernel(slots, den, vel, mask, near, *rest):
    many_x, many_y, many_z = slots
    count = many_x + many_y + many_x * many_y
    from_z, rest = rest[:many_z], rest[many_z + 1 + count :]
    z_set, first, packets, faces, shares = rest[0], rest[1], rest[2 : 2 + count], rest[-2], rest[-1]
    to_x, y_lines, to_xy = packets[:many_x], packets[many_x : many_x + many_y], packets[many_x + many_y :]
    to_y = rest[2 + count : -2]
    ext_x, ext_y = first.shape[1] - 4, near.shape[1]
    spot = lane_ids() % GROUP
    px, py, pz = parity_of("gx"), parity_of("gy"), parity_of("gz")

    z_set[OWN_LOW] = near[0]
    z_set[OWN_HIGH] = near[1]

    def taken(slot, tile):
        if tile == 1:
            return pltpu.roll(from_z[slot][0], LANES - GROUP // 2, 1)
        return from_z[slot][tile // 2]

    for tile in range(3):
        even = taken(0, tile)
        odd = taken(1, tile) if many_z > 1 else jnp.zeros_like(even)
        z_set[ABOVE + tile] = jnp.where(pz == 0, even, odd)
        z_set[BELOW + tile] = jnp.where(pz == 0, odd, even)

    for j in Z_UP + Z_DOWN:
        up = VELOCITIES[j][2] > 0
        group = (Z_UP if up else Z_DOWN).index(j)
        last = LANES - 1 if up else 0
        for part in range(ext_y // 8):
            halo = z_set[(ABOVE if up else BELOW) + 1, pl.ds(8 * part, 8), :]
            for x in range(ext_x):
                edge = pltpu.roll(halo, (last - 2 - GROUP * group - x) % LANES, 1)
                first[j, 2 + x, pl.ds(8 + 8 * part, 8), last : last + 1] = edge[:, last : last + 1]


    sub = lax.broadcasted_iota(jnp.int32, (8, LANES), 0)
    loaded = []
    for side, part in itertools.product(range(2), range(ext_y // 8)):
        toward, x = 1 - 2 * side, ext_x - 1 if side else 0
        pulled = []
        for j in range(19):
            cx, cy, _ = VELOCITIES[j]
            if cx == -toward:
                pulled.append(jnp.zeros((8, LANES), jnp.float32))
                continue
            value = first[j, x + 2 + cx, pl.ds(8 + 8 * part + cy, 8), :]
            if cy == -1 and part == 0:
                value = jnp.where(sub == 0, 0.0, value)
            if cy == 1 and part == ext_y // 8 - 1:
                value = jnp.where(sub == 7, 0.0, value)
            pulled.append(value)
        at = (x, pl.ds(8 * part, 8), slice(None))
        here = [den[(1, *at)], vel[(1, 0, *at)], vel[(1, 1, *at)], vel[(1, 2, *at)], mask[at] > 0]
        loaded.append((side, part, pulled, here))
    for side, part, pulled, (rho, ux, uy, uz, fluid) in loaded:
        wanted = pops(0, 1 - 2 * side)
        after, _ = collide(pulled, 1.0 / rho, rho, ux, uy, uz, None, wanted)
        for line, j in enumerate(wanted):
            shares[side, line, pl.ds(8 * part, 8), :] = jnp.where(fluid, after[j], 0.0)

    pack_lines((mask,), first, packets, many_x, many_y, lambda kind, index: not is_flat(kind, index), shares)

    for side in range(2):
        for part in range(ext_y // 8):
            rows = pl.ds(8 * part, 8)
            value = jnp.zeros((8, LANES), jnp.float32)
            for tile in range(Z_TILES):
                start = ext_x if side else 2
                moved = pltpu.roll(z_set[tile, rows, :], (2 * tile - start) % LANES, 1)
                value = jnp.where(spot // 2 == tile, moved, value)
            faces[side, rows, :] = value

    def add_xy(slot_x, slot_y, side_x, side_y):
        start = ext_y - 2 if side_y else 0
        to_xy[many_x * slot_y + slot_x][EDGE // 8, 0:2, :] = faces[side_x, start : start + 2, :]

    def add_y(slot, side):
        toward = 1 - 2 * side
        lines = {name: line for line, name in enumerate(face_lines(1, toward))}
        pulled = []
        for j in range(19):
            cx, cy, _ = VELOCITIES[j]
            if cy == -toward:
                pulled.append(jnp.zeros((8, LANES), jnp.float32))
                continue
            value = y_lines[slot][lines[("pop", j, abs(cy))]]
            if cx:
                value = jnp.where(sub == (7 if cx > 0 else 0), 0.0, pltpu.roll(value, -cx % 8, 0))
            pulled.append(value)
        rho, ux, uy, uz, kind = [y_lines[slot][lines[("field", k, 0)]] for k in range(5)]
        after, _ = collide(pulled, 1.0 / rho, rho, ux, uy, uz, None, pops(1, toward))
        full, ends = side_lines(1, toward)
        for line, (what, index) in enumerate(full):
            if what == "share":
                to_y[slot][line] = jnp.where(kind > 1.5, after[pops(1, toward)[index]], 0.0)
            else:
                to_y[slot][line] = y_lines[slot][lines[(what, index, 0)]]
        for spot, (index, depth, end) in enumerate(ends):
            x = ext_x - 1 if end else 0
            to_y[slot][SIDE - 1, spot : spot + 1, :] = y_lines[slot][lines[("pop", index, depth)], x : x + 1, :]
        start = ext_y - 2 if side else 0
        for tile in range(Z_TILES):
            row = 2 * tile % 8
            to_y[slot][SIDE + tile // 4, row : row + 2, :] = z_set[tile, start : start + 2, :]

    def add_x(slot, side):
        to_x[slot][SIDE] = faces[side]

    for slot_y in range(many_y):
        there_y = has_partner("gy", slot_y)
        pl.when(there_y)(lambda: on_side(py, slot_y, functools.partial(add_y, slot_y)))

        @pl.when(jnp.logical_not(there_y))
        def _():
            to_y[slot_y][...] = jnp.zeros(to_y[slot_y].shape, jnp.float32)

        for slot_x in range(many_x):
            pl.when(there_y & has_partner("gx", slot_x))(
                lambda: on_side(
                    py,
                    slot_y,
                    lambda side_y: on_side(px, slot_x, lambda side_x: add_xy(slot_x, slot_y, side_x, side_y)),
                )
            )
    for slot_x in range(many_x):
        pl.when(has_partner("gx", slot_x))(lambda: on_side(px, slot_x, functools.partial(add_x, slot_x)))


def collide(pulled, inverse, rho, ux, uy, uz, fluid, wanted):
    total = {}
    diff = {}
    for j in range(1, 19, 2):
        total[j] = pulled[j] + pulled[j + 1]
        diff[j] = pulled[j] - pulled[j + 1]
    in_xy, in_xz, in_yz = total[7] + total[9], total[11] + total[13], total[15] + total[17]
    two_x, two_y, two_z = total[1] + total[1], total[3] + total[3], total[5] + total[5]
    count = (12.0 * pulled[0] + (two_x + two_y)) + (two_z + (in_xy + (in_xz + in_yz)))
    flow_x = (diff[1] + diff[1]) + ((diff[7] + diff[9]) + (diff[11] + diff[13]))
    flow_y = (diff[3] + diff[3]) + ((diff[7] - diff[9]) + (diff[15] + diff[17]))
    flow_z = (diff[5] + diff[5]) + ((diff[11] - diff[13]) + (diff[15] - diff[17]))
    xx, yy, zz = two_x + (in_xy + in_xz), two_y + (in_xy + in_yz), two_z + (in_xz + in_yz)
    xy, xz, yz = total[7] - total[9], total[11] - total[13], total[15] - total[17]
    push_x = xx * ux + xy * uy + xz * uz
    push_y = xy * ux + yy * uy + yz * uz
    push_z = xz * ux + yz * uy + zz * uz
    usq = ux * ux + uy * uy + uz * uz
    push = ux * push_x + uy * push_y + uz * push_z
    base = count * (OMEGA / 36.0 + (OMEGA / 24.0) * usq) - (OMEGA / 8.0) * push - ux * inverse
    along_x = (OMEGA / 12.0) * (flow_x + 3.0 * push_x - ux * count) + inverse
    along_y = (OMEGA / 12.0) * (flow_y + 3.0 * push_y - uy * count)
    along_z = (OMEGA / 12.0) * (flow_z + 3.0 * push_z - uz * count)
    parts = {
        1: along_x,
        3: along_y,
        5: along_z,
        7: along_x + along_y,
        9: along_x - along_y,
        11: along_x + along_z,
        13: along_x - along_z,
        15: along_y + along_z,
        17: along_y - along_z,
    }
    out = {}
    for j in wanted:
        if j == 0:
            shift = base
        elif j % 2:
            shift = base + parts[j]
        else:
            shift = base - parts[j - 1]
        out[j] = (1.0 - OMEGA) * pulled[j] + shift
        if fluid is not None:
            out[j] = jnp.where(fluid, out[j], pulled[OPPOSITE[j]])
    change = (-1.0 / 6.0) * rho * (flow_x * ux + flow_y * uy + flow_z * uz)
    return out, change if fluid is None else jnp.where(fluid, change, 0.0)


def only(value, row):
    return jnp.where(lax.broadcasted_iota(jnp.int32, (8, LANES), 0) == row, value, 0.0)


class Plane:
    def across(self, shares, side, line):
        return shares[side, line, pl.ds(8 + self.row, 8), :]

    def rim(self, shares, line, toward):
        if toward != (-1 if self.row < 0 else 1):
            return 0.0
        return only(shares[line, self.x, pl.ds(8 + self.row, 8), :], 0 if toward < 0 else 1)

    def __init__(self, x, row):
        self.x, self.row = x, row

    def load(self, ref, lead, margin, cx=0, cy=0):
        return ref[lead, self.x + margin + cx, pl.ds(8 + self.row + cy, 8), :]

    def store(self, ref, lead, margin, value):
        ref[lead, self.x + margin, pl.ds(8 + self.row, 8), :] = value


class Rim:
    def __init__(self, x, ext_y):
        self.x, self.ext_y = x, ext_y

    def across(self, shares, side, line):
        upper, lower = shares[side, line, pl.ds(8 + self.ext_y - 1, 8), :], shares[side, line, pl.ds(1, 8), :]
        return jnp.where(lax.broadcasted_iota(jnp.int32, (8, LANES), 0) < 4, upper, lower)

    def rim(self, shares, line, toward):
        start = 1 if toward < 0 else 8 + self.ext_y - 1
        return only(shares[line, self.x, pl.ds(start, 8), :], 6 if toward < 0 else 1)

    def load(self, ref, lead, margin, cx=0, cy=0):
        at = self.x + margin + cx
        upper = ref[lead, at, pl.ds(8 + self.ext_y - 1 + cy, 8), :]
        lower = ref[lead, at, pl.ds(1 + cy, 8), :]
        return jnp.where(lax.broadcasted_iota(jnp.int32, (8, LANES), 0) < 4, upper, lower)

    def store(self, ref, lead, margin, value):
        at = self.x + margin
        ref[lead, at, pl.ds(8 + self.ext_y - 1, 2), :] = value[0:2]
        ref[lead, at, pl.ds(7, 2), :] = value[6:8]


def first_step(first, fields, second, change, tiles, outside=True, shares=None, y_shares=None):
    loaded = [
        (
            [tile.load(first, j, 2, *VELOCITIES[j][:2]) for j in range(19)],
            [tile.load(fields, k, 1) for k in range(5)],
        )
        for tile in tiles
    ]
    done = [
        collide(pulled, 1.0 / rho, rho, ux, uy, uz, kind > 1.5, range(19))
        for pulled, (rho, ux, uy, uz, kind) in loaded
    ]
    for tile, (_, here), (after, gain) in zip(tiles, loaded, done):
        inside = here[KIND] > 0.5
        side = None if shares is None else {-1: 0, second.shape[1] - 2: 1}.get(tile.x)
        for j in range(19):
            value = after[j]
            if side is not None and VELOCITIES[j][0] == 2 * side - 1:
                value = value + tile.across(shares, side, pops(0, 2 * side - 1).index(j))
            if side is None and y_shares is not None and VELOCITIES[j][1]:
                value = value + tile.rim(y_shares, pops(1, VELOCITIES[j][1]).index(j), VELOCITIES[j][1])
            if outside:
                value = jnp.where(inside, value, 0.0)
            cz = VELOCITIES[j][2]
            tile.store(second, j, 1, pltpu.roll(value, -cz % LANES, 1) if cz else value)
        tile.store(change, 0, 1, gain)


def inner_kernel(den, vel, mask, first, fields, second, change):
    refs = (None, den, vel, mask)
    ext_x, ext_y, _ = mask.shape
    every = slice(None)
    for k in range(5):
        fields[k, 1 : 1 + ext_x, pl.ds(8, ext_y), :] = field_of(refs, "field", k, (every, every, every))

    many = 3 if (ext_x - 2) % 3 == 0 else 1

    @pl.loop(0, (ext_x - 2) // many)
    def _(group):
        tiles = [Plane(many * group + at + 1, 1 + 8 * part) for at in range(many) for part in range(ext_y // 8)]
        first_step(first, fields, second, change, tiles, outside=False)


def put_row(first, fields, kind, index, x, y, value):
    row = y + 8
    if kind == "pop":
        first[index, x + 2, row : row + 1, :] = value
    else:
        fields[index, x + 1, row : row + 1, :] = value


def place_z(z_first, value, start, size, side, ext_x):
    rows = pl.ds(start, size)
    spot = lane_ids()[:size] % GROUP
    inside = spot >= 2 + ext_x if side else spot < 2
    for tile in range(Z_TILES):
        shift = (2 + ext_x if side else 0) - 2 * tile
        moved = pltpu.roll(value, shift % LANES, 1)[:size]
        z_first[tile, rows, :] = jnp.where(inside, moved, z_first[tile, rows, :])


def z_step(z_first, z_second, starts):
    lane = lane_ids()
    loaded = []
    for row in starts:

        def both(low_tile, high_tile, group, cx, cy):
            rows = pl.ds(8 + row + cy, 8)
            low = pltpu.roll(z_first[low_tile, rows, :], (-GROUP * group - cx) % LANES, 1)
            high = pltpu.roll(z_first[high_tile, rows, :], (LANES // 2 - GROUP * group - cx) % LANES, 1)
            return jnp.where(lane < LANES // 2, low, high)

        pulled = []
        for j in range(19):
            cx, cy, cz = VELOCITIES[j]
            if cz == 0:
                tile, group = Z_PLACE[("pop", j)]
                pulled.append(both(BELOW + tile, ABOVE + tile, group, cx, cy))
            elif cz == 1:
                pulled.append(both(OWN_LOW, ABOVE + 2, Z_UP.index(j), cx, cy))
            else:
                pulled.append(both(BELOW + 2, OWN_HIGH, Z_DOWN.index(j), cx, cy))
        places = [Z_PLACE[("field", k)] for k in range(5)]
        loaded.append((pulled, [both(BELOW + tile, ABOVE + tile, group, 0, 0) for tile, group in places]))
    done = [
        collide(pulled, 1.0 / rho, rho, ux, uy, uz, kind > 1.5, Z_UP + Z_DOWN)[0]
        for pulled, (rho, ux, uy, uz, kind) in loaded
    ]
    for row, (_, here), after in zip(starts, loaded, done):
        for group in range(5):
            value = jnp.where(lane < LANES // 2, after[Z_DOWN[group]], after[Z_UP[group]])
            z_second[group, pl.ds(8 + row, 8), :] = jnp.where(here[KIND] > 0.5, value, 0.0)


def second_step(refs, second, z_second, change, held, held_sens, planes):
    den, vel, mask = refs
    _, ext_y, _ = mask.shape
    lane = lane_ids()
    every = slice(None)
    loaded = []
    for x, part in itertools.product(planes, range(ext_y // 8)):
        row = 8 + 8 * part
        pulled = []
        for j in range(19):
            cx, cy, cz = VELOCITIES[j]
            rows = pl.ds(row + cy, 8)
            value = second[j, x + 1 + cx, rows, :]
            if cz == 1:
                edge = z_second[Z_UP.index(j), rows, :]
                edge = pltpu.roll(edge, LANES // 2 - 3 - cx - x, 1)
                value = jnp.where(lane == LANES - 1, edge, value)
            elif cz == -1:
                edge = z_second[Z_DOWN.index(j), rows, :]
                edge = pltpu.roll(edge, LANES - 2 - cx - x, 1)
                value = jnp.where(lane == 0, edge, value)
            pulled.append(value)
        at = (x, pl.ds(8 * part, 8), every)
        rho = den[(0, *at)]
        here = [1.0 / rho, rho, vel[(0, 0, *at)], vel[(0, 1, *at)], vel[(0, 2, *at)], mask[at] > 0]
        loaded.append((at, pulled, here, change[0, x + 1, pl.ds(row, 8), :]))
    done = [collide(pulled, *here, range(19)) for _, pulled, here, _ in loaded]
    for (at, _, _, before), (after, gain) in zip(loaded, done):
        for j in range(19):
            held[(j, *at)] = after[j]
        held_sens[at] = before + gain


def side_kernel(slots, den, vel, mask, z_set, *rest):
    many_x, many_y = slots
    from_x, from_y = rest[4 : 4 + many_x], rest[4 + many_x : 4 + many_x + many_y]
    first, fields, second, change, z_first, z_second, shares, y_shares, held, held_sens = rest[-10:]
    _, ext_y, _ = z_set.shape
    ext_x = change.shape[1] - 2
    inner = pl.ds(8, ext_y)
    put = functools.partial(put_row, first, fields)
    z_first[:, inner, :] = z_set[...]

    def place_y(slot, side):
        packet = from_y[slot]
        toward = 2 * side - 1
        near = ext_y if side else -1
        nothing = jnp.zeros((1, LANES), jnp.float32)
        full, ends = side_lines(1, toward)
        for x in range(ext_x):
            for j in pops(1, 0):
                put("pop", j, x, near, nothing)
            for j in pops(1, toward):
                put("pop", j, x, near + toward, nothing)
            put("field", RHO, x, near, jnp.full((1, LANES), jnp.inf, jnp.float32))
            for line, (kind, index) in enumerate(full):
                if kind == "share":
                    y_shares[index, x, near + 8 : near + 9, :] = packet[line, x : x + 1, :]
                else:
                    put(kind, index, x, near, packet[line, x : x + 1, :])
        for spot, (index, depth, end) in enumerate(ends):
            put("pop", index, ext_x - 1 if end else 0, near + toward * depth, packet[SIDE - 1, spot : spot + 1, :])
        start = 8 + ext_y if side else 6
        for tile in range(Z_TILES):
            row = 2 * tile % 8
            z_first[tile, start : start + 2, :] = packet[SIDE + tile // 4, row : row + 2, :]
        if many_y == 1:
            clear_y(1 - side)

    def clear_y(side):
        nothing = jnp.zeros((1, LANES), jnp.float32)
        y = ext_y if side else -1
        for x in range(-2, ext_x + 2):
            for j in pops(1, 2 * side - 1):
                put("pop", j, x, y, nothing)
        for x in range(-1, ext_x + 1):
            put("field", KIND, x, y, nothing)
        start = 8 + ext_y if side else 6
        for tile in range(Z_TILES):
            z_first[tile, start : start + 2, :] = jnp.zeros((2, LANES), jnp.float32)

    def place_x(slot, side):
        packet = from_x[slot]
        toward = 2 * side - 1
        near = ext_x if side else -1
        nothing = jnp.zeros((ext_y, LANES), jnp.float32)
        for j in pops(0, 0):
            first[j, near + 2, inner, :] = nothing
        for j in pops(0, toward):
            first[j, near + toward + 2, inner, :] = nothing
        fields[RHO, near + 1, inner, :] = jnp.full((ext_y, LANES), jnp.inf, jnp.float32)
        full, ends = side_lines(0, toward)
        for line, (kind, index) in enumerate(full):
            if kind == "pop":
                first[index, near + 2, inner, :] = packet[line]
            elif kind == "share":
                shares[side, index, inner, :] = packet[line]
            else:
                fields[index, near + 1, inner, :] = packet[line]
        for spot, (index, depth, end) in enumerate(ends):
            put("pop", index, near + toward * depth, ext_y - 1 if end else 0, packet[SIDE - 1, spot : spot + 1, :])
        for part in range(ext_y // 8):
            place_z(z_first, packet[SIDE, pl.ds(8 * part, 8), :], 8 + 8 * part, 8, side, ext_x)

    shares[:, :, pl.ds(0, 8), :] = jnp.zeros((2, 5, 8, LANES), jnp.float32)
    shares[:, :, pl.ds(8 + ext_y, 8), :] = jnp.zeros((2, 5, 8, LANES), jnp.float32)
    for slot_y in range(many_y):
        on_side(parity_of("gy"), slot_y, functools.partial(place_y, slot_y))
    for slot_x in range(many_x):
        on_side(parity_of("gx"), slot_x, functools.partial(place_x, slot_x))

    starts = range(1, ext_y, 8)
    first_step(first, fields, second, change, [Plane(x, row) for x in (0, ext_x - 1) for row in starts], outside=False)
    first_step(first, fields, second, change, [Plane(x, row) for x in (-1, ext_x) for row in starts], shares=shares)
    z_step(z_first, z_second, range(7, ext_y - 8, 8))
    many = 3 if (ext_x - 2) % 3 == 0 else 1

    @pl.loop(0, (ext_x - 2) // many)
    def _(group):
        tiles = [Rim(many * group + at + 1, ext_y) for at in range(many)]
        first_step(first, fields, second, change, tiles, y_shares=y_shares)

    z_step(z_first, z_second, (-1, ext_y - 1))
    second_step((den, vel, mask), second, z_second, change, held, held_sens, range(2, ext_x - 2))


def last_kernel(slots, den, vel, mask, *rest):
    many_x, many_y = slots
    from_xy = rest[10 : 10 + many_x * many_y]
    out, sens, first, fields, second, change, z_first, z_second, shares, y_shares, held, held_sens, sems = rest[-13:]
    ext_x, ext_y, _ = mask.shape
    lane = lane_ids()
    every = slice(None)
    px, py = parity_of("gx"), parity_of("gy")

    def copies(x):
        return (
            pltpu.make_async_copy(held.at[:, x], out.at[:, x], sems.at[0, x]),
            pltpu.make_async_copy(held_sens.at[x], sens.at[x], sems.at[1, x]),
        )

    for x in range(2, ext_x - 2):
        for copy in copies(x):
            copy.start()

    def place_xy(slot_x, slot_y, side_x, side_y):
        packet = from_xy[many_x * slot_y + slot_x]
        for line, (kind, index, far_x, far_y) in enumerate(edge_lines(2 * side_x - 1, 2 * side_y - 1)):
            x = ext_x + far_x if side_x else -1 - far_x
            y = ext_y + far_y if side_y else -1 - far_y
            put_row(first, fields, kind, index, x, y, packet[line // 8, line % 8 : line % 8 + 1, :])
        place_z(z_first, packet[EDGE // 8], 8 + ext_y if side_y else 6, 2, side_x, ext_x)

    for slot_x in range(many_x):
        for slot_y in range(many_y):
            on_side(
                py,
                slot_y,
                lambda side_y: on_side(px, slot_x, lambda side_x: place_xy(slot_x, slot_y, side_x, side_y)),
            )

    for pair in ((-1, 0), (ext_x - 1, ext_x)):
        tiles = [Rim(x, ext_y) for x in pair]
        first_step(first, fields, second, change, tiles, shares=shares, y_shares=y_shares)

    z_step(z_first, z_second, (-1, ext_y - 1))

    planes = [0, 1, ext_x - 2, ext_x - 1]
    for pair in (planes[:2], planes[2:]):
        second_step((den, vel, mask), second, z_second, change, held, held_sens, pair)
        for x in pair:
            for copy in copies(x):
                copy.start()

    for x in range(ext_x):
        for copy in copies(x):
            copy.wait()


def shards(adjoint, density, velocity, pore_mask):
    ext_x, ext_y, ext_z = pore_mask.shape
    assert ext_z == LANES and ext_y % 8 == 0 and ext_x + 4 <= GROUP and ext_x == 8
    many_x = 2
    many_y, many_z = [1 if lax.axis_size(axis) == 2 else 2 for axis in ("gy", "gz")]
    vmem = pl.BlockSpec(memory_space=pltpu.VMEM)
    hbm = pl.BlockSpec(memory_space=pltpu.HBM)
    inputs = (adjoint, density, velocity, pore_mask)

    def array(*shape):
        return jax.ShapeDtypeStruct(shape, jnp.float32)

    def call(kernel, name, operands, shapes, limit, **more):
        more.setdefault("out_specs", [vmem] * len(shapes))
        more.setdefault("in_specs", [vmem] * len(operands))
        params = pltpu.CompilerParams(vmem_limit_bytes=limit * 1024 * 1024)
        return pl.pallas_call(kernel, out_shape=shapes, compiler_params=params, name=name, **more)(*operands)

    def partners(axis, slot):
        found = {}
        for at in range(slot, lax.axis_size(axis) - 1, 2):
            found[at], found[at + 1] = at + 1, at
        return found

    def ends(axis):
        last = lax.axis_size(axis) - 1
        return {0: last, last: 0}

    def swap(value, spares, *places):
        tables = {axis: partners(axis, slot) for axis, slot in places}
        axes = [axis for axis in ("gx", "gy", "gz") if axis in tables or axis in dict(spares)]
        sizes = [lax.axis_size(axis) for axis in axes]
        pairs = []
        for at in itertools.product(*[range(size) for size in sizes]):
            to = [tables.get(axis, {}).get(spot, spot) for axis, spot in zip(axes, at)]
            for spare, table in spares:
                if tuple(to) == at:
                    to = [table.get(spot, spot) if axis == spare else spot for axis, spot in zip(axes, at)]
            flat = []
            for spots in (at, to):
                index = 0
                for size, spot in zip(sizes, spots):
                    index = index * size + spot
                flat.append(index)
            pairs.append(tuple(flat))
        return lax.ppermute(value, tuple(axes), pairs)

    loaded = [jax.ShapeDtypeStruct(value.shape, value.dtype) for value in inputs]
    *held, near, a_z, b_z = (
        *call(
            functools.partial(pack_z_kernel, many_z),
            "pack_z",
            [pltpu.with_memory_space_constraint(value, pltpu.HBM) for value in inputs],
            loaded + [array(2, ext_y, LANES)] + [array(2, ext_y, LANES)] * many_z,
            8,
            in_specs=[hbm] * 4,
            scratch_shapes=[pltpu.SemaphoreType.DMA((7,))],
        ),
        *[None] * (2 - many_z),
    )
    from_z = [swap(value, [("gx", partners("gx", 0))], ("gz", slot)) for slot, value in enumerate((a_z, b_z)[:many_z])]

    rows = ext_y + 16
    adj, den, vel, mask = held
    shapes = (
        [array(19, ext_x + 4, rows, LANES)]
        + [array(SIDE + 1, ext_y, LANES)] * many_x
        + [array(FACE, ext_x, LANES)] * many_y
        + [array(EDGE // 8 + 1, 8, LANES)] * (many_x * many_y)
    )
    shifted = call(
        functools.partial(shift_kernel, (many_x, many_y)),
        "shift",
        (adj, den, vel, mask),
        shapes,
        8,
        cost_estimate=pl.CostEstimate(flops=1_000_000, bytes_accessed=2_500_000, transcendentals=0),
    )
    z_set, first, *packets = call(
        functools.partial(pack_xy_kernel, (many_x, many_y, many_z)),
        "pack_xy",
        (den, vel, mask, near, *from_z, *shifted),
        [array(Z_TILES, ext_y, LANES)] + shapes + [array(SIDE + 2, ext_x, LANES)] * many_y,
        8,
        input_output_aliases={4 + many_z + at: 1 + at for at in range(len(shapes))},
        scratch_shapes=[
            pltpu.VMEM((2, ext_y, LANES), jnp.float32),
            pltpu.VMEM((2, 5, ext_y, LANES), jnp.float32),
        ],
    )
    to_x, to_xy, to_y = packets[:many_x], packets[many_x + many_y : -many_y], packets[-many_y:]
    from_xy = [
        swap(to_xy[many_x * slot_y + slot_x], [], ("gx", slot_x), ("gy", slot_y))
        for slot_y in range(many_y)
        for slot_x in range(many_x)
    ]
    from_y = [swap(value, [("gz", partners("gz", 0))], ("gy", slot)) for slot, value in enumerate(to_y)]
    spares = [("gx", ends("gx"))]
    if lax.axis_size("gz") > 2:
        top = lax.axis_size("gz") - 1
        spares = [("gz", {top - 1: top, top: top - 1})] + spares
    from_x = [swap(value, spares, ("gx", slot)) for slot, value in enumerate(to_x)]

    fields, second, change = call(
        inner_kernel,
        "inner_step",
        (den, vel, mask, first),
        [array(5, ext_x + 2, rows, LANES), array(19, ext_x + 2, rows, LANES), array(1, ext_x + 2, rows, LANES)],
        8,
        cost_estimate=pl.CostEstimate(flops=40_000_000, bytes_accessed=8_000_000, transcendentals=0),
    )
    inout = (first, fields, second, change)
    inout = call(
        functools.partial(side_kernel, (many_x, many_y)),
        "side_step",
        (den, vel, mask, z_set, *inout, *from_x, *from_y),
        [array(*value.shape) for value in inout] + [array(Z_TILES, rows, LANES), array(5, rows, LANES), array(2, 5, rows, LANES), array(5, ext_x, rows, LANES)]
        + [array(19, ext_x, ext_y, LANES), array(ext_x, ext_y, LANES)],
        8,
        input_output_aliases={4 + at: at for at in range(4)},
        cost_estimate=pl.CostEstimate(flops=40_000_000, bytes_accessed=8_000_000, transcendentals=0),
    )
    return call(
        functools.partial(last_kernel, (many_x, many_y)),
        "last_steps",
        (den, vel, mask, *inout, *from_xy),
        [array(19, ext_x, ext_y, LANES), array(ext_x, ext_y, LANES)] + [array(*value.shape) for value in inout],
        8,
        out_specs=[hbm] * 2 + [vmem] * 10,
        input_output_aliases={3 + at: 2 + at for at in range(10)},
        scratch_shapes=[pltpu.SemaphoreType.DMA((2, ext_x))],
    )[:2]


def solution(mesh):
    placed = (
        P(None, "gx", "gy", "gz"),
        P(None, "gx", "gy", "gz"),
        P(None, None, "gx", "gy", "gz"),
        P("gx", "gy", "gz"),
    )

    def whole(*arrays):
        return tuple(shards(*arrays))

    return jax.shard_map(
        whole,
        mesh=mesh,
        in_specs=placed,
        out_specs=(P(None, "gx", "gy", "gz"), P("gx", "gy", "gz")),
        check_vma=False,
    )
```

```python
import functools
import itertools

import jax
import jax.numpy as jnp
from jax import lax
from jax.experimental import pallas as pl
from jax.experimental.pallas import tpu as pltpu
from jax.sharding import PartitionSpec as P

VELOCITIES = [
    (0, 0, 0),
    (1, 0, 0),
    (-1, 0, 0),
    (0, 1, 0),
    (0, -1, 0),
    (0, 0, 1),
    (0, 0, -1),
    (1, 1, 0),
    (-1, -1, 0),
    (1, -1, 0),
    (-1, 1, 0),
    (1, 0, 1),
    (-1, 0, -1),
    (1, 0, -1),
    (-1, 0, 1),
    (0, 1, 1),
    (0, -1, -1),
    (0, 1, -1),
    (0, -1, 1),
]
OPPOSITE = [0, 2, 1, 4, 3, 6, 5, 8, 7, 10, 9, 12, 11, 14, 13, 16, 15, 18, 17]
OMEGA = 1.25
LANES = 128
GROUP = 16


def pops(axis, sign):
    return [j for j in range(19) if VELOCITIES[j][axis] == sign]


def mirrored(j):
    cx, cy, cz = VELOCITIES[j]
    return VELOCITIES.index((cx, cy, -cz))


Z_FLAT = pops(2, 0)
Z_UP = pops(2, 1)
Z_DOWN = [mirrored(j) for j in Z_UP]
RHO, UX, UY, UZ, KIND = range(5)
Z_PLACE = {("pop", j): (0, g) for g, j in enumerate(Z_FLAT[:8])}
Z_PLACE[("pop", Z_FLAT[8])] = (1, 5)
Z_PLACE[("field", RHO)] = (1, 6)
Z_PLACE[("field", KIND)] = (1, 7)
Z_PLACE[("field", UX)] = (2, 5)
Z_PLACE[("field", UY)] = (2, 6)
Z_PLACE[("field", UZ)] = (2, 7)
BELOW, ABOVE, OWN_LOW, OWN_HIGH, Z_TILES = 0, 3, 6, 7, 8


def face_lines(axis, toward):
    near = pops(axis, 0) + pops(axis, toward)
    lines = [("pop", j, 0) for j in near] + [("field", k, 0) for k in range(5)]
    return lines + [("pop", j, 1) for j in pops(axis, toward)]


def edge_lines(toward_x, toward_y):
    lines = [("field", k, 0, 0) for k in range(5)]
    for j in range(19):
        cx, cy, _ = VELOCITIES[j]
        if cx not in (0, toward_x) or cy not in (0, toward_y):
            continue
        lines.append(("pop", j, 0, 0))
        if cx:
            lines.append(("pop", j, 1, 0))
        if cy:
            lines.append(("pop", j, 0, 1))
        if cx and cy:
            lines.append(("pop", j, 1, 1))
    return lines


FACE = 24
EDGE = 24
SIDE = 15


def side_lines(axis, toward):
    full = [("pop", j) for j in pops(axis, toward)] + [("share", p) for p in range(5)]
    full += [("field", k) for k in (UX, UY, UZ, KIND)]
    ends = []
    for end in range(2):
        for j in pops(1 - axis, 1 - 2 * end):
            across = VELOCITIES[j][axis]
            if across in (0, toward):
                ends.append((j, abs(across), end))
    return full, ends


def lane_ids():
    return lax.broadcasted_iota(jnp.int32, (8, LANES), 1)


def field_of(refs, kind, index, at):
    adj, den, vel, mask = refs
    if kind == "pop":
        return adj[(index, *at)]
    if index == RHO:
        return den[(1, *at)]
    if index == KIND:
        return (mask[at] + 1).astype(jnp.float32)
    return vel[(1, index - UX, *at)]


def parity_of(axis):
    return lax.rem(lax.axis_index(axis), 2)


def on_side(parity, slot, act):
    @pl.when(parity == slot)
    def _():
        act(1)

    @pl.when(parity != slot)
    def _():
        act(0)


def has_partner(axis, slot):
    at = lax.axis_index(axis)
    to = at + jnp.where(lax.rem(at, 2) == slot, 1, -1)
    return (to >= 0) & (to < lax.axis_size(axis))


def pack_z_kernel(slots, adj_in, den_in, vel_in, mask_in, adj, den, vel, mask, near, *rest):
    packets, sems = rest[:slots], rest[slots]
    refs = (adj, den, vel, mask)
    ext_x, ext_y, _ = mask.shape
    starts = range(0, 19, 3)
    fields = [
        pltpu.make_async_copy(source, target, sems.at[at])
        for at, (source, target) in enumerate([(den_in, den), (vel_in, vel), (mask_in, mask)])
    ]
    loads = [
        pltpu.make_async_copy(adj_in.at[start : min(start + 3, 19)], adj.at[start : min(start + 3, 19)], sems.at[3 + at])
        for at, start in enumerate(starts)
    ]
    for load in fields + loads:
        load.start()
    lane = lane_ids()
    parity = parity_of("gz")
    parts = range(ext_y // 8)
    zero = jnp.zeros((8, LANES), jnp.float32)
    lows, highs = [[zero] * 3 for _ in parts], [[zero] * 3 for _ in parts]
    far_low, far_high = [zero for _ in parts], [zero for _ in parts]

    def gather(kind, index):
        for x, part in itertools.product(range(ext_x), parts):
            value = field_of(refs, kind, index, (x, pl.ds(8 * part, 8), slice(None)))
            if kind == "pop" and VELOCITIES[index][2] == 1:
                spot = GROUP * Z_UP.index(index) + 2 + x
                moved = pltpu.roll(value, spot, 1)
                lows[part][1] = jnp.where(lane == spot, moved, lows[part][1])
                far_low[part] = jnp.where(lane == spot + 1, moved, far_low[part])
            elif kind == "pop" and VELOCITIES[index][2] == -1:
                spot = GROUP * Z_DOWN.index(index) + 2 + x
                moved = pltpu.roll(value, spot, 1)
                highs[part][1] = jnp.where(lane == spot - 1, moved, highs[part][1])
                far_high[part] = jnp.where(lane == spot - 2, moved, far_high[part])
            else:
                tile, group = Z_PLACE[(kind, index)]
                spot = GROUP * group + 2 + x
                moved = pltpu.roll(value, spot, 1)
                lows[part][tile] = jnp.where(lane == spot, moved, lows[part][tile])
                highs[part][tile] = jnp.where(lane == spot - 1, moved, highs[part][tile])

    for load in fields:
        load.wait()
    for k in range(5):
        gather("field", k)
    for start, load in zip(starts, loads):
        load.wait()
        for j in range(start, min(start + 3, 19)):
            gather("pop", j)
    for part in parts:
        rows = pl.ds(8 * part, 8)
        low = lows[part]
        high = [pltpu.roll(tile, 1, 1) for tile in highs[part]]
        low[2] = jnp.where(lane < 5 * GROUP, pltpu.roll(far_low[part], LANES - 1, 1), low[2])
        high[2] = jnp.where(lane < 5 * GROUP, pltpu.roll(far_high[part], 2, 1), high[2])
        near[0, rows, :] = low[1]
        near[1, rows, :] = high[1]
        for slot in range(slots):
            there = has_partner("gz", slot)
            sent = [jnp.where(there, jnp.where(parity == slot, up, down), 0.0) for up, down in zip(high, low)]
            mine = (lane + (GROUP - 2)) % GROUP < GROUP // 2
            packets[slot][0, rows, :] = jnp.where(mine, sent[0], pltpu.roll(sent[1], GROUP // 2, 1))
            packets[slot][1, rows, :] = sent[2]


def pack_lines(refs, first, packets, many_x, many_y, wanted, shares):
    to_x, y_lines = packets[:many_x], packets[many_x : many_x + many_y]
    to_xy = packets[many_x + many_y :]
    ext_x, ext_y, _ = refs[-1].shape
    every = slice(None)
    px, py = parity_of("gx"), parity_of("gy")

    def line_of(kind, index, x, y):
        if kind == "pop":
            return first[index, x + 2, y + 8 : y + 9, :]
        return field_of(refs, kind, index, (x, slice(y, y + 1), every))

    def pack_xy(slot_x, slot_y, side_x, side_y):
        packet = to_xy[many_x * slot_y + slot_x]
        for line, (kind, index, far_x, far_y) in enumerate(edge_lines(1 - 2 * side_x, 1 - 2 * side_y)):
            if wanted(kind, index):
                x = ext_x - 1 - far_x if side_x else far_x
                y = ext_y - 1 - far_y if side_y else far_y
                packet[line // 8, line % 8 : line % 8 + 1, :] = line_of(kind, index, x, y)

    def pack_y(slot, side):
        for line, (kind, index, depth) in enumerate(face_lines(1, 1 - 2 * side)):
            if wanted(kind, index):
                y = ext_y - 1 - depth if side else depth
                for x in range(ext_x):
                    y_lines[slot][line, x : x + 1, :] = line_of(kind, index, x, y)

    def pack_x(slot, side):
        full, ends = side_lines(0, 1 - 2 * side)
        for line, (kind, index) in enumerate(full):
            if kind == "field" and wanted(kind, index):
                to_x[slot][line] = field_of(refs, kind, index, (ext_x - 1 if side else 0, every, every))
            elif kind == "pop" and wanted(kind, index):
                to_x[slot][line] = first[index, (ext_x - 1 if side else 0) + 2, pl.ds(8, ext_y), :]
            elif kind == "share" and shares is not None:
                to_x[slot][line] = shares[side, index]
        for spot, (index, depth, end) in enumerate(ends):
            if wanted("pop", index):
                x = ext_x - 1 - depth if side else depth
                to_x[slot][SIDE - 1, spot : spot + 1, :] = line_of("pop", index, x, ext_y - 1 if end else 0)

    def when_there(there, packet, act):
        pl.when(there)(act)
        if shares is None:

            @pl.when(jnp.logical_not(there))
            def _():
                packet[...] = jnp.zeros(packet.shape, jnp.float32)

    for slot_y in range(many_y):
        there_y = has_partner("gy", slot_y)
        when_there(there_y, y_lines[slot_y], lambda: on_side(py, slot_y, functools.partial(pack_y, slot_y)))
        for slot_x in range(many_x):
            when_there(
                there_y & has_partner("gx", slot_x),
                to_xy[many_x * slot_y + slot_x],
                lambda: on_side(
                    py,
                    slot_y,
                    lambda side_y: on_side(px, slot_x, lambda side_x: pack_xy(slot_x, slot_y, side_x, side_y)),
                ),
            )
    for slot_x in range(many_x):
        when_there(
            has_partner("gx", slot_x), to_x[slot_x], lambda: on_side(px, slot_x, functools.partial(pack_x, slot_x))
        )


def is_flat(kind, index):
    return kind == "field" or VELOCITIES[index][2] == 0


def shift_kernel(slots, adj, den, vel, mask, first, *packets):
    many_x, many_y = slots
    _, ext_x, ext_y, _ = adj.shape
    for j in range(19):
        cz = VELOCITIES[j][2]
        for x, part in itertools.product(range(ext_x), range(ext_y // 8)):
            value = adj[j, x, pl.ds(8 * part, 8), :]
            first[j, 2 + x, pl.ds(8 + 8 * part, 8), :] = pltpu.roll(value, -cz % LANES, 1) if cz else value
    pack_lines((None, den, vel, mask), first, packets, many_x, many_y, is_flat, None)


def pack_xy_kernel(slots, den, vel, mask, near, *rest):
    many_x, many_y, many_z = slots
    count = many_x + many_y + many_x * many_y
    from_z, rest = rest[:many_z], rest[many_z + 1 + count :]
    z_set, first, packets, faces, shares = rest[0], rest[1], rest[2 : 2 + count], rest[-2], rest[-1]
    to_x, y_lines, to_xy = packets[:many_x], packets[many_x : many_x + many_y], packets[many_x + many_y :]
    to_y = rest[2 + count : -2]
    ext_x, ext_y = first.shape[1] - 4, near.shape[1]
    spot = lane_ids() % GROUP
    px, py, pz = parity_of("gx"), parity_of("gy"), parity_of("gz")

    z_set[OWN_LOW] = near[0]
    z_set[OWN_HIGH] = near[1]

    def taken(slot, tile):
        if tile == 1:
            return pltpu.roll(from_z[slot][0], LANES - GROUP // 2, 1)
        return from_z[slot][tile // 2]

    for tile in range(3):
        even = taken(0, tile)
        odd = taken(1, tile) if many_z > 1 else jnp.zeros_like(even)
        z_set[ABOVE + tile] = jnp.where(pz == 0, even, odd)
        z_set[BELOW + tile] = jnp.where(pz == 0, odd, even)

    for j in Z_UP + Z_DOWN:
        up = VELOCITIES[j][2] > 0
        group = (Z_UP if up else Z_DOWN).index(j)
        last = LANES - 1 if up else 0
        for part in range(ext_y // 8):
            halo = z_set[(ABOVE if up else BELOW) + 1, pl.ds(8 * part, 8), :]
            for x in range(ext_x):
                edge = pltpu.roll(halo, (last - 2 - GROUP * group - x) % LANES, 1)
                first[j, 2 + x, pl.ds(8 + 8 * part, 8), last : last + 1] = edge[:, last : last + 1]


    sub = lax.broadcasted_iota(jnp.int32, (8, LANES), 0)
    loaded = []
    for side, part in itertools.product(range(2), range(ext_y // 8)):
        toward, x = 1 - 2 * side, ext_x - 1 if side else 0
        pulled = []
        for j in range(19):
            cx, cy, _ = VELOCITIES[j]
            if cx == -toward:
                pulled.append(jnp.zeros((8, LANES), jnp.float32))
                continue
            value = first[j, x + 2 + cx, pl.ds(8 + 8 * part + cy, 8), :]
            if cy == -1 and part == 0:
                value = jnp.where(sub == 0, 0.0, value)
            if cy == 1 and part == ext_y // 8 - 1:
                value = jnp.where(sub == 7, 0.0, value)
            pulled.append(value)
        at = (x, pl.ds(8 * part, 8), slice(None))
        here = [den[(1, *at)], vel[(1, 0, *at)], vel[(1, 1, *at)], vel[(1, 2, *at)], mask[at] > 0]
        loaded.append((side, part, pulled, here))
    for side, part, pulled, (rho, ux, uy, uz, fluid) in loaded:
        wanted = pops(0, 1 - 2 * side)
        after, _ = collide(pulled, 1.0 / rho, rho, ux, uy, uz, None, wanted)
        for line, j in enumerate(wanted):
            shares[side, line, pl.ds(8 * part, 8), :] = jnp.where(fluid, after[j], 0.0)

    pack_lines((mask,), first, packets, many_x, many_y, lambda kind, index: not is_flat(kind, index), shares)

    for side in range(2):
        for part in range(ext_y // 8):
            rows = pl.ds(8 * part, 8)
            value = jnp.zeros((8, LANES), jnp.float32)
            for tile in range(Z_TILES):
                start = ext_x if side else 2
                moved = pltpu.roll(z_set[tile, rows, :], (2 * tile - start) % LANES, 1)
                value = jnp.where(spot // 2 == tile, moved, value)
            faces[side, rows, :] = value

    def add_xy(slot_x, slot_y, side_x, side_y):
        start = ext_y - 2 if side_y else 0
        to_xy[many_x * slot_y + slot_x][EDGE // 8, 0:2, :] = faces[side_x, start : start + 2, :]

    def add_y(slot, side):
        toward = 1 - 2 * side
        lines = {name: line for line, name in enumerate(face_lines(1, toward))}
        pulled = []
        for j in range(19):
            cx, cy, _ = VELOCITIES[j]
            if cy == -toward:
                pulled.append(jnp.zeros((8, LANES), jnp.float32))
                continue
            value = y_lines[slot][lines[("pop", j, abs(cy))]]
            if cx:
                value = jnp.where(sub == (7 if cx > 0 else 0), 0.0, pltpu.roll(value, -cx % 8, 0))
            pulled.append(value)
        rho, ux, uy, uz, kind = [y_lines[slot][lines[("field", k, 0)]] for k in range(5)]
        after, _ = collide(pulled, 1.0 / rho, rho, ux, uy, uz, None, pops(1, toward))
        full, ends = side_lines(1, toward)
        for line, (what, index) in enumerate(full):
            if what == "share":
                to_y[slot][line] = jnp.where(kind > 1.5, after[pops(1, toward)[index]], 0.0)
            else:
                to_y[slot][line] = y_lines[slot][lines[(what, index, 0)]]
        for spot, (index, depth, end) in enumerate(ends):
            x = ext_x - 1 if end else 0
            to_y[slot][SIDE - 1, spot : spot + 1, :] = y_lines[slot][lines[("pop", index, depth)], x : x + 1, :]
        start = ext_y - 2 if side else 0
        for tile in range(Z_TILES):
            row = 2 * tile % 8
            to_y[slot][SIDE + tile // 4, row : row + 2, :] = z_set[tile, start : start + 2, :]

    def add_x(slot, side):
        to_x[slot][SIDE] = faces[side]

    for slot_y in range(many_y):
        there_y = has_partner("gy", slot_y)
        pl.when(there_y)(lambda: on_side(py, slot_y, functools.partial(add_y, slot_y)))

        @pl.when(jnp.logical_not(there_y))
        def _():
            to_y[slot_y][...] = jnp.zeros(to_y[slot_y].shape, jnp.float32)

        for slot_x in range(many_x):
            pl.when(there_y & has_partner("gx", slot_x))(
                lambda: on_side(
                    py,
                    slot_y,
                    lambda side_y: on_side(px, slot_x, lambda side_x: add_xy(slot_x, slot_y, side_x, side_y)),
                )
            )
    for slot_x in range(many_x):
        pl.when(has_partner("gx", slot_x))(lambda: on_side(px, slot_x, functools.partial(add_x, slot_x)))


def collide(pulled, inverse, rho, ux, uy, uz, fluid, wanted):
    total = {}
    diff = {}
    for j in range(1, 19, 2):
        total[j] = pulled[j] + pulled[j + 1]
        diff[j] = pulled[j] - pulled[j + 1]
    in_xy, in_xz, in_yz = total[7] + total[9], total[11] + total[13], total[15] + total[17]
    two_x, two_y, two_z = total[1] + total[1], total[3] + total[3], total[5] + total[5]
    count = (12.0 * pulled[0] + (two_x + two_y)) + (two_z + (in_xy + (in_xz + in_yz)))
    flow_x = (diff[1] + diff[1]) + ((diff[7] + diff[9]) + (diff[11] + diff[13]))
    flow_y = (diff[3] + diff[3]) + ((diff[7] - diff[9]) + (diff[15] + diff[17]))
    flow_z = (diff[5] + diff[5]) + ((diff[11] - diff[13]) + (diff[15] - diff[17]))
    xx, yy, zz = two_x + (in_xy + in_xz), two_y + (in_xy + in_yz), two_z + (in_xz + in_yz)
    xy, xz, yz = total[7] - total[9], total[11] - total[13], total[15] - total[17]
    push_x = xx * ux + xy * uy + xz * uz
    push_y = xy * ux + yy * uy + yz * uz
    push_z = xz * ux + yz * uy + zz * uz
    usq = ux * ux + uy * uy + uz * uz
    push = ux * push_x + uy * push_y + uz * push_z
    base = count * (OMEGA / 36.0 + (OMEGA / 24.0) * usq) - (OMEGA / 8.0) * push - ux * inverse
    along_x = (OMEGA / 12.0) * (flow_x + 3.0 * push_x - ux * count) + inverse
    along_y = (OMEGA / 12.0) * (flow_y + 3.0 * push_y - uy * count)
    along_z = (OMEGA / 12.0) * (flow_z + 3.0 * push_z - uz * count)
    parts = {
        1: along_x,
        3: along_y,
        5: along_z,
        7: along_x + along_y,
        9: along_x - along_y,
        11: along_x + along_z,
        13: along_x - along_z,
        15: along_y + along_z,
        17: along_y - along_z,
    }
    out = {}
    for j in wanted:
        if j == 0:
            shift = base
        elif j % 2:
            shift = base + parts[j]
        else:
            shift = base - parts[j - 1]
        out[j] = (1.0 - OMEGA) * pulled[j] + shift
        if fluid is not None:
            out[j] = jnp.where(fluid, out[j], pulled[OPPOSITE[j]])
    change = (-1.0 / 6.0) * rho * (flow_x * ux + flow_y * uy + flow_z * uz)
    return out, change if fluid is None else jnp.where(fluid, change, 0.0)


def only(value, row):
    return jnp.where(lax.broadcasted_iota(jnp.int32, (8, LANES), 0) == row, value, 0.0)


class Plane:
    def across(self, shares, side, line):
        return shares[side, line, pl.ds(8 + self.row, 8), :]

    def rim(self, shares, line, toward):
        if toward != (-1 if self.row < 0 else 1):
            return 0.0
        return only(shares[line, self.x, pl.ds(8 + self.row, 8), :], 0 if toward < 0 else 1)

    def __init__(self, x, row):
        self.x, self.row = x, row

    def load(self, ref, lead, margin, cx=0, cy=0):
        return ref[lead, self.x + margin + cx, pl.ds(8 + self.row + cy, 8), :]

    def store(self, ref, lead, margin, value):
        ref[lead, self.x + margin, pl.ds(8 + self.row, 8), :] = value


class Rim:
    def __init__(self, x, ext_y):
        self.x, self.ext_y = x, ext_y

    def across(self, shares, side, line):
        upper, lower = shares[side, line, pl.ds(8 + self.ext_y - 1, 8), :], shares[side, line, pl.ds(1, 8), :]
        return jnp.where(lax.broadcasted_iota(jnp.int32, (8, LANES), 0) < 4, upper, lower)

    def rim(self, shares, line, toward):
        start = 1 if toward < 0 else 8 + self.ext_y - 1
        return only(shares[line, self.x, pl.ds(start, 8), :], 6 if toward < 0 else 1)

    def load(self, ref, lead, margin, cx=0, cy=0):
        at = self.x + margin + cx
        upper = ref[lead, at, pl.ds(8 + self.ext_y - 1 + cy, 8), :]
        lower = ref[lead, at, pl.ds(1 + cy, 8), :]
        return jnp.where(lax.broadcasted_iota(jnp.int32, (8, LANES), 0) < 4, upper, lower)

    def store(self, ref, lead, margin, value):
        at = self.x + margin
        ref[lead, at, pl.ds(8 + self.ext_y - 1, 2), :] = value[0:2]
        ref[lead, at, pl.ds(7, 2), :] = value[6:8]


def first_step(first, fields, second, change, tiles, outside=True, shares=None, y_shares=None):
    loaded = [
        (
            [tile.load(first, j, 2, *VELOCITIES[j][:2]) for j in range(19)],
            [tile.load(fields, k, 1) for k in range(5)],
        )
        for tile in tiles
    ]
    done = [
        collide(pulled, 1.0 / rho, rho, ux, uy, uz, kind > 1.5, range(19))
        for pulled, (rho, ux, uy, uz, kind) in loaded
    ]
    for tile, (_, here), (after, gain) in zip(tiles, loaded, done):
        inside = here[KIND] > 0.5
        side = None if shares is None else {-1: 0, second.shape[1] - 2: 1}.get(tile.x)
        for j in range(19):
            value = after[j]
            if side is not None and VELOCITIES[j][0] == 2 * side - 1:
                value = value + tile.across(shares, side, pops(0, 2 * side - 1).index(j))
            if side is None and y_shares is not None and VELOCITIES[j][1]:
                value = value + tile.rim(y_shares, pops(1, VELOCITIES[j][1]).index(j), VELOCITIES[j][1])
            if outside:
                value = jnp.where(inside, value, 0.0)
            cz = VELOCITIES[j][2]
            tile.store(second, j, 1, pltpu.roll(value, -cz % LANES, 1) if cz else value)
        tile.store(change, 0, 1, gain)


def inner_kernel(den, vel, mask, first, fields, second, change):
    refs = (None, den, vel, mask)
    ext_x, ext_y, _ = mask.shape
    every = slice(None)
    for k in range(5):
        fields[k, 1 : 1 + ext_x, pl.ds(8, ext_y), :] = field_of(refs, "field", k, (every, every, every))

    many = 3 if (ext_x - 2) % 3 == 0 else 1

    @pl.loop(0, (ext_x - 2) // many)
    def _(group):
        tiles = [Plane(many * group + at + 1, 1 + 8 * part) for at in range(many) for part in range(ext_y // 8)]
        first_step(first, fields, second, change, tiles, outside=False)


def put_row(first, fields, kind, index, x, y, value):
    row = y + 8
    if kind == "pop":
        first[index, x + 2, row : row + 1, :] = value
    else:
        fields[index, x + 1, row : row + 1, :] = value


def place_z(z_first, value, start, size, side, ext_x):
    rows = pl.ds(start, size)
    spot = lane_ids()[:size] % GROUP
    inside = spot >= 2 + ext_x if side else spot < 2
    for tile in range(Z_TILES):
        shift = (2 + ext_x if side else 0) - 2 * tile
        moved = pltpu.roll(value, shift % LANES, 1)[:size]
        z_first[tile, rows, :] = jnp.where(inside, moved, z_first[tile, rows, :])


def z_step(z_first, z_second, starts):
    lane = lane_ids()
    loaded = []
    for row in starts:

        def both(low_tile, high_tile, group, cx, cy):
            rows = pl.ds(8 + row + cy, 8)
            low = pltpu.roll(z_first[low_tile, rows, :], (-GROUP * group - cx) % LANES, 1)
            high = pltpu.roll(z_first[high_tile, rows, :], (LANES // 2 - GROUP * group - cx) % LANES, 1)
            return jnp.where(lane < LANES // 2, low, high)

        pulled = []
        for j in range(19):
            cx, cy, cz = VELOCITIES[j]
            if cz == 0:
                tile, group = Z_PLACE[("pop", j)]
                pulled.append(both(BELOW + tile, ABOVE + tile, group, cx, cy))
            elif cz == 1:
                pulled.append(both(OWN_LOW, ABOVE + 2, Z_UP.index(j), cx, cy))
            else:
                pulled.append(both(BELOW + 2, OWN_HIGH, Z_DOWN.index(j), cx, cy))
        places = [Z_PLACE[("field", k)] for k in range(5)]
        loaded.append((pulled, [both(BELOW + tile, ABOVE + tile, group, 0, 0) for tile, group in places]))
    done = [
        collide(pulled, 1.0 / rho, rho, ux, uy, uz, kind > 1.5, Z_UP + Z_DOWN)[0]
        for pulled, (rho, ux, uy, uz, kind) in loaded
    ]
    for row, (_, here), after in zip(starts, loaded, done):
        for group in range(5):
            value = jnp.where(lane < LANES // 2, after[Z_DOWN[group]], after[Z_UP[group]])
            z_second[group, pl.ds(8 + row, 8), :] = jnp.where(here[KIND] > 0.5, value, 0.0)


def second_step(refs, second, z_second, change, held, held_sens, planes):
    den, vel, mask = refs
    _, ext_y, _ = mask.shape
    lane = lane_ids()
    every = slice(None)
    loaded = []
    for x, part in itertools.product(planes, range(ext_y // 8)):
        row = 8 + 8 * part
        pulled = []
        for j in range(19):
            cx, cy, cz = VELOCITIES[j]
            rows = pl.ds(row + cy, 8)
            value = second[j, x + 1 + cx, rows, :]
            if cz == 1:
                edge = z_second[Z_UP.index(j), rows, :]
                edge = pltpu.roll(edge, LANES // 2 - 3 - cx - x, 1)
                value = jnp.where(lane == LANES - 1, edge, value)
            elif cz == -1:
                edge = z_second[Z_DOWN.index(j), rows, :]
                edge = pltpu.roll(edge, LANES - 2 - cx - x, 1)
                value = jnp.where(lane == 0, edge, value)
            pulled.append(value)
        at = (x, pl.ds(8 * part, 8), every)
        rho = den[(0, *at)]
        here = [1.0 / rho, rho, vel[(0, 0, *at)], vel[(0, 1, *at)], vel[(0, 2, *at)], mask[at] > 0]
        loaded.append((at, pulled, here, change[0, x + 1, pl.ds(row, 8), :]))
    done = [collide(pulled, *here, range(19)) for _, pulled, here, _ in loaded]
    for (at, _, _, before), (after, gain) in zip(loaded, done):
        for j in range(19):
            held[(j, *at)] = after[j]
        held_sens[at] = before + gain


def side_kernel(slots, den, vel, mask, z_set, *rest):
    many_x, many_y = slots
    from_x, from_y = rest[4 : 4 + many_x], rest[4 + many_x : 4 + many_x + many_y]
    first, fields, second, change, z_first, z_second, shares, y_shares, held, held_sens = rest[-10:]
    _, ext_y, _ = z_set.shape
    ext_x = change.shape[1] - 2
    inner = pl.ds(8, ext_y)
    put = functools.partial(put_row, first, fields)
    z_first[:, inner, :] = z_set[...]

    def place_y(slot, side):
        packet = from_y[slot]
        toward = 2 * side - 1
        near = ext_y if side else -1
        nothing = jnp.zeros((1, LANES), jnp.float32)
        full, ends = side_lines(1, toward)
        for x in range(ext_x):
            for j in pops(1, 0):
                put("pop", j, x, near, nothing)
            for j in pops(1, toward):
                put("pop", j, x, near + toward, nothing)
            put("field", RHO, x, near, jnp.full((1, LANES), jnp.inf, jnp.float32))
            for line, (kind, index) in enumerate(full):
                if kind == "share":
                    y_shares[index, x, near + 8 : near + 9, :] = packet[line, x : x + 1, :]
                else:
                    put(kind, index, x, near, packet[line, x : x + 1, :])
        for spot, (index, depth, end) in enumerate(ends):
            put("pop", index, ext_x - 1 if end else 0, near + toward * depth, packet[SIDE - 1, spot : spot + 1, :])
        start = 8 + ext_y if side else 6
        for tile in range(Z_TILES):
            row = 2 * tile % 8
            z_first[tile, start : start + 2, :] = packet[SIDE + tile // 4, row : row + 2, :]
        if many_y == 1:
            clear_y(1 - side)

    def clear_y(side):
        nothing = jnp.zeros((1, LANES), jnp.float32)
        y = ext_y if side else -1
        for x in range(-2, ext_x + 2):
            for j in pops(1, 2 * side - 1):
                put("pop", j, x, y, nothing)
        for x in range(-1, ext_x + 1):
            put("field", KIND, x, y, nothing)
        start = 8 + ext_y if side else 6
        for tile in range(Z_TILES):
            z_first[tile, start : start + 2, :] = jnp.zeros((2, LANES), jnp.float32)

    def place_x(slot, side):
        packet = from_x[slot]
        toward = 2 * side - 1
        near = ext_x if side else -1
        nothing = jnp.zeros((ext_y, LANES), jnp.float32)
        for j in pops(0, 0):
            first[j, near + 2, inner, :] = nothing
        for j in pops(0, toward):
            first[j, near + toward + 2, inner, :] = nothing
        fields[RHO, near + 1, inner, :] = jnp.full((ext_y, LANES), jnp.inf, jnp.float32)
        full, ends = side_lines(0, toward)
        for line, (kind, index) in enumerate(full):
            if kind == "pop":
                first[index, near + 2, inner, :] = packet[line]
            elif kind == "share":
                shares[side, index, inner, :] = packet[line]
            else:
                fields[index, near + 1, inner, :] = packet[line]
        for spot, (index, depth, end) in enumerate(ends):
            put("pop", index, near + toward * depth, ext_y - 1 if end else 0, packet[SIDE - 1, spot : spot + 1, :])
        for part in range(ext_y // 8):
            place_z(z_first, packet[SIDE, pl.ds(8 * part, 8), :], 8 + 8 * part, 8, side, ext_x)

    shares[:, :, pl.ds(0, 8), :] = jnp.zeros((2, 5, 8, LANES), jnp.float32)
    shares[:, :, pl.ds(8 + ext_y, 8), :] = jnp.zeros((2, 5, 8, LANES), jnp.float32)
    for slot_y in range(many_y):
        on_side(parity_of("gy"), slot_y, functools.partial(place_y, slot_y))
    for slot_x in range(many_x):
        on_side(parity_of("gx"), slot_x, functools.partial(place_x, slot_x))

    starts = range(1, ext_y, 8)
    first_step(first, fields, second, change, [Plane(x, row) for x in (0, ext_x - 1) for row in starts], outside=False)
    first_step(first, fields, second, change, [Plane(x, row) for x in (-1, ext_x) for row in starts], shares=shares)
    z_step(z_first, z_second, range(7, ext_y - 8, 8))
    many = 3 if (ext_x - 2) % 3 == 0 else 1

    @pl.loop(0, (ext_x - 2) // many)
    def _(group):
        tiles = [Rim(many * group + at + 1, ext_y) for at in range(many)]
        first_step(first, fields, second, change, tiles, y_shares=y_shares)

    z_step(z_first, z_second, (-1, ext_y - 1))
    second_step((den, vel, mask), second, z_second, change, held, held_sens, range(2, ext_x - 2))


def last_kernel(slots, den, vel, mask, *rest):
    many_x, many_y = slots
    from_xy = rest[10 : 10 + many_x * many_y]
    out, sens, first, fields, second, change, z_first, z_second, shares, y_shares, held, held_sens, sems = rest[-13:]
    ext_x, ext_y, _ = mask.shape
    lane = lane_ids()
    every = slice(None)
    px, py = parity_of("gx"), parity_of("gy")

    def copies(x):
        return (
            pltpu.make_async_copy(held.at[:, x], out.at[:, x], sems.at[0, x]),
            pltpu.make_async_copy(held_sens.at[x], sens.at[x], sems.at[1, x]),
        )

    for x in range(2, ext_x - 2):
        for copy in copies(x):
            copy.start()

    def place_xy(slot_x, slot_y, side_x, side_y):
        packet = from_xy[many_x * slot_y + slot_x]
        for line, (kind, index, far_x, far_y) in enumerate(edge_lines(2 * side_x - 1, 2 * side_y - 1)):
            x = ext_x + far_x if side_x else -1 - far_x
            y = ext_y + far_y if side_y else -1 - far_y
            put_row(first, fields, kind, index, x, y, packet[line // 8, line % 8 : line % 8 + 1, :])
        place_z(z_first, packet[EDGE // 8], 8 + ext_y if side_y else 6, 2, side_x, ext_x)

    for slot_x in range(many_x):
        for slot_y in range(many_y):
            on_side(
                py,
                slot_y,
                lambda side_y: on_side(px, slot_x, lambda side_x: place_xy(slot_x, slot_y, side_x, side_y)),
            )

    for pair in ((-1, 0), (ext_x - 1, ext_x)):
        tiles = [Rim(x, ext_y) for x in pair]
        first_step(first, fields, second, change, tiles, shares=shares, y_shares=y_shares)

    z_step(z_first, z_second, (-1, ext_y - 1))

    planes = [0, 1, ext_x - 2, ext_x - 1]
    for pair in (planes[:2], planes[2:]):
        second_step((den, vel, mask), second, z_second, change, held, held_sens, pair)
        for x in pair:
            for copy in copies(x):
                copy.start()

    for x in range(ext_x):
        for copy in copies(x):
            copy.wait()


def shards(adjoint, density, velocity, pore_mask):
    ext_x, ext_y, ext_z = pore_mask.shape
    assert ext_z == LANES and ext_y % 8 == 0 and ext_x + 4 <= GROUP and ext_x == 8
    many_x = 2
    many_y, many_z = [1 if lax.axis_size(axis) == 2 else 2 for axis in ("gy", "gz")]
    vmem = pl.BlockSpec(memory_space=pltpu.VMEM)
    hbm = pl.BlockSpec(memory_space=pltpu.HBM)
    inputs = (adjoint, density, velocity, pore_mask)

    def array(*shape):
        return jax.ShapeDtypeStruct(shape, jnp.float32)

    def call(kernel, name, operands, shapes, limit, **more):
        more.setdefault("out_specs", [vmem] * len(shapes))
        more.setdefault("in_specs", [vmem] * len(operands))
        params = pltpu.CompilerParams(vmem_limit_bytes=limit * 1024 * 1024)
        return pl.pallas_call(kernel, out_shape=shapes, compiler_params=params, name=name, **more)(*operands)

    def partners(axis, slot):
        found = {}
        for at in range(slot, lax.axis_size(axis) - 1, 2):
            found[at], found[at + 1] = at + 1, at
        return found

    def ends(axis):
        last = lax.axis_size(axis) - 1
        return {0: last, last: 0}

    def swap(value, spares, *places):
        tables = {axis: partners(axis, slot) for axis, slot in places}
        axes = [axis for axis in ("gx", "gy", "gz") if axis in tables or axis in dict(spares)]
        sizes = [lax.axis_size(axis) for axis in axes]
        pairs = []
        for at in itertools.product(*[range(size) for size in sizes]):
            to = [tables.get(axis, {}).get(spot, spot) for axis, spot in zip(axes, at)]
            for spare, table in spares:
                if tuple(to) == at:
                    to = [table.get(spot, spot) if axis == spare else spot for axis, spot in zip(axes, at)]
            flat = []
            for spots in (at, to):
                index = 0
                for size, spot in zip(sizes, spots):
                    index = index * size + spot
                flat.append(index)
            pairs.append(tuple(flat))
        return lax.ppermute(value, tuple(axes), pairs)

    loaded = [jax.ShapeDtypeStruct(value.shape, value.dtype) for value in inputs]
    *held, near, a_z, b_z = (
        *call(
            functools.partial(pack_z_kernel, many_z),
            "pack_z",
            [pltpu.with_memory_space_constraint(value, pltpu.HBM) for value in inputs],
            loaded + [array(2, ext_y, LANES)] + [array(2, ext_y, LANES)] * many_z,
            8,
            in_specs=[hbm] * 4,
            scratch_shapes=[pltpu.SemaphoreType.DMA((10,))],
        ),
        *[None] * (2 - many_z),
    )
    from_z = [swap(value, [("gx", partners("gx", 0))], ("gz", slot)) for slot, value in enumerate((a_z, b_z)[:many_z])]

    rows = ext_y + 16
    adj, den, vel, mask = held
    shapes = (
        [array(19, ext_x + 4, rows, LANES)]
        + [array(SIDE + 1, ext_y, LANES)] * many_x
        + [array(FACE, ext_x, LANES)] * many_y
        + [array(EDGE // 8 + 1, 8, LANES)] * (many_x * many_y)
    )
    shifted = call(
        functools.partial(shift_kernel, (many_x, many_y)),
        "shift",
        (adj, den, vel, mask),
        shapes,
        8,
        cost_estimate=pl.CostEstimate(flops=1_000_000, bytes_accessed=2_500_000, transcendentals=0),
    )
    z_set, first, *packets = call(
        functools.partial(pack_xy_kernel, (many_x, many_y, many_z)),
        "pack_xy",
        (den, vel, mask, near, *from_z, *shifted),
        [array(Z_TILES, ext_y, LANES)] + shapes + [array(SIDE + 2, ext_x, LANES)] * many_y,
        8,
        input_output_aliases={4 + many_z + at: 1 + at for at in range(len(shapes))},
        scratch_shapes=[
            pltpu.VMEM((2, ext_y, LANES), jnp.float32),
            pltpu.VMEM((2, 5, ext_y, LANES), jnp.float32),
        ],
    )
    to_x, to_xy, to_y = packets[:many_x], packets[many_x + many_y : -many_y], packets[-many_y:]
    from_xy = [
        swap(to_xy[many_x * slot_y + slot_x], [], ("gx", slot_x), ("gy", slot_y))
        for slot_y in range(many_y)
        for slot_x in range(many_x)
    ]
    from_y = [swap(value, [("gz", partners("gz", 0))], ("gy", slot)) for slot, value in enumerate(to_y)]
    spares = [("gx", ends("gx"))]
    if lax.axis_size("gz") > 2:
        top = lax.axis_size("gz") - 1
        spares = [("gz", {top - 1: top, top: top - 1})] + spares
    from_x = [swap(value, spares, ("gx", slot)) for slot, value in enumerate(to_x)]

    fields, second, change = call(
        inner_kernel,
        "inner_step",
        (den, vel, mask, first),
        [array(5, ext_x + 2, rows, LANES), array(19, ext_x + 2, rows, LANES), array(1, ext_x + 2, rows, LANES)],
        8,
        cost_estimate=pl.CostEstimate(flops=40_000_000, bytes_accessed=8_000_000, transcendentals=0),
    )
    inout = (first, fields, second, change)
    inout = call(
        functools.partial(side_kernel, (many_x, many_y)),
        "side_step",
        (den, vel, mask, z_set, *inout, *from_x, *from_y),
        [array(*value.shape) for value in inout] + [array(Z_TILES, rows, LANES), array(5, rows, LANES), array(2, 5, rows, LANES), array(5, ext_x, rows, LANES)]
        + [array(19, ext_x, ext_y, LANES), array(ext_x, ext_y, LANES)],
        8,
        input_output_aliases={4 + at: at for at in range(4)},
        cost_estimate=pl.CostEstimate(flops=40_000_000, bytes_accessed=8_000_000, transcendentals=0),
    )
    return call(
        functools.partial(last_kernel, (many_x, many_y)),
        "last_steps",
        (den, vel, mask, *inout, *from_xy),
        [array(19, ext_x, ext_y, LANES), array(ext_x, ext_y, LANES)] + [array(*value.shape) for value in inout],
        8,
        out_specs=[hbm] * 2 + [vmem] * 10,
        input_output_aliases={3 + at: 2 + at for at in range(10)},
        scratch_shapes=[pltpu.SemaphoreType.DMA((2, ext_x))],
    )[:2]


def solution(mesh):
    placed = (
        P(None, "gx", "gy", "gz"),
        P(None, "gx", "gy", "gz"),
        P(None, None, "gx", "gy", "gz"),
        P("gx", "gy", "gz"),
    )

    def whole(*arrays):
        return tuple(shards(*arrays))

    return jax.shard_map(
        whole,
        mesh=mesh,
        in_specs=placed,
        out_specs=(P(None, "gx", "gy", "gz"), P("gx", "gy", "gz")),
        check_vma=False,
    )
```

```python
import functools
import itertools

import jax
import jax.numpy as jnp
from jax import lax
from jax.experimental import pallas as pl
from jax.experimental.pallas import tpu as pltpu
from jax.sharding import PartitionSpec as P

VELOCITIES = [
    (0, 0, 0),
    (1, 0, 0),
    (-1, 0, 0),
    (0, 1, 0),
    (0, -1, 0),
    (0, 0, 1),
    (0, 0, -1),
    (1, 1, 0),
    (-1, -1, 0),
    (1, -1, 0),
    (-1, 1, 0),
    (1, 0, 1),
    (-1, 0, -1),
    (1, 0, -1),
    (-1, 0, 1),
    (0, 1, 1),
    (0, -1, -1),
    (0, 1, -1),
    (0, -1, 1),
]
OPPOSITE = [0, 2, 1, 4, 3, 6, 5, 8, 7, 10, 9, 12, 11, 14, 13, 16, 15, 18, 17]
OMEGA = 1.25
LANES = 128
GROUP = 16


def pops(axis, sign):
    return [j for j in range(19) if VELOCITIES[j][axis] == sign]


def mirrored(j):
    cx, cy, cz = VELOCITIES[j]
    return VELOCITIES.index((cx, cy, -cz))


Z_FLAT = pops(2, 0)
Z_UP = pops(2, 1)
Z_DOWN = [mirrored(j) for j in Z_UP]
RHO, UX, UY, UZ, KIND = range(5)
Z_PLACE = {("pop", j): (0, g) for g, j in enumerate(Z_FLAT[:8])}
Z_PLACE[("pop", Z_FLAT[8])] = (1, 5)
Z_PLACE[("field", RHO)] = (1, 6)
Z_PLACE[("field", KIND)] = (1, 7)
Z_PLACE[("field", UX)] = (2, 5)
Z_PLACE[("field", UY)] = (2, 6)
Z_PLACE[("field", UZ)] = (2, 7)
BELOW, ABOVE, OWN_LOW, OWN_HIGH, Z_TILES = 0, 3, 6, 7, 8


def face_lines(axis, toward):
    near = pops(axis, 0) + pops(axis, toward)
    lines = [("pop", j, 0) for j in near] + [("field", k, 0) for k in range(5)]
    return lines + [("pop", j, 1) for j in pops(axis, toward)]


def edge_lines(toward_x, toward_y):
    lines = [("field", k, 0, 0) for k in range(5)]
    for j in range(19):
        cx, cy, _ = VELOCITIES[j]
        if cx not in (0, toward_x) or cy not in (0, toward_y):
            continue
        lines.append(("pop", j, 0, 0))
        if cx:
            lines.append(("pop", j, 1, 0))
        if cy:
            lines.append(("pop", j, 0, 1))
        if cx and cy:
            lines.append(("pop", j, 1, 1))
    return lines


FACE = 24
EDGE = 24
SIDE = 15


def side_lines(axis, toward):
    full = [("pop", j) for j in pops(axis, toward)] + [("share", p) for p in range(5)]
    full += [("field", k) for k in (UX, UY, UZ, KIND)]
    ends = []
    for end in range(2):
        for j in pops(1 - axis, 1 - 2 * end):
            across = VELOCITIES[j][axis]
            if across in (0, toward):
                ends.append((j, abs(across), end))
    return full, ends


def lane_ids():
    return lax.broadcasted_iota(jnp.int32, (8, LANES), 1)


def field_of(refs, kind, index, at):
    adj, den, vel, mask = refs
    if kind == "pop":
        return adj[(index, *at)]
    if index == RHO:
        return den[(1, *at)]
    if index == KIND:
        return (mask[at] + 1).astype(jnp.float32)
    return vel[(1, index - UX, *at)]


def parity_of(axis):
    return lax.rem(lax.axis_index(axis), 2)


def on_side(parity, slot, act):
    @pl.when(parity == slot)
    def _():
        act(1)

    @pl.when(parity != slot)
    def _():
        act(0)


def has_partner(axis, slot):
    at = lax.axis_index(axis)
    to = at + jnp.where(lax.rem(at, 2) == slot, 1, -1)
    return (to >= 0) & (to < lax.axis_size(axis))


def pack_z_kernel(slots, adj_in, den_in, vel_in, mask_in, adj, den, vel, mask, near, *rest):
    packets, sems = rest[:slots], rest[slots]
    refs = (adj, den, vel, mask)
    ext_x, ext_y, _ = mask.shape
    starts = range(0, 19, 10)
    loads = [
        pltpu.make_async_copy(adj_in.at[start : min(start + 10, 19)], adj.at[start : min(start + 10, 19)], sems.at[at])
        for at, start in enumerate(starts)
    ] + [
        pltpu.make_async_copy(source, target, sems.at[len(starts) + at])
        for at, (source, target) in enumerate([(den_in, den), (vel_in, vel), (mask_in, mask)])
    ]
    for load in loads:
        load.start()
    lane = lane_ids()
    parity = parity_of("gz")
    parts = range(ext_y // 8)
    zero = jnp.zeros((8, LANES), jnp.float32)
    lows, highs = [[zero] * 3 for _ in parts], [[zero] * 3 for _ in parts]
    far_low, far_high = [zero for _ in parts], [zero for _ in parts]

    def gather(kind, index):
        for x, part in itertools.product(range(ext_x), parts):
            value = field_of(refs, kind, index, (x, pl.ds(8 * part, 8), slice(None)))
            if kind == "pop" and VELOCITIES[index][2] == 1:
                spot = GROUP * Z_UP.index(index) + 2 + x
                moved = pltpu.roll(value, spot, 1)
                lows[part][1] = jnp.where(lane == spot, moved, lows[part][1])
                far_low[part] = jnp.where(lane == spot + 1, moved, far_low[part])
            elif kind == "pop" and VELOCITIES[index][2] == -1:
                spot = GROUP * Z_DOWN.index(index) + 2 + x
                moved = pltpu.roll(value, spot, 1)
                highs[part][1] = jnp.where(lane == spot - 1, moved, highs[part][1])
                far_high[part] = jnp.where(lane == spot - 2, moved, far_high[part])
            else:
                tile, group = Z_PLACE[(kind, index)]
                spot = GROUP * group + 2 + x
                moved = pltpu.roll(value, spot, 1)
                lows[part][tile] = jnp.where(lane == spot, moved, lows[part][tile])
                highs[part][tile] = jnp.where(lane == spot - 1, moved, highs[part][tile])

    for start, load in zip(starts, loads):
        load.wait()
        for j in range(start, min(start + 10, 19)):
            gather("pop", j)
    for load in loads[len(starts) :]:
        load.wait()
    for k in range(5):
        gather("field", k)
    for part in parts:
        rows = pl.ds(8 * part, 8)
        low = lows[part]
        high = [pltpu.roll(tile, 1, 1) for tile in highs[part]]
        low[2] = jnp.where(lane < 5 * GROUP, pltpu.roll(far_low[part], LANES - 1, 1), low[2])
        high[2] = jnp.where(lane < 5 * GROUP, pltpu.roll(far_high[part], 2, 1), high[2])
        near[0, rows, :] = low[1]
        near[1, rows, :] = high[1]
        for slot in range(slots):
            there = has_partner("gz", slot)
            sent = [jnp.where(there, jnp.where(parity == slot, up, down), 0.0) for up, down in zip(high, low)]
            mine = (lane + (GROUP - 2)) % GROUP < GROUP // 2
            packets[slot][0, rows, :] = jnp.where(mine, sent[0], pltpu.roll(sent[1], GROUP // 2, 1))
            packets[slot][1, rows, :] = sent[2]


def pack_lines(refs, first, packets, many_x, many_y, wanted, shares):
    to_x, y_lines = packets[:many_x], packets[many_x : many_x + many_y]
    to_xy = packets[many_x + many_y :]
    ext_x, ext_y, _ = refs[-1].shape
    every = slice(None)
    px, py = parity_of("gx"), parity_of("gy")

    def line_of(kind, index, x, y):
        if kind == "pop":
            return first[index, x + 2, y + 8 : y + 9, :]
        return field_of(refs, kind, index, (x, slice(y, y + 1), every))

    def pack_xy(slot_x, slot_y, side_x, side_y):
        packet = to_xy[many_x * slot_y + slot_x]
        for line, (kind, index, far_x, far_y) in enumerate(edge_lines(1 - 2 * side_x, 1 - 2 * side_y)):
            if wanted(kind, index):
                x = ext_x - 1 - far_x if side_x else far_x
                y = ext_y - 1 - far_y if side_y else far_y
                packet[line // 8, line % 8 : line % 8 + 1, :] = line_of(kind, index, x, y)

    def pack_y(slot, side):
        for line, (kind, index, depth) in enumerate(face_lines(1, 1 - 2 * side)):
            if wanted(kind, index):
                y = ext_y - 1 - depth if side else depth
                for x in range(ext_x):
                    y_lines[slot][line, x : x + 1, :] = line_of(kind, index, x, y)

    def pack_x(slot, side):
        full, ends = side_lines(0, 1 - 2 * side)
        for line, (kind, index) in enumerate(full):
            if kind == "field" and wanted(kind, index):
                to_x[slot][line] = field_of(refs, kind, index, (ext_x - 1 if side else 0, every, every))
            elif kind == "pop" and wanted(kind, index):
                to_x[slot][line] = first[index, (ext_x - 1 if side else 0) + 2, pl.ds(8, ext_y), :]
            elif kind == "share" and shares is not None:
                to_x[slot][line] = shares[side, index]
        for spot, (index, depth, end) in enumerate(ends):
            if wanted("pop", index):
                x = ext_x - 1 - depth if side else depth
                to_x[slot][SIDE - 1, spot : spot + 1, :] = line_of("pop", index, x, ext_y - 1 if end else 0)

    def when_there(there, packet, act):
        pl.when(there)(act)
        if shares is None:

            @pl.when(jnp.logical_not(there))
            def _():
                packet[...] = jnp.zeros(packet.shape, jnp.float32)

    for slot_y in range(many_y):
        there_y = has_partner("gy", slot_y)
        when_there(there_y, y_lines[slot_y], lambda: on_side(py, slot_y, functools.partial(pack_y, slot_y)))
        for slot_x in range(many_x):
            when_there(
                there_y & has_partner("gx", slot_x),
                to_xy[many_x * slot_y + slot_x],
                lambda: on_side(
                    py,
                    slot_y,
                    lambda side_y: on_side(px, slot_x, lambda side_x: pack_xy(slot_x, slot_y, side_x, side_y)),
                ),
            )
    for slot_x in range(many_x):
        when_there(
            has_partner("gx", slot_x), to_x[slot_x], lambda: on_side(px, slot_x, functools.partial(pack_x, slot_x))
        )


def is_flat(kind, index):
    return kind == "field" or VELOCITIES[index][2] == 0


def shift_kernel(slots, adj, den, vel, mask, first, *packets):
    many_x, many_y = slots
    _, ext_x, ext_y, _ = adj.shape
    for j in range(19):
        cz = VELOCITIES[j][2]
        for x, part in itertools.product(range(ext_x), range(ext_y // 8)):
            value = adj[j, x, pl.ds(8 * part, 8), :]
            first[j, 2 + x, pl.ds(8 + 8 * part, 8), :] = pltpu.roll(value, -cz % LANES, 1) if cz else value
    pack_lines((None, den, vel, mask), first, packets, many_x, many_y, is_flat, None)


def pack_xy_kernel(slots, den, vel, mask, near, *rest):
    many_x, many_y, many_z = slots
    count = many_x + many_y + many_x * many_y
    from_z, rest = rest[:many_z], rest[many_z + 1 + count :]
    z_set, first, packets, faces, shares = rest[0], rest[1], rest[2 : 2 + count], rest[-2], rest[-1]
    to_x, y_lines, to_xy = packets[:many_x], packets[many_x : many_x + many_y], packets[many_x + many_y :]
    to_y = rest[2 + count : -2]
    ext_x, ext_y = first.shape[1] - 4, near.shape[1]
    spot = lane_ids() % GROUP
    px, py, pz = parity_of("gx"), parity_of("gy"), parity_of("gz")

    z_set[OWN_LOW] = near[0]
    z_set[OWN_HIGH] = near[1]

    def taken(slot, tile):
        if tile == 1:
            return pltpu.roll(from_z[slot][0], LANES - GROUP // 2, 1)
        return from_z[slot][tile // 2]

    for tile in range(3):
        even = taken(0, tile)
        odd = taken(1, tile) if many_z > 1 else jnp.zeros_like(even)
        z_set[ABOVE + tile] = jnp.where(pz == 0, even, odd)
        z_set[BELOW + tile] = jnp.where(pz == 0, odd, even)

    for j in Z_UP + Z_DOWN:
        up = VELOCITIES[j][2] > 0
        group = (Z_UP if up else Z_DOWN).index(j)
        last = LANES - 1 if up else 0
        for part in range(ext_y // 8):
            halo = z_set[(ABOVE if up else BELOW) + 1, pl.ds(8 * part, 8), :]
            for x in range(ext_x):
                edge = pltpu.roll(halo, (last - 2 - GROUP * group - x) % LANES, 1)
                first[j, 2 + x, pl.ds(8 + 8 * part, 8), last : last + 1] = edge[:, last : last + 1]


    sub = lax.broadcasted_iota(jnp.int32, (8, LANES), 0)
    loaded = []
    for side, part in itertools.product(range(2), range(ext_y // 8)):
        toward, x = 1 - 2 * side, ext_x - 1 if side else 0
        pulled = []
        for j in range(19):
            cx, cy, _ = VELOCITIES[j]
            if cx == -toward:
                pulled.append(jnp.zeros((8, LANES), jnp.float32))
                continue
            value = first[j, x + 2 + cx, pl.ds(8 + 8 * part + cy, 8), :]
            if cy == -1 and part == 0:
                value = jnp.where(sub == 0, 0.0, value)
            if cy == 1 and part == ext_y // 8 - 1:
                value = jnp.where(sub == 7, 0.0, value)
            pulled.append(value)
        at = (x, pl.ds(8 * part, 8), slice(None))
        here = [den[(1, *at)], vel[(1, 0, *at)], vel[(1, 1, *at)], vel[(1, 2, *at)], mask[at] > 0]
        loaded.append((side, part, pulled, here))
    for side, part, pulled, (rho, ux, uy, uz, fluid) in loaded:
        wanted = pops(0, 1 - 2 * side)
        after, _ = collide(pulled, 1.0 / rho, rho, ux, uy, uz, None, wanted)
        for line, j in enumerate(wanted):
            shares[side, line, pl.ds(8 * part, 8), :] = jnp.where(fluid, after[j], 0.0)

    pack_lines((mask,), first, packets, many_x, many_y, lambda kind, index: not is_flat(kind, index), shares)

    for side in range(2):
        for part in range(ext_y // 8):
            rows = pl.ds(8 * part, 8)
            value = jnp.zeros((8, LANES), jnp.float32)
            for tile in range(Z_TILES):
                start = ext_x if side else 2
                moved = pltpu.roll(z_set[tile, rows, :], (2 * tile - start) % LANES, 1)
                value = jnp.where(spot // 2 == tile, moved, value)
            faces[side, rows, :] = value

    def add_xy(slot_x, slot_y, side_x, side_y):
        start = ext_y - 2 if side_y else 0
        to_xy[many_x * slot_y + slot_x][EDGE // 8, 0:2, :] = faces[side_x, start : start + 2, :]

    def add_y(slot, side):
        toward = 1 - 2 * side
        lines = {name: line for line, name in enumerate(face_lines(1, toward))}
        pulled = []
        for j in range(19):
            cx, cy, _ = VELOCITIES[j]
            if cy == -toward:
                pulled.append(jnp.zeros((8, LANES), jnp.float32))
                continue
            value = y_lines[slot][lines[("pop", j, abs(cy))]]
            if cx:
                value = jnp.where(sub == (7 if cx > 0 else 0), 0.0, pltpu.roll(value, -cx % 8, 0))
            pulled.append(value)
        rho, ux, uy, uz, kind = [y_lines[slot][lines[("field", k, 0)]] for k in range(5)]
        after, _ = collide(pulled, 1.0 / rho, rho, ux, uy, uz, None, pops(1, toward))
        full, ends = side_lines(1, toward)
        for line, (what, index) in enumerate(full):
            if what == "share":
                to_y[slot][line] = jnp.where(kind > 1.5, after[pops(1, toward)[index]], 0.0)
            else:
                to_y[slot][line] = y_lines[slot][lines[(what, index, 0)]]
        for spot, (index, depth, end) in enumerate(ends):
            x = ext_x - 1 if end else 0
            to_y[slot][SIDE - 1, spot : spot + 1, :] = y_lines[slot][lines[("pop", index, depth)], x : x + 1, :]
        start = ext_y - 2 if side else 0
        for tile in range(Z_TILES):
            row = 2 * tile % 8
            to_y[slot][SIDE + tile // 4, row : row + 2, :] = z_set[tile, start : start + 2, :]

    def add_x(slot, side):
        to_x[slot][SIDE] = faces[side]

    for slot_y in range(many_y):
        there_y = has_partner("gy", slot_y)
        pl.when(there_y)(lambda: on_side(py, slot_y, functools.partial(add_y, slot_y)))

        @pl.when(jnp.logical_not(there_y))
        def _():
            to_y[slot_y][...] = jnp.zeros(to_y[slot_y].shape, jnp.float32)

        for slot_x in range(many_x):
            pl.when(there_y & has_partner("gx", slot_x))(
                lambda: on_side(
                    py,
                    slot_y,
                    lambda side_y: on_side(px, slot_x, lambda side_x: add_xy(slot_x, slot_y, side_x, side_y)),
                )
            )
    for slot_x in range(many_x):
        pl.when(has_partner("gx", slot_x))(lambda: on_side(px, slot_x, functools.partial(add_x, slot_x)))


def collide(pulled, inverse, rho, ux, uy, uz, fluid, wanted):
    total = {}
    diff = {}
    for j in range(1, 19, 2):
        total[j] = pulled[j] + pulled[j + 1]
        diff[j] = pulled[j] - pulled[j + 1]
    in_xy, in_xz, in_yz = total[7] + total[9], total[11] + total[13], total[15] + total[17]
    two_x, two_y, two_z = total[1] + total[1], total[3] + total[3], total[5] + total[5]
    count = (12.0 * pulled[0] + (two_x + two_y)) + (two_z + (in_xy + (in_xz + in_yz)))
    flow_x = (diff[1] + diff[1]) + ((diff[7] + diff[9]) + (diff[11] + diff[13]))
    flow_y = (diff[3] + diff[3]) + ((diff[7] - diff[9]) + (diff[15] + diff[17]))
    flow_z = (diff[5] + diff[5]) + ((diff[11] - diff[13]) + (diff[15] - diff[17]))
    xx, yy, zz = two_x + (in_xy + in_xz), two_y + (in_xy + in_yz), two_z + (in_xz + in_yz)
    xy, xz, yz = total[7] - total[9], total[11] - total[13], total[15] - total[17]
    push_x = xx * ux + xy * uy + xz * uz
    push_y = xy * ux + yy * uy + yz * uz
    push_z = xz * ux + yz * uy + zz * uz
    usq = ux * ux + uy * uy + uz * uz
    push = ux * push_x + uy * push_y + uz * push_z
    base = count * (OMEGA / 36.0 + (OMEGA / 24.0) * usq) - (OMEGA / 8.0) * push - ux * inverse
    along_x = (OMEGA / 12.0) * (flow_x + 3.0 * push_x - ux * count) + inverse
    along_y = (OMEGA / 12.0) * (flow_y + 3.0 * push_y - uy * count)
    along_z = (OMEGA / 12.0) * (flow_z + 3.0 * push_z - uz * count)
    parts = {
        1: along_x,
        3: along_y,
        5: along_z,
        7: along_x + along_y,
        9: along_x - along_y,
        11: along_x + along_z,
        13: along_x - along_z,
        15: along_y + along_z,
        17: along_y - along_z,
    }
    out = {}
    for j in wanted:
        if j == 0:
            shift = base
        elif j % 2:
            shift = base + parts[j]
        else:
            shift = base - parts[j - 1]
        out[j] = (1.0 - OMEGA) * pulled[j] + shift
        if fluid is not None:
            out[j] = jnp.where(fluid, out[j], pulled[OPPOSITE[j]])
    change = (-1.0 / 6.0) * rho * (flow_x * ux + flow_y * uy + flow_z * uz)
    return out, change if fluid is None else jnp.where(fluid, change, 0.0)


def only(value, row):
    return jnp.where(lax.broadcasted_iota(jnp.int32, (8, LANES), 0) == row, value, 0.0)


class Plane:
    def across(self, shares, side, line):
        return shares[side, line, pl.ds(8 + self.row, 8), :]

    def rim(self, shares, line, toward):
        if toward != (-1 if self.row < 0 else 1):
            return 0.0
        return only(shares[line, self.x, pl.ds(8 + self.row, 8), :], 0 if toward < 0 else 1)

    def __init__(self, x, row):
        self.x, self.row = x, row

    def load(self, ref, lead, margin, cx=0, cy=0):
        return ref[lead, self.x + margin + cx, pl.ds(8 + self.row + cy, 8), :]

    def store(self, ref, lead, margin, value):
        ref[lead, self.x + margin, pl.ds(8 + self.row, 8), :] = value


class Rim:
    def __init__(self, x, ext_y):
        self.x, self.ext_y = x, ext_y

    def across(self, shares, side, line):
        upper, lower = shares[side, line, pl.ds(8 + self.ext_y - 1, 8), :], shares[side, line, pl.ds(1, 8), :]
        return jnp.where(lax.broadcasted_iota(jnp.int32, (8, LANES), 0) < 4, upper, lower)

    def rim(self, shares, line, toward):
        start = 1 if toward < 0 else 8 + self.ext_y - 1
        return only(shares[line, self.x, pl.ds(start, 8), :], 6 if toward < 0 else 1)

    def load(self, ref, lead, margin, cx=0, cy=0):
        at = self.x + margin + cx
        upper = ref[lead, at, pl.ds(8 + self.ext_y - 1 + cy, 8), :]
        lower = ref[lead, at, pl.ds(1 + cy, 8), :]
        return jnp.where(lax.broadcasted_iota(jnp.int32, (8, LANES), 0) < 4, upper, lower)

    def store(self, ref, lead, margin, value):
        at = self.x + margin
        ref[lead, at, pl.ds(8 + self.ext_y - 1, 2), :] = value[0:2]
        ref[lead, at, pl.ds(7, 2), :] = value[6:8]


def first_step(first, fields, second, change, tiles, outside=True, shares=None, y_shares=None):
    loaded = [
        (
            [tile.load(first, j, 2, *VELOCITIES[j][:2]) for j in range(19)],
            [tile.load(fields, k, 1) for k in range(5)],
        )
        for tile in tiles
    ]
    done = [
        collide(pulled, 1.0 / rho, rho, ux, uy, uz, kind > 1.5, range(19))
        for pulled, (rho, ux, uy, uz, kind) in loaded
    ]
    for tile, (_, here), (after, gain) in zip(tiles, loaded, done):
        inside = here[KIND] > 0.5
        side = None if shares is None else {-1: 0, second.shape[1] - 2: 1}.get(tile.x)
        for j in range(19):
            value = after[j]
            if side is not None and VELOCITIES[j][0] == 2 * side - 1:
                value = value + tile.across(shares, side, pops(0, 2 * side - 1).index(j))
            if side is None and y_shares is not None and VELOCITIES[j][1]:
                value = value + tile.rim(y_shares, pops(1, VELOCITIES[j][1]).index(j), VELOCITIES[j][1])
            if outside:
                value = jnp.where(inside, value, 0.0)
            cz = VELOCITIES[j][2]
            tile.store(second, j, 1, pltpu.roll(value, -cz % LANES, 1) if cz else value)
        tile.store(change, 0, 1, gain)


def inner_kernel(den, vel, mask, first, fields, second, change):
    refs = (None, den, vel, mask)
    ext_x, ext_y, _ = mask.shape
    every = slice(None)
    for k in range(5):
        fields[k, 1 : 1 + ext_x, pl.ds(8, ext_y), :] = field_of(refs, "field", k, (every, every, every))

    many = 3 if (ext_x - 2) % 3 == 0 else 1

    @pl.loop(0, (ext_x - 2) // many)
    def _(group):
        tiles = [Plane(many * group + at + 1, 1 + 8 * part) for at in range(many) for part in range(ext_y // 8)]
        first_step(first, fields, second, change, tiles, outside=False)


def put_row(first, fields, kind, index, x, y, value):
    row = y + 8
    if kind == "pop":
        first[index, x + 2, row : row + 1, :] = value
    else:
        fields[index, x + 1, row : row + 1, :] = value


def place_z(z_first, value, start, size, side, ext_x):
    rows = pl.ds(start, size)
    spot = lane_ids()[:size] % GROUP
    inside = spot >= 2 + ext_x if side else spot < 2
    for tile in range(Z_TILES):
        shift = (2 + ext_x if side else 0) - 2 * tile
        moved = pltpu.roll(value, shift % LANES, 1)[:size]
        z_first[tile, rows, :] = jnp.where(inside, moved, z_first[tile, rows, :])


def z_step(z_first, z_second, starts):
    lane = lane_ids()
    loaded = []
    for row in starts:

        def both(low_tile, high_tile, group, cx, cy):
            rows = pl.ds(8 + row + cy, 8)
            low = pltpu.roll(z_first[low_tile, rows, :], (-GROUP * group - cx) % LANES, 1)
            high = pltpu.roll(z_first[high_tile, rows, :], (LANES // 2 - GROUP * group - cx) % LANES, 1)
            return jnp.where(lane < LANES // 2, low, high)

        pulled = []
        for j in range(19):
            cx, cy, cz = VELOCITIES[j]
            if cz == 0:
                tile, group = Z_PLACE[("pop", j)]
                pulled.append(both(BELOW + tile, ABOVE + tile, group, cx, cy))
            elif cz == 1:
                pulled.append(both(OWN_LOW, ABOVE + 2, Z_UP.index(j), cx, cy))
            else:
                pulled.append(both(BELOW + 2, OWN_HIGH, Z_DOWN.index(j), cx, cy))
        places = [Z_PLACE[("field", k)] for k in range(5)]
        loaded.append((pulled, [both(BELOW + tile, ABOVE + tile, group, 0, 0) for tile, group in places]))
    done = [
        collide(pulled, 1.0 / rho, rho, ux, uy, uz, kind > 1.5, Z_UP + Z_DOWN)[0]
        for pulled, (rho, ux, uy, uz, kind) in loaded
    ]
    for row, (_, here), after in zip(starts, loaded, done):
        for group in range(5):
            value = jnp.where(lane < LANES // 2, after[Z_DOWN[group]], after[Z_UP[group]])
            z_second[group, pl.ds(8 + row, 8), :] = jnp.where(here[KIND] > 0.5, value, 0.0)


def second_step(refs, second, z_second, change, held, held_sens, planes):
    den, vel, mask = refs
    _, ext_y, _ = mask.shape
    lane = lane_ids()
    every = slice(None)
    loaded = []
    for x, part in itertools.product(planes, range(ext_y // 8)):
        row = 8 + 8 * part
        pulled = []
        for j in range(19):
            cx, cy, cz = VELOCITIES[j]
            rows = pl.ds(row + cy, 8)
            value = second[j, x + 1 + cx, rows, :]
            if cz == 1:
                edge = z_second[Z_UP.index(j), rows, :]
                edge = pltpu.roll(edge, LANES // 2 - 3 - cx - x, 1)
                value = jnp.where(lane == LANES - 1, edge, value)
            elif cz == -1:
                edge = z_second[Z_DOWN.index(j), rows, :]
                edge = pltpu.roll(edge, LANES - 2 - cx - x, 1)
                value = jnp.where(lane == 0, edge, value)
            pulled.append(value)
        at = (x, pl.ds(8 * part, 8), every)
        rho = den[(0, *at)]
        here = [1.0 / rho, rho, vel[(0, 0, *at)], vel[(0, 1, *at)], vel[(0, 2, *at)], mask[at] > 0]
        loaded.append((at, pulled, here, change[0, x + 1, pl.ds(row, 8), :]))
    done = [collide(pulled, *here, range(19)) for _, pulled, here, _ in loaded]
    for (at, _, _, before), (after, gain) in zip(loaded, done):
        for j in range(19):
            held[(j, *at)] = after[j]
        held_sens[at] = before + gain


def side_kernel(slots, den, vel, mask, z_set, *rest):
    many_x, many_y = slots
    from_x, from_y = rest[4 : 4 + many_x], rest[4 + many_x : 4 + many_x + many_y]
    first, fields, second, change, z_first, z_second, shares, y_shares, held, held_sens = rest[-10:]
    _, ext_y, _ = z_set.shape
    ext_x = change.shape[1] - 2
    inner = pl.ds(8, ext_y)
    put = functools.partial(put_row, first, fields)
    z_first[:, inner, :] = z_set[...]

    def place_y(slot, side):
        packet = from_y[slot]
        toward = 2 * side - 1
        near = ext_y if side else -1
        nothing = jnp.zeros((1, LANES), jnp.float32)
        full, ends = side_lines(1, toward)
        for x in range(ext_x):
            for j in pops(1, 0):
                put("pop", j, x, near, nothing)
            for j in pops(1, toward):
                put("pop", j, x, near + toward, nothing)
            put("field", RHO, x, near, jnp.full((1, LANES), jnp.inf, jnp.float32))
            for line, (kind, index) in enumerate(full):
                if kind == "share":
                    y_shares[index, x, near + 8 : near + 9, :] = packet[line, x : x + 1, :]
                else:
                    put(kind, index, x, near, packet[line, x : x + 1, :])
        for spot, (index, depth, end) in enumerate(ends):
            put("pop", index, ext_x - 1 if end else 0, near + toward * depth, packet[SIDE - 1, spot : spot + 1, :])
        start = 8 + ext_y if side else 6
        for tile in range(Z_TILES):
            row = 2 * tile % 8
            z_first[tile, start : start + 2, :] = packet[SIDE + tile // 4, row : row + 2, :]
        if many_y == 1:
            clear_y(1 - side)

    def clear_y(side):
        nothing = jnp.zeros((1, LANES), jnp.float32)
        y = ext_y if side else -1
        for x in range(-2, ext_x + 2):
            for j in pops(1, 2 * side - 1):
                put("pop", j, x, y, nothing)
        for x in range(-1, ext_x + 1):
            put("field", KIND, x, y, nothing)
        start = 8 + ext_y if side else 6
        for tile in range(Z_TILES):
            z_first[tile, start : start + 2, :] = jnp.zeros((2, LANES), jnp.float32)

    def place_x(slot, side):
        packet = from_x[slot]
        toward = 2 * side - 1
        near = ext_x if side else -1
        nothing = jnp.zeros((ext_y, LANES), jnp.float32)
        for j in pops(0, 0):
            first[j, near + 2, inner, :] = nothing
        for j in pops(0, toward):
            first[j, near + toward + 2, inner, :] = nothing
        fields[RHO, near + 1, inner, :] = jnp.full((ext_y, LANES), jnp.inf, jnp.float32)
        full, ends = side_lines(0, toward)
        for line, (kind, index) in enumerate(full):
            if kind == "pop":
                first[index, near + 2, inner, :] = packet[line]
            elif kind == "share":
                shares[side, index, inner, :] = packet[line]
            else:
                fields[index, near + 1, inner, :] = packet[line]
        for spot, (index, depth, end) in enumerate(ends):
            put("pop", index, near + toward * depth, ext_y - 1 if end else 0, packet[SIDE - 1, spot : spot + 1, :])
        for part in range(ext_y // 8):
            place_z(z_first, packet[SIDE, pl.ds(8 * part, 8), :], 8 + 8 * part, 8, side, ext_x)

    shares[:, :, pl.ds(0, 8), :] = jnp.zeros((2, 5, 8, LANES), jnp.float32)
    shares[:, :, pl.ds(8 + ext_y, 8), :] = jnp.zeros((2, 5, 8, LANES), jnp.float32)
    for slot_y in range(many_y):
        on_side(parity_of("gy"), slot_y, functools.partial(place_y, slot_y))
    for slot_x in range(many_x):
        on_side(parity_of("gx"), slot_x, functools.partial(place_x, slot_x))

    starts = range(1, ext_y, 8)
    first_step(first, fields, second, change, [Plane(x, row) for x in (0, ext_x - 1) for row in starts], outside=False)
    first_step(first, fields, second, change, [Plane(x, row) for x in (-1, ext_x) for row in starts], shares=shares)
    z_step(z_first, z_second, range(7, ext_y - 8, 8))
    many = 3 if (ext_x - 2) % 3 == 0 else 1

    @pl.loop(0, (ext_x - 2) // many)
    def _(group):
        tiles = [Rim(many * group + at + 1, ext_y) for at in range(many)]
        first_step(first, fields, second, change, tiles, y_shares=y_shares)

    z_step(z_first, z_second, (-1, ext_y - 1))
    second_step((den, vel, mask), second, z_second, change, held, held_sens, range(2, ext_x - 2))


def last_kernel(slots, den, vel, mask, *rest):
    many_x, many_y = slots
    from_xy = rest[10 : 10 + many_x * many_y]
    out, sens, first, fields, second, change, z_first, z_second, shares, y_shares, held, held_sens, sems = rest[-13:]
    ext_x, ext_y, _ = mask.shape
    lane = lane_ids()
    every = slice(None)
    px, py = parity_of("gx"), parity_of("gy")

    def copies(x):
        return (
            pltpu.make_async_copy(held.at[:, x], out.at[:, x], sems.at[0, x]),
            pltpu.make_async_copy(held_sens.at[x], sens.at[x], sems.at[1, x]),
        )

    for x in range(2, ext_x - 2):
        for copy in copies(x):
            copy.start()

    def place_xy(slot_x, slot_y, side_x, side_y):
        packet = from_xy[many_x * slot_y + slot_x]
        for line, (kind, index, far_x, far_y) in enumerate(edge_lines(2 * side_x - 1, 2 * side_y - 1)):
            x = ext_x + far_x if side_x else -1 - far_x
            y = ext_y + far_y if side_y else -1 - far_y
            put_row(first, fields, kind, index, x, y, packet[line // 8, line % 8 : line % 8 + 1, :])
        place_z(z_first, packet[EDGE // 8], 8 + ext_y if side_y else 6, 2, side_x, ext_x)

    for slot_x in range(many_x):
        for slot_y in range(many_y):
            on_side(
                py,
                slot_y,
                lambda side_y: on_side(px, slot_x, lambda side_x: place_xy(slot_x, slot_y, side_x, side_y)),
            )

    for pair in ((-1, 0), (ext_x - 1, ext_x)):
        tiles = [Rim(x, ext_y) for x in pair]
        first_step(first, fields, second, change, tiles, shares=shares, y_shares=y_shares)

    z_step(z_first, z_second, (-1, ext_y - 1))

    planes = [0, 1, ext_x - 2, ext_x - 1]
    for pair in (planes[:2], planes[2:]):
        second_step((den, vel, mask), second, z_second, change, held, held_sens, pair)
        for x in pair:
            for copy in copies(x):
                copy.start()

    for x in range(ext_x):
        for copy in copies(x):
            copy.wait()


def shards(adjoint, density, velocity, pore_mask):
    ext_x, ext_y, ext_z = pore_mask.shape
    assert ext_z == LANES and ext_y % 8 == 0 and ext_x + 4 <= GROUP and ext_x == 8
    many_x = 2
    many_y, many_z = [1 if lax.axis_size(axis) == 2 else 2 for axis in ("gy", "gz")]
    vmem = pl.BlockSpec(memory_space=pltpu.VMEM)
    hbm = pl.BlockSpec(memory_space=pltpu.HBM)
    inputs = (adjoint, density, velocity, pore_mask)

    def array(*shape):
        return jax.ShapeDtypeStruct(shape, jnp.float32)

    def call(kernel, name, operands, shapes, limit, **more):
        more.setdefault("out_specs", [vmem] * len(shapes))
        more.setdefault("in_specs", [vmem] * len(operands))
        params = pltpu.CompilerParams(vmem_limit_bytes=limit * 1024 * 1024)
        return pl.pallas_call(kernel, out_shape=shapes, compiler_params=params, name=name, **more)(*operands)

    def partners(axis, slot):
        found = {}
        for at in range(slot, lax.axis_size(axis) - 1, 2):
            found[at], found[at + 1] = at + 1, at
        return found

    def ends(axis):
        last = lax.axis_size(axis) - 1
        return {0: last, last: 0}

    def swap(value, spares, *places):
        tables = {axis: partners(axis, slot) for axis, slot in places}
        axes = [axis for axis in ("gx", "gy", "gz") if axis in tables or axis in dict(spares)]
        sizes = [lax.axis_size(axis) for axis in axes]
        pairs = []
        for at in itertools.product(*[range(size) for size in sizes]):
            to = [tables.get(axis, {}).get(spot, spot) for axis, spot in zip(axes, at)]
            for spare, table in spares:
                if tuple(to) == at:
                    to = [table.get(spot, spot) if axis == spare else spot for axis, spot in zip(axes, at)]
            flat = []
            for spots in (at, to):
                index = 0
                for size, spot in zip(sizes, spots):
                    index = index * size + spot
                flat.append(index)
            pairs.append(tuple(flat))
        return lax.ppermute(value, tuple(axes), pairs)

    loaded = [jax.ShapeDtypeStruct(value.shape, value.dtype) for value in inputs]
    *held, near, a_z, b_z = (
        *call(
            functools.partial(pack_z_kernel, many_z),
            "pack_z",
            [pltpu.with_memory_space_constraint(value, pltpu.HBM) for value in inputs],
            loaded + [array(2, ext_y, LANES)] + [array(2, ext_y, LANES)] * many_z,
            8,
            in_specs=[hbm] * 4,
            scratch_shapes=[pltpu.SemaphoreType.DMA((5,))],
        ),
        *[None] * (2 - many_z),
    )
    from_z = [swap(value, [("gx", partners("gx", 0))], ("gz", slot)) for slot, value in enumerate((a_z, b_z)[:many_z])]

    rows = ext_y + 16
    adj, den, vel, mask = held
    shapes = (
        [array(19, ext_x + 4, rows, LANES)]
        + [array(SIDE + 1, ext_y, LANES)] * many_x
        + [array(FACE, ext_x, LANES)] * many_y
        + [array(EDGE // 8 + 1, 8, LANES)] * (many_x * many_y)
    )
    shifted = call(
        functools.partial(shift_kernel, (many_x, many_y)),
        "shift",
        (adj, den, vel, mask),
        shapes,
        8,
        cost_estimate=pl.CostEstimate(flops=1_000_000, bytes_accessed=2_500_000, transcendentals=0),
    )
    z_set, first, *packets = call(
        functools.partial(pack_xy_kernel, (many_x, many_y, many_z)),
        "pack_xy",
        (den, vel, mask, near, *from_z, *shifted),
        [array(Z_TILES, ext_y, LANES)] + shapes + [array(SIDE + 2, ext_x, LANES)] * many_y,
        8,
        input_output_aliases={4 + many_z + at: 1 + at for at in range(len(shapes))},
        scratch_shapes=[
            pltpu.VMEM((2, ext_y, LANES), jnp.float32),
            pltpu.VMEM((2, 5, ext_y, LANES), jnp.float32),
        ],
    )
    to_x, to_xy, to_y = packets[:many_x], packets[many_x + many_y : -many_y], packets[-many_y:]
    from_xy = [
        swap(to_xy[many_x * slot_y + slot_x], [], ("gx", slot_x), ("gy", slot_y))
        for slot_y in range(many_y)
        for slot_x in range(many_x)
    ]
    from_y = [swap(value, [("gz", partners("gz", 0))], ("gy", slot)) for slot, value in enumerate(to_y)]
    spares = [("gx", ends("gx"))]
    if lax.axis_size("gz") > 2:
        top = lax.axis_size("gz") - 1
        spares = [("gz", {top - 1: top, top: top - 1})] + spares
    from_x = [swap(value, spares, ("gx", slot)) for slot, value in enumerate(to_x)]

    fields, second, change = call(
        inner_kernel,
        "inner_step",
        (den, vel, mask, first),
        [array(5, ext_x + 2, rows, LANES), array(19, ext_x + 2, rows, LANES), array(1, ext_x + 2, rows, LANES)],
        8,
        cost_estimate=pl.CostEstimate(flops=40_000_000, bytes_accessed=8_000_000, transcendentals=0),
    )
    inout = (first, fields, second, change)
    inout = call(
        functools.partial(side_kernel, (many_x, many_y)),
        "side_step",
        (den, vel, mask, z_set, *inout, *from_x, *from_y),
        [array(*value.shape) for value in inout] + [array(Z_TILES, rows, LANES), array(5, rows, LANES), array(2, 5, rows, LANES), array(5, ext_x, rows, LANES)]
        + [array(19, ext_x, ext_y, LANES), array(ext_x, ext_y, LANES)],
        8,
        input_output_aliases={4 + at: at for at in range(4)},
        cost_estimate=pl.CostEstimate(flops=40_000_000, bytes_accessed=8_000_000, transcendentals=0),
    )
    return call(
        functools.partial(last_kernel, (many_x, many_y)),
        "last_steps",
        (den, vel, mask, *inout, *from_xy),
        [array(19, ext_x, ext_y, LANES), array(ext_x, ext_y, LANES)] + [array(*value.shape) for value in inout],
        8,
        out_specs=[hbm] * 2 + [vmem] * 10,
        input_output_aliases={3 + at: 2 + at for at in range(10)},
        scratch_shapes=[pltpu.SemaphoreType.DMA((2, ext_x))],
    )[:2]


def solution(mesh):
    placed = (
        P(None, "gx", "gy", "gz"),
        P(None, "gx", "gy", "gz"),
        P(None, None, "gx", "gy", "gz"),
        P("gx", "gy", "gz"),
    )

    def whole(*arrays):
        return tuple(shards(*arrays))

    return jax.shard_map(
        whole,
        mesh=mesh,
        in_specs=placed,
        out_specs=(P(None, "gx", "gy", "gz"), P("gx", "gy", "gz")),
        check_vma=False,
    )
```
